32 devices in a mesh: dp: 8 (over y, x, core), sp: 4 (over z).
Axes of the slice: x: 2, y: 2, z: 4, core: 2. Of those that a mesh axis runs over, the one named last changes fastest.
Arguments:
- tokens: bfloat16 [8, 4096, 768], P('dp', 'sp'), may hold values from -6 to 6
- qkv_weight: bfloat16 [768, 2304], P(('dp', 'sp')), may hold values from -0.21875 to 0.21875
- query_value_bias: bfloat16 [2, 768], P(None, ('dp', 'sp')), may hold values from -3 to 3
- out_weight: bfloat16 [768, 768], P(('dp', 'sp')), may hold values from -1.75 to 1.75
- out_bias: bfloat16 [768], P(('dp', 'sp')), may hold values from -3 to 3
- norm1_gain: bfloat16 [768], P(('dp', 'sp')), may hold values from 0.099609375 to 1.8984375
- norm1_bias: bfloat16 [768], P(('dp', 'sp')), may hold values from -3 to 3
- up_weight: bfloat16 [768, 3072], P(('dp', 'sp')), may hold values from -0.21875 to 0.21875
- up_bias: bfloat16 [3072], P(('dp', 'sp')), may hold values from -3 to 3
- down_weight: bfloat16 [3072, 768], P(('dp', 'sp')), may hold values from -0.109375 to 0.109375
- down_bias: bfloat16 [768], P(('dp', 'sp')), may hold values from -3 to 3
- norm2_gain: bfloat16 [768], P(('dp', 'sp')), may hold values from 0.099609375 to 1.8984375
- norm2_bias: bfloat16 [768], P(('dp', 'sp')), may hold values from -3 to 3
- rand_blocks: int32 [8, 12, 62, 3], P('dp', 'sp'), may hold values from 1 to 62, as said below
- out_grad: bfloat16 [8, 4096, 768], P('dp', 'sp'), may hold values from -6 to 6
Outputs:
- layer_out: bfloat16 [8, 4096, 768], P('dp', 'sp')
- input_grad: float32 [8, 4096, 768], P('dp', 'sp')
- qkv_weight_grad: float32 [768, 2304], P(('dp', 'sp'))
- query_value_bias_grad: float32 [2, 768], P(None, ('dp', 'sp'))
- out_weight_grad: float32 [768, 768], P(('dp', 'sp'))
- out_bias_grad: float32 [768], P(('dp', 'sp'))
- norm1_gain_grad: float32 [768], P(('dp', 'sp'))
- norm1_bias_grad: float32 [768], P(('dp', 'sp'))
- up_weight_grad: float32 [768, 3072], P(('dp', 'sp'))
- up_bias_grad: float32 [3072], P(('dp', 'sp'))
- down_weight_grad: float32 [3072, 768], P(('dp', 'sp'))
- down_bias_grad: float32 [768], P(('dp', 'sp'))
- norm2_gain_grad: float32 [768], P(('dp', 'sp'))
- norm2_bias_grad: float32 [768], P(('dp', 'sp'))
The draws below stay inside these ranges and needn't reach their ends.
Inputs may be any that keep to these rules, and one draw needn't show every extreme that they name: For middle query block i, the 3 entries of rand_blocks[b, h, i - 1] are distinct and none of them is i - 1, i, i + 1, 0 or 63.
All inputs are finite; a program needn't handle non-finite values.
Results may differ from the reference program's by a relative error of at most 0.013.
Values may be sent and summed in bfloat16 or wider, within the bound.
A program may use at most 256 MiB of HBM per device.

```python
import jax
import jax.numpy as jnp
from jax import lax

D = 768
HEADS = 12
HEAD_DIM = 64
FF = 3072
BLOCK = 64
RANDOM = 3
LEN = 4096
NB = 64
BATCH = 8


def draw_rand_blocks(key, part):
    query_rows = jnp.arange(1, NB - 1, dtype=jnp.int32)[:, None]
    columns = jnp.arange(NB, dtype=jnp.int32)[None, :]
    banned = (columns == 0) | (columns == NB - 1) | (jnp.abs(columns - query_rows) <= 1)
    ranks = jax.random.randint(key, (BATCH, HEADS, NB - 2, NB), 0, 1 << 20, dtype=jnp.int32) * NB + columns
    ranks = jnp.where(banned, jnp.full_like(ranks, -1), ranks)
    values, picks = lax.top_k(ranks, RANDOM)
    return picks.astype(jnp.int32)


def levels(own_key, extent, shards, least, high):
    level, own = 1.0, jax.random.fold_in(own_key, 6)
    for dim, parts in shards:
        steps = jnp.exp(jax.random.uniform(jax.random.fold_in(own, dim), (parts,), jnp.float32, least / len(shards), high / len(shards)))
        level = level * jnp.repeat(steps, extent[dim] // parts).reshape([-1 if axis == dim else 1 for axis in range(len(extent))])
    return level


def bell_draw(rng, extent, spread, bound, shards=(), kind=jnp.bfloat16):
    values = spread * jax.random.normal(rng, extent, jnp.float32)
    if shards:
        values = values * levels(rng, extent, shards, -0.22, 0.18)
    return jnp.clip(values, -bound, bound).astype(kind)


def setup_inputs(seed: int = 0) -> dict:
    key_of = jax.random.split(jax.random.key(seed), 16)
    return {
        "tokens": bell_draw(key_of[0], (BATCH, LEN, D), 1.0, 6.0, ((0, 8), (1, 4))),
        "qkv_weight": bell_draw(key_of[1], (D, 3 * D), D ** -0.5, 0.21875, ((0, 32),)),
        "query_value_bias": bell_draw(key_of[2], (2, D), 0.5, 3.0, ((1, 32),)),
        "out_weight": bell_draw(key_of[3], (D, D), (D // 64) ** -0.5, 1.75, ((0, 32),)),
        "out_bias": bell_draw(key_of[4], (D,), 0.5, 3.0, ((0, 32),)),
        "norm1_gain": jnp.clip(1.0 + 0.18 * jax.random.normal(key_of[5], (D,), jnp.float32), 0.099609375, 1.8984375).astype(jnp.bfloat16),
        "norm1_bias": bell_draw(key_of[6], (D,), 0.5, 3.0, ((0, 32),)),
        "up_weight": bell_draw(key_of[7], (D, FF), D ** -0.5, 0.21875, ((0, 32),)),
        "up_bias": bell_draw(key_of[8], (FF,), 0.5, 3.0, ((0, 32),)),
        "down_weight": bell_draw(key_of[9], (FF, D), FF ** -0.5, 0.109375, ((0, 32),)),
        "down_bias": bell_draw(key_of[10], (D,), 0.5, 3.0, ((0, 32),)),
        "norm2_gain": jnp.clip(1.0 + 0.18 * jax.random.normal(key_of[11], (D,), jnp.float32), 0.099609375, 1.8984375).astype(jnp.bfloat16),
        "norm2_bias": bell_draw(key_of[12], (D,), 0.5, 3.0, ((0, 32),)),
        "rand_blocks": draw_rand_blocks(jax.random.fold_in(key_of[15], 71), 0),
        "out_grad": bell_draw(key_of[14], (BATCH, LEN, D), 1.0, 6.0, ((0, 8), (1, 4))),
    }


@jax.custom_vjp
def reduced_precision_cast(v):
    return lax.optimization_barrier(v.astype(jnp.bfloat16)).astype(jnp.float32)

@jax.custom_vjp
def reduced_precision_gradient(v):
    return v

def low_keep(v):
    return (reduced_precision_cast(v), None)

def low_pass(kept, grad):
    return (grad,)

def back_keep(v):
    return (v, None)

def back_low(kept, grad):
    return (reduced_precision_cast(grad),)
reduced_precision_cast.defvjp(low_keep, low_pass)
reduced_precision_gradient.defvjp(back_keep, back_low)
highest_precision_mode = lax.Precision.HIGHEST
norm_eps = 1e-05
masked_score = -1e+30

def key_table(rand_head, blocks):
    position = jnp.arange(blocks, dtype=jnp.int32)
    window = jnp.stack([jnp.maximum(position - 1, 0), position, jnp.minimum(position + 1, blocks - 1)], axis=1)
    global_cols = jnp.stack([jnp.zeros_like(position), jnp.full_like(position, blocks - 1)], axis=1)
    padding = jnp.zeros((1, rand_head.shape[1]), jnp.int32)
    random_cols = jnp.concatenate([padding, rand_head.astype(jnp.int32), padding], axis=0)
    return jnp.concatenate([window, global_cols, random_cols], axis=1)

def duplicate_mask(blocks, slots):
    position = jnp.arange(blocks, dtype=jnp.int32)[:, None]
    column = jnp.arange(slots, dtype=jnp.int32)[None, :]
    return (position == 1) & (column == 3) | (position == blocks - 2) & (column == 4)

def head_attention(queries, keys_in, values_in, rand_head):
    blocks = LEN // BLOCK
    score_scale_factor = HEAD_DIM ** (-0.5)
    table_full = key_table(rand_head, blocks)
    table_mid = table_full[1:-1]
    mask_mid = jnp.repeat(duplicate_mask(blocks, table_full.shape[1])[1:-1], BLOCK, axis=1)[:, None, :]
    blocked_query_rows = queries.reshape(blocks, BLOCK, HEAD_DIM)
    key_blocks = keys_in.reshape(blocks, BLOCK, HEAD_DIM)
    value_blocks = values_in.reshape(blocks, BLOCK, HEAD_DIM)
    selected_key_blocks = key_blocks[table_mid].reshape(blocks - 2, -1, HEAD_DIM)
    selected_value_blocks = value_blocks[table_mid].reshape(blocks - 2, -1, HEAD_DIM)
    middle_unscaled_scores = reduced_precision_gradient(score_scale_factor * jnp.einsum('gjf,gcf->gjc', blocked_query_rows[1:-1], selected_key_blocks, precision=highest_precision_mode))
    mid_scores = jnp.where(mask_mid, jnp.full_like(middle_unscaled_scores, masked_score), middle_unscaled_scores)
    middle_attention_probs = jnp.exp(mid_scores - jax.nn.logsumexp(mid_scores, axis=2, keepdims=True))
    middle_context_output = jnp.einsum('xah,xho->xao', reduced_precision_cast(middle_attention_probs), selected_value_blocks, precision=highest_precision_mode)
    global_rows = jnp.concatenate([blocked_query_rows[0], blocked_query_rows[-1]], axis=0)
    glob_scores = reduced_precision_gradient(score_scale_factor * jnp.dot(global_rows, keys_in.T, precision=highest_precision_mode))
    glob_probs = jnp.exp(glob_scores - jax.nn.logsumexp(glob_scores, axis=1, keepdims=True))
    glob_out = jnp.dot(reduced_precision_cast(glob_probs), values_in, precision=highest_precision_mode)
    return jnp.concatenate([glob_out[:BLOCK], middle_context_output.reshape(-1, HEAD_DIM), glob_out[BLOCK:]], axis=0)

def layer_norm(resid, gain, shift):
    center = resid - lax.optimization_barrier(jnp.mean(resid, axis=1, keepdims=True))
    rstd = lax.rsqrt(lax.optimization_barrier(jnp.mean(center * center, axis=1, keepdims=True)) + norm_eps)
    return center * rstd * gain + shift

def layer(inputs, qkv_weight, query_value_bias, out_weight, out_bias, norm1_gain, norm1_bias, up_weight, up_bias, down_weight, down_bias, norm2_gain, norm2_bias, rand_seq):
    bias_cols = jnp.concatenate([query_value_bias[0], jnp.zeros((D,), jnp.float32), query_value_bias[1]])
    raw = jnp.dot(inputs, qkv_weight, precision=highest_precision_mode) + bias_cols
    packed = reduced_precision_cast(reduced_precision_gradient(raw)).reshape(LEN, 3, HEADS, HEAD_DIM)
    queries = jnp.transpose(packed[:, 0], (1, 0, 2))
    keys_in = jnp.transpose(packed[:, 1], (1, 0, 2))
    values_in = jnp.transpose(packed[:, 2], (1, 0, 2))
    attend = jax.checkpoint(head_attention)
    heads_out = lax.map(lambda operands: attend(*operands), (queries, keys_in, values_in, rand_seq))
    context = reduced_precision_cast(reduced_precision_gradient(jnp.transpose(heads_out, (1, 0, 2)).reshape(LEN, D)))
    attn_proj = reduced_precision_gradient(jnp.dot(context, out_weight, precision=highest_precision_mode) + out_bias)
    hidden1 = layer_norm(inputs + attn_proj, norm1_gain, norm1_bias)
    pre = reduced_precision_gradient(jnp.dot(reduced_precision_cast(hidden1), up_weight, precision=highest_precision_mode) + up_bias)
    act = reduced_precision_cast(jax.nn.gelu(pre, approximate=True))
    ffn_out = reduced_precision_gradient(jnp.dot(act, down_weight, precision=highest_precision_mode) + down_bias)
    return layer_norm(hidden1 + ffn_out, norm2_gain, norm2_bias)

def reference(tokens, qkv_weight, query_value_bias, out_weight, out_bias, norm1_gain, norm1_bias, up_weight, up_bias, down_weight, down_bias, norm2_gain, norm2_bias, rand_blocks, out_grad):
    params = tuple((p.astype(jnp.float32) for p in (qkv_weight, query_value_bias, out_weight, out_bias, norm1_gain, norm1_bias, up_weight, up_bias, down_weight, down_bias, norm2_gain, norm2_bias)))

    def one_sequence(running, item):
        seq_tokens, rand_seq, seq_cot = item

        def forward(inputs, *weights):
            return layer(inputs, *weights, rand_seq)
        result, pullback = jax.vjp(forward, seq_tokens.astype(jnp.float32), *params)
        grads = pullback(seq_cot.astype(jnp.float32))
        running = tuple((acc + grad for acc, grad in zip(running, grads[1:])))
        return (running, (result.astype(jnp.bfloat16), grads[0]))
    start = tuple((jnp.zeros_like(p) for p in params))
    totals, (outputs, input_grads) = lax.scan(one_sequence, start, (tokens, rand_blocks, out_grad))
    return (outputs, input_grads, totals[0], totals[1], totals[2], totals[3], totals[4], totals[5], totals[6], totals[7], totals[8], totals[9], totals[10], totals[11])
```

```python
from functools import partial

import jax
import jax.numpy as jnp
import numpy as np
from jax import lax
from jax.experimental import pallas as pl
from jax.experimental.pallas import tpu as pltpu
from jax.sharding import Mesh
from jax.sharding import PartitionSpec as P

HEAD_DIM = 64
BLOCK = 64
LANES = 128
SLOT = 4 * HEAD_DIM
EPS = 1e-05
MASKED = -1e30
ALL = ("c", "core", "zh", "zl")
GROUP = ("core", "zl")
REST = ("c", "zh")
CHUNK = 512
ROWS = 256
VMEM_BYTES = 60 * 1024 * 1024

f32 = jnp.float32
bf16 = jnp.bfloat16
NT = (((1,), (1,)), ((), ()))
TN = (((0,), (0,)), ((), ()))


def dot(a, b):
    return jnp.dot(a, b, preferred_element_type=f32)


def dot_nt(a, b):
    return lax.dot_general(a, b, NT, preferred_element_type=f32)


def dot_tn(a, b):
    return lax.dot_general(a, b, TN, preferred_element_type=f32)


def rows_at(start, size):
    return pl.ds(pl.multiple_of(start, size), size)


def listed(ref, rand_ref, head, i, blocks, randoms, cols):
    parts = [
        ref[0:BLOCK, cols],
        ref[(blocks - 1) * BLOCK : blocks * BLOCK, cols],
        ref[pl.ds(pl.multiple_of((i - 1) * BLOCK, BLOCK), 3 * BLOCK), cols],
    ]
    base = (head * (blocks - 2) + i - 1) * randoms
    for r in range(randoms):
        parts.append(ref[rows_at(rand_ref[base + r] * BLOCK, BLOCK), cols])
    return jnp.concatenate(parts, axis=0)


def mask_globals(s, i, blocks):
    lane = lax.broadcasted_iota(jnp.int32, (BLOCK, LANES), 1)
    low = lane < BLOCK
    dead = (low & (i == 1)) | (~low & (i == blocks - 2))
    return jnp.concatenate([jnp.where(dead, MASKED, s[:, :LANES]), s[:, LANES:]], axis=1)


def attend_kernel(heads, randoms, rand_ref, x_ref, w_ref, b_ref, qkv_ref, res_ref, ctx_ref):
    length = x_ref.shape[0]
    blocks = length // BLOCK
    last = (blocks - 1) * BLOCK

    def project(t, carry):
        rows = rows_at(t * CHUNK, CHUNK)
        qkv_ref[rows, :] = (dot(x_ref[rows, :], w_ref[...]) + b_ref[...]).astype(bf16)
        return carry

    lax.fori_loop(0, length // CHUNK, project, 0)

    def middle(i, carry):
        rows = rows_at(i * BLOCK, BLOCK)
        lane = lax.broadcasted_iota(jnp.int32, (BLOCK, LANES), 1)
        for h in range(heads):
            at = h * SLOT
            kv = listed(qkv_ref, rand_ref, h, i, blocks, randoms, slice(at + LANES, at + SLOT))
            s = mask_globals(dot_nt(qkv_ref[rows, at : at + LANES], kv), i, blocks)
            top = jnp.max(s, axis=1, keepdims=True)
            e = jnp.exp(s - top)
            total = jnp.sum(e, axis=1, keepdims=True)
            o = dot(e.astype(bf16), kv) / total
            res_ref[h, rows, :] = jnp.where(lane < HEAD_DIM, top + jnp.log(total), o)
        return carry

    lax.fori_loop(1, blocks - 1, middle, 0)

    for h in range(heads):
        at = h * SLOT
        q = jnp.concatenate(
            [qkv_ref[0:BLOCK, at : at + LANES], qkv_ref[last : last + BLOCK, at : at + LANES]], axis=0
        )

        def whole(t, carry, at=at, q=q):
            top, total, acc = carry
            kv = qkv_ref[rows_at(t * CHUNK, CHUNK), at + LANES : at + SLOT]
            s = dot_nt(q, kv)
            new = jnp.maximum(top, jnp.max(s, axis=1, keepdims=True))
            fade = jnp.exp(top - new)
            e = jnp.exp(s - new)
            total = total * fade + jnp.sum(e, axis=1, keepdims=True)
            return new, total, acc * fade + dot(e.astype(bf16), kv)

        top, total, acc = lax.fori_loop(
            0,
            length // CHUNK,
            whole,
            (
                jnp.full((2 * BLOCK, 1), MASKED, f32),
                jnp.zeros((2 * BLOCK, 1), f32),
                jnp.zeros((2 * BLOCK, LANES), f32),
            ),
        )
        lane = lax.broadcasted_iota(jnp.int32, (2 * BLOCK, LANES), 1)
        both = jnp.where(lane < HEAD_DIM, top + jnp.log(total), acc / total)
        res_ref[h, 0:BLOCK, :] = both[:BLOCK]
        res_ref[h, last : last + BLOCK, :] = both[BLOCK:]

    per_quarter = ctx_ref.shape[1]

    def pack(t, carry):
        part, piece = t // per_quarter, t % per_quarter
        lane = lax.broadcasted_iota(jnp.int32, (BLOCK, LANES), 1)
        low = lane < HEAD_DIM
        for n in range(ROWS // BLOCK):
            rows = rows_at(t * ROWS + n * BLOCK, BLOCK)
            first = pltpu.roll(res_ref[0, rows, :], HEAD_DIM, 1)
            pair = jnp.where(low, first, res_ref[1, rows, :])
            ctx_ref[part, piece, n * BLOCK : (n + 1) * BLOCK, :] = pair.astype(bf16)
        for n in range(ROWS // (2 * BLOCK)):
            rows = rows_at(t * ROWS + 2 * n * BLOCK, BLOCK)
            odd = rows_at(t * ROWS + (2 * n + 1) * BLOCK, BLOCK)
            first = pltpu.roll(res_ref[2, rows, :], HEAD_DIM, 1)
            both = jnp.where(low, first, res_ref[2, odd, :])
            ctx_ref[part, piece, ROWS + n * BLOCK : ROWS + (n + 1) * BLOCK, :] = both.astype(bf16)
        return carry

    lax.fori_loop(0, length // ROWS, pack, 0)


def attend(rand, x, w, b, parts, heads):
    length = x.shape[0]
    randoms = rand.size // (heads * (length // BLOCK - 2))
    vmem = pl.BlockSpec(memory_space=pltpu.VMEM)
    return pl.pallas_call(
        partial(attend_kernel, heads, randoms),
        out_shape=(
            jax.ShapeDtypeStruct((length, heads * SLOT), bf16),
            jax.ShapeDtypeStruct((heads, length, LANES), f32),
            jax.ShapeDtypeStruct((parts, length // parts // ROWS, ROWS * 3 // 2, LANES), bf16),
        ),
        in_specs=[pl.BlockSpec(memory_space=pltpu.SMEM), vmem, vmem, vmem],
        out_specs=(vmem, vmem, vmem),
        compiler_params=pltpu.CompilerParams(vmem_limit_bytes=VMEM_BYTES),
        name="attend",
    )(rand, x, w, b)


def attend_back_kernel(
    heads, randoms, rand_ref, qkv_ref, res_ref, dctx_ref, draw_ref, sums_ref, *scratch
):
    dout, acc = scratch[:heads], scratch[heads:]
    length = qkv_ref.shape[0]
    blocks = length // BLOCK
    last = (blocks - 1) * BLOCK
    per_quarter = dctx_ref.shape[1]

    def unpack(t, carry):
        part, piece = t // per_quarter, t % per_quarter
        lane = lax.broadcasted_iota(jnp.int32, (BLOCK, LANES), 1)
        low = lane < HEAD_DIM
        for n in range(ROWS // BLOCK):
            rows = rows_at(t * ROWS + n * BLOCK, BLOCK)
            pair = dctx_ref[part, piece, n * BLOCK : (n + 1) * BLOCK, :].astype(f32)
            dout[0][rows, :] = jnp.where(low, 0.0, pltpu.roll(pair, HEAD_DIM, 1)).astype(bf16)
            dout[1][rows, :] = jnp.where(low, 0.0, pair).astype(bf16)
        for n in range(ROWS // (2 * BLOCK)):
            rows = rows_at(t * ROWS + 2 * n * BLOCK, BLOCK)
            odd = rows_at(t * ROWS + (2 * n + 1) * BLOCK, BLOCK)
            both = dctx_ref[part, piece, ROWS + n * BLOCK : ROWS + (n + 1) * BLOCK, :].astype(f32)
            dout[2][rows, :] = jnp.where(low, 0.0, pltpu.roll(both, HEAD_DIM, 1)).astype(bf16)
            dout[2][odd, :] = jnp.where(low, 0.0, both).astype(bf16)
        return carry

    lax.fori_loop(0, length // ROWS, unpack, 0)

    step = 256
    for h in range(heads):
        at = h * SLOT
        q = jnp.concatenate(
            [qkv_ref[0:BLOCK, at : at + LANES], qkv_ref[last : last + BLOCK, at : at + LANES]], axis=0
        )
        g = jnp.concatenate([dout[h][0:BLOCK, :], dout[h][last : last + BLOCK, :]], axis=0)
        res = jnp.concatenate([res_ref[h, 0:BLOCK, :], res_ref[h, last : last + BLOCK, :]], axis=0)
        log_total = res[:, 0:1]
        delta = jnp.sum(g.astype(f32) * res, axis=1, keepdims=True)
        both = jnp.concatenate([q, g], axis=0)

        def whole(t, dq, at=at, h=h, both=both, log_total=log_total, delta=delta):
            rows = rows_at(t * step, step)
            kv = qkv_ref[rows, at + LANES : at + SLOT]
            sd = dot_nt(both, kv)
            p = jnp.exp(sd[: 2 * BLOCK] - log_total)
            ds = (p * (sd[2 * BLOCK :] - delta)).astype(bf16)
            acc[h][rows, :] = dot_tn(jnp.concatenate([ds, p.astype(bf16)], axis=0), both)
            return dq + dot(ds, kv)

        dq = lax.fori_loop(0, length // step, whole, jnp.zeros((2 * BLOCK, LANES), f32))
        lane = lax.broadcasted_iota(jnp.int32, (2 * BLOCK, LANES), 1)
        dq = jnp.where(lane < HEAD_DIM, dq, 0.0).astype(bf16)
        draw_ref[0:BLOCK, at : at + LANES] = dq[:BLOCK]
        draw_ref[last : last + BLOCK, at : at + LANES] = dq[BLOCK:]

    def middle(i, carry):
        rows = rows_at(i * BLOCK, BLOCK)
        lane = lax.broadcasted_iota(jnp.int32, (BLOCK, LANES), 1)
        for h in range(heads):
            at = h * SLOT
            kv = listed(qkv_ref, rand_ref, h, i, blocks, randoms, slice(at + LANES, at + SLOT))
            g = dout[h][rows, :]
            res = res_ref[h, rows, :]
            both = jnp.concatenate([qkv_ref[rows, at : at + LANES], g], axis=0)
            delta = jnp.sum(g.astype(f32) * res, axis=1, keepdims=True)
            sd = dot_nt(both, kv)
            p = jnp.exp(mask_globals(sd[:BLOCK], i, blocks) - res[:, 0:1])
            ds = (p * (sd[BLOCK:] - delta)).astype(bf16)
            dkv = dot_tn(jnp.concatenate([ds, p.astype(bf16)], axis=0), both)
            dq = dot(ds, kv)
            draw_ref[rows, at : at + LANES] = jnp.where(lane < HEAD_DIM, dq, 0.0).astype(bf16)
            acc[h][0:BLOCK, :] += dkv[0:BLOCK]
            acc[h][last : last + BLOCK, :] += dkv[BLOCK : 2 * BLOCK]
            near = pl.ds(pl.multiple_of((i - 1) * BLOCK, BLOCK), 3 * BLOCK)
            acc[h][near, :] += dkv[2 * BLOCK : 5 * BLOCK]
            base = (h * (blocks - 2) + i - 1) * randoms
            for r in range(randoms):
                far = rows_at(rand_ref[base + r] * BLOCK, BLOCK)
                acc[h][far, :] += dkv[(5 + r) * BLOCK : (6 + r) * BLOCK]
        return carry

    lax.fori_loop(1, blocks - 1, middle, 0)
    sums_ref[...] = jnp.zeros_like(sums_ref)

    def finish(t, carry):
        rows = rows_at(t * CHUNK, CHUNK)
        for h in range(heads):
            at = h * SLOT
            draw_ref[rows, at + LANES : at + SLOT] = acc[h][rows, :].astype(bf16)
        sums_ref[0:1, :] += jnp.sum(draw_ref[rows, :].astype(f32), axis=0, keepdims=True)
        return carry

    lax.fori_loop(0, length // CHUNK, finish, 0)


def attend_back(rand, qkv, res, dctx, heads):
    length = qkv.shape[0]
    randoms = rand.size // (heads * (length // BLOCK - 2))
    vmem = pl.BlockSpec(memory_space=pltpu.VMEM)
    return pl.pallas_call(
        partial(attend_back_kernel, heads, randoms),
        out_shape=(
            jax.ShapeDtypeStruct((length, heads * SLOT), bf16),
            jax.ShapeDtypeStruct((8, heads * SLOT), f32),
        ),
        in_specs=[pl.BlockSpec(memory_space=pltpu.SMEM), vmem, vmem, vmem],
        out_specs=(vmem, vmem),
        scratch_shapes=[pltpu.VMEM((length, LANES), bf16)] * heads
        + [pltpu.VMEM((length, LANES), f32)] * heads,
        compiler_params=pltpu.CompilerParams(vmem_limit_bytes=VMEM_BYTES),
        name="attend_back",
    )(rand, qkv, res, dctx)


def mean_of(a):
    return jnp.mean(a, axis=1, keepdims=True)


def norm(r):
    center = r - mean_of(r)
    rstd = lax.rsqrt(mean_of(center * center) + EPS)
    return center * rstd, rstd


def norm_back(dn, n, rstd):
    return rstd * (dn - mean_of(dn) - n * mean_of(dn * n))


def rowsum(a):
    return jnp.sum(a, axis=0, keepdims=True)


def chain_kernel(
    groups,
    ctx_ref,
    tok_ref,
    og_ref,
    wo_ref,
    wu_ref,
    wd_ref,
    vec_ref,
    bu_ref,
    out_ref,
    dres_ref,
    dctx_ref,
    mix_ref,
    hid_ref,
    act_ref,
    dpre_ref,
    dffn_ref,
    dproj_ref,
    gvec_ref,
    gbu_ref,
    slope_ref,
    wop_ref,
):
    width = tok_ref.shape[1]
    hidden = wu_ref.shape[1]
    wide = 3 * HEAD_DIM
    step = pl.program_id(0)

    @pl.when(step == 0)
    def _():
        for g in range(groups):
            wop_ref[g * LANES : (g + 1) * LANES, :] = wo_ref[g * wide : g * wide + LANES, :]
            to = groups * LANES + g * HEAD_DIM
            wop_ref[to : to + HEAD_DIM, :] = wo_ref[g * wide + LANES : (g + 1) * wide, :]
        gvec_ref[...] = jnp.zeros_like(gvec_ref)
        gbu_ref[...] = jnp.zeros_like(gbu_ref)

    low = lax.broadcasted_iota(jnp.int32, (BLOCK, LANES), 1) < HEAD_DIM
    for g in range(groups):
        mix_ref[:, g * LANES : (g + 1) * LANES] = ctx_ref[g, 0, :ROWS, :]
    for g in range(0, groups, 2):
        to = groups * LANES + g * HEAD_DIM
        for n in range(ROWS // (2 * BLOCK)):
            at = ROWS + n * BLOCK
            a = ctx_ref[g, 0, at : at + BLOCK, :].astype(f32)
            b = ctx_ref[g + 1, 0, at : at + BLOCK, :].astype(f32)
            even = jnp.where(low, a, pltpu.roll(b, HEAD_DIM, 1))
            odd = jnp.where(low, pltpu.roll(a, HEAD_DIM, 1), b)
            r = 2 * n * BLOCK
            mix_ref[r : r + BLOCK, to : to + LANES] = even.astype(bf16)
            mix_ref[r + BLOCK : r + 2 * BLOCK, to : to + LANES] = odd.astype(bf16)

    bo, g1, s1 = vec_ref[0:1, :], vec_ref[1:2, :], vec_ref[2:3, :]
    bd, g2, s2 = vec_ref[3:4, :], vec_ref[4:5, :], vec_ref[5:6, :]
    n1, rstd1 = norm(tok_ref[...].astype(f32) + dot(mix_ref[...], wop_ref[...]) + bo)
    hid = n1 * g1 + s1
    hid_low = hid.astype(bf16)
    hid_ref[...] = hid_low
    scale = np.sqrt(2.0 / np.pi).astype(np.float32)

    def up(f, carry):
        cols = rows_at(f * CHUNK, CHUNK)
        u = dot(hid_low, wu_ref[:, cols]) + bu_ref[:, cols]
        square = u * u
        t = jnp.tanh(scale * (u + 0.044715 * (u * square)))
        half = 0.5 * (1.0 + t)
        act_ref[:, cols] = (u * half).astype(bf16)
        slope = half + 0.5 * u * (1.0 - t * t) * (scale * (1.0 + (3 * 0.044715) * square))
        slope_ref[:, cols] = slope.astype(bf16)
        return carry

    lax.fori_loop(0, hidden // CHUNK, up, 0)
    n2, rstd2 = norm(hid + dot(act_ref[...], wd_ref[...]) + bd)
    out_ref[...] = (n2 * g2 + s2).astype(bf16)
    og = og_ref[...].astype(f32)
    gvec_ref[4:5, :] += rowsum(og * n2)
    gvec_ref[5:6, :] += rowsum(og)
    dres2 = norm_back(og * g2, n2, rstd2)
    dffn = dres2.astype(bf16)
    dffn_ref[...] = dffn
    gvec_ref[3:4, :] += rowsum(dffn.astype(f32))

    def down_back(f, carry):
        cols = rows_at(f * CHUNK, CHUNK)
        dact = dot_nt(dffn, wd_ref[cols, :])
        dpre = (dact * slope_ref[:, cols].astype(f32)).astype(bf16)
        dpre_ref[:, cols] = dpre
        gbu_ref[0:1, cols] += rowsum(dpre.astype(f32))
        return carry

    lax.fori_loop(0, hidden // CHUNK, down_back, 0)
    dh = dres2 + dot_nt(dpre_ref[...], wu_ref[...])
    gvec_ref[1:2, :] += rowsum(dh * n1)
    gvec_ref[2:3, :] += rowsum(dh)
    dres1 = norm_back(dh * g1, n1, rstd1)
    dres_ref[...] = dres1
    dproj = dres1.astype(bf16)
    dproj_ref[...] = dproj
    gvec_ref[0:1, :] += rowsum(dproj.astype(f32))
    dmix = dot_nt(dproj, wop_ref[...])
    for g in range(groups):
        dctx_ref[g, 0, :ROWS, :] = dmix[:, g * LANES : (g + 1) * LANES].astype(bf16)
    for g in range(0, groups, 2):
        to = groups * LANES + g * HEAD_DIM
        for n in range(ROWS // (2 * BLOCK)):
            at = ROWS + n * BLOCK
            r = 2 * n * BLOCK
            even = dmix[r : r + BLOCK, to : to + LANES]
            odd = dmix[r + BLOCK : r + 2 * BLOCK, to : to + LANES]
            a = jnp.where(low, even, pltpu.roll(odd, HEAD_DIM, 1))
            b = jnp.where(low, pltpu.roll(even, HEAD_DIM, 1), odd)
            dctx_ref[g, 0, at : at + BLOCK, :] = a.astype(bf16)
            dctx_ref[g + 1, 0, at : at + BLOCK, :] = b.astype(bf16)


def chain(ctx, tok, og, wo, wu, wd, vec, bu):
    rows, width = tok.shape
    hidden = wu.shape[1]
    groups = ctx.shape[0]
    once = pl.Buffered(1)

    def tiled(cols):
        return pl.BlockSpec((ROWS, cols), lambda t: (t, 0))

    def fixed(shape):
        return pl.BlockSpec(shape, lambda t: (0, 0), pipeline_mode=once)

    packed = pl.BlockSpec((groups, 1) + ctx.shape[2:], lambda t: (0, t, 0, 0))
    shape = jax.ShapeDtypeStruct
    return pl.pallas_call(
        partial(chain_kernel, groups),
        grid=(rows // ROWS,),
        out_shape=(
            shape((rows, width), bf16),
            shape((rows, width), f32),
            shape(ctx.shape, bf16),
            shape((rows, width), bf16),
            shape((rows, width), bf16),
            shape((rows, hidden), bf16),
            shape((rows, hidden), bf16),
            shape((rows, width), bf16),
            shape((rows, width), bf16),
            shape((8, width), f32),
            shape((8, hidden), f32),
        ),
        in_specs=[
            packed,
            tiled(width),
            tiled(width),
            fixed(wo.shape),
            fixed(wu.shape),
            fixed(wd.shape),
            fixed(vec.shape),
            fixed(bu.shape),
        ],
        out_specs=(
            tiled(width),
            tiled(width),
            packed,
            tiled(width),
            tiled(width),
            tiled(hidden),
            tiled(hidden),
            tiled(width),
            tiled(width),
            pl.BlockSpec((8, width), lambda t: (0, 0)),
            pl.BlockSpec((8, hidden), lambda t: (0, 0)),
        ),
        scratch_shapes=[pltpu.VMEM((ROWS, hidden), bf16), pltpu.VMEM(wo.shape, bf16)],
        compiler_params=pltpu.CompilerParams(vmem_limit_bytes=VMEM_BYTES),
        name="chain",
    )(ctx, tok, og, wo, wu, wd, vec, bu)


def per_device(
    tokens,
    qkv_weight,
    query_value_bias,
    out_weight,
    out_bias,
    norm1_gain,
    norm1_bias,
    up_weight,
    up_bias,
    down_weight,
    down_bias,
    norm2_gain,
    norm2_bias,
    rand_blocks,
    out_grad,
):
    members = lax.axis_size(GROUP)
    devices = lax.axis_size(ALL)
    swap = [(0, 0), (1, 2), (2, 1), (3, 3)]

    def move(a):
        return lax.ppermute(a, ("core", "zh"), swap)

    tok = move(tokens[0])
    og = move(out_grad[0])
    rand = move(rand_blocks[0])
    heads = rand.shape[0]
    rows, width = tok.shape
    cols = heads * HEAD_DIM
    group = lax.axis_index(GROUP)

    x = lax.all_gather(tok, GROUP, axis=0, tiled=True)
    w_qkv = lax.all_gather(qkv_weight, ALL, axis=0, tiled=True)
    w_out = lax.all_gather(out_weight, ALL, axis=0, tiled=True)
    w_up = lax.all_gather(up_weight, ALL, axis=0, tiled=True)
    w_down = lax.all_gather(down_weight, ALL, axis=0, tiled=True)
    own = width // devices
    small = jnp.concatenate(
        [
            query_value_bias[0],
            query_value_bias[1],
            out_bias,
            norm1_gain,
            norm1_bias,
            down_bias,
            norm2_gain,
            norm2_bias,
            up_bias,
        ]
    )
    small = lax.all_gather(small, ALL, axis=0).astype(f32)
    vecs = jnp.transpose(small[:, : 8 * own].reshape(devices, 8, own), (1, 0, 2)).reshape(8, width)
    bias_up = small[:, 8 * own :].reshape(1, -1)

    def lay_out(a):
        a = a.reshape(a.shape[:-2] + (3, heads, HEAD_DIM))
        q, k, v = a[..., 0, :, :], a[..., 1, :, :], a[..., 2, :, :]
        q = q * jnp.asarray(HEAD_DIM**-0.5, a.dtype)
        laid = jnp.stack([q, jnp.zeros_like(q), k, v], axis=-2)
        return laid.reshape(laid.shape[:-3] + (heads * SLOT,))

    w_own = lax.dynamic_slice_in_dim(
        w_qkv.reshape(width, 3, members, cols), group, 1, axis=2
    ).reshape(width, 3, cols)
    w_own = lay_out(w_own)
    bias3 = jnp.stack([vecs[0], jnp.zeros_like(vecs[0]), vecs[1]]).reshape(3, members, cols)
    b_own = lay_out(lax.dynamic_slice_in_dim(bias3, group, 1, axis=1).reshape(1, 3, cols))
    rand_flat = rand.reshape(-1)

    qkv, res, ctx_send = attend(rand_flat, x, w_own, b_own, members, heads)
    ctx = lax.all_to_all(ctx_send, GROUP, split_axis=0, concat_axis=0, tiled=True)
    chain_vecs = jnp.concatenate([vecs[2:8], jnp.zeros((2, width), f32)], axis=0)
    out, dres1, dctx_send, mix, hid, act, dpre, dffn, dproj, gvec, gbu = chain(
        ctx, tok, og, w_out, w_up, w_down, chain_vecs, bias_up
    )
    dctx = lax.all_to_all(dctx_send, GROUP, split_axis=0, concat_axis=0, tiled=True)
    out = move(out)

    g_down = dot_tn(act, dffn).astype(bf16)
    g_up = dot_tn(hid, dpre).astype(bf16)
    g_mix = dot_tn(mix, dproj).astype(bf16)
    pairs = g_mix[: members * LANES].reshape(members, LANES, width)
    thirds = g_mix[members * LANES :].reshape(members, HEAD_DIM, width)
    g_out = jnp.concatenate([pairs, thirds], axis=1).reshape(width, width)

    def scatter(a):
        return lax.psum_scatter(a, ALL, scatter_dimension=0, tiled=True).astype(f32)

    g_down, g_up, g_out = scatter(g_down), scatter(g_up), scatter(g_out)

    draw, sums = attend_back(rand_flat, qkv, res, dctx, heads)
    dx = dot_nt(draw, w_own).astype(bf16)
    dx = lax.psum_scatter(dx, GROUP, scatter_dimension=0, tiled=True)
    input_grad = move((dres1 + dx.astype(f32)).astype(bf16)).astype(f32)

    def strip(a):
        a = a.reshape(a.shape[:-1] + (heads, 4, HEAD_DIM))
        q, k, v = a[..., 0, :] * (HEAD_DIM**-0.5), a[..., 2, :], a[..., 3, :]
        return jnp.stack([q, k, v], axis=-3).reshape(a.shape[:-3] + (3, cols))

    g_qkv = strip(dot_tn(x, draw)).reshape(-1, 2, 2, members // 2, own, 3 * cols)
    g_qkv = jnp.transpose(g_qkv, (0, 2, 1, 3, 4, 5)).reshape(-1, members, own, 3 * cols)
    g_qkv = g_qkv.reshape(-1, 3 * cols).astype(bf16)
    g_qkv = lax.psum_scatter(g_qkv, REST, scatter_dimension=0, tiled=True)
    g_qkv = g_qkv.reshape(members, own, 3 * cols)
    g_qkv = lax.all_to_all(g_qkv, GROUP, split_axis=0, concat_axis=0, tiled=True).astype(f32)
    g_qkv = jnp.transpose(g_qkv.reshape(members, own, 3, cols), (1, 2, 0, 3)).reshape(own, -1)

    col_sums = strip(sums[0:1])[0]
    pair = jnp.stack([col_sums[0], col_sums[2]]).reshape(2, 1, cols)
    mine = (jnp.arange(members) == group)[None, :, None]
    pair = jnp.where(mine, pair, 0.0).reshape(2, width)
    vec_grads = jnp.concatenate([pair, gvec[0:6]], axis=0).reshape(8, devices, own)
    vec_grads = jnp.transpose(vec_grads, (1, 0, 2)).reshape(devices, 8 * own)
    vec_grads = jnp.concatenate([vec_grads, gbu[0].reshape(devices, -1)], axis=1)
    vec_grads = lax.psum_scatter(vec_grads, ALL, scatter_dimension=0, tiled=True)[0]
    v8 = vec_grads[: 8 * own].reshape(8, own)
    return (
        out[None],
        input_grad[None],
        g_qkv,
        v8[0:2],
        g_out,
        v8[2],
        v8[3],
        v8[4],
        g_up,
        vec_grads[8 * own :],
        g_down,
        v8[5],
        v8[6],
        v8[7],
    )


def solution(mesh):
    dp, sp = mesh.shape["dp"], mesh.shape["sp"]
    fine = Mesh(mesh.devices.reshape(dp // 2, 2, 2, sp // 2), ALL)
    dp, sp = ("c", "core"), ("zh", "zl")
    act = P(dp, sp, None)
    mat = P(ALL, None)
    pair = P(None, ALL)
    vec = P(ALL)
    rand = P(dp, sp, None, None)
    return jax.shard_map(
        per_device,
        mesh=fine,
        in_specs=(act, mat, pair, mat, vec, vec, vec, mat, vec, mat, vec, vec, vec, rand, act),
        out_specs=(act, act, mat, pair, mat, vec, vec, vec, mat, vec, mat, vec, vec, vec),
        check_vma=False,
    )
```

```python
from functools import partial

import jax
import jax.numpy as jnp
import numpy as np
from jax import lax
from jax.experimental import pallas as pl
from jax.experimental.pallas import tpu as pltpu
from jax.sharding import Mesh
from jax.sharding import PartitionSpec as P

HEAD_DIM = 64
BLOCK = 64
LANES = 128
SLOT = 4 * HEAD_DIM
EPS = 1e-05
MASKED = -1e30
ALL = ("c", "core", "zh", "zl")
GROUP = ("core", "zl")
REST = ("c", "zh")
CHUNK = 512
ROWS = 256
VMEM_BYTES = 60 * 1024 * 1024

f32 = jnp.float32
bf16 = jnp.bfloat16
NT = (((1,), (1,)), ((), ()))
TN = (((0,), (0,)), ((), ()))


def dot(a, b):
    return jnp.dot(a, b, preferred_element_type=f32)


def dot_nt(a, b):
    return lax.dot_general(a, b, NT, preferred_element_type=f32)


def dot_tn(a, b):
    return lax.dot_general(a, b, TN, preferred_element_type=f32)


def rows_at(start, size):
    return pl.ds(pl.multiple_of(start, size), size)


def listed(ref, rand_ref, head, i, blocks, randoms, cols):
    parts = [
        ref[0:BLOCK, cols],
        ref[(blocks - 1) * BLOCK : blocks * BLOCK, cols],
        ref[pl.ds(pl.multiple_of((i - 1) * BLOCK, BLOCK), 3 * BLOCK), cols],
    ]
    base = (head * (blocks - 2) + i - 1) * randoms
    for r in range(randoms):
        parts.append(ref[rows_at(rand_ref[base + r] * BLOCK, BLOCK), cols])
    return jnp.concatenate(parts, axis=0)


def mask_globals(s, i, blocks):
    lane = lax.broadcasted_iota(jnp.int32, (BLOCK, LANES), 1)
    low = lane < BLOCK
    dead = (low & (i == 1)) | (~low & (i == blocks - 2))
    return jnp.concatenate([jnp.where(dead, MASKED, s[:, :LANES]), s[:, LANES:]], axis=1)


def attend_kernel(heads, randoms, rand_ref, x_ref, w_ref, b_ref, qkv_ref, res_ref, ctx_ref):
    length = x_ref.shape[0]
    blocks = length // BLOCK
    last = (blocks - 1) * BLOCK

    def project(t, carry):
        rows = rows_at(t * CHUNK, CHUNK)
        qkv_ref[rows, :] = (dot(x_ref[rows, :], w_ref[...]) + b_ref[...]).astype(bf16)
        return carry

    lax.fori_loop(0, length // CHUNK, project, 0)

    def middle(i, carry):
        rows = rows_at(i * BLOCK, BLOCK)
        lane = lax.broadcasted_iota(jnp.int32, (BLOCK, LANES), 1)
        for h in range(heads):
            at = h * SLOT
            kv = listed(qkv_ref, rand_ref, h, i, blocks, randoms, slice(at + LANES, at + SLOT))
            s = mask_globals(dot_nt(qkv_ref[rows, at : at + LANES], kv), i, blocks)
            top = jnp.max(s, axis=1, keepdims=True)
            e = jnp.exp(s - top)
            total = jnp.sum(e, axis=1, keepdims=True)
            o = dot(e.astype(bf16), kv) / total
            res_ref[h, rows, :] = jnp.where(lane < HEAD_DIM, top + jnp.log(total), o)
        return carry

    lax.fori_loop(1, blocks - 1, middle, 0)

    for h in range(heads):
        at = h * SLOT
        q = jnp.concatenate(
            [qkv_ref[0:BLOCK, at : at + LANES], qkv_ref[last : last + BLOCK, at : at + LANES]], axis=0
        )

        def whole(t, carry, at=at, q=q):
            top, total, acc = carry
            kv = qkv_ref[rows_at(t * CHUNK, CHUNK), at + LANES : at + SLOT]
            s = dot_nt(q, kv)
            new = jnp.maximum(top, jnp.max(s, axis=1, keepdims=True))
            fade = jnp.exp(top - new)
            e = jnp.exp(s - new)
            total = total * fade + jnp.sum(e, axis=1, keepdims=True)
            return new, total, acc * fade + dot(e.astype(bf16), kv)

        top, total, acc = lax.fori_loop(
            0,
            length // CHUNK,
            whole,
            (
                jnp.full((2 * BLOCK, 1), MASKED, f32),
                jnp.zeros((2 * BLOCK, 1), f32),
                jnp.zeros((2 * BLOCK, LANES), f32),
            ),
        )
        lane = lax.broadcasted_iota(jnp.int32, (2 * BLOCK, LANES), 1)
        both = jnp.where(lane < HEAD_DIM, top + jnp.log(total), acc / total)
        res_ref[h, 0:BLOCK, :] = both[:BLOCK]
        res_ref[h, last : last + BLOCK, :] = both[BLOCK:]

    per_quarter = ctx_ref.shape[1]

    def pack(t, carry):
        part, piece = t // per_quarter, t % per_quarter
        lane = lax.broadcasted_iota(jnp.int32, (BLOCK, LANES), 1)
        low = lane < HEAD_DIM
        for n in range(ROWS // BLOCK):
            rows = rows_at(t * ROWS + n * BLOCK, BLOCK)
            first = pltpu.roll(res_ref[0, rows, :], HEAD_DIM, 1)
            pair = jnp.where(low, first, res_ref[1, rows, :])
            ctx_ref[part, piece, n * BLOCK : (n + 1) * BLOCK, :] = pair.astype(bf16)
        for n in range(ROWS // (2 * BLOCK)):
            rows = rows_at(t * ROWS + 2 * n * BLOCK, BLOCK)
            odd = rows_at(t * ROWS + (2 * n + 1) * BLOCK, BLOCK)
            first = pltpu.roll(res_ref[2, rows, :], HEAD_DIM, 1)
            both = jnp.where(low, first, res_ref[2, odd, :])
            ctx_ref[part, piece, ROWS + n * BLOCK : ROWS + (n + 1) * BLOCK, :] = both.astype(bf16)
        return carry

    lax.fori_loop(0, length // ROWS, pack, 0)


def attend(rand, x, w, b, parts, heads):
    length = x.shape[0]
    randoms = rand.size // (heads * (length // BLOCK - 2))
    vmem = pl.BlockSpec(memory_space=pltpu.VMEM)
    return pl.pallas_call(
        partial(attend_kernel, heads, randoms),
        out_shape=(
            jax.ShapeDtypeStruct((length, heads * SLOT), bf16),
            jax.ShapeDtypeStruct((heads, length, LANES), f32),
            jax.ShapeDtypeStruct((parts, length // parts // ROWS, ROWS * 3 // 2, LANES), bf16),
        ),
        in_specs=[pl.BlockSpec(memory_space=pltpu.SMEM), vmem, vmem, vmem],
        out_specs=(vmem, vmem, vmem),
        compiler_params=pltpu.CompilerParams(vmem_limit_bytes=VMEM_BYTES),
        name="attend",
    )(rand, x, w, b)


def attend_back_kernel(
    heads, randoms, rand_ref, qkv_ref, res_ref, dctx_ref, draw_ref, sums_ref, *scratch
):
    dout, acc = scratch[:heads], scratch[heads:]
    length = qkv_ref.shape[0]
    blocks = length // BLOCK
    last = (blocks - 1) * BLOCK
    per_quarter = dctx_ref.shape[1]

    def unpack(t, carry):
        part, piece = t // per_quarter, t % per_quarter
        lane = lax.broadcasted_iota(jnp.int32, (BLOCK, LANES), 1)
        low = lane < HEAD_DIM
        for n in range(ROWS // BLOCK):
            rows = rows_at(t * ROWS + n * BLOCK, BLOCK)
            pair = dctx_ref[part, piece, n * BLOCK : (n + 1) * BLOCK, :].astype(f32)
            dout[0][rows, :] = jnp.where(low, 0.0, pltpu.roll(pair, HEAD_DIM, 1)).astype(bf16)
            dout[1][rows, :] = jnp.where(low, 0.0, pair).astype(bf16)
        for n in range(ROWS // (2 * BLOCK)):
            rows = rows_at(t * ROWS + 2 * n * BLOCK, BLOCK)
            odd = rows_at(t * ROWS + (2 * n + 1) * BLOCK, BLOCK)
            both = dctx_ref[part, piece, ROWS + n * BLOCK : ROWS + (n + 1) * BLOCK, :].astype(f32)
            dout[2][rows, :] = jnp.where(low, 0.0, pltpu.roll(both, HEAD_DIM, 1)).astype(bf16)
            dout[2][odd, :] = jnp.where(low, 0.0, both).astype(bf16)
        return carry

    lax.fori_loop(0, length // ROWS, unpack, 0)

    step = 256
    for h in range(heads):
        at = h * SLOT
        q = jnp.concatenate(
            [qkv_ref[0:BLOCK, at : at + LANES], qkv_ref[last : last + BLOCK, at : at + LANES]], axis=0
        )
        g = jnp.concatenate([dout[h][0:BLOCK, :], dout[h][last : last + BLOCK, :]], axis=0)
        res = jnp.concatenate([res_ref[h, 0:BLOCK, :], res_ref[h, last : last + BLOCK, :]], axis=0)
        log_total = res[:, 0:1]
        delta = jnp.sum(g.astype(f32) * res, axis=1, keepdims=True)
        both = jnp.concatenate([q, g], axis=0)

        def whole(t, dq, at=at, h=h, both=both, log_total=log_total, delta=delta):
            rows = rows_at(t * step, step)
            kv = qkv_ref[rows, at + LANES : at + SLOT]
            sd = dot_nt(both, kv)
            p = jnp.exp(sd[: 2 * BLOCK] - log_total)
            ds = (p * (sd[2 * BLOCK :] - delta)).astype(bf16)
            acc[h][rows, :] = dot_tn(jnp.concatenate([ds, p.astype(bf16)], axis=0), both)
            return dq + dot(ds, kv)

        dq = lax.fori_loop(0, length // step, whole, jnp.zeros((2 * BLOCK, LANES), f32))
        lane = lax.broadcasted_iota(jnp.int32, (2 * BLOCK, LANES), 1)
        dq = jnp.where(lane < HEAD_DIM, dq, 0.0).astype(bf16)
        draw_ref[0:BLOCK, at : at + LANES] = dq[:BLOCK]
        draw_ref[last : last + BLOCK, at : at + LANES] = dq[BLOCK:]

    def middle(i, carry):
        rows = rows_at(i * BLOCK, BLOCK)
        lane = lax.broadcasted_iota(jnp.int32, (BLOCK, LANES), 1)
        for h in range(heads):
            at = h * SLOT
            kv = listed(qkv_ref, rand_ref, h, i, blocks, randoms, slice(at + LANES, at + SLOT))
            g = dout[h][rows, :]
            res = res_ref[h, rows, :]
            both = jnp.concatenate([qkv_ref[rows, at : at + LANES], g], axis=0)
            delta = jnp.sum(g.astype(f32) * res, axis=1, keepdims=True)
            sd = dot_nt(both, kv)
            p = jnp.exp(mask_globals(sd[:BLOCK], i, blocks) - res[:, 0:1])
            ds = (p * (sd[BLOCK:] - delta)).astype(bf16)
            dkv = dot_tn(jnp.concatenate([ds, p.astype(bf16)], axis=0), both)
            dq = dot(ds, kv)
            draw_ref[rows, at : at + LANES] = jnp.where(lane < HEAD_DIM, dq, 0.0).astype(bf16)
            acc[h][0:BLOCK, :] += dkv[0:BLOCK]
            acc[h][last : last + BLOCK, :] += dkv[BLOCK : 2 * BLOCK]
            near = pl.ds(pl.multiple_of((i - 1) * BLOCK, BLOCK), 3 * BLOCK)
            acc[h][near, :] += dkv[2 * BLOCK : 5 * BLOCK]
            base = (h * (blocks - 2) + i - 1) * randoms
            for r in range(randoms):
                far = rows_at(rand_ref[base + r] * BLOCK, BLOCK)
                acc[h][far, :] += dkv[(5 + r) * BLOCK : (6 + r) * BLOCK]
        return carry

    lax.fori_loop(1, blocks - 1, middle, 0)
    sums_ref[...] = jnp.zeros_like(sums_ref)

    def finish(t, carry):
        rows = rows_at(t * CHUNK, CHUNK)
        for h in range(heads):
            at = h * SLOT
            draw_ref[rows, at + LANES : at + SLOT] = acc[h][rows, :].astype(bf16)
        sums_ref[0:1, :] += jnp.sum(draw_ref[rows, :].astype(f32), axis=0, keepdims=True)
        return carry

    lax.fori_loop(0, length // CHUNK, finish, 0)


def attend_back(rand, qkv, res, dctx, heads):
    length = qkv.shape[0]
    randoms = rand.size // (heads * (length // BLOCK - 2))
    vmem = pl.BlockSpec(memory_space=pltpu.VMEM)
    return pl.pallas_call(
        partial(attend_back_kernel, heads, randoms),
        out_shape=(
            jax.ShapeDtypeStruct((length, heads * SLOT), bf16),
            jax.ShapeDtypeStruct((8, heads * SLOT), f32),
        ),
        in_specs=[pl.BlockSpec(memory_space=pltpu.SMEM), vmem, vmem, vmem],
        out_specs=(vmem, vmem),
        scratch_shapes=[pltpu.VMEM((length, LANES), bf16)] * heads
        + [pltpu.VMEM((length, LANES), f32)] * heads,
        compiler_params=pltpu.CompilerParams(vmem_limit_bytes=VMEM_BYTES),
        name="attend_back",
    )(rand, qkv, res, dctx)


def mean_of(a):
    return jnp.mean(a, axis=1, keepdims=True)


def norm(r):
    center = r - mean_of(r)
    rstd = lax.rsqrt(mean_of(center * center) + EPS)
    return center * rstd, rstd


def norm_back(dn, n, rstd):
    return rstd * (dn - mean_of(dn) - n * mean_of(dn * n))


def rowsum(a):
    return jnp.sum(a, axis=0, keepdims=True)


def chain_kernel(
    groups,
    ctx_ref,
    tok_ref,
    og_ref,
    wo_ref,
    wu_ref,
    wd_ref,
    vec_ref,
    bu_ref,
    out_ref,
    dres_ref,
    dctx_ref,
    mix_ref,
    hid_ref,
    act_ref,
    dpre_ref,
    dffn_ref,
    dproj_ref,
    gvec_ref,
    gbu_ref,
    slope_ref,
    wop_ref,
):
    width = tok_ref.shape[1]
    hidden = wu_ref.shape[1]
    wide = 3 * HEAD_DIM
    step = pl.program_id(0)

    @pl.when(step == 0)
    def _():
        for g in range(groups):
            wop_ref[g * LANES : (g + 1) * LANES, :] = wo_ref[g * wide : g * wide + LANES, :]
            to = groups * LANES + g * HEAD_DIM
            wop_ref[to : to + HEAD_DIM, :] = wo_ref[g * wide + LANES : (g + 1) * wide, :]
        gvec_ref[...] = jnp.zeros_like(gvec_ref)
        gbu_ref[...] = jnp.zeros_like(gbu_ref)

    low = lax.broadcasted_iota(jnp.int32, (BLOCK, LANES), 1) < HEAD_DIM
    for g in range(groups):
        mix_ref[:, g * LANES : (g + 1) * LANES] = ctx_ref[g, 0, :ROWS, :]
    for g in range(0, groups, 2):
        to = groups * LANES + g * HEAD_DIM
        for n in range(ROWS // (2 * BLOCK)):
            at = ROWS + n * BLOCK
            a = ctx_ref[g, 0, at : at + BLOCK, :].astype(f32)
            b = ctx_ref[g + 1, 0, at : at + BLOCK, :].astype(f32)
            even = jnp.where(low, a, pltpu.roll(b, HEAD_DIM, 1))
            odd = jnp.where(low, pltpu.roll(a, HEAD_DIM, 1), b)
            r = 2 * n * BLOCK
            mix_ref[r : r + BLOCK, to : to + LANES] = even.astype(bf16)
            mix_ref[r + BLOCK : r + 2 * BLOCK, to : to + LANES] = odd.astype(bf16)

    bo, g1, s1 = vec_ref[0:1, :], vec_ref[1:2, :], vec_ref[2:3, :]
    bd, g2, s2 = vec_ref[3:4, :], vec_ref[4:5, :], vec_ref[5:6, :]
    n1, rstd1 = norm(tok_ref[...].astype(f32) + dot(mix_ref[...], wop_ref[...]) + bo)
    hid = n1 * g1 + s1
    hid_low = hid.astype(bf16)
    hid_ref[...] = hid_low
    scale = np.sqrt(2.0 / np.pi).astype(np.float32)

    def up(f, carry):
        cols = rows_at(f * CHUNK, CHUNK)
        u = dot(hid_low, wu_ref[:, cols]) + bu_ref[:, cols]
        square = u * u
        t = jnp.tanh(scale * (u + 0.044715 * (u * square)))
        half = 0.5 * (1.0 + t)
        act_ref[:, cols] = (u * half).astype(bf16)
        slope = half + 0.5 * u * (1.0 - t * t) * (scale * (1.0 + (3 * 0.044715) * square))
        slope_ref[:, cols] = slope.astype(bf16)
        return carry

    lax.fori_loop(0, hidden // CHUNK, up, 0)
    n2, rstd2 = norm(hid + dot(act_ref[...], wd_ref[...]) + bd)
    out_ref[...] = (n2 * g2 + s2).astype(bf16)
    og = og_ref[...].astype(f32)
    gvec_ref[4:5, :] += rowsum(og * n2)
    gvec_ref[5:6, :] += rowsum(og)
    dres2 = norm_back(og * g2, n2, rstd2)
    dffn = dres2.astype(bf16)
    dffn_ref[...] = dffn
    gvec_ref[3:4, :] += rowsum(dffn.astype(f32))

    def down_back(f, carry):
        cols = rows_at(f * CHUNK, CHUNK)
        dact = dot_nt(dffn, wd_ref[cols, :])
        dpre = (dact * slope_ref[:, cols].astype(f32)).astype(bf16)
        dpre_ref[:, cols] = dpre
        gbu_ref[0:1, cols] += rowsum(dpre.astype(f32))
        return carry

    lax.fori_loop(0, hidden // CHUNK, down_back, 0)
    dh = dres2 + dot_nt(dpre_ref[...], wu_ref[...])
    gvec_ref[1:2, :] += rowsum(dh * n1)
    gvec_ref[2:3, :] += rowsum(dh)
    dres1 = norm_back(dh * g1, n1, rstd1)
    dres_ref[...] = dres1
    dproj = dres1.astype(bf16)
    dproj_ref[...] = dproj
    gvec_ref[0:1, :] += rowsum(dproj.astype(f32))
    dmix = dot_nt(dproj, wop_ref[...])
    for g in range(groups):
        dctx_ref[g, 0, :ROWS, :] = dmix[:, g * LANES : (g + 1) * LANES].astype(bf16)
    for g in range(0, groups, 2):
        to = groups * LANES + g * HEAD_DIM
        for n in range(ROWS // (2 * BLOCK)):
            at = ROWS + n * BLOCK
            r = 2 * n * BLOCK
            even = dmix[r : r + BLOCK, to : to + LANES]
            odd = dmix[r + BLOCK : r + 2 * BLOCK, to : to + LANES]
            a = jnp.where(low, even, pltpu.roll(odd, HEAD_DIM, 1))
            b = jnp.where(low, pltpu.roll(even, HEAD_DIM, 1), odd)
            dctx_ref[g, 0, at : at + BLOCK, :] = a.astype(bf16)
            dctx_ref[g + 1, 0, at : at + BLOCK, :] = b.astype(bf16)


def chain(ctx, tok, og, wo, wu, wd, vec, bu):
    rows, width = tok.shape
    hidden = wu.shape[1]
    groups = ctx.shape[0]
    once = pl.Buffered(1)

    def tiled(cols):
        return pl.BlockSpec((ROWS, cols), lambda t: (t, 0))

    def fixed(shape):
        return pl.BlockSpec(shape, lambda t: (0, 0), pipeline_mode=once)

    packed = pl.BlockSpec((groups, 1) + ctx.shape[2:], lambda t: (0, t, 0, 0))
    shape = jax.ShapeDtypeStruct
    return pl.pallas_call(
        partial(chain_kernel, groups),
        grid=(rows // ROWS,),
        out_shape=(
            shape((rows, width), bf16),
            shape((rows, width), f32),
            shape(ctx.shape, bf16),
            shape((rows, width), bf16),
            shape((rows, width), bf16),
            shape((rows, hidden), bf16),
            shape((rows, hidden), bf16),
            shape((rows, width), bf16),
            shape((rows, width), bf16),
            shape((8, width), f32),
            shape((8, hidden), f32),
        ),
        in_specs=[
            packed,
            tiled(width),
            tiled(width),
            fixed(wo.shape),
            fixed(wu.shape),
            fixed(wd.shape),
            fixed(vec.shape),
            fixed(bu.shape),
        ],
        out_specs=(
            tiled(width),
            tiled(width),
            packed,
            tiled(width),
            tiled(width),
            tiled(hidden),
            tiled(hidden),
            tiled(width),
            tiled(width),
            pl.BlockSpec((8, width), lambda t: (0, 0)),
            pl.BlockSpec((8, hidden), lambda t: (0, 0)),
        ),
        scratch_shapes=[pltpu.VMEM((ROWS, hidden), bf16), pltpu.VMEM(wo.shape, bf16)],
        compiler_params=pltpu.CompilerParams(vmem_limit_bytes=VMEM_BYTES),
        name="chain",
    )(ctx, tok, og, wo, wu, wd, vec, bu)


MESH = pl.DeviceIdType.MESH


def run_phases(items):
    step = 0
    live = list(items)
    while live:
        after = []
        for first, phases in live:
            if first > step or next(phases, None) is not None:
                after.append((first, phases))
        live = after
        step += 1


class Where:
    def __init__(self):
        c, core, zh, zl = (lax.axis_index(a) for a in ALL)
        self.y, self.x, self.core, self.zh, self.zl = c // 2, c % 2, core, zh, zl
        self.z = zh * 2 + zl
        self.by_x = (self.y * 2 + 1 - self.x, core, zh, zl)
        self.by_y = ((1 - self.y) * 2 + self.x, core, zh, zl)
        self.by_core = (c, 1 - core, zh, zl)
        self.by_zl = (c, core, zh, 1 - zl)
        self.by_zh = (c, core, 1 - zh, zl)
        self.by_mid = (c, core, 1 - zh, 1 - zl)
        self.by_swap = (c, 1 - core, 1 - zh, zl)
        self.inner = zh != zl
        self.stays = core == zh

    def greet(self):
        barrier = pltpu.get_barrier_semaphore()
        others = (self.by_x, self.by_y, self.by_core, self.by_zl, self.by_zh, self.by_mid, self.by_swap)
        for other in others:
            pl.semaphore_signal(barrier, inc=1, device_id=other, device_id_type=MESH)
        pl.semaphore_wait(barrier, len(others))


class Copies:
    def __init__(self, send, recv, local):
        self.send, self.recv, self.local_sems = send, recv, local
        self.n = self.m = 0

    def remote(self, src, dst, device):
        n = self.n
        self.n += 1
        return pltpu.make_async_remote_copy(
            src_ref=src,
            dst_ref=dst,
            send_sem=self.send.at[n],
            recv_sem=self.recv.at[n],
            device_id=device,
            device_id_type=MESH,
        )

    def local(self, src, dst):
        m = self.m
        self.m += 1
        return pltpu.make_async_copy(src, dst, self.local_sems.at[m])


def gather_item(me, copies, shard, full, cols, x_first):
    y, x, core, zh, zl = me.y, me.x, me.core, me.zh, me.zl
    mine = shard.at[:, cols]
    own = copies.local(mine, full.at[y, x, core, me.z, :, cols])
    first = copies.remote(mine, full.at[y, x, core, me.z, :, cols], me.by_zl)
    own.start()
    first.start()
    yield 1
    own.wait()
    first.wait()
    pair = full.at[y, x, core, pl.ds(zh * 2, 2), :, cols]
    pair_far = full.at[y, x, core, pl.ds((1 - zh) * 2, 2), :, cols]
    middle = copies.remote(pair, pair, me.by_mid)
    onward = copies.remote(pair_far, pair_far, me.by_zl)

    @pl.when(me.inner)
    def _():
        middle.start()

    yield 1

    @pl.when(me.inner)
    def _():
        middle.wait()
        onward.start()

    yield 1

    @pl.when(me.inner)
    def _():
        onward.wait_send()

    @pl.when(jnp.logical_not(me.inner))
    def _():
        onward.wait_recv()

    line = full.at[y, x, core, :, :, cols]
    near = copies.remote(line, line, me.by_x if x_first else me.by_y)
    near.start()
    across = [copies.remote(line, line, me.by_core)]
    across[0].start()
    yield 1
    near.wait()
    if x_first:
        block = full.at[y, :, core, :, :, cols]
        got = full.at[y, 1 - x, core, :, :, cols]
        rest = full.at[1 - y, :, core, :, :, cols]
    else:
        block = full.at[:, x, core, :, :, cols]
        got = full.at[1 - y, x, core, :, :, cols]
        rest = full.at[:, 1 - x, core, :, :, cols]
    far = copies.remote(block, block, me.by_y if x_first else me.by_x)
    far.start()
    across.append(copies.remote(got, got, me.by_core))
    across[1].start()
    yield 1
    far.wait()
    across.append(copies.remote(rest, rest, me.by_core))
    across[2].start()
    yield 1
    for copy in across:
        copy.wait()


def tokens_item(me, copies, tok, x_all, piece):
    place = me.core * 2 + me.zl
    there = (1 - me.core) * 2 + me.zl
    out = copies.remote(tok.at[piece], x_all.at[there, piece], me.by_swap)
    keep = copies.local(tok.at[piece], x_all.at[place, piece])

    @pl.when(me.stays)
    def _():
        keep.start()

    @pl.when(jnp.logical_not(me.stays))
    def _():
        out.start()

    yield 1

    @pl.when(me.stays)
    def _():
        keep.wait()

    @pl.when(jnp.logical_not(me.stays))
    def _():
        out.wait()

    held = x_all.at[place, piece]
    along = copies.remote(held, held, me.by_zl)
    along.start()
    over = copies.remote(held, held, me.by_core)
    over.start()
    yield 1
    along.wait()
    came = x_all.at[me.core * 2 + 1 - me.zl, piece]
    onto = copies.remote(came, came, me.by_core)
    onto.start()
    yield 1
    over.wait()
    onto.wait()


def exchange_item(me, copies, src, dst):
    out = copies.remote(src, dst, me.by_swap)
    keep = copies.local(src, dst)

    @pl.when(me.stays)
    def _():
        keep.start()

    @pl.when(jnp.logical_not(me.stays))
    def _():
        out.start()

    yield 1

    @pl.when(me.stays)
    def _():
        keep.wait()

    @pl.when(jnp.logical_not(me.stays))
    def _():
        out.wait()


PIECES = 4


def gather_kernel(
    tok, og, qkv, w_out, up, down, small, x_all, og_all, qkv_all, out_all, up_all, down_all, small_all, *sems
):
    me = Where()
    me.greet()
    copies = Copies(*sems)
    items = []

    def halves(first, shard, full):
        half = shard.shape[1] // 2
        for n in range(2):
            items.append((first, gather_item(me, copies, shard, full, slice(n * half, (n + 1) * half), n == 0)))

    items.append((0, gather_item(me, copies, small, small_all, slice(0, LANES), True)))
    for piece in range(PIECES):
        items.append((piece, tokens_item(me, copies, tok, x_all, piece)))
        if piece == 0:
            halves(0, qkv, qkv_all)
    halves(1, w_out, out_all)
    halves(2, up, up_all)
    halves(3, down, down_all)
    items.append((4, exchange_item(me, copies, og, og_all)))
    items.sort(key=lambda item: item[0])
    run_phases(items)


def gather(tok, og, mats, small, members):
    rows, width = tok.shape
    hbm = pl.BlockSpec(memory_space=pltpu.HBM)
    shape = jax.ShapeDtypeStruct
    tok = tok.reshape(PIECES, rows // PIECES, width)
    outs = [shape((members,) + tok.shape, bf16), shape(og.shape, bf16)]
    outs += [shape((2, 2, 2, 4) + a.shape, bf16) for a in (*mats, small)]
    return pl.pallas_call(
        gather_kernel,
        out_shape=tuple(outs),
        in_specs=[hbm] * 7,
        out_specs=(hbm,) * 7,
        scratch_shapes=[
            pltpu.SemaphoreType.DMA((112,)),
            pltpu.SemaphoreType.DMA((112,)),
            pltpu.SemaphoreType.DMA((16,)),
        ],
        compiler_params=pltpu.CompilerParams(
            collective_id=0, has_side_effects=True, vmem_limit_bytes=VMEM_BYTES
        ),
        name="gather",
    )(tok, og, *mats, small)


def per_device(
    tokens,
    qkv_weight,
    query_value_bias,
    out_weight,
    out_bias,
    norm1_gain,
    norm1_bias,
    up_weight,
    up_bias,
    down_weight,
    down_bias,
    norm2_gain,
    norm2_bias,
    rand_blocks,
    out_grad,
):
    members = lax.axis_size(GROUP)
    devices = lax.axis_size(ALL)
    swap = [(0, 0), (1, 2), (2, 1), (3, 3)]

    def move(a):
        return lax.ppermute(a, ("core", "zh"), swap)

    rand = move(rand_blocks[0])
    heads = rand.shape[0]
    rows, width = tokens.shape[1:]
    cols = heads * HEAD_DIM
    group = lax.axis_index(GROUP)
    own = width // devices
    small = jnp.concatenate(
        [
            query_value_bias[0],
            query_value_bias[1],
            out_bias,
            norm1_gain,
            norm1_bias,
            down_bias,
            norm2_gain,
            norm2_bias,
            up_bias,
        ]
    )
    mats = (qkv_weight, out_weight, up_weight, down_weight)
    direct = lax.axis_size("c") == 4 and members == 4 and own % 8 == 0
    if direct:
        count = small.shape[0]
        padded = jnp.pad(small, (0, 16 * LANES - count)).reshape(16, LANES)
        x, og, *full, small = gather(tokens[0], out_grad[0], mats, padded, members)
        x = x.reshape(members * rows, width)
        tok = lax.dynamic_slice_in_dim(x, group * rows, rows, axis=0)
        w_qkv, w_out, w_up, w_down = (a.reshape(-1, a.shape[-1]) for a in full)
        small = small.reshape(devices, -1)[:, :count].astype(f32)
    else:
        tok = move(tokens[0])
        og = move(out_grad[0])
        x = lax.all_gather(tok, GROUP, axis=0, tiled=True)
        w_qkv, w_out, w_up, w_down = (lax.all_gather(a, ALL, axis=0, tiled=True) for a in mats)
        small = lax.all_gather(small, ALL, axis=0).astype(f32)
    vecs = jnp.transpose(small[:, : 8 * own].reshape(devices, 8, own), (1, 0, 2)).reshape(8, width)
    bias_up = small[:, 8 * own :].reshape(1, -1)

    def lay_out(a):
        a = a.reshape(a.shape[:-2] + (3, heads, HEAD_DIM))
        q, k, v = a[..., 0, :, :], a[..., 1, :, :], a[..., 2, :, :]
        q = q * jnp.asarray(HEAD_DIM**-0.5, a.dtype)
        laid = jnp.stack([q, jnp.zeros_like(q), k, v], axis=-2)
        return laid.reshape(laid.shape[:-3] + (heads * SLOT,))

    w_own = lax.dynamic_slice_in_dim(
        w_qkv.reshape(width, 3, members, cols), group, 1, axis=2
    ).reshape(width, 3, cols)
    w_own = lay_out(w_own)
    bias3 = jnp.stack([vecs[0], jnp.zeros_like(vecs[0]), vecs[1]]).reshape(3, members, cols)
    b_own = lay_out(lax.dynamic_slice_in_dim(bias3, group, 1, axis=1).reshape(1, 3, cols))
    rand_flat = rand.reshape(-1)

    qkv, res, ctx_send = attend(rand_flat, x, w_own, b_own, members, heads)
    ctx = lax.all_to_all(ctx_send, GROUP, split_axis=0, concat_axis=0, tiled=True)
    chain_vecs = jnp.concatenate([vecs[2:8], jnp.zeros((2, width), f32)], axis=0)
    out, dres1, dctx_send, mix, hid, act, dpre, dffn, dproj, gvec, gbu = chain(
        ctx, tok, og, w_out, w_up, w_down, chain_vecs, bias_up
    )
    dctx = lax.all_to_all(dctx_send, GROUP, split_axis=0, concat_axis=0, tiled=True)
    out = move(out)

    g_down = dot_tn(act, dffn).astype(bf16)
    g_up = dot_tn(hid, dpre).astype(bf16)
    g_mix = dot_tn(mix, dproj).astype(bf16)
    pairs = g_mix[: members * LANES].reshape(members, LANES, width)
    thirds = g_mix[members * LANES :].reshape(members, HEAD_DIM, width)
    g_out = jnp.concatenate([pairs, thirds], axis=1).reshape(width, width)

    def scatter(a):
        return lax.psum_scatter(a, ALL, scatter_dimension=0, tiled=True).astype(f32)

    g_down, g_up, g_out = scatter(g_down), scatter(g_up), scatter(g_out)

    draw, sums = attend_back(rand_flat, qkv, res, dctx, heads)
    dx = dot_nt(draw, w_own).astype(bf16)
    dx = lax.psum_scatter(dx, GROUP, scatter_dimension=0, tiled=True)
    input_grad = move((dres1 + dx.astype(f32)).astype(bf16)).astype(f32)

    def strip(a):
        a = a.reshape(a.shape[:-1] + (heads, 4, HEAD_DIM))
        q, k, v = a[..., 0, :] * (HEAD_DIM**-0.5), a[..., 2, :], a[..., 3, :]
        return jnp.stack([q, k, v], axis=-3).reshape(a.shape[:-3] + (3, cols))

    g_qkv = strip(dot_tn(x, draw)).reshape(-1, 2, 2, members // 2, own, 3 * cols)
    g_qkv = jnp.transpose(g_qkv, (0, 2, 1, 3, 4, 5)).reshape(-1, members, own, 3 * cols)
    g_qkv = g_qkv.reshape(-1, 3 * cols).astype(bf16)
    g_qkv = lax.psum_scatter(g_qkv, REST, scatter_dimension=0, tiled=True)
    g_qkv = g_qkv.reshape(members, own, 3 * cols)
    g_qkv = lax.all_to_all(g_qkv, GROUP, split_axis=0, concat_axis=0, tiled=True).astype(f32)
    g_qkv = jnp.transpose(g_qkv.reshape(members, own, 3, cols), (1, 2, 0, 3)).reshape(own, -1)

    col_sums = strip(sums[0:1])[0]
    pair = jnp.stack([col_sums[0], col_sums[2]]).reshape(2, 1, cols)
    mine = (jnp.arange(members) == group)[None, :, None]
    pair = jnp.where(mine, pair, 0.0).reshape(2, width)
    vec_grads = jnp.concatenate([pair, gvec[0:6]], axis=0).reshape(8, devices, own)
    vec_grads = jnp.transpose(vec_grads, (1, 0, 2)).reshape(devices, 8 * own)
    vec_grads = jnp.concatenate([vec_grads, gbu[0].reshape(devices, -1)], axis=1)
    vec_grads = lax.psum_scatter(vec_grads, ALL, scatter_dimension=0, tiled=True)[0]
    v8 = vec_grads[: 8 * own].reshape(8, own)
    return (
        out[None],
        input_grad[None],
        g_qkv,
        v8[0:2],
        g_out,
        v8[2],
        v8[3],
        v8[4],
        g_up,
        vec_grads[8 * own :],
        g_down,
        v8[5],
        v8[6],
        v8[7],
    )


def solution(mesh):
    dp, sp = mesh.shape["dp"], mesh.shape["sp"]
    fine = Mesh(mesh.devices.reshape(dp // 2, 2, 2, sp // 2), ALL)
    dp, sp = ("c", "core"), ("zh", "zl")
    act = P(dp, sp, None)
    mat = P(ALL, None)
    pair = P(None, ALL)
    vec = P(ALL)
    rand = P(dp, sp, None, None)
    return jax.shard_map(
        per_device,
        mesh=fine,
        in_specs=(act, mat, pair, mat, vec, vec, vec, mat, vec, mat, vec, vec, vec, rand, act),
        out_specs=(act, act, mat, pair, mat, vec, vec, vec, mat, vec, mat, vec, vec, vec),
        check_vma=False,
    )
```

```python
from functools import partial

import jax
import jax.numpy as jnp
import numpy as np
from jax import lax
from jax.experimental import pallas as pl
from jax.experimental.pallas import tpu as pltpu
from jax.sharding import Mesh
from jax.sharding import PartitionSpec as P

HEAD_DIM = 64
BLOCK = 64
LANES = 128
SLOT = 4 * HEAD_DIM
EPS = 1e-05
MASKED = -1e30
ALL = ("c", "core", "zh", "zl")
GROUP = ("core", "zl")
REST = ("c", "zh")
CHUNK = 512
ROWS = 256
VMEM_BYTES = 60 * 1024 * 1024

f32 = jnp.float32
bf16 = jnp.bfloat16
NT = (((1,), (1,)), ((), ()))
TN = (((0,), (0,)), ((), ()))


def dot(a, b):
    return jnp.dot(a, b, preferred_element_type=f32)


def dot_nt(a, b):
    return lax.dot_general(a, b, NT, preferred_element_type=f32)


def dot_tn(a, b):
    return lax.dot_general(a, b, TN, preferred_element_type=f32)


def rows_at(start, size):
    return pl.ds(pl.multiple_of(start, size), size)


def listed(ref, rand_ref, head, i, blocks, randoms, cols):
    parts = [
        ref[0:BLOCK, cols],
        ref[(blocks - 1) * BLOCK : blocks * BLOCK, cols],
        ref[pl.ds(pl.multiple_of((i - 1) * BLOCK, BLOCK), 3 * BLOCK), cols],
    ]
    base = (head * (blocks - 2) + i - 1) * randoms
    for r in range(randoms):
        parts.append(ref[rows_at(rand_ref[base + r] * BLOCK, BLOCK), cols])
    return jnp.concatenate(parts, axis=0)


def mask_globals(s, i, blocks):
    lane = lax.broadcasted_iota(jnp.int32, (BLOCK, LANES), 1)
    low = lane < BLOCK
    dead = (low & (i == 1)) | (~low & (i == blocks - 2))
    return jnp.concatenate([jnp.where(dead, MASKED, s[:, :LANES]), s[:, LANES:]], axis=1)


def attend_kernel(heads, randoms, rand_ref, x_ref, w_ref, b_ref, qkv_ref, res_ref, ctx_ref):
    length = x_ref.shape[0]
    blocks = length // BLOCK
    last = (blocks - 1) * BLOCK

    def project(t, carry):
        rows = rows_at(t * CHUNK, CHUNK)
        qkv_ref[rows, :] = (dot(x_ref[rows, :], w_ref[...]) + b_ref[...]).astype(bf16)
        return carry

    lax.fori_loop(0, length // CHUNK, project, 0)

    def middle(i, carry):
        rows = rows_at(i * BLOCK, BLOCK)
        lane = lax.broadcasted_iota(jnp.int32, (BLOCK, LANES), 1)
        for h in range(heads):
            at = h * SLOT
            kv = listed(qkv_ref, rand_ref, h, i, blocks, randoms, slice(at + LANES, at + SLOT))
            s = mask_globals(dot_nt(qkv_ref[rows, at : at + LANES], kv), i, blocks)
            top = jnp.max(s, axis=1, keepdims=True)
            e = jnp.exp(s - top)
            total = jnp.sum(e, axis=1, keepdims=True)
            o = dot(e.astype(bf16), kv) / total
            res_ref[h, rows, :] = jnp.where(lane < HEAD_DIM, top + jnp.log(total), o)
        return carry

    lax.fori_loop(1, blocks - 1, middle, 0)

    for h in range(heads):
        at = h * SLOT
        q = jnp.concatenate(
            [qkv_ref[0:BLOCK, at : at + LANES], qkv_ref[last : last + BLOCK, at : at + LANES]], axis=0
        )

        def whole(t, carry, at=at, q=q):
            top, total, acc = carry
            kv = qkv_ref[rows_at(t * CHUNK, CHUNK), at + LANES : at + SLOT]
            s = dot_nt(q, kv)
            new = jnp.maximum(top, jnp.max(s, axis=1, keepdims=True))
            fade = jnp.exp(top - new)
            e = jnp.exp(s - new)
            total = total * fade + jnp.sum(e, axis=1, keepdims=True)
            return new, total, acc * fade + dot(e.astype(bf16), kv)

        top, total, acc = lax.fori_loop(
            0,
            length // CHUNK,
            whole,
            (
                jnp.full((2 * BLOCK, 1), MASKED, f32),
                jnp.zeros((2 * BLOCK, 1), f32),
                jnp.zeros((2 * BLOCK, LANES), f32),
            ),
        )
        lane = lax.broadcasted_iota(jnp.int32, (2 * BLOCK, LANES), 1)
        both = jnp.where(lane < HEAD_DIM, top + jnp.log(total), acc / total)
        res_ref[h, 0:BLOCK, :] = both[:BLOCK]
        res_ref[h, last : last + BLOCK, :] = both[BLOCK:]

    per_quarter = ctx_ref.shape[1]

    def pack(t, carry):
        part, piece = t // per_quarter, t % per_quarter
        lane = lax.broadcasted_iota(jnp.int32, (BLOCK, LANES), 1)
        low = lane < HEAD_DIM
        for n in range(ROWS // BLOCK):
            rows = rows_at(t * ROWS + n * BLOCK, BLOCK)
            first = pltpu.roll(res_ref[0, rows, :], HEAD_DIM, 1)
            pair = jnp.where(low, first, res_ref[1, rows, :])
            ctx_ref[part, piece, n * BLOCK : (n + 1) * BLOCK, :] = pair.astype(bf16)
        for n in range(ROWS // (2 * BLOCK)):
            rows = rows_at(t * ROWS + 2 * n * BLOCK, BLOCK)
            odd = rows_at(t * ROWS + (2 * n + 1) * BLOCK, BLOCK)
            first = pltpu.roll(res_ref[2, rows, :], HEAD_DIM, 1)
            both = jnp.where(low, first, res_ref[2, odd, :])
            ctx_ref[part, piece, ROWS + n * BLOCK : ROWS + (n + 1) * BLOCK, :] = both.astype(bf16)
        return carry

    lax.fori_loop(0, length // ROWS, pack, 0)


def attend(rand, x, w, b, parts, heads):
    length = x.shape[0]
    randoms = rand.size // (heads * (length // BLOCK - 2))
    vmem = pl.BlockSpec(memory_space=pltpu.VMEM)
    return pl.pallas_call(
        partial(attend_kernel, heads, randoms),
        out_shape=(
            jax.ShapeDtypeStruct((length, heads * SLOT), bf16),
            jax.ShapeDtypeStruct((heads, length, LANES), f32),
            jax.ShapeDtypeStruct((parts, length // parts // ROWS, ROWS * 3 // 2, LANES), bf16),
        ),
        in_specs=[pl.BlockSpec(memory_space=pltpu.SMEM), vmem, vmem, vmem],
        out_specs=(vmem, vmem, vmem),
        compiler_params=pltpu.CompilerParams(vmem_limit_bytes=VMEM_BYTES),
        name="attend",
    )(rand, x, w, b)


def attend_back_kernel(
    heads, randoms, rand_ref, qkv_ref, res_ref, dctx_ref, draw_ref, sums_ref, *scratch
):
    dout, acc = scratch[:heads], scratch[heads:]
    length = qkv_ref.shape[0]
    blocks = length // BLOCK
    last = (blocks - 1) * BLOCK
    per_quarter = dctx_ref.shape[1]

    def unpack(t, carry):
        part, piece = t // per_quarter, t % per_quarter
        lane = lax.broadcasted_iota(jnp.int32, (BLOCK, LANES), 1)
        low = lane < HEAD_DIM
        for n in range(ROWS // BLOCK):
            rows = rows_at(t * ROWS + n * BLOCK, BLOCK)
            pair = dctx_ref[part, piece, n * BLOCK : (n + 1) * BLOCK, :].astype(f32)
            dout[0][rows, :] = jnp.where(low, 0.0, pltpu.roll(pair, HEAD_DIM, 1)).astype(bf16)
            dout[1][rows, :] = jnp.where(low, 0.0, pair).astype(bf16)
        for n in range(ROWS // (2 * BLOCK)):
            rows = rows_at(t * ROWS + 2 * n * BLOCK, BLOCK)
            odd = rows_at(t * ROWS + (2 * n + 1) * BLOCK, BLOCK)
            both = dctx_ref[part, piece, ROWS + n * BLOCK : ROWS + (n + 1) * BLOCK, :].astype(f32)
            dout[2][rows, :] = jnp.where(low, 0.0, pltpu.roll(both, HEAD_DIM, 1)).astype(bf16)
            dout[2][odd, :] = jnp.where(low, 0.0, both).astype(bf16)
        return carry

    lax.fori_loop(0, length // ROWS, unpack, 0)

    step = 256
    for h in range(heads):
        at = h * SLOT
        q = jnp.concatenate(
            [qkv_ref[0:BLOCK, at : at + LANES], qkv_ref[last : last + BLOCK, at : at + LANES]], axis=0
        )
        g = jnp.concatenate([dout[h][0:BLOCK, :], dout[h][last : last + BLOCK, :]], axis=0)
        res = jnp.concatenate([res_ref[h, 0:BLOCK, :], res_ref[h, last : last + BLOCK, :]], axis=0)
        log_total = res[:, 0:1]
        delta = jnp.sum(g.astype(f32) * res, axis=1, keepdims=True)
        both = jnp.concatenate([q, g], axis=0)

        def whole(t, dq, at=at, h=h, both=both, log_total=log_total, delta=delta):
            rows = rows_at(t * step, step)
            kv = qkv_ref[rows, at + LANES : at + SLOT]
            sd = dot_nt(both, kv)
            p = jnp.exp(sd[: 2 * BLOCK] - log_total)
            ds = (p * (sd[2 * BLOCK :] - delta)).astype(bf16)
            acc[h][rows, :] = dot_tn(jnp.concatenate([ds, p.astype(bf16)], axis=0), both)
            return dq + dot(ds, kv)

        dq = lax.fori_loop(0, length // step, whole, jnp.zeros((2 * BLOCK, LANES), f32))
        lane = lax.broadcasted_iota(jnp.int32, (2 * BLOCK, LANES), 1)
        dq = jnp.where(lane < HEAD_DIM, dq, 0.0).astype(bf16)
        draw_ref[0:BLOCK, at : at + LANES] = dq[:BLOCK]
        draw_ref[last : last + BLOCK, at : at + LANES] = dq[BLOCK:]

    def middle(i, carry):
        rows = rows_at(i * BLOCK, BLOCK)
        lane = lax.broadcasted_iota(jnp.int32, (BLOCK, LANES), 1)
        for h in range(heads):
            at = h * SLOT
            kv = listed(qkv_ref, rand_ref, h, i, blocks, randoms, slice(at + LANES, at + SLOT))
            g = dout[h][rows, :]
            res = res_ref[h, rows, :]
            both = jnp.concatenate([qkv_ref[rows, at : at + LANES], g], axis=0)
            delta = jnp.sum(g.astype(f32) * res, axis=1, keepdims=True)
            sd = dot_nt(both, kv)
            p = jnp.exp(mask_globals(sd[:BLOCK], i, blocks) - res[:, 0:1])
            ds = (p * (sd[BLOCK:] - delta)).astype(bf16)
            dkv = dot_tn(jnp.concatenate([ds, p.astype(bf16)], axis=0), both)
            dq = dot(ds, kv)
            draw_ref[rows, at : at + LANES] = jnp.where(lane < HEAD_DIM, dq, 0.0).astype(bf16)
            acc[h][0:BLOCK, :] += dkv[0:BLOCK]
            acc[h][last : last + BLOCK, :] += dkv[BLOCK : 2 * BLOCK]
            near = pl.ds(pl.multiple_of((i - 1) * BLOCK, BLOCK), 3 * BLOCK)
            acc[h][near, :] += dkv[2 * BLOCK : 5 * BLOCK]
            base = (h * (blocks - 2) + i - 1) * randoms
            for r in range(randoms):
                far = rows_at(rand_ref[base + r] * BLOCK, BLOCK)
                acc[h][far, :] += dkv[(5 + r) * BLOCK : (6 + r) * BLOCK]
        return carry

    lax.fori_loop(1, blocks - 1, middle, 0)
    sums_ref[...] = jnp.zeros_like(sums_ref)

    def finish(t, carry):
        rows = rows_at(t * CHUNK, CHUNK)
        for h in range(heads):
            at = h * SLOT
            draw_ref[rows, at + LANES : at + SLOT] = acc[h][rows, :].astype(bf16)
        sums_ref[0:1, :] += jnp.sum(draw_ref[rows, :].astype(f32), axis=0, keepdims=True)
        return carry

    lax.fori_loop(0, length // CHUNK, finish, 0)


def attend_back(rand, qkv, res, dctx, heads):
    length = qkv.shape[0]
    randoms = rand.size // (heads * (length // BLOCK - 2))
    vmem = pl.BlockSpec(memory_space=pltpu.VMEM)
    return pl.pallas_call(
        partial(attend_back_kernel, heads, randoms),
        out_shape=(
            jax.ShapeDtypeStruct((length, heads * SLOT), bf16),
            jax.ShapeDtypeStruct((8, heads * SLOT), f32),
        ),
        in_specs=[pl.BlockSpec(memory_space=pltpu.SMEM), vmem, vmem, vmem],
        out_specs=(vmem, vmem),
        scratch_shapes=[pltpu.VMEM((length, LANES), bf16)] * heads
        + [pltpu.VMEM((length, LANES), f32)] * heads,
        compiler_params=pltpu.CompilerParams(vmem_limit_bytes=VMEM_BYTES),
        name="attend_back",
    )(rand, qkv, res, dctx)


def mean_of(a):
    return jnp.mean(a, axis=1, keepdims=True)


def norm(r):
    center = r - mean_of(r)
    rstd = lax.rsqrt(mean_of(center * center) + EPS)
    return center * rstd, rstd


def norm_back(dn, n, rstd):
    return rstd * (dn - mean_of(dn) - n * mean_of(dn * n))


def rowsum(a):
    return jnp.sum(a, axis=0, keepdims=True)


def chain_kernel(
    groups,
    ctx_ref,
    tok_ref,
    og_ref,
    wo_ref,
    wu_ref,
    wd_ref,
    vec_ref,
    bu_ref,
    out_ref,
    dres_ref,
    dctx_ref,
    mix_ref,
    hid_ref,
    act_ref,
    dpre_ref,
    dffn_ref,
    dproj_ref,
    gvec_ref,
    gbu_ref,
    slope_ref,
    wop_ref,
):
    width = tok_ref.shape[1]
    hidden = wu_ref.shape[1]
    wide = 3 * HEAD_DIM
    step = pl.program_id(0)

    @pl.when(step == 0)
    def _():
        for g in range(groups):
            wop_ref[g * LANES : (g + 1) * LANES, :] = wo_ref[g * wide : g * wide + LANES, :]
            to = groups * LANES + g * HEAD_DIM
            wop_ref[to : to + HEAD_DIM, :] = wo_ref[g * wide + LANES : (g + 1) * wide, :]
        gvec_ref[...] = jnp.zeros_like(gvec_ref)
        gbu_ref[...] = jnp.zeros_like(gbu_ref)

    low = lax.broadcasted_iota(jnp.int32, (BLOCK, LANES), 1) < HEAD_DIM
    for g in range(groups):
        mix_ref[:, g * LANES : (g + 1) * LANES] = ctx_ref[g, 0, :ROWS, :]
    for g in range(0, groups, 2):
        to = groups * LANES + g * HEAD_DIM
        for n in range(ROWS // (2 * BLOCK)):
            at = ROWS + n * BLOCK
            a = ctx_ref[g, 0, at : at + BLOCK, :].astype(f32)
            b = ctx_ref[g + 1, 0, at : at + BLOCK, :].astype(f32)
            even = jnp.where(low, a, pltpu.roll(b, HEAD_DIM, 1))
            odd = jnp.where(low, pltpu.roll(a, HEAD_DIM, 1), b)
            r = 2 * n * BLOCK
            mix_ref[r : r + BLOCK, to : to + LANES] = even.astype(bf16)
            mix_ref[r + BLOCK : r + 2 * BLOCK, to : to + LANES] = odd.astype(bf16)

    bo, g1, s1 = vec_ref[0:1, :], vec_ref[1:2, :], vec_ref[2:3, :]
    bd, g2, s2 = vec_ref[3:4, :], vec_ref[4:5, :], vec_ref[5:6, :]
    n1, rstd1 = norm(tok_ref[...].astype(f32) + dot(mix_ref[...], wop_ref[...]) + bo)
    hid = n1 * g1 + s1
    hid_low = hid.astype(bf16)
    hid_ref[...] = hid_low
    scale = np.sqrt(2.0 / np.pi).astype(np.float32)

    def up(f, carry):
        cols = rows_at(f * CHUNK, CHUNK)
        u = dot(hid_low, wu_ref[:, cols]) + bu_ref[:, cols]
        square = u * u
        t = jnp.tanh(scale * (u + 0.044715 * (u * square)))
        half = 0.5 * (1.0 + t)
        act_ref[:, cols] = (u * half).astype(bf16)
        slope = half + 0.5 * u * (1.0 - t * t) * (scale * (1.0 + (3 * 0.044715) * square))
        slope_ref[:, cols] = slope.astype(bf16)
        return carry

    lax.fori_loop(0, hidden // CHUNK, up, 0)
    n2, rstd2 = norm(hid + dot(act_ref[...], wd_ref[...]) + bd)
    out_ref[...] = (n2 * g2 + s2).astype(bf16)
    og = og_ref[...].astype(f32)
    gvec_ref[4:5, :] += rowsum(og * n2)
    gvec_ref[5:6, :] += rowsum(og)
    dres2 = norm_back(og * g2, n2, rstd2)
    dffn = dres2.astype(bf16)
    dffn_ref[...] = dffn
    gvec_ref[3:4, :] += rowsum(dffn.astype(f32))

    def down_back(f, carry):
        cols = rows_at(f * CHUNK, CHUNK)
        dact = dot_nt(dffn, wd_ref[cols, :])
        dpre = (dact * slope_ref[:, cols].astype(f32)).astype(bf16)
        dpre_ref[:, cols] = dpre
        gbu_ref[0:1, cols] += rowsum(dpre.astype(f32))
        return carry

    lax.fori_loop(0, hidden // CHUNK, down_back, 0)
    dh = dres2 + dot_nt(dpre_ref[...], wu_ref[...])
    gvec_ref[1:2, :] += rowsum(dh * n1)
    gvec_ref[2:3, :] += rowsum(dh)
    dres1 = norm_back(dh * g1, n1, rstd1)
    dres_ref[...] = dres1
    dproj = dres1.astype(bf16)
    dproj_ref[...] = dproj
    gvec_ref[0:1, :] += rowsum(dproj.astype(f32))
    dmix = dot_nt(dproj, wop_ref[...])
    for g in range(groups):
        dctx_ref[g, 0, :ROWS, :] = dmix[:, g * LANES : (g + 1) * LANES].astype(bf16)
    for g in range(0, groups, 2):
        to = groups * LANES + g * HEAD_DIM
        for n in range(ROWS // (2 * BLOCK)):
            at = ROWS + n * BLOCK
            r = 2 * n * BLOCK
            even = dmix[r : r + BLOCK, to : to + LANES]
            odd = dmix[r + BLOCK : r + 2 * BLOCK, to : to + LANES]
            a = jnp.where(low, even, pltpu.roll(odd, HEAD_DIM, 1))
            b = jnp.where(low, pltpu.roll(even, HEAD_DIM, 1), odd)
            dctx_ref[g, 0, at : at + BLOCK, :] = a.astype(bf16)
            dctx_ref[g + 1, 0, at : at + BLOCK, :] = b.astype(bf16)


def chain(ctx, tok, og, wo, wu, wd, vec, bu):
    rows, width = tok.shape
    hidden = wu.shape[1]
    groups = ctx.shape[0]
    once = pl.Buffered(1)

    def tiled(cols):
        return pl.BlockSpec((ROWS, cols), lambda t: (t, 0))

    def fixed(shape):
        return pl.BlockSpec(shape, lambda t: (0, 0), pipeline_mode=once)

    packed = pl.BlockSpec((groups, 1) + ctx.shape[2:], lambda t: (0, t, 0, 0))
    shape = jax.ShapeDtypeStruct
    return pl.pallas_call(
        partial(chain_kernel, groups),
        grid=(rows // ROWS,),
        out_shape=(
            shape((rows, width), bf16),
            shape((rows, width), f32),
            shape(ctx.shape, bf16),
            shape((rows, width), bf16),
            shape((rows, width), bf16),
            shape((rows, hidden), bf16),
            shape((rows, hidden), bf16),
            shape((rows, width), bf16),
            shape((rows, width), bf16),
            shape((8, width), f32),
            shape((8, hidden), f32),
        ),
        in_specs=[
            packed,
            tiled(width),
            tiled(width),
            fixed(wo.shape),
            fixed(wu.shape),
            fixed(wd.shape),
            fixed(vec.shape),
            fixed(bu.shape),
        ],
        out_specs=(
            tiled(width),
            tiled(width),
            packed,
            tiled(width),
            tiled(width),
            tiled(hidden),
            tiled(hidden),
            tiled(width),
            tiled(width),
            pl.BlockSpec((8, width), lambda t: (0, 0)),
            pl.BlockSpec((8, hidden), lambda t: (0, 0)),
        ),
        scratch_shapes=[pltpu.VMEM((ROWS, hidden), bf16), pltpu.VMEM(wo.shape, bf16)],
        compiler_params=pltpu.CompilerParams(vmem_limit_bytes=VMEM_BYTES),
        name="chain",
    )(ctx, tok, og, wo, wu, wd, vec, bu)


MESH = pl.DeviceIdType.MESH


def run_phases(items):
    step = 0
    live = list(items)
    while live:
        after = []
        for first, phases in live:
            if first > step or next(phases, None) is not None:
                after.append((first, phases))
        live = after
        step += 1


class Where:
    def __init__(self):
        c, core, zh, zl = (lax.axis_index(a) for a in ALL)
        self.y, self.x, self.core, self.zh, self.zl = c // 2, c % 2, core, zh, zl
        self.z = zh * 2 + zl
        self.by_x = (self.y * 2 + 1 - self.x, core, zh, zl)
        self.by_y = ((1 - self.y) * 2 + self.x, core, zh, zl)
        self.by_core = (c, 1 - core, zh, zl)
        self.by_zl = (c, core, zh, 1 - zl)
        self.by_zh = (c, core, 1 - zh, zl)
        self.by_mid = (c, core, 1 - zh, 1 - zl)
        self.by_swap = (c, 1 - core, 1 - zh, zl)
        self.by_both = (c, 1 - core, zh, 1 - zl)
        self.inner = zh != zl
        self.stays = core == zh

    def greet(self):
        barrier = pltpu.get_barrier_semaphore()
        others = (self.by_x, self.by_y, self.by_core, self.by_zl)
        others += (self.by_zh, self.by_mid, self.by_swap, self.by_both)
        for other in others:
            pl.semaphore_signal(barrier, inc=1, device_id=other, device_id_type=MESH)
        pl.semaphore_wait(barrier, len(others))


class Copies:
    def __init__(self, send, recv, local):
        self.send, self.recv, self.local_sems = send, recv, local
        self.n = self.m = 0

    def remote(self, src, dst, device):
        n = self.n
        self.n += 1
        return pltpu.make_async_remote_copy(
            src_ref=src,
            dst_ref=dst,
            send_sem=self.send.at[n],
            recv_sem=self.recv.at[n],
            device_id=device,
            device_id_type=MESH,
        )

    def local(self, src, dst):
        m = self.m
        self.m += 1
        return pltpu.make_async_copy(src, dst, self.local_sems.at[m])


def gather_item(me, copies, shard, full, cols, x_first):
    y, x, core, zh, zl = me.y, me.x, me.core, me.zh, me.zl
    mine = shard.at[:, cols]
    own = copies.local(mine, full.at[y, x, core, me.z, :, cols])
    first = copies.remote(mine, full.at[y, x, core, me.z, :, cols], me.by_zl)
    own.start()
    first.start()
    yield 1
    own.wait()
    first.wait()
    pair = full.at[y, x, core, pl.ds(zh * 2, 2), :, cols]
    pair_far = full.at[y, x, core, pl.ds((1 - zh) * 2, 2), :, cols]
    middle = copies.remote(pair, pair, me.by_mid)
    onward = copies.remote(pair_far, pair_far, me.by_zl)

    @pl.when(me.inner)
    def _():
        middle.start()

    yield 1

    @pl.when(me.inner)
    def _():
        middle.wait()
        onward.start()

    yield 1

    @pl.when(me.inner)
    def _():
        onward.wait_send()

    @pl.when(jnp.logical_not(me.inner))
    def _():
        onward.wait_recv()

    line = full.at[y, x, core, :, :, cols]
    near = copies.remote(line, line, me.by_x if x_first else me.by_y)
    near.start()
    across = [copies.remote(line, line, me.by_core)]
    across[0].start()
    yield 1
    near.wait()
    if x_first:
        block = full.at[y, :, core, :, :, cols]
        got = full.at[y, 1 - x, core, :, :, cols]
        rest = full.at[1 - y, :, core, :, :, cols]
    else:
        block = full.at[:, x, core, :, :, cols]
        got = full.at[1 - y, x, core, :, :, cols]
        rest = full.at[:, 1 - x, core, :, :, cols]
    far = copies.remote(block, block, me.by_y if x_first else me.by_x)
    far.start()
    across.append(copies.remote(got, got, me.by_core))
    across[1].start()
    yield 1
    far.wait()
    across.append(copies.remote(rest, rest, me.by_core))
    across[2].start()
    yield 1
    for copy in across:
        copy.wait()


def tokens_item(me, copies, tok, x_all, piece):
    place = me.core * 2 + me.zl
    there = (1 - me.core) * 2 + me.zl
    out = copies.remote(tok.at[piece], x_all.at[there, piece], me.by_swap)
    keep = copies.local(tok.at[piece], x_all.at[place, piece])

    @pl.when(me.stays)
    def _():
        keep.start()

    @pl.when(jnp.logical_not(me.stays))
    def _():
        out.start()

    yield 1

    @pl.when(me.stays)
    def _():
        keep.wait()

    @pl.when(jnp.logical_not(me.stays))
    def _():
        out.wait()

    held = x_all.at[place, piece]
    along = copies.remote(held, held, me.by_zl)
    along.start()
    over = copies.remote(held, held, me.by_core)
    over.start()
    yield 1
    along.wait()
    came = x_all.at[me.core * 2 + 1 - me.zl, piece]
    onto = copies.remote(came, came, me.by_core)
    onto.start()
    yield 1
    over.wait()
    onto.wait()


def exchange_item(me, copies, src, dst):
    out = copies.remote(src, dst, me.by_swap)
    keep = copies.local(src, dst)

    @pl.when(me.stays)
    def _():
        keep.start()

    @pl.when(jnp.logical_not(me.stays))
    def _():
        out.start()

    yield 1

    @pl.when(me.stays)
    def _():
        keep.wait()

    @pl.when(jnp.logical_not(me.stays))
    def _():
        out.wait()


PIECES = 4


def gather_kernel(
    tok, og, qkv, w_out, up, down, small, x_all, og_all, qkv_all, out_all, up_all, down_all, small_all, *sems
):
    me = Where()
    me.greet()
    copies = Copies(*sems)
    items = []

    def halves(first, shard, full):
        half = shard.shape[1] // 2
        for n in range(2):
            items.append((first, gather_item(me, copies, shard, full, slice(n * half, (n + 1) * half), n == 0)))

    items.append((0, gather_item(me, copies, small, small_all, slice(0, LANES), True)))
    for piece in range(PIECES):
        items.append((piece, tokens_item(me, copies, tok, x_all, piece)))
        if piece == 0:
            halves(0, qkv, qkv_all)
    halves(1, w_out, out_all)
    halves(2, up, up_all)
    halves(3, down, down_all)
    items.append((4, exchange_item(me, copies, og, og_all)))
    items.sort(key=lambda item: item[0])
    run_phases(items)


def gather(tok, og, mats, small, members):
    rows, width = tok.shape
    hbm = pl.BlockSpec(memory_space=pltpu.HBM)
    shape = jax.ShapeDtypeStruct
    tok = tok.reshape(PIECES, rows // PIECES, width)
    outs = [shape((members,) + tok.shape, bf16), shape(og.shape, bf16)]
    outs += [shape((2, 2, 2, 4) + a.shape, bf16) for a in (*mats, small)]
    return pl.pallas_call(
        gather_kernel,
        out_shape=tuple(outs),
        in_specs=[hbm] * 7,
        out_specs=(hbm,) * 7,
        scratch_shapes=[
            pltpu.SemaphoreType.DMA((112,)),
            pltpu.SemaphoreType.DMA((112,)),
            pltpu.SemaphoreType.DMA((16,)),
        ],
        compiler_params=pltpu.CompilerParams(
            collective_id=0, has_side_effects=True, vmem_limit_bytes=VMEM_BYTES
        ),
        name="gather",
    )(tok, og, *mats, small)


def add_rows(dst, a, b, rows):
    step = next(n for n in (48, 32, 24, 16, 8) if rows % n == 0)

    def body(t, carry):
        at = rows_at(t * step, step)
        dst[at, :] = (a[at, :].astype(f32) + b[at, :].astype(f32)).astype(dst.dtype)
        return carry

    lax.fori_loop(0, rows // step, body, 0)


def scatter_item(me, copies, src, cols, acc, from_core, from_first, from_second, from_zh, part, from_zl, out, x_first):
    y, x, core, zh, zl = me.y, me.x, me.core, me.zh, me.zl
    rows = acc.shape[2]
    own = copies.local(src.at[:, :, core, :, cols], acc)
    over = copies.remote(src.at[:, :, 1 - core, :, cols], from_core, me.by_core)
    own.start()
    over.start()
    yield 1
    own.wait()
    over.wait()
    for a in range(2):
        for b in range(2):
            add_rows(acc.at[a, b], acc.at[a, b], from_core.at[a, b], rows)
    if x_first:
        first = copies.remote(acc.at[:, 1 - x], from_first, me.by_x)
    else:
        first = copies.remote(acc.at[1 - y], from_first, me.by_y)
    first.start()
    yield 1
    first.wait()
    for a in range(2):
        block = acc.at[a, x] if x_first else acc.at[y, a]
        add_rows(block, block, from_first.at[a], rows)
    if x_first:
        second = copies.remote(acc.at[1 - y, x], from_second, me.by_y)
    else:
        second = copies.remote(acc.at[y, 1 - x], from_second, me.by_x)
    second.start()
    yield 1
    second.wait()
    block = acc.at[y, x]
    add_rows(block, block, from_second, rows)
    half = rows // 2
    third = copies.remote(block.at[rows_at((1 - zh) * half, half)], from_zh, me.by_zh)
    third.start()
    yield 1
    third.wait()
    add_rows(part, block.at[rows_at(zh * half, half)], from_zh, half)
    last = half // 2
    fourth = copies.remote(part.at[rows_at((1 - zl) * last, last)], from_zl, me.by_zl)
    fourth.start()
    yield 1
    fourth.wait()
    add_rows(out, part.at[rows_at(zl * last, last)], from_zl, last)


def scatter_buffers(rows, cols, kind):
    return [
        pltpu.VMEM((2, 2, rows, cols), kind),
        pltpu.VMEM((2, 2, rows, cols), kind),
        pltpu.VMEM((2, rows, cols), kind),
        pltpu.VMEM((rows, cols), kind),
        pltpu.VMEM((rows // 2, cols), kind),
        pltpu.VMEM((rows // 2, cols), f32),
        pltpu.VMEM((rows // 4, cols), f32),
    ]


def own_columns_item(me, copies, src, acc, from_x, from_y, from_zh, part, out):
    y, x, core, zh, zl = me.y, me.x, me.core, me.zh, me.zl
    rows = src.shape[4]
    keep = copies.local(src.at[:, x], acc)
    first = copies.remote(src.at[:, 1 - x], from_x, me.by_x)
    keep.start()
    first.start()
    yield 1
    keep.wait()
    first.wait()
    for a in range(2):
        for b in range(2):
            for c in range(2):
                add_rows(acc.at[a, b, c], acc.at[a, b, c], from_x.at[a, b, c], rows)
    second = copies.remote(acc.at[1 - y], from_y, me.by_y)
    second.start()
    yield 1
    second.wait()
    for b in range(2):
        for c in range(2):
            block = acc.at[y, b, c]
            add_rows(block, block, from_y.at[b, c], rows)
    third = copies.remote(acc.at[y, :, 1 - zh], from_zh, me.by_zh)
    third.start()
    yield 1
    third.wait()
    half = rows // 2
    for b in range(2):
        add_rows(part.at[b], acc.at[y, b, zh], from_zh.at[b], rows)
    place = core * 2 + zl
    mine = rows_at(zl * half, half)
    other = rows_at((1 - zl) * half, half)
    keep = copies.local(part.at[core, mine], out.at[place])
    keep.start()
    moves = [
        copies.remote(part.at[core, other], out.at[place], me.by_zl),
        copies.remote(part.at[1 - core, mine], out.at[place], me.by_core),
        copies.remote(part.at[1 - core, other], out.at[place], me.by_both),
    ]
    for move in moves:
        move.start()
    yield 1
    keep.wait()
    for move in moves:
        move.wait()


def input_grad_item(me, copies, dx, dres, piece, acc, from_core, from_zl, res, send, out):
    core, zl = me.core, me.zl
    rows = acc.shape[1]
    keep = copies.local(dx.at[core, :, piece], acc)
    more = copies.local(dres.at[piece], res)
    over = copies.remote(dx.at[1 - core, :, piece], from_core, me.by_core)
    keep.start()
    more.start()
    over.start()
    yield 1
    keep.wait()
    over.wait()
    add_rows(acc.at[1 - zl], acc.at[1 - zl], from_core.at[1 - zl], rows)
    along = copies.remote(acc.at[1 - zl], from_zl, me.by_zl)
    along.start()
    add_rows(acc.at[zl], acc.at[zl], from_core.at[zl], rows)
    more.wait()
    add_rows(res, res, acc.at[zl], rows)
    yield 1
    along.wait()
    add_rows(send, res, from_zl, rows)
    yield from exchange_item(me, copies, send, out.at[piece])


SPLITS = ((0, 2), (1, 4), (2, 1), (3, 1))


def scatter_kernel(*refs):
    down, up, proj, vecs, qkv, dx, dres = refs[:7]
    outs = refs[7:13]
    sems, scratch = refs[13:16], list(refs[16:])
    me = Where()
    me.greet()
    copies = Copies(*sems)
    items = []

    def take(n):
        got = scratch[:n]
        del scratch[:n]
        return got

    for piece in range(PIECES):
        items.append((piece, input_grad_item(me, copies, dx, dres, piece, *take(5), outs[5])))
    items.append((0, own_columns_item(me, copies, qkv, *take(5), outs[4])))
    step = 0
    for n, splits in SPLITS:
        src = refs[n]
        width = src.shape[4] // splits
        for part in range(splits):
            cols = slice(part * width, (part + 1) * width)
            item = scatter_item(me, copies, src, cols, *take(7), outs[n].at[:, cols], step % 2 == 0)
            items.append((step // 2, item))
            step += 1
    items.sort(key=lambda item: item[0])
    run_phases(items)


def scatter(down, up, proj, vecs, qkv, dx, dres):
    hbm = pl.BlockSpec(memory_space=pltpu.HBM)
    vmem = pl.BlockSpec(memory_space=pltpu.VMEM)
    shape = jax.ShapeDtypeStruct
    grads = (down, up, proj, vecs)
    outs = [shape((a.shape[3] // 4, a.shape[4]), f32) for a in grads]
    rows, cols = qkv.shape[4:]
    outs.append(shape((4, rows // 2, cols), f32))
    outs.append(shape(dres.shape, bf16))
    buffers = []
    for _ in range(PIECES):
        tile = dres.shape[1:]
        buffers += [
            pltpu.VMEM((2,) + tile, bf16),
            pltpu.VMEM((2,) + tile, bf16),
            pltpu.VMEM(tile, bf16),
            pltpu.VMEM(tile, f32),
            pltpu.VMEM(tile, bf16),
        ]
    buffers += [
        pltpu.VMEM((2, 2, 2, rows, cols), bf16),
        pltpu.VMEM((2, 2, 2, rows, cols), bf16),
        pltpu.VMEM((2, 2, rows, cols), bf16),
        pltpu.VMEM((2, rows, cols), bf16),
        pltpu.VMEM((2, rows, cols), f32),
    ]
    for n, splits in SPLITS:
        a = grads[n]
        for _ in range(splits):
            buffers += scatter_buffers(a.shape[3], a.shape[4] // splits, a.dtype)
    return pl.pallas_call(
        scatter_kernel,
        out_shape=tuple(outs),
        in_specs=[hbm] * 7,
        out_specs=(vmem,) * 5 + (hbm,),
        scratch_shapes=[
            pltpu.SemaphoreType.DMA((80,)),
            pltpu.SemaphoreType.DMA((80,)),
            pltpu.SemaphoreType.DMA((32,)),
        ]
        + buffers,
        compiler_params=pltpu.CompilerParams(
            collective_id=1, has_side_effects=True, vmem_limit_bytes=VMEM_BYTES
        ),
        name="scatter",
    )(down, up, proj, vecs, qkv, dx, dres)


def per_device(
    tokens,
    qkv_weight,
    query_value_bias,
    out_weight,
    out_bias,
    norm1_gain,
    norm1_bias,
    up_weight,
    up_bias,
    down_weight,
    down_bias,
    norm2_gain,
    norm2_bias,
    rand_blocks,
    out_grad,
):
    members = lax.axis_size(GROUP)
    devices = lax.axis_size(ALL)
    swap = [(0, 0), (1, 2), (2, 1), (3, 3)]

    def move(a):
        return lax.ppermute(a, ("core", "zh"), swap)

    rand = move(rand_blocks[0])
    heads = rand.shape[0]
    rows, width = tokens.shape[1:]
    cols = heads * HEAD_DIM
    group = lax.axis_index(GROUP)
    own = width // devices
    small = jnp.concatenate(
        [
            query_value_bias[0],
            query_value_bias[1],
            out_bias,
            norm1_gain,
            norm1_bias,
            down_bias,
            norm2_gain,
            norm2_bias,
            up_bias,
        ]
    )
    mats = (qkv_weight, out_weight, up_weight, down_weight)
    direct = lax.axis_size("c") == 4 and members == 4 and own % 8 == 0
    if direct:
        count = small.shape[0]
        padded = jnp.pad(small, (0, 16 * LANES - count)).reshape(16, LANES)
        x, og, *full, small = gather(tokens[0], out_grad[0], mats, padded, members)
        x = x.reshape(members * rows, width)
        tok = lax.dynamic_slice_in_dim(x, group * rows, rows, axis=0)
        w_qkv, w_out, w_up, w_down = (a.reshape(-1, a.shape[-1]) for a in full)
        small = small.reshape(devices, -1)[:, :count].astype(f32)
    else:
        tok = move(tokens[0])
        og = move(out_grad[0])
        x = lax.all_gather(tok, GROUP, axis=0, tiled=True)
        w_qkv, w_out, w_up, w_down = (lax.all_gather(a, ALL, axis=0, tiled=True) for a in mats)
        small = lax.all_gather(small, ALL, axis=0).astype(f32)
    vecs = jnp.transpose(small[:, : 8 * own].reshape(devices, 8, own), (1, 0, 2)).reshape(8, width)
    bias_up = small[:, 8 * own :].reshape(1, -1)

    def lay_out(a):
        a = a.reshape(a.shape[:-2] + (3, heads, HEAD_DIM))
        q, k, v = a[..., 0, :, :], a[..., 1, :, :], a[..., 2, :, :]
        q = q * jnp.asarray(HEAD_DIM**-0.5, a.dtype)
        laid = jnp.stack([q, jnp.zeros_like(q), k, v], axis=-2)
        return laid.reshape(laid.shape[:-3] + (heads * SLOT,))

    w_own = lax.dynamic_slice_in_dim(
        w_qkv.reshape(width, 3, members, cols), group, 1, axis=2
    ).reshape(width, 3, cols)
    w_own = lay_out(w_own)
    bias3 = jnp.stack([vecs[0], jnp.zeros_like(vecs[0]), vecs[1]]).reshape(3, members, cols)
    b_own = lay_out(lax.dynamic_slice_in_dim(bias3, group, 1, axis=1).reshape(1, 3, cols))
    rand_flat = rand.reshape(-1)

    qkv, res, ctx_send = attend(rand_flat, x, w_own, b_own, members, heads)
    ctx = lax.all_to_all(ctx_send, GROUP, split_axis=0, concat_axis=0, tiled=True)
    chain_vecs = jnp.concatenate([vecs[2:8], jnp.zeros((2, width), f32)], axis=0)
    out, dres1, dctx_send, mix, hid, act, dpre, dffn, dproj, gvec, gbu = chain(
        ctx, tok, og, w_out, w_up, w_down, chain_vecs, bias_up
    )
    dctx = lax.all_to_all(dctx_send, GROUP, split_axis=0, concat_axis=0, tiled=True)
    out = move(out)

    g_down = dot_tn(act, dffn).astype(bf16)
    g_up = dot_tn(hid, dpre).astype(bf16)
    g_mix = dot_tn(mix, dproj).astype(bf16)
    pairs = g_mix[: members * LANES].reshape(members, LANES, width)
    thirds = g_mix[members * LANES :].reshape(members, HEAD_DIM, width)
    g_out = jnp.concatenate([pairs, thirds], axis=1).reshape(width, width)

    draw, sums = attend_back(rand_flat, qkv, res, dctx, heads)
    dx = dot_nt(draw, w_own).astype(bf16)
    g_qkv = dot_tn(x, draw)

    def strip(a):
        a = a.reshape(a.shape[:-1] + (heads, 4, HEAD_DIM))
        q, k, v = a[..., 0, :] * (HEAD_DIM**-0.5), a[..., 2, :], a[..., 3, :]
        return jnp.stack([q, k, v], axis=-3).reshape(a.shape[:-3] + (3, cols))

    col_sums = strip(sums[0:1])[0]
    pair = jnp.stack([col_sums[0], col_sums[2]]).reshape(2, 1, cols)
    mine = (jnp.arange(members) == group)[None, :, None]
    pair = jnp.where(mine, pair, 0.0).reshape(2, width)
    vec_grads = jnp.concatenate([pair, gvec[0:6]], axis=0).reshape(8, devices, own)
    vec_grads = jnp.transpose(vec_grads, (1, 0, 2)).reshape(devices, 8 * own)
    vec_grads = jnp.concatenate([vec_grads, gbu[0].reshape(devices, -1)], axis=1)
    count = vec_grads.shape[1]

    if direct:
        lines = 8
        padded = jnp.pad(vec_grads, ((0, 0), (0, lines * LANES - count)))
        g_down, g_up, g_out, vec_grads, g_qkv, input_grad = scatter(
            g_down.reshape(2, 2, 2, -1, width),
            g_up.reshape(2, 2, 2, -1, g_up.shape[1]),
            g_out.reshape(2, 2, 2, -1, width),
            padded.reshape(2, 2, 2, 4 * lines, LANES),
            g_qkv.astype(bf16).reshape(2, 2, 2, 2, 2 * own, -1),
            dx.reshape(2, 2, PIECES, -1, width),
            dres1.reshape(PIECES, -1, width),
        )
        vec_grads = vec_grads.reshape(-1)[:count]
        input_grad = input_grad.reshape(rows, width).astype(f32)
        g_qkv = strip(g_qkv)
    else:

        def reduce(a):
            return lax.psum_scatter(a, ALL, scatter_dimension=0, tiled=True).astype(f32)

        g_down, g_up, g_out, vec_grads = reduce(g_down), reduce(g_up), reduce(g_out), reduce(vec_grads)[0]
        dx = lax.psum_scatter(dx, GROUP, scatter_dimension=0, tiled=True)
        input_grad = move((dres1 + dx.astype(f32)).astype(bf16)).astype(f32)
        g_qkv = strip(g_qkv).reshape(-1, 2, 2, members // 2, own, 3 * cols)
        g_qkv = jnp.transpose(g_qkv, (0, 2, 1, 3, 4, 5)).reshape(-1, members, own, 3 * cols)
        g_qkv = g_qkv.reshape(-1, 3 * cols).astype(bf16)
        g_qkv = lax.psum_scatter(g_qkv, REST, scatter_dimension=0, tiled=True)
        g_qkv = g_qkv.reshape(members, own, 3 * cols)
        g_qkv = lax.all_to_all(g_qkv, GROUP, split_axis=0, concat_axis=0, tiled=True).astype(f32)
    g_qkv = jnp.transpose(g_qkv.reshape(members, own, 3, cols), (1, 2, 0, 3)).reshape(own, -1)
    v8 = vec_grads[: 8 * own].reshape(8, own)
    return (
        out[None],
        input_grad[None],
        g_qkv,
        v8[0:2],
        g_out,
        v8[2],
        v8[3],
        v8[4],
        g_up,
        vec_grads[8 * own :],
        g_down,
        v8[5],
        v8[6],
        v8[7],
    )


def solution(mesh):
    dp, sp = mesh.shape["dp"], mesh.shape["sp"]
    fine = Mesh(mesh.devices.reshape(dp // 2, 2, 2, sp // 2), ALL)
    dp, sp = ("c", "core"), ("zh", "zl")
    act = P(dp, sp, None)
    mat = P(ALL, None)
    pair = P(None, ALL)
    vec = P(ALL)
    rand = P(dp, sp, None, None)
    return jax.shard_map(
        per_device,
        mesh=fine,
        in_specs=(act, mat, pair, mat, vec, vec, vec, mat, vec, mat, vec, vec, vec, rand, act),
        out_specs=(act, act, mat, pair, mat, vec, vec, vec, mat, vec, mat, vec, vec, vec),
        check_vma=False,
    )
```

```python
from functools import partial

import jax
import jax.numpy as jnp
import numpy as np
from jax import lax
from jax.experimental import pallas as pl
from jax.experimental.pallas import tpu as pltpu
from jax.sharding import Mesh
from jax.sharding import PartitionSpec as P

HEAD_DIM = 64
BLOCK = 64
LANES = 128
SLOT = 4 * HEAD_DIM
EPS = 1e-05
MASKED = -1e30
ALL = ("c", "core", "zh", "zl")
GROUP = ("core", "zl")
REST = ("c", "zh")
CHUNK = 512
ROWS = 256
PAIR = 2
PAIR_BACK = 2
VMEM_BYTES = 60 * 1024 * 1024

f32 = jnp.float32
bf16 = jnp.bfloat16
NT = (((1,), (1,)), ((), ()))
TN = (((0,), (0,)), ((), ()))


def dot(a, b):
    return jnp.dot(a, b, preferred_element_type=f32)


def dot_nt(a, b):
    return lax.dot_general(a, b, NT, preferred_element_type=f32)


def dot_tn(a, b):
    return lax.dot_general(a, b, TN, preferred_element_type=f32)


def rows_at(start, size):
    return pl.ds(pl.multiple_of(start, size), size)


def listed(ref, rand_ref, head, i, blocks, randoms):
    cols = slice(head * SLOT + LANES, head * SLOT + SLOT)
    near = jnp.clip(i - 1, 0, blocks - 3)
    parts = [ref[0, :, cols], ref[blocks - 1, :, cols]]
    parts += [ref[near + n, :, cols] for n in range(3)]
    base = (head * (blocks - 2) + near) * randoms
    parts += [ref[rand_ref[base + r], :, cols] for r in range(randoms)]
    return jnp.concatenate(parts, axis=0)


def keys_values(ref, head, t, size):
    cols = slice(head * SLOT + LANES, head * SLOT + SLOT)
    return ref[pl.ds(t * (size // BLOCK), size // BLOCK), :, cols].reshape(size, LANES)


def mask_globals(s, i, blocks):
    lane = lax.broadcasted_iota(jnp.int32, (BLOCK, LANES), 1)
    low = lane < BLOCK
    dead = (low & (i == 1)) | (~low & (i == blocks - 2))
    return jnp.concatenate([jnp.where(dead, MASKED, s[:, :LANES]), s[:, LANES:]], axis=1)


def middle_blocks(qkv_ref, rand_ref, res_ref, first, heads, randoms, blocks):
    lane = lax.broadcasted_iota(jnp.int32, (BLOCK, LANES), 1)
    work = [(first + n, h) for n in range(PAIR) for h in range(heads)]
    kvs = [listed(qkv_ref, rand_ref, h, i, blocks, randoms) for i, h in work]
    qs = [qkv_ref[i, :, h * SLOT : h * SLOT + LANES] for i, h in work]
    ss = [mask_globals(dot_nt(q, kv), i, blocks) for q, kv, (i, h) in zip(qs, kvs, work)]
    tops = [jnp.max(s, axis=1, keepdims=True) for s in ss]
    es = [jnp.exp(s - top) for s, top in zip(ss, tops)]
    totals = [jnp.sum(e, axis=1, keepdims=True) for e in es]
    os = [dot(e.astype(bf16), kv) for e, kv in zip(es, kvs)]
    for o, top, total, (i, h) in zip(os, tops, totals, work):
        both = jnp.where(lane < HEAD_DIM, top + jnp.log(total), o / total)
        res_ref[h, rows_at(i * BLOCK, BLOCK), :] = both


def global_blocks(qkv_ref, heads, length):
    last = length // BLOCK - 1

    def ends(h):
        cols = slice(h * SLOT, h * SLOT + LANES)
        return jnp.concatenate([qkv_ref[0, :, cols], qkv_ref[last, :, cols]], axis=0)

    qs = [ends(h) for h in range(heads)]

    def whole(t, carry):
        kvs = [keys_values(qkv_ref, h, t, CHUNK) for h in range(heads)]
        ss = [dot_nt(q, kv) for q, kv in zip(qs, kvs)]
        news = [jnp.maximum(c[0], jnp.max(s, axis=1, keepdims=True)) for c, s in zip(carry, ss)]
        fades = [jnp.exp(c[0] - new) for c, new in zip(carry, news)]
        es = [jnp.exp(s - new) for s, new in zip(ss, news)]
        sums = [jnp.sum(e, axis=1, keepdims=True) for e in es]
        os = [dot(e.astype(bf16), kv) for e, kv in zip(es, kvs)]
        return tuple(
            (new, c[1] * fade + total, c[2] * fade + o)
            for c, new, fade, total, o in zip(carry, news, fades, sums, os)
        )

    start = (
        jnp.full((2 * BLOCK, 1), MASKED, f32),
        jnp.zeros((2 * BLOCK, 1), f32),
        jnp.zeros((2 * BLOCK, LANES), f32),
    )
    done = lax.fori_loop(0, length // CHUNK, whole, (start,) * heads)
    lane = lax.broadcasted_iota(jnp.int32, (2 * BLOCK, LANES), 1)
    return [jnp.where(lane < HEAD_DIM, top + jnp.log(total), acc / total) for top, total, acc in done]


def pack_rows(res_ref, ctx_ref, start, part, piece):
    low = lax.broadcasted_iota(jnp.int32, (BLOCK, LANES), 1) < HEAD_DIM
    for n in range(ROWS // BLOCK):
        rows = rows_at(start + n * BLOCK, BLOCK)
        first = pltpu.roll(res_ref[0, rows, :], HEAD_DIM, 1)
        pair = jnp.where(low, first, res_ref[1, rows, :])
        ctx_ref[part, piece, n * BLOCK : (n + 1) * BLOCK, :] = pair.astype(bf16)
    for n in range(ROWS // (2 * BLOCK)):
        rows = rows_at(start + 2 * n * BLOCK, BLOCK)
        odd = rows_at(start + (2 * n + 1) * BLOCK, BLOCK)
        first = pltpu.roll(res_ref[2, rows, :], HEAD_DIM, 1)
        both = jnp.where(low, first, res_ref[2, odd, :])
        ctx_ref[part, piece, ROWS + n * BLOCK : ROWS + (n + 1) * BLOCK, :] = both.astype(bf16)


def attend_kernel(heads, randoms, rand_ref, x_ref, w_ref, b_ref, qkv_ref, res_ref, ctx_ref):
    length = x_ref.shape[0]
    blocks = length // BLOCK

    def project(t, carry):
        raw = dot(x_ref[rows_at(t * CHUNK, CHUNK), :], w_ref[...]) + b_ref[...]
        step = CHUNK // BLOCK
        qkv_ref[pl.ds(t * step, step)] = raw.astype(bf16).reshape(step, BLOCK, raw.shape[1])
        return carry

    lax.fori_loop(0, length // CHUNK, project, 0)

    def middle(t, carry):
        middle_blocks(qkv_ref, rand_ref, res_ref, t * PAIR, heads, randoms, blocks)
        return carry

    lax.fori_loop(0, blocks // PAIR, middle, 0)
    for h, both in enumerate(global_blocks(qkv_ref, heads, length)):
        res_ref[h, 0:BLOCK, :] = both[:BLOCK]
        res_ref[h, length - BLOCK : length, :] = both[BLOCK:]
    per_quarter = ctx_ref.shape[1]

    def pack(t, carry):
        pack_rows(res_ref, ctx_ref, t * ROWS, t // per_quarter, t % per_quarter)
        return carry

    lax.fori_loop(0, length // ROWS, pack, 0)


def attend(rand, x, w, b, parts, heads):
    length = x.shape[0]
    randoms = rand.size // (heads * (length // BLOCK - 2))
    vmem = pl.BlockSpec(memory_space=pltpu.VMEM)
    return pl.pallas_call(
        partial(attend_kernel, heads, randoms),
        out_shape=(
            jax.ShapeDtypeStruct((length // BLOCK, BLOCK, heads * SLOT), bf16),
            jax.ShapeDtypeStruct((heads, length, LANES), f32),
            jax.ShapeDtypeStruct((parts, length // parts // ROWS, ROWS * 3 // 2, LANES), bf16),
        ),
        in_specs=[pl.BlockSpec(memory_space=pltpu.SMEM), vmem, vmem, vmem],
        out_specs=(vmem, vmem, vmem),
        compiler_params=pltpu.CompilerParams(vmem_limit_bytes=VMEM_BYTES),
        name="attend",
    )(rand, x, w, b)


def attend_back_kernel(
    heads, randoms, rand_ref, qkv_ref, res_ref, dctx_ref, draw_ref, sums_ref, *scratch
):
    dout, acc = scratch[:heads], scratch[heads:]
    blocks = qkv_ref.shape[0]
    length = blocks * BLOCK
    last = (blocks - 1) * BLOCK
    per_quarter = dctx_ref.shape[1]

    def unpack(t, carry):
        part, piece = t // per_quarter, t % per_quarter
        lane = lax.broadcasted_iota(jnp.int32, (BLOCK, LANES), 1)
        low = lane < HEAD_DIM
        for n in range(ROWS // BLOCK):
            rows = rows_at(t * ROWS + n * BLOCK, BLOCK)
            pair = dctx_ref[part, piece, n * BLOCK : (n + 1) * BLOCK, :].astype(f32)
            dout[0][rows, :] = jnp.where(low, 0.0, pltpu.roll(pair, HEAD_DIM, 1)).astype(bf16)
            dout[1][rows, :] = jnp.where(low, 0.0, pair).astype(bf16)
        for n in range(ROWS // (2 * BLOCK)):
            rows = rows_at(t * ROWS + 2 * n * BLOCK, BLOCK)
            odd = rows_at(t * ROWS + (2 * n + 1) * BLOCK, BLOCK)
            both = dctx_ref[part, piece, ROWS + n * BLOCK : ROWS + (n + 1) * BLOCK, :].astype(f32)
            dout[2][rows, :] = jnp.where(low, 0.0, pltpu.roll(both, HEAD_DIM, 1)).astype(bf16)
            dout[2][odd, :] = jnp.where(low, 0.0, both).astype(bf16)
        return carry

    lax.fori_loop(0, length // ROWS, unpack, 0)

    step = 256

    def ends(ref, cols):
        return jnp.concatenate([ref[0:BLOCK, cols], ref[last : last + BLOCK, cols]], axis=0)

    every = slice(0, LANES)
    gs = [ends(dout[h], every) for h in range(heads)]
    reses = [ends(res_ref.at[h], every) for h in range(heads)]
    alls = [
        jnp.concatenate(
            [qkv_ref[n, :, h * SLOT : h * SLOT + LANES] for n in (0, blocks - 1)] + [gs[h]], axis=0
        )
        for h in range(heads)
    ]
    logs = [res[:, 0:1] for res in reses]
    deltas = [jnp.sum(g.astype(f32) * res, axis=1, keepdims=True) for g, res in zip(gs, reses)]

    def whole(t, dqs):
        rows = rows_at(t * step, step)
        kvs = [keys_values(qkv_ref, h, t, step) for h in range(heads)]
        sds = [dot_nt(both, kv) for both, kv in zip(alls, kvs)]
        ps = [jnp.exp(sd[: 2 * BLOCK] - log) for sd, log in zip(sds, logs)]
        dss = [(p * (sd[2 * BLOCK :] - d)).astype(bf16) for p, sd, d in zip(ps, sds, deltas)]
        dkvs = [
            dot_tn(jnp.concatenate([ds, p.astype(bf16)], axis=0), both)
            for ds, p, both in zip(dss, ps, alls)
        ]
        news = tuple(dq + dot(ds, kv) for dq, ds, kv in zip(dqs, dss, kvs))
        for h in range(heads):
            acc[h][rows, :] = dkvs[h]
        return news

    dqs = lax.fori_loop(
        0, length // step, whole, (jnp.zeros((2 * BLOCK, LANES), f32),) * heads
    )
    for h in range(heads):
        cols = slice(h * SLOT, h * SLOT + LANES)
        lane = lax.broadcasted_iota(jnp.int32, (2 * BLOCK, LANES), 1)
        dq = jnp.where(lane < HEAD_DIM, dqs[h], 0.0).astype(bf16)
        draw_ref[0:BLOCK, cols] = dq[:BLOCK]
        draw_ref[last : last + BLOCK, cols] = dq[BLOCK:]

    def middle(t, carry):
        lane = lax.broadcasted_iota(jnp.int32, (BLOCK, LANES), 1)
        work = [(1 + t * PAIR_BACK + n, h) for n in range(PAIR_BACK) for h in range(heads)]
        kvs = [listed(qkv_ref, rand_ref, h, i, blocks, randoms) for i, h in work]
        places = [(rows_at(i * BLOCK, BLOCK), slice(h * SLOT, h * SLOT + LANES)) for i, h in work]
        gs = [dout[h][rows, :] for (rows, _), (_, h) in zip(places, work)]
        reses = [res_ref[h, rows, :] for (rows, _), (_, h) in zip(places, work)]
        alls = [
            jnp.concatenate([qkv_ref[i, :, cols], g], axis=0)
            for (_, cols), (i, _), g in zip(places, work, gs)
        ]
        sds = [dot_nt(both, kv) for both, kv in zip(alls, kvs)]
        deltas = [jnp.sum(g.astype(f32) * res, axis=1, keepdims=True) for g, res in zip(gs, reses)]
        ps = [
            jnp.exp(mask_globals(sd[:BLOCK], i, blocks) - res[:, 0:1])
            for sd, res, (i, h) in zip(sds, reses, work)
        ]
        dss = [(p * (sd[BLOCK:] - d)).astype(bf16) for p, sd, d in zip(ps, sds, deltas)]
        dkvs = [
            dot_tn(jnp.concatenate([ds, p.astype(bf16)], axis=0), both)
            for ds, p, both in zip(dss, ps, alls)
        ]
        dqs = [dot(ds, kv) for ds, kv in zip(dss, kvs)]
        for dq, (rows, cols) in zip(dqs, places):
            draw_ref[rows, cols] = jnp.where(lane < HEAD_DIM, dq, 0.0).astype(bf16)
        for dkv, (i, h) in zip(dkvs, work):
            acc[h][0:BLOCK, :] += dkv[0:BLOCK]
            acc[h][last : last + BLOCK, :] += dkv[BLOCK : 2 * BLOCK]
            near = pl.ds(pl.multiple_of((i - 1) * BLOCK, BLOCK), 3 * BLOCK)
            acc[h][near, :] += dkv[2 * BLOCK : 5 * BLOCK]
            base = (h * (blocks - 2) + i - 1) * randoms
            for r in range(randoms):
                far = rows_at(rand_ref[base + r] * BLOCK, BLOCK)
                acc[h][far, :] += dkv[(5 + r) * BLOCK : (6 + r) * BLOCK]
        return carry

    lax.fori_loop(0, (blocks - 2) // PAIR_BACK, middle, 0)
    sums_ref[...] = jnp.zeros_like(sums_ref)

    def finish(t, carry):
        rows = rows_at(t * CHUNK, CHUNK)
        for h in range(heads):
            at = h * SLOT
            draw_ref[rows, at + LANES : at + SLOT] = acc[h][rows, :].astype(bf16)
        sums_ref[0:1, :] += jnp.sum(draw_ref[rows, :].astype(f32), axis=0, keepdims=True)
        return carry

    lax.fori_loop(0, length // CHUNK, finish, 0)


def attend_back(rand, qkv, res, dctx, heads):
    length = qkv.shape[0] * BLOCK
    randoms = rand.size // (heads * (length // BLOCK - 2))
    vmem = pl.BlockSpec(memory_space=pltpu.VMEM)
    return pl.pallas_call(
        partial(attend_back_kernel, heads, randoms),
        out_shape=(
            jax.ShapeDtypeStruct((length, heads * SLOT), bf16),
            jax.ShapeDtypeStruct((8, heads * SLOT), f32),
        ),
        in_specs=[pl.BlockSpec(memory_space=pltpu.SMEM), vmem, vmem, vmem],
        out_specs=(vmem, vmem),
        scratch_shapes=[pltpu.VMEM((length, LANES), bf16)] * heads
        + [pltpu.VMEM((length, LANES), f32)] * heads,
        compiler_params=pltpu.CompilerParams(vmem_limit_bytes=VMEM_BYTES),
        name="attend_back",
    )(rand, qkv, res, dctx)


def mean_of(a):
    return jnp.mean(a, axis=1, keepdims=True)


def norm(r):
    center = r - mean_of(r)
    rstd = lax.rsqrt(mean_of(center * center) + EPS)
    return center * rstd, rstd


def norm_back(dn, n, rstd):
    return rstd * (dn - mean_of(dn) - n * mean_of(dn * n))


def rowsum(a):
    return jnp.sum(a, axis=0, keepdims=True)


def chain_kernel(
    groups,
    ctx_ref,
    tok_ref,
    og_ref,
    wo_ref,
    wu_ref,
    wd_ref,
    vec_ref,
    bu_ref,
    out_ref,
    dres_ref,
    dctx_ref,
    mix_ref,
    hid_ref,
    act_ref,
    dpre_ref,
    dffn_ref,
    dproj_ref,
    gvec_ref,
    gbu_ref,
    slope_ref,
    wop_ref,
):
    width = tok_ref.shape[1]
    hidden = wu_ref.shape[1]
    wide = 3 * HEAD_DIM
    step = pl.program_id(0)

    @pl.when(step == 0)
    def _():
        for g in range(groups):
            wop_ref[g * LANES : (g + 1) * LANES, :] = wo_ref[g * wide : g * wide + LANES, :]
            to = groups * LANES + g * HEAD_DIM
            wop_ref[to : to + HEAD_DIM, :] = wo_ref[g * wide + LANES : (g + 1) * wide, :]
        gvec_ref[...] = jnp.zeros_like(gvec_ref)
        gbu_ref[...] = jnp.zeros_like(gbu_ref)

    low = lax.broadcasted_iota(jnp.int32, (BLOCK, LANES), 1) < HEAD_DIM
    for g in range(groups):
        mix_ref[:, g * LANES : (g + 1) * LANES] = ctx_ref[g, 0, :ROWS, :]
    for g in range(0, groups, 2):
        to = groups * LANES + g * HEAD_DIM
        for n in range(ROWS // (2 * BLOCK)):
            at = ROWS + n * BLOCK
            a = ctx_ref[g, 0, at : at + BLOCK, :].astype(f32)
            b = ctx_ref[g + 1, 0, at : at + BLOCK, :].astype(f32)
            even = jnp.where(low, a, pltpu.roll(b, HEAD_DIM, 1))
            odd = jnp.where(low, pltpu.roll(a, HEAD_DIM, 1), b)
            r = 2 * n * BLOCK
            mix_ref[r : r + BLOCK, to : to + LANES] = even.astype(bf16)
            mix_ref[r + BLOCK : r + 2 * BLOCK, to : to + LANES] = odd.astype(bf16)

    bo, g1, s1 = vec_ref[0:1, :], vec_ref[1:2, :], vec_ref[2:3, :]
    bd, g2, s2 = vec_ref[3:4, :], vec_ref[4:5, :], vec_ref[5:6, :]
    n1, rstd1 = norm(tok_ref[...].astype(f32) + dot(mix_ref[...], wop_ref[...]) + bo)
    hid = n1 * g1 + s1
    hid_low = hid.astype(bf16)
    hid_ref[...] = hid_low
    scale = np.sqrt(2.0 / np.pi).astype(np.float32)

    def up(f, carry):
        cols = rows_at(f * CHUNK, CHUNK)
        u = dot(hid_low, wu_ref[:, cols]) + bu_ref[:, cols]
        square = u * u
        t = jnp.tanh(scale * (u + 0.044715 * (u * square)))
        half = 0.5 * (1.0 + t)
        act_ref[:, cols] = (u * half).astype(bf16)
        slope = half + 0.5 * u * (1.0 - t * t) * (scale * (1.0 + (3 * 0.044715) * square))
        slope_ref[:, cols] = slope.astype(bf16)
        return carry

    lax.fori_loop(0, hidden // CHUNK, up, 0)
    n2, rstd2 = norm(hid + dot(act_ref[...], wd_ref[...]) + bd)
    out_ref[...] = (n2 * g2 + s2).astype(bf16)
    og = og_ref[...].astype(f32)
    gvec_ref[4:5, :] += rowsum(og * n2)
    gvec_ref[5:6, :] += rowsum(og)
    dres2 = norm_back(og * g2, n2, rstd2)
    dffn = dres2.astype(bf16)
    dffn_ref[...] = dffn
    gvec_ref[3:4, :] += rowsum(dffn.astype(f32))

    def down_back(f, carry):
        cols = rows_at(f * CHUNK, CHUNK)
        dact = dot_nt(dffn, wd_ref[cols, :])
        dpre = (dact * slope_ref[:, cols].astype(f32)).astype(bf16)
        dpre_ref[:, cols] = dpre
        gbu_ref[0:1, cols] += rowsum(dpre.astype(f32))
        return carry

    lax.fori_loop(0, hidden // CHUNK, down_back, 0)
    dh = dres2 + dot_nt(dpre_ref[...], wu_ref[...])
    gvec_ref[1:2, :] += rowsum(dh * n1)
    gvec_ref[2:3, :] += rowsum(dh)
    dres1 = norm_back(dh * g1, n1, rstd1)
    dres_ref[...] = dres1
    dproj = dres1.astype(bf16)
    dproj_ref[...] = dproj
    gvec_ref[0:1, :] += rowsum(dproj.astype(f32))
    dmix = dot_nt(dproj, wop_ref[...])
    for g in range(groups):
        dctx_ref[g, 0, :ROWS, :] = dmix[:, g * LANES : (g + 1) * LANES].astype(bf16)
    for g in range(0, groups, 2):
        to = groups * LANES + g * HEAD_DIM
        for n in range(ROWS // (2 * BLOCK)):
            at = ROWS + n * BLOCK
            r = 2 * n * BLOCK
            even = dmix[r : r + BLOCK, to : to + LANES]
            odd = dmix[r + BLOCK : r + 2 * BLOCK, to : to + LANES]
            a = jnp.where(low, even, pltpu.roll(odd, HEAD_DIM, 1))
            b = jnp.where(low, pltpu.roll(even, HEAD_DIM, 1), odd)
            dctx_ref[g, 0, at : at + BLOCK, :] = a.astype(bf16)
            dctx_ref[g + 1, 0, at : at + BLOCK, :] = b.astype(bf16)


def chain(ctx, tok, og, wo, wu, wd, vec, bu):
    rows, width = tok.shape
    hidden = wu.shape[1]
    groups = ctx.shape[0]
    once = pl.Buffered(1)

    def tiled(cols):
        return pl.BlockSpec((ROWS, cols), lambda t: (t, 0))

    def fixed(shape):
        return pl.BlockSpec(shape, lambda t: (0, 0), pipeline_mode=once)

    packed = pl.BlockSpec((groups, 1) + ctx.shape[2:], lambda t: (0, t, 0, 0))
    shape = jax.ShapeDtypeStruct
    return pl.pallas_call(
        partial(chain_kernel, groups),
        grid=(rows // ROWS,),
        out_shape=(
            shape((rows, width), bf16),
            shape((rows, width), f32),
            shape(ctx.shape, bf16),
            shape((rows, width), bf16),
            shape((rows, width), bf16),
            shape((rows, hidden), bf16),
            shape((rows, hidden), bf16),
            shape((rows, width), bf16),
            shape((rows, width), bf16),
            shape((8, width), f32),
            shape((8, hidden), f32),
        ),
        in_specs=[
            packed,
            tiled(width),
            tiled(width),
            fixed(wo.shape),
            fixed(wu.shape),
            fixed(wd.shape),
            fixed(vec.shape),
            fixed(bu.shape),
        ],
        out_specs=(
            tiled(width),
            tiled(width),
            packed,
            tiled(width),
            tiled(width),
            tiled(hidden),
            tiled(hidden),
            tiled(width),
            tiled(width),
            pl.BlockSpec((8, width), lambda t: (0, 0)),
            pl.BlockSpec((8, hidden), lambda t: (0, 0)),
        ),
        scratch_shapes=[pltpu.VMEM((ROWS, hidden), bf16), pltpu.VMEM(wo.shape, bf16)],
        compiler_params=pltpu.CompilerParams(vmem_limit_bytes=VMEM_BYTES),
        name="chain",
    )(ctx, tok, og, wo, wu, wd, vec, bu)


MESH = pl.DeviceIdType.MESH


def run_phases(items):
    step = 0
    live = list(items)
    while live:
        after = []
        for first, phases in live:
            if first > step or next(phases, None) is not None:
                after.append((first, phases))
        live = after
        step += 1


class Where:
    def __init__(self):
        c, core, zh, zl = (lax.axis_index(a) for a in ALL)
        self.y, self.x, self.core, self.zh, self.zl = c // 2, c % 2, core, zh, zl
        self.z = zh * 2 + zl
        self.by_x = (self.y * 2 + 1 - self.x, core, zh, zl)
        self.by_y = ((1 - self.y) * 2 + self.x, core, zh, zl)
        self.by_core = (c, 1 - core, zh, zl)
        self.by_zl = (c, core, zh, 1 - zl)
        self.by_zh = (c, core, 1 - zh, zl)
        self.by_mid = (c, core, 1 - zh, 1 - zl)
        self.by_swap = (c, 1 - core, 1 - zh, zl)
        self.by_both = (c, 1 - core, zh, 1 - zl)
        self.inner = zh != zl
        self.stays = core == zh

    def greet(self):
        barrier = pltpu.get_barrier_semaphore()
        others = (self.by_x, self.by_y, self.by_core, self.by_zl)
        others += (self.by_zh, self.by_mid, self.by_swap, self.by_both)
        for other in others:
            pl.semaphore_signal(barrier, inc=1, device_id=other, device_id_type=MESH)
        pl.semaphore_wait(barrier, len(others))


class Copies:
    def __init__(self, send, recv, local):
        self.send, self.recv, self.local_sems = send, recv, local
        self.n = self.m = 0

    def remote(self, src, dst, device):
        n = self.n
        self.n += 1
        return pltpu.make_async_remote_copy(
            src_ref=src,
            dst_ref=dst,
            send_sem=self.send.at[n],
            recv_sem=self.recv.at[n],
            device_id=device,
            device_id_type=MESH,
        )

    def local(self, src, dst):
        m = self.m
        self.m += 1
        return pltpu.make_async_copy(src, dst, self.local_sems.at[m])


def gather_item(me, copies, shard, full, cols, x_first):
    y, x, core, zh, zl = me.y, me.x, me.core, me.zh, me.zl
    mine = shard.at[:, cols]
    own = copies.local(mine, full.at[y, x, core, me.z, :, cols])
    first = copies.remote(mine, full.at[y, x, core, me.z, :, cols], me.by_zl)
    own.start()
    first.start()
    yield 1
    own.wait()
    first.wait()
    pair = full.at[y, x, core, pl.ds(zh * 2, 2), :, cols]
    pair_far = full.at[y, x, core, pl.ds((1 - zh) * 2, 2), :, cols]
    middle = copies.remote(pair, pair, me.by_mid)
    onward = copies.remote(pair_far, pair_far, me.by_zl)

    @pl.when(me.inner)
    def _():
        middle.start()

    yield 1

    @pl.when(me.inner)
    def _():
        middle.wait()
        onward.start()

    yield 1

    @pl.when(me.inner)
    def _():
        onward.wait_send()

    @pl.when(jnp.logical_not(me.inner))
    def _():
        onward.wait_recv()

    line = full.at[y, x, core, :, :, cols]
    near = copies.remote(line, line, me.by_x if x_first else me.by_y)
    near.start()
    across = [copies.remote(line, line, me.by_core)]
    across[0].start()
    yield 1
    near.wait()
    if x_first:
        block = full.at[y, :, core, :, :, cols]
        got = full.at[y, 1 - x, core, :, :, cols]
        rest = full.at[1 - y, :, core, :, :, cols]
    else:
        block = full.at[:, x, core, :, :, cols]
        got = full.at[1 - y, x, core, :, :, cols]
        rest = full.at[:, 1 - x, core, :, :, cols]
    far = copies.remote(block, block, me.by_y if x_first else me.by_x)
    far.start()
    across.append(copies.remote(got, got, me.by_core))
    across[1].start()
    yield 1
    far.wait()
    across.append(copies.remote(rest, rest, me.by_core))
    across[2].start()
    yield 1
    for copy in across:
        copy.wait()


def tokens_item(me, copies, tok, x_all, piece):
    place = me.core * 2 + me.zl
    there = (1 - me.core) * 2 + me.zl
    out = copies.remote(tok.at[piece], x_all.at[there, piece], me.by_swap)
    keep = copies.local(tok.at[piece], x_all.at[place, piece])

    @pl.when(me.stays)
    def _():
        keep.start()

    @pl.when(jnp.logical_not(me.stays))
    def _():
        out.start()

    yield 1

    @pl.when(me.stays)
    def _():
        keep.wait()

    @pl.when(jnp.logical_not(me.stays))
    def _():
        out.wait()

    held = x_all.at[place, piece]
    along = copies.remote(held, held, me.by_zl)
    along.start()
    over = copies.remote(held, held, me.by_core)
    over.start()
    yield 1
    along.wait()
    came = x_all.at[me.core * 2 + 1 - me.zl, piece]
    onto = copies.remote(came, came, me.by_core)
    onto.start()
    yield 1
    over.wait()
    onto.wait()


def exchange_item(me, copies, src, dst):
    out = copies.remote(src, dst, me.by_swap)
    keep = copies.local(src, dst)

    @pl.when(me.stays)
    def _():
        keep.start()

    @pl.when(jnp.logical_not(me.stays))
    def _():
        out.start()

    yield 1

    @pl.when(me.stays)
    def _():
        keep.wait()

    @pl.when(jnp.logical_not(me.stays))
    def _():
        out.wait()


PIECES = 4


def weight_item(me, copies, src, parts, whole, bias):
    y, x, core, zh, zl = me.y, me.x, me.core, me.zh, me.zl
    place = core * 2 + zl
    keep = copies.local(src.at[place], parts.at[place])
    moves = [
        copies.remote(src.at[core * 2 + 1 - zl], parts.at[place], me.by_zl),
        copies.remote(src.at[(1 - core) * 2 + zl], parts.at[place], me.by_core),
        copies.remote(src.at[(1 - core) * 2 + 1 - zl], parts.at[place], me.by_both),
    ]
    keep.start()
    for move in moves:
        move.start()
    yield 1
    keep.wait()
    for move in moves:
        move.wait()
    own = whole.shape[4] // 2
    for b in range(2):
        both = jnp.concatenate([parts[2 * b, :own, :], parts[2 * b + 1, :own, :]], axis=0)
        whole[y, x, b, zh] = both.astype(bf16)
    tail = pl.ds(own, 8)
    bias[y, x, zh] = parts[0, tail, :] + parts[1, tail, :] + parts[2, tail, :] + parts[3, tail, :]
    for spot, bias_spot, other in (
        (whole.at[y, x, :, zh], bias.at[y, x, zh], me.by_zh),
        (whole.at[y, x], bias.at[y, x], me.by_x),
        (whole.at[y], bias.at[y], me.by_y),
    ):
        moves = [copies.remote(spot, spot, other), copies.remote(bias_spot, bias_spot, other)]
        for move in moves:
            move.start()
        yield 1
        for move in moves:
            move.wait()


def finish(*generators):
    for phases in generators:
        for _ in phases:
            pass


def front_kernel(heads, randoms, *refs):
    rand_ref, tok, og, wq, w_out, up, down, small = refs[:8]
    x_hbm, tok_own, og_own, w_own, qkv_hbm, res_hbm, ctx_all, out_all, up_all, down_all, small_all = refs[8:19]
    x_all, parts, whole, bias, qkv_ref, res_ref, ends_ref, ctx_ref = refs[19:27]
    me = Where()
    me.greet()
    copies = Copies(*refs[27:])
    blocks = qkv_ref.shape[0]
    length = blocks * BLOCK
    quarter = length // 4
    core, zl = me.core, me.zl
    place = core * 2 + zl
    near = core * 2 + 1 - zl
    beside = (1 - core) * 2 + zl
    across = (1 - core) * 2 + 1 - zl

    weights = weight_item(me, copies, wq, parts, whole, bias)
    tokens = [tokens_item(me, copies, tok, x_all, piece) for piece in range(PIECES)]
    smalls = gather_item(me, copies, small, small_all, slice(0, LANES), True)
    later = []
    turn = 0
    for shard, full, splits, first in ((w_out, out_all, 1, 0), (up, up_all, 4, 0), (down, down_all, 2, 1)):
        width = shard.shape[1] // splits
        for n in range(splits):
            cols = slice(n * width, (n + 1) * width)
            later.append((first + n, gather_item(me, copies, shard, full, cols, turn % 2 == 0)))
            turn += 1
    later.append((4, exchange_item(me, copies, og, og_own)))
    later.append((1, smalls))
    state = {"step": 0, "live": later}

    def advance():
        after = []
        for first, phases in state["live"]:
            if first > state["step"] or next(phases, None) is not None:
                after.append((first, phases))
        state["live"] = after
        state["step"] += 1

    outs = []

    def write(src, dst):
        copy = copies.local(src, dst)
        copy.start()
        outs.append(copy)

    def project(where):
        bias_row = jnp.sum(bias[...].reshape(-1, 8, bias.shape[-1]), axis=0)[0:1]
        matrix = whole[...].reshape(-1, whole.shape[-1])
        for piece in range(PIECES):
            raw = dot(x_all[where, piece], matrix) + bias_row
            step = ROWS // BLOCK
            at = (where * PIECES + piece) * step
            qkv_ref[pl.ds(at, step)] = raw.astype(bf16).reshape(step, BLOCK, raw.shape[1])

    next(weights)
    for item in tokens:
        next(item)
    next(weights)
    for item in tokens:
        next(item)
    next(weights)
    next(weights)
    finish(weights)
    write(whole, w_own)
    write(x_all.at[place], tok_own)
    project(place)
    for item in tokens:
        next(item)
    advance()
    project(near)
    finish(*tokens)
    project(beside)
    advance()
    project(across)
    write(x_all, x_hbm)
    write(qkv_ref, qkv_hbm)
    for h, both in enumerate(global_blocks(qkv_ref, heads, length)):
        ends_ref[h] = both
    advance()

    def middle(t, carry):
        middle_blocks(qkv_ref, rand_ref, res_ref, t * PAIR, heads, randoms, blocks)
        return carry

    sends = []
    turns = quarter // BLOCK // PAIR
    for where, other in ((across, me.by_both), (near, me.by_zl), (beside, me.by_core), (place, None)):
        half = turns // 2
        lax.fori_loop(where * turns, where * turns + half, middle, 0)
        advance()
        lax.fori_loop(where * turns + half, (where + 1) * turns, middle, 0)

        @pl.when(where == 0)
        def _():
            for h in range(heads):
                res_ref[h, 0:BLOCK, :] = ends_ref[h, 0:BLOCK, :]

        @pl.when(where == 3)
        def _():
            for h in range(heads):
                res_ref[h, length - BLOCK : length, :] = ends_ref[h, BLOCK : 2 * BLOCK, :]

        for piece in range(PIECES):
            pack_rows(res_ref, ctx_ref, where * quarter + piece * ROWS, where, piece)
        rows = rows_at(where * quarter, quarter)
        write(res_ref.at[:, rows], res_hbm.at[:, rows])
        if other is None:
            write(ctx_ref.at[where], ctx_all.at[place])
        else:
            send = copies.remote(ctx_ref.at[where], ctx_all.at[place], other)
            send.start()
            sends.append(send)
        advance()
    while state["live"]:
        advance()
    for copy in sends + outs:
        copy.wait()


def front(rand, tok, og, wq, mats, small, heads):
    rows, width = tok.shape
    members = 4
    length = rows * members
    randoms = rand.size // (heads * (length // BLOCK - 2))
    hbm = pl.BlockSpec(memory_space=pltpu.HBM)
    shape = jax.ShapeDtypeStruct
    tok = tok.reshape(PIECES, rows // PIECES, width)
    cols = heads * SLOT
    own = mats[0].shape[0]
    packed = (members, rows // ROWS, ROWS * 3 // 2, LANES)
    outs = [
        shape((members,) + tok.shape, bf16),
        shape(tok.shape, bf16),
        shape(og.shape, bf16),
        shape((2, 2, 2, 2, 2 * own, cols), bf16),
        shape((length // BLOCK, BLOCK, cols), bf16),
        shape((heads, length, LANES), f32),
        shape(packed, bf16),
    ]
    outs += [shape((2, 2, 2, 4) + a.shape, bf16) for a in (*mats, small)]
    return pl.pallas_call(
        partial(front_kernel, heads, randoms),
        out_shape=tuple(outs),
        in_specs=[pl.BlockSpec(memory_space=pltpu.SMEM)] + [hbm] * 7,
        out_specs=(hbm,) * 11,
        scratch_shapes=[
            pltpu.VMEM((members,) + tok.shape, bf16),
            pltpu.VMEM(wq.shape, f32),
            pltpu.VMEM((2, 2, 2, 2, 2 * own, cols), bf16),
            pltpu.VMEM((2, 2, 2, 8, cols), f32),
            pltpu.VMEM((length // BLOCK, BLOCK, cols), bf16),
            pltpu.VMEM((heads, length, LANES), f32),
            pltpu.VMEM((heads, 2 * BLOCK, LANES), f32),
            pltpu.VMEM(packed, bf16),
            pltpu.SemaphoreType.DMA((112,)),
            pltpu.SemaphoreType.DMA((112,)),
            pltpu.SemaphoreType.DMA((32,)),
        ],
        compiler_params=pltpu.CompilerParams(
            collective_id=0, has_side_effects=True, vmem_limit_bytes=VMEM_BYTES
        ),
        name="front",
    )(rand, tok, og, wq, *mats, small)


def add_rows(dst, a, b, rows):
    step = next(n for n in (48, 32, 24, 16, 8) if rows % n == 0)

    def body(t, carry):
        at = rows_at(t * step, step)
        dst[at, :] = (a[at, :].astype(f32) + b[at, :].astype(f32)).astype(dst.dtype)
        return carry

    lax.fori_loop(0, rows // step, body, 0)


def scatter_item(me, copies, src, cols, acc, from_core, from_first, from_second, from_zh, part, from_zl, out, x_first):
    y, x, core, zh, zl = me.y, me.x, me.core, me.zh, me.zl
    rows = acc.shape[2]
    own = copies.local(src.at[:, :, core, :, cols], acc)
    over = copies.remote(src.at[:, :, 1 - core, :, cols], from_core, me.by_core)
    own.start()
    over.start()
    yield 1
    own.wait()
    over.wait()
    for a in range(2):
        for b in range(2):
            add_rows(acc.at[a, b], acc.at[a, b], from_core.at[a, b], rows)
    if x_first:
        first = copies.remote(acc.at[:, 1 - x], from_first, me.by_x)
    else:
        first = copies.remote(acc.at[1 - y], from_first, me.by_y)
    first.start()
    yield 1
    first.wait()
    for a in range(2):
        block = acc.at[a, x] if x_first else acc.at[y, a]
        add_rows(block, block, from_first.at[a], rows)
    if x_first:
        second = copies.remote(acc.at[1 - y, x], from_second, me.by_y)
    else:
        second = copies.remote(acc.at[y, 1 - x], from_second, me.by_x)
    second.start()
    yield 1
    second.wait()
    block = acc.at[y, x]
    add_rows(block, block, from_second, rows)
    half = rows // 2
    third = copies.remote(block.at[rows_at((1 - zh) * half, half)], from_zh, me.by_zh)
    third.start()
    yield 1
    third.wait()
    add_rows(part, block.at[rows_at(zh * half, half)], from_zh, half)
    last = half // 2
    fourth = copies.remote(part.at[rows_at((1 - zl) * last, last)], from_zl, me.by_zl)
    fourth.start()
    yield 1
    fourth.wait()
    add_rows(out, part.at[rows_at(zl * last, last)], from_zl, last)


def scatter_buffers(rows, cols, kind):
    return [
        pltpu.VMEM((2, 2, rows, cols), kind),
        pltpu.VMEM((2, 2, rows, cols), kind),
        pltpu.VMEM((2, rows, cols), kind),
        pltpu.VMEM((rows, cols), kind),
        pltpu.VMEM((rows // 2, cols), kind),
        pltpu.VMEM((rows // 2, cols), f32),
        pltpu.VMEM((rows // 4, cols), f32),
    ]


def own_columns_item(me, copies, src, acc, from_x, from_y, from_zh, part, out):
    y, x, core, zh, zl = me.y, me.x, me.core, me.zh, me.zl
    rows = src.shape[4]
    keep = copies.local(src.at[:, x], acc)
    first = copies.remote(src.at[:, 1 - x], from_x, me.by_x)
    keep.start()
    first.start()
    yield 1
    keep.wait()
    first.wait()
    for a in range(2):
        for b in range(2):
            for c in range(2):
                add_rows(acc.at[a, b, c], acc.at[a, b, c], from_x.at[a, b, c], rows)
    second = copies.remote(acc.at[1 - y], from_y, me.by_y)
    second.start()
    yield 1
    second.wait()
    for b in range(2):
        for c in range(2):
            block = acc.at[y, b, c]
            add_rows(block, block, from_y.at[b, c], rows)
    third = copies.remote(acc.at[y, :, 1 - zh], from_zh, me.by_zh)
    third.start()
    yield 1
    third.wait()
    half = rows // 2
    for b in range(2):
        add_rows(part.at[b], acc.at[y, b, zh], from_zh.at[b], rows)
    place = core * 2 + zl
    mine = rows_at(zl * half, half)
    other = rows_at((1 - zl) * half, half)
    keep = copies.local(part.at[core, mine], out.at[place])
    keep.start()
    moves = [
        copies.remote(part.at[core, other], out.at[place], me.by_zl),
        copies.remote(part.at[1 - core, mine], out.at[place], me.by_core),
        copies.remote(part.at[1 - core, other], out.at[place], me.by_both),
    ]
    for move in moves:
        move.start()
    yield 1
    keep.wait()
    for move in moves:
        move.wait()


def input_grad_item(me, copies, dx, dres, piece, acc, from_core, from_zl, res, send, out):
    core, zl = me.core, me.zl
    rows = acc.shape[1]
    keep = copies.local(dx.at[core, :, piece], acc)
    more = copies.local(dres.at[piece], res)
    over = copies.remote(dx.at[1 - core, :, piece], from_core, me.by_core)
    keep.start()
    more.start()
    over.start()
    yield 1
    keep.wait()
    over.wait()
    add_rows(acc.at[1 - zl], acc.at[1 - zl], from_core.at[1 - zl], rows)
    along = copies.remote(acc.at[1 - zl], from_zl, me.by_zl)
    along.start()
    add_rows(acc.at[zl], acc.at[zl], from_core.at[zl], rows)
    more.wait()
    add_rows(res, res, acc.at[zl], rows)
    yield 1
    along.wait()
    add_rows(send, res, from_zl, rows)
    yield from exchange_item(me, copies, send, out.at[piece])


SPLITS = ((0, 2), (1, 4), (2, 1), (3, 1))


def scatter_kernel(*refs):
    down, up, proj, vecs, qkv, dx, dres = refs[:7]
    outs = refs[7:13]
    sems, scratch = refs[13:16], list(refs[16:])
    me = Where()
    me.greet()
    copies = Copies(*sems)
    items = []

    def take(n):
        got = scratch[:n]
        del scratch[:n]
        return got

    for piece in range(PIECES):
        items.append((piece, input_grad_item(me, copies, dx, dres, piece, *take(5), outs[5])))
    items.append((0, own_columns_item(me, copies, qkv, *take(5), outs[4])))
    step = 0
    for n, splits in SPLITS:
        src = refs[n]
        width = src.shape[4] // splits
        for part in range(splits):
            cols = slice(part * width, (part + 1) * width)
            item = scatter_item(me, copies, src, cols, *take(7), outs[n].at[:, cols], step % 2 == 0)
            items.append((step // 2, item))
            step += 1
    items.sort(key=lambda item: item[0])
    run_phases(items)


def scatter(down, up, proj, vecs, qkv, dx, dres):
    hbm = pl.BlockSpec(memory_space=pltpu.HBM)
    vmem = pl.BlockSpec(memory_space=pltpu.VMEM)
    shape = jax.ShapeDtypeStruct
    grads = (down, up, proj, vecs)
    outs = [shape((a.shape[3] // 4, a.shape[4]), f32) for a in grads]
    rows, cols = qkv.shape[4:]
    outs.append(shape((4, rows // 2, cols), f32))
    outs.append(shape(dres.shape, bf16))
    buffers = []
    for _ in range(PIECES):
        tile = dres.shape[1:]
        buffers += [
            pltpu.VMEM((2,) + tile, bf16),
            pltpu.VMEM((2,) + tile, bf16),
            pltpu.VMEM(tile, bf16),
            pltpu.VMEM(tile, f32),
            pltpu.VMEM(tile, bf16),
        ]
    buffers += [
        pltpu.VMEM((2, 2, 2, rows, cols), bf16),
        pltpu.VMEM((2, 2, 2, rows, cols), bf16),
        pltpu.VMEM((2, 2, rows, cols), bf16),
        pltpu.VMEM((2, rows, cols), bf16),
        pltpu.VMEM((2, rows, cols), f32),
    ]
    for n, splits in SPLITS:
        a = grads[n]
        for _ in range(splits):
            buffers += scatter_buffers(a.shape[3], a.shape[4] // splits, a.dtype)
    return pl.pallas_call(
        scatter_kernel,
        out_shape=tuple(outs),
        in_specs=[hbm] * 7,
        out_specs=(vmem,) * 5 + (hbm,),
        scratch_shapes=[
            pltpu.SemaphoreType.DMA((80,)),
            pltpu.SemaphoreType.DMA((80,)),
            pltpu.SemaphoreType.DMA((32,)),
        ]
        + buffers,
        compiler_params=pltpu.CompilerParams(
            collective_id=1, has_side_effects=True, vmem_limit_bytes=VMEM_BYTES
        ),
        name="scatter",
    )(down, up, proj, vecs, qkv, dx, dres)


def per_device(
    tokens,
    qkv_weight,
    query_value_bias,
    out_weight,
    out_bias,
    norm1_gain,
    norm1_bias,
    up_weight,
    up_bias,
    down_weight,
    down_bias,
    norm2_gain,
    norm2_bias,
    rand_blocks,
    out_grad,
):
    members = lax.axis_size(GROUP)
    devices = lax.axis_size(ALL)
    swap = [(0, 0), (1, 2), (2, 1), (3, 3)]

    def move(a):
        return lax.ppermute(a, ("core", "zh"), swap)

    rand = move(rand_blocks[0])
    heads = rand.shape[0]
    rows, width = tokens.shape[1:]
    cols = heads * HEAD_DIM
    group = lax.axis_index(GROUP)
    own = width // devices
    rand_flat = rand.reshape(-1)

    def lay_out(a):
        a = a.reshape(a.shape[:-2] + (3, heads, HEAD_DIM))
        q, k, v = a[..., 0, :, :], a[..., 1, :, :], a[..., 2, :, :]
        q = q * jnp.asarray(HEAD_DIM**-0.5, a.dtype)
        laid = jnp.stack([q, jnp.zeros_like(q), k, v], axis=-2)
        return laid.reshape(laid.shape[:-3] + (heads * SLOT,))

    bias_part = jnp.stack([query_value_bias[0], jnp.zeros((own,), bf16), query_value_bias[1]])
    small = [out_bias, norm1_gain, norm1_bias, down_bias, norm2_gain, norm2_bias, up_bias]
    small = jnp.concatenate(small)
    direct = lax.axis_size("c") == 4 and members == 4 and own % 8 == 0
    if direct:
        count = small.shape[0]
        padded = jnp.pad(small, (0, 16 * LANES - count)).reshape(16, LANES)
        spread = lax.dynamic_update_slice(
            jnp.zeros((3, width), f32), bias_part.astype(f32), (0, lax.axis_index(ALL) * own)
        )
        spread = lay_out(jnp.transpose(spread.reshape(3, members, cols), (1, 0, 2)))
        wq = jnp.transpose(qkv_weight.astype(f32).reshape(own, 3, members, cols), (2, 0, 1, 3))
        wq = jnp.concatenate([lay_out(wq), spread[:, None], jnp.zeros((members, 7, heads * SLOT), f32)], axis=1)
        mats = (out_weight, up_weight, down_weight)
        x, tok, og, w_own, qkv, res, ctx, *full = front(
            rand_flat, tokens[0], out_grad[0], wq, mats, padded, heads
        )
        x, tok = x.reshape(-1, width), tok.reshape(-1, width)
        w_own = w_own.reshape(width, -1)
        w_out, w_up, w_down = (a.reshape(-1, a.shape[-1]) for a in full[:3])
        small = full[3].reshape(devices, -1)[:, :count].astype(f32)
    else:
        tok = move(tokens[0])
        og = move(out_grad[0])
        x = lax.all_gather(tok, GROUP, axis=0, tiled=True)
        mats = (qkv_weight, out_weight, up_weight, down_weight)
        w_qkv, w_out, w_up, w_down = (lax.all_gather(a, ALL, axis=0, tiled=True) for a in mats)
        small = lax.all_gather(small, ALL, axis=0).astype(f32)
        w_own = lax.dynamic_slice_in_dim(
            w_qkv.reshape(width, 3, members, cols), group, 1, axis=2
        ).reshape(width, 3, cols)
        w_own = lay_out(w_own)
        bias3 = lax.all_gather(bias_part, ALL, axis=1, tiled=True).astype(f32).reshape(3, members, cols)
        b_own = lay_out(lax.dynamic_slice_in_dim(bias3, group, 1, axis=1).reshape(1, 3, cols))
        qkv, res, ctx_send = attend(rand_flat, x, w_own, b_own, members, heads)
        ctx = lax.all_to_all(ctx_send, GROUP, split_axis=0, concat_axis=0, tiled=True)
    vecs = jnp.transpose(small[:, : 6 * own].reshape(devices, 6, own), (1, 0, 2)).reshape(6, width)
    bias_up = small[:, 6 * own :].reshape(1, -1)
    chain_vecs = jnp.concatenate([vecs, jnp.zeros((2, width), f32)], axis=0)
    out, dres1, dctx_send, mix, hid, act, dpre, dffn, dproj, gvec, gbu = chain(
        ctx, tok, og, w_out, w_up, w_down, chain_vecs, bias_up
    )
    dctx = lax.all_to_all(dctx_send, GROUP, split_axis=0, concat_axis=0, tiled=True)
    out = move(out)

    g_down = dot_tn(act, dffn).astype(bf16)
    g_up = dot_tn(hid, dpre).astype(bf16)
    g_mix = dot_tn(mix, dproj).astype(bf16)
    pairs = g_mix[: members * LANES].reshape(members, LANES, width)
    thirds = g_mix[members * LANES :].reshape(members, HEAD_DIM, width)
    g_out = jnp.concatenate([pairs, thirds], axis=1).reshape(width, width)

    draw, sums = attend_back(rand_flat, qkv, res, dctx, heads)
    dx = dot_nt(draw, w_own).astype(bf16)
    g_qkv = dot_tn(x, draw)

    def strip(a):
        a = a.reshape(a.shape[:-1] + (heads, 4, HEAD_DIM))
        q, k, v = a[..., 0, :] * (HEAD_DIM**-0.5), a[..., 2, :], a[..., 3, :]
        return jnp.stack([q, k, v], axis=-3).reshape(a.shape[:-3] + (3, cols))

    col_sums = strip(sums[0:1])[0]
    pair = jnp.stack([col_sums[0], col_sums[2]]).reshape(2, 1, cols)
    mine = (jnp.arange(members) == group)[None, :, None]
    pair = jnp.where(mine, pair, 0.0).reshape(2, width)
    vec_grads = jnp.concatenate([pair, gvec[0:6]], axis=0).reshape(8, devices, own)
    vec_grads = jnp.transpose(vec_grads, (1, 0, 2)).reshape(devices, 8 * own)
    vec_grads = jnp.concatenate([vec_grads, gbu[0].reshape(devices, -1)], axis=1)
    count = vec_grads.shape[1]

    if direct:
        lines = 8
        padded = jnp.pad(vec_grads, ((0, 0), (0, lines * LANES - count)))
        g_down, g_up, g_out, vec_grads, g_qkv, input_grad = scatter(
            g_down.reshape(2, 2, 2, -1, width),
            g_up.reshape(2, 2, 2, -1, g_up.shape[1]),
            g_out.reshape(2, 2, 2, -1, width),
            padded.reshape(2, 2, 2, 4 * lines, LANES),
            g_qkv.astype(bf16).reshape(2, 2, 2, 2, 2 * own, -1),
            dx.reshape(2, 2, PIECES, -1, width),
            dres1.reshape(PIECES, -1, width),
        )
        vec_grads = vec_grads.reshape(-1)[:count]
        input_grad = input_grad.reshape(rows, width).astype(f32)
        g_qkv = strip(g_qkv)
    else:

        def reduce(a):
            return lax.psum_scatter(a, ALL, scatter_dimension=0, tiled=True).astype(f32)

        g_down, g_up, g_out, vec_grads = reduce(g_down), reduce(g_up), reduce(g_out), reduce(vec_grads)[0]
        dx = lax.psum_scatter(dx, GROUP, scatter_dimension=0, tiled=True)
        input_grad = move((dres1 + dx.astype(f32)).astype(bf16)).astype(f32)
        g_qkv = strip(g_qkv).reshape(-1, 2, 2, members // 2, own, 3 * cols)
        g_qkv = jnp.transpose(g_qkv, (0, 2, 1, 3, 4, 5)).reshape(-1, members, own, 3 * cols)
        g_qkv = g_qkv.reshape(-1, 3 * cols).astype(bf16)
        g_qkv = lax.psum_scatter(g_qkv, REST, scatter_dimension=0, tiled=True)
        g_qkv = g_qkv.reshape(members, own, 3 * cols)
        g_qkv = lax.all_to_all(g_qkv, GROUP, split_axis=0, concat_axis=0, tiled=True).astype(f32)
    g_qkv = jnp.transpose(g_qkv.reshape(members, own, 3, cols), (1, 2, 0, 3)).reshape(own, -1)
    v8 = vec_grads[: 8 * own].reshape(8, own)
    return (
        out[None],
        input_grad[None],
        g_qkv,
        v8[0:2],
        g_out,
        v8[2],
        v8[3],
        v8[4],
        g_up,
        vec_grads[8 * own :],
        g_down,
        v8[5],
        v8[6],
        v8[7],
    )


def solution(mesh):
    dp, sp = mesh.shape["dp"], mesh.shape["sp"]
    fine = Mesh(mesh.devices.reshape(dp // 2, 2, 2, sp // 2), ALL)
    dp, sp = ("c", "core"), ("zh", "zl")
    act = P(dp, sp, None)
    mat = P(ALL, None)
    pair = P(None, ALL)
    vec = P(ALL)
    rand = P(dp, sp, None, None)
    return jax.shard_map(
        per_device,
        mesh=fine,
        in_specs=(act, mat, pair, mat, vec, vec, vec, mat, vec, mat, vec, vec, vec, rand, act),
        out_specs=(act, act, mat, pair, mat, vec, vec, vec, mat, vec, mat, vec, vec, vec),
        check_vma=False,
    )
```

```python
from functools import partial

import jax
import jax.numpy as jnp
import numpy as np
from jax import lax
from jax.experimental import pallas as pl
from jax.experimental.pallas import tpu as pltpu
from jax.sharding import Mesh
from jax.sharding import PartitionSpec as P

HEAD_DIM = 64
BLOCK = 64
LANES = 128
SLOT = 4 * HEAD_DIM
EPS = 1e-05
MASKED = -1e30
ALL = ("c", "core", "zh", "zl")
GROUP = ("core", "zl")
REST = ("c", "zh")
CHUNK = 512
ROWS = 256
PAIR = 2
SUBS = 1
PAIR_BACK = 2
VMEM_BYTES = 60 * 1024 * 1024

f32 = jnp.float32
bf16 = jnp.bfloat16
NT = (((1,), (1,)), ((), ()))
TN = (((0,), (0,)), ((), ()))


def dot(a, b):
    return jnp.dot(a, b, preferred_element_type=f32)


def dot_nt(a, b):
    return lax.dot_general(a, b, NT, preferred_element_type=f32)


def dot_tn(a, b):
    return lax.dot_general(a, b, TN, preferred_element_type=f32)


def rows_at(start, size):
    return pl.ds(pl.multiple_of(start, size), size)


def listed(ref, rand_ref, head, i, blocks, randoms):
    cols = slice(head * SLOT + LANES, head * SLOT + SLOT)
    near = jnp.clip(i - 1, 0, blocks - 3)
    parts = [ref[0, :, cols], ref[blocks - 1, :, cols]]
    parts += [ref[near + n, :, cols] for n in range(3)]
    base = (head * (blocks - 2) + near) * randoms
    parts += [ref[rand_ref[base + r], :, cols] for r in range(randoms)]
    return jnp.concatenate(parts, axis=0)


def keys_values(ref, head, t, size):
    cols = slice(head * SLOT + LANES, head * SLOT + SLOT)
    return ref[pl.ds(t * (size // BLOCK), size // BLOCK), :, cols].reshape(size, LANES)


def mask_globals(s, i, blocks):
    lane = lax.broadcasted_iota(jnp.int32, (BLOCK, LANES), 1)
    low = lane < BLOCK
    dead = (low & (i == 1)) | (~low & (i == blocks - 2))
    return jnp.concatenate([jnp.where(dead, MASKED, s[:, :LANES]), s[:, LANES:]], axis=1)


def middle_blocks(qkv_ref, rand_ref, res_ref, first, heads, randoms, blocks):
    lane = lax.broadcasted_iota(jnp.int32, (BLOCK, LANES), 1)
    work = [(first + n, h) for n in range(PAIR) for h in range(heads)]
    kvs = [listed(qkv_ref, rand_ref, h, i, blocks, randoms) for i, h in work]
    qs = [qkv_ref[i, :, h * SLOT : h * SLOT + LANES] for i, h in work]
    ss = [mask_globals(dot_nt(q, kv), i, blocks) for q, kv, (i, h) in zip(qs, kvs, work)]
    tops = [jnp.max(s, axis=1, keepdims=True) for s in ss]
    es = [jnp.exp(s - top) for s, top in zip(ss, tops)]
    totals = [jnp.sum(e, axis=1, keepdims=True) for e in es]
    os = [dot(e.astype(bf16), kv) for e, kv in zip(es, kvs)]
    for o, top, total, (i, h) in zip(os, tops, totals, work):
        both = jnp.where(lane < HEAD_DIM, top + jnp.log(total), o / total)
        res_ref[h, rows_at(i * BLOCK, BLOCK), :] = both


def global_blocks(qkv_ref, heads, length):
    last = length // BLOCK - 1

    def ends(h):
        cols = slice(h * SLOT, h * SLOT + LANES)
        return jnp.concatenate([qkv_ref[0, :, cols], qkv_ref[last, :, cols]], axis=0)

    qs = [ends(h) for h in range(heads)]

    def whole(t, carry):
        kvs = [keys_values(qkv_ref, h, t, CHUNK) for h in range(heads)]
        ss = [dot_nt(q, kv) for q, kv in zip(qs, kvs)]
        news = [jnp.maximum(c[0], jnp.max(s, axis=1, keepdims=True)) for c, s in zip(carry, ss)]
        fades = [jnp.exp(c[0] - new) for c, new in zip(carry, news)]
        es = [jnp.exp(s - new) for s, new in zip(ss, news)]
        sums = [jnp.sum(e, axis=1, keepdims=True) for e in es]
        os = [dot(e.astype(bf16), kv) for e, kv in zip(es, kvs)]
        return tuple(
            (new, c[1] * fade + total, c[2] * fade + o)
            for c, new, fade, total, o in zip(carry, news, fades, sums, os)
        )

    start = (
        jnp.full((2 * BLOCK, 1), MASKED, f32),
        jnp.zeros((2 * BLOCK, 1), f32),
        jnp.zeros((2 * BLOCK, LANES), f32),
    )
    done = lax.fori_loop(0, length // CHUNK, whole, (start,) * heads)
    lane = lax.broadcasted_iota(jnp.int32, (2 * BLOCK, LANES), 1)
    return [jnp.where(lane < HEAD_DIM, top + jnp.log(total), acc / total) for top, total, acc in done]


def pack_rows(res_ref, ctx_ref, start, part, piece):
    low = lax.broadcasted_iota(jnp.int32, (BLOCK, LANES), 1) < HEAD_DIM
    for n in range(ROWS // BLOCK):
        rows = rows_at(start + n * BLOCK, BLOCK)
        first = pltpu.roll(res_ref[0, rows, :], HEAD_DIM, 1)
        pair = jnp.where(low, first, res_ref[1, rows, :])
        ctx_ref[part, piece, n * BLOCK : (n + 1) * BLOCK, :] = pair.astype(bf16)
    for n in range(ROWS // (2 * BLOCK)):
        rows = rows_at(start + 2 * n * BLOCK, BLOCK)
        odd = rows_at(start + (2 * n + 1) * BLOCK, BLOCK)
        first = pltpu.roll(res_ref[2, rows, :], HEAD_DIM, 1)
        both = jnp.where(low, first, res_ref[2, odd, :])
        ctx_ref[part, piece, ROWS + n * BLOCK : ROWS + (n + 1) * BLOCK, :] = both.astype(bf16)


def attend_kernel(heads, randoms, rand_ref, x_ref, w_ref, b_ref, qkv_ref, res_ref, ctx_ref):
    length = x_ref.shape[0]
    blocks = length // BLOCK

    def project(t, carry):
        raw = dot(x_ref[rows_at(t * CHUNK, CHUNK), :], w_ref[...]) + b_ref[...]
        step = CHUNK // BLOCK
        qkv_ref[pl.ds(t * step, step)] = raw.astype(bf16).reshape(step, BLOCK, raw.shape[1])
        return carry

    lax.fori_loop(0, length // CHUNK, project, 0)

    def middle(t, carry):
        middle_blocks(qkv_ref, rand_ref, res_ref, t * PAIR, heads, randoms, blocks)
        return carry

    lax.fori_loop(0, blocks // PAIR, middle, 0)
    for h, both in enumerate(global_blocks(qkv_ref, heads, length)):
        res_ref[h, 0:BLOCK, :] = both[:BLOCK]
        res_ref[h, length - BLOCK : length, :] = both[BLOCK:]
    per_quarter = ctx_ref.shape[1]

    def pack(t, carry):
        pack_rows(res_ref, ctx_ref, t * ROWS, t // per_quarter, t % per_quarter)
        return carry

    lax.fori_loop(0, length // ROWS, pack, 0)


def attend(rand, x, w, b, parts, heads):
    length = x.shape[0]
    randoms = rand.size // (heads * (length // BLOCK - 2))
    vmem = pl.BlockSpec(memory_space=pltpu.VMEM)
    return pl.pallas_call(
        partial(attend_kernel, heads, randoms),
        out_shape=(
            jax.ShapeDtypeStruct((length // BLOCK, BLOCK, heads * SLOT), bf16),
            jax.ShapeDtypeStruct((heads, length, LANES), f32),
            jax.ShapeDtypeStruct((parts, length // parts // ROWS, ROWS * 3 // 2, LANES), bf16),
        ),
        in_specs=[pl.BlockSpec(memory_space=pltpu.SMEM), vmem, vmem, vmem],
        out_specs=(vmem, vmem, vmem),
        compiler_params=pltpu.CompilerParams(vmem_limit_bytes=VMEM_BYTES),
        name="attend",
    )(rand, x, w, b)


def attend_back_kernel(
    heads, randoms, rand_ref, qkv_ref, res_ref, dctx_ref, draw_ref, sums_ref, *scratch
):
    dout, acc = scratch[:heads], scratch[heads:]
    blocks = qkv_ref.shape[0]
    length = blocks * BLOCK
    last = (blocks - 1) * BLOCK
    per_quarter = dctx_ref.shape[1]

    def unpack(t, carry):
        part, piece = t // per_quarter, t % per_quarter
        lane = lax.broadcasted_iota(jnp.int32, (BLOCK, LANES), 1)
        low = lane < HEAD_DIM
        for n in range(ROWS // BLOCK):
            rows = rows_at(t * ROWS + n * BLOCK, BLOCK)
            pair = dctx_ref[part, piece, n * BLOCK : (n + 1) * BLOCK, :].astype(f32)
            dout[0][rows, :] = jnp.where(low, 0.0, pltpu.roll(pair, HEAD_DIM, 1)).astype(bf16)
            dout[1][rows, :] = jnp.where(low, 0.0, pair).astype(bf16)
        for n in range(ROWS // (2 * BLOCK)):
            rows = rows_at(t * ROWS + 2 * n * BLOCK, BLOCK)
            odd = rows_at(t * ROWS + (2 * n + 1) * BLOCK, BLOCK)
            both = dctx_ref[part, piece, ROWS + n * BLOCK : ROWS + (n + 1) * BLOCK, :].astype(f32)
            dout[2][rows, :] = jnp.where(low, 0.0, pltpu.roll(both, HEAD_DIM, 1)).astype(bf16)
            dout[2][odd, :] = jnp.where(low, 0.0, both).astype(bf16)
        return carry

    lax.fori_loop(0, length // ROWS, unpack, 0)

    step = 256

    def ends(ref, cols):
        return jnp.concatenate([ref[0:BLOCK, cols], ref[last : last + BLOCK, cols]], axis=0)

    every = slice(0, LANES)
    gs = [ends(dout[h], every) for h in range(heads)]
    reses = [ends(res_ref.at[h], every) for h in range(heads)]
    alls = [
        jnp.concatenate(
            [qkv_ref[n, :, h * SLOT : h * SLOT + LANES] for n in (0, blocks - 1)] + [gs[h]], axis=0
        )
        for h in range(heads)
    ]
    logs = [res[:, 0:1] for res in reses]
    deltas = [jnp.sum(g.astype(f32) * res, axis=1, keepdims=True) for g, res in zip(gs, reses)]

    def whole(t, dqs):
        rows = rows_at(t * step, step)
        kvs = [keys_values(qkv_ref, h, t, step) for h in range(heads)]
        sds = [dot_nt(both, kv) for both, kv in zip(alls, kvs)]
        ps = [jnp.exp(sd[: 2 * BLOCK] - log) for sd, log in zip(sds, logs)]
        dss = [(p * (sd[2 * BLOCK :] - d)).astype(bf16) for p, sd, d in zip(ps, sds, deltas)]
        dkvs = [
            dot_tn(jnp.concatenate([ds, p.astype(bf16)], axis=0), both)
            for ds, p, both in zip(dss, ps, alls)
        ]
        news = tuple(dq + dot(ds, kv) for dq, ds, kv in zip(dqs, dss, kvs))
        for h in range(heads):
            acc[h][rows, :] = dkvs[h]
        return news

    dqs = lax.fori_loop(
        0, length // step, whole, (jnp.zeros((2 * BLOCK, LANES), f32),) * heads
    )
    for h in range(heads):
        cols = slice(h * SLOT, h * SLOT + LANES)
        lane = lax.broadcasted_iota(jnp.int32, (2 * BLOCK, LANES), 1)
        dq = jnp.where(lane < HEAD_DIM, dqs[h], 0.0).astype(bf16)
        draw_ref[0:BLOCK, cols] = dq[:BLOCK]
        draw_ref[last : last + BLOCK, cols] = dq[BLOCK:]

    def middle(t, carry):
        lane = lax.broadcasted_iota(jnp.int32, (BLOCK, LANES), 1)
        work = [(1 + t * PAIR_BACK + n, h) for n in range(PAIR_BACK) for h in range(heads)]
        kvs = [listed(qkv_ref, rand_ref, h, i, blocks, randoms) for i, h in work]
        places = [(rows_at(i * BLOCK, BLOCK), slice(h * SLOT, h * SLOT + LANES)) for i, h in work]
        gs = [dout[h][rows, :] for (rows, _), (_, h) in zip(places, work)]
        reses = [res_ref[h, rows, :] for (rows, _), (_, h) in zip(places, work)]
        alls = [
            jnp.concatenate([qkv_ref[i, :, cols], g], axis=0)
            for (_, cols), (i, _), g in zip(places, work, gs)
        ]
        sds = [dot_nt(both, kv) for both, kv in zip(alls, kvs)]
        deltas = [jnp.sum(g.astype(f32) * res, axis=1, keepdims=True) for g, res in zip(gs, reses)]
        ps = [
            jnp.exp(mask_globals(sd[:BLOCK], i, blocks) - res[:, 0:1])
            for sd, res, (i, h) in zip(sds, reses, work)
        ]
        dss = [(p * (sd[BLOCK:] - d)).astype(bf16) for p, sd, d in zip(ps, sds, deltas)]
        dkvs = [
            dot_tn(jnp.concatenate([ds, p.astype(bf16)], axis=0), both)
            for ds, p, both in zip(dss, ps, alls)
        ]
        dqs = [dot(ds, kv) for ds, kv in zip(dss, kvs)]
        for dq, (rows, cols) in zip(dqs, places):
            draw_ref[rows, cols] = jnp.where(lane < HEAD_DIM, dq, 0.0).astype(bf16)
        for dkv, (i, h) in zip(dkvs, work):
            acc[h][0:BLOCK, :] += dkv[0:BLOCK]
            acc[h][last : last + BLOCK, :] += dkv[BLOCK : 2 * BLOCK]
            near = pl.ds(pl.multiple_of((i - 1) * BLOCK, BLOCK), 3 * BLOCK)
            acc[h][near, :] += dkv[2 * BLOCK : 5 * BLOCK]
            base = (h * (blocks - 2) + i - 1) * randoms
            for r in range(randoms):
                far = rows_at(rand_ref[base + r] * BLOCK, BLOCK)
                acc[h][far, :] += dkv[(5 + r) * BLOCK : (6 + r) * BLOCK]
        return carry

    lax.fori_loop(0, (blocks - 2) // PAIR_BACK, middle, 0)
    sums_ref[...] = jnp.zeros_like(sums_ref)

    def finish(t, carry):
        rows = rows_at(t * CHUNK, CHUNK)
        for h in range(heads):
            at = h * SLOT
            draw_ref[rows, at + LANES : at + SLOT] = acc[h][rows, :].astype(bf16)
        sums_ref[0:1, :] += jnp.sum(draw_ref[rows, :].astype(f32), axis=0, keepdims=True)
        return carry

    lax.fori_loop(0, length // CHUNK, finish, 0)


def attend_back(rand, qkv, res, dctx, heads):
    length = qkv.shape[0] * BLOCK
    randoms = rand.size // (heads * (length // BLOCK - 2))
    vmem = pl.BlockSpec(memory_space=pltpu.VMEM)
    return pl.pallas_call(
        partial(attend_back_kernel, heads, randoms),
        out_shape=(
            jax.ShapeDtypeStruct((length, heads * SLOT), bf16),
            jax.ShapeDtypeStruct((8, heads * SLOT), f32),
        ),
        in_specs=[pl.BlockSpec(memory_space=pltpu.SMEM), vmem, vmem, vmem],
        out_specs=(vmem, vmem),
        scratch_shapes=[pltpu.VMEM((length, LANES), bf16)] * heads
        + [pltpu.VMEM((length, LANES), f32)] * heads,
        compiler_params=pltpu.CompilerParams(vmem_limit_bytes=VMEM_BYTES),
        name="attend_back",
    )(rand, qkv, res, dctx)


def mean_of(a):
    return jnp.mean(a, axis=1, keepdims=True)


def norm(r):
    center = r - mean_of(r)
    rstd = lax.rsqrt(mean_of(center * center) + EPS)
    return center * rstd, rstd


def norm_back(dn, n, rstd):
    return rstd * (dn - mean_of(dn) - n * mean_of(dn * n))


def rowsum(a):
    return jnp.sum(a, axis=0, keepdims=True)


MESH = pl.DeviceIdType.MESH


def run_phases(items):
    step = 0
    live = list(items)
    while live:
        after = []
        for first, phases in live:
            if first > step or next(phases, None) is not None:
                after.append((first, phases))
        live = after
        step += 1


class Where:
    def __init__(self):
        c, core, zh, zl = (lax.axis_index(a) for a in ALL)
        self.y, self.x, self.core, self.zh, self.zl = c // 2, c % 2, core, zh, zl
        self.z = zh * 2 + zl
        self.by_x = (self.y * 2 + 1 - self.x, core, zh, zl)
        self.by_y = ((1 - self.y) * 2 + self.x, core, zh, zl)
        self.by_core = (c, 1 - core, zh, zl)
        self.by_zl = (c, core, zh, 1 - zl)
        self.by_zh = (c, core, 1 - zh, zl)
        self.by_mid = (c, core, 1 - zh, 1 - zl)
        self.by_swap = (c, 1 - core, 1 - zh, zl)
        self.by_both = (c, 1 - core, zh, 1 - zl)
        self.inner = zh != zl
        self.stays = core == zh

    def greet(self):
        barrier = pltpu.get_barrier_semaphore()
        others = (self.by_x, self.by_y, self.by_core, self.by_zl)
        others += (self.by_zh, self.by_mid, self.by_swap, self.by_both)
        for other in others:
            pl.semaphore_signal(barrier, inc=1, device_id=other, device_id_type=MESH)
        pl.semaphore_wait(barrier, len(others))


class Copies:
    def __init__(self, send, recv, local):
        self.send, self.recv, self.local_sems = send, recv, local
        self.n = self.m = 0

    def remote(self, src, dst, device):
        n = self.n
        self.n += 1
        return pltpu.make_async_remote_copy(
            src_ref=src,
            dst_ref=dst,
            send_sem=self.send.at[n],
            recv_sem=self.recv.at[n],
            device_id=device,
            device_id_type=MESH,
        )

    def local(self, src, dst):
        m = self.m
        self.m += 1
        return pltpu.make_async_copy(src, dst, self.local_sems.at[m])


def chain_kernel(
    groups,
    direct,
    ctx_ref,
    tok_ref,
    og_ref,
    wo_ref,
    wu_ref,
    wd_ref,
    vec_ref,
    bu_ref,
    out_ref,
    dres_ref,
    dctx_ref,
    mix_ref,
    hid_ref,
    act_ref,
    dpre_ref,
    dffn_ref,
    dproj_ref,
    gvec_ref,
    gbu_ref,
    slope_ref,
    wop_ref,
    *stage,
):
    width = tok_ref.shape[1]
    hidden = wu_ref.shape[1]
    wide = 3 * HEAD_DIM
    step = pl.program_id(0)
    if direct:
        me = Where()
        out_far, dctx_far = out_ref, dctx_ref
        out_stage, dctx_stage, send, recv, local = stage
        out_ref, dctx_ref = out_stage.at[step], dctx_stage.at[step]

        @pl.when(step == 0)
        def _():
            me.greet()

    def transfers(t):
        place = me.core * 2 + me.zl
        near, beside = me.core * 2 + 1 - me.zl, (1 - me.core) * 2 + me.zl
        across = (1 - me.core) * 2 + 1 - me.zl
        others = ((near, me.by_zl), (beside, me.by_core), (across, me.by_both))
        remote = [
            pltpu.make_async_remote_copy(
                src_ref=dctx_stage.at[t, where],
                dst_ref=dctx_far.at[place, pl.ds(t * SUBS, SUBS)],
                send_sem=send.at[t, n],
                recv_sem=recv.at[t, n],
                device_id=other,
                device_id_type=MESH,
            )
            for n, (where, other) in enumerate(others)
        ]
        swap = pltpu.make_async_remote_copy(
            src_ref=out_stage.at[t],
            dst_ref=out_far.at[t],
            send_sem=send.at[t, 3],
            recv_sem=recv.at[t, 3],
            device_id=me.by_swap,
            device_id_type=MESH,
        )
        keep = pltpu.make_async_copy(out_stage.at[t], out_far.at[t], local.at[t, 0])
        own = pltpu.make_async_copy(
            dctx_stage.at[t, place], dctx_far.at[place, pl.ds(t * SUBS, SUBS)], local.at[t, 1]
        )
        return remote, own, swap, keep

    @pl.when(step == 0)
    def _():
        for g in range(groups):
            wop_ref[g * LANES : (g + 1) * LANES, :] = wo_ref[g * wide : g * wide + LANES, :]
            to = groups * LANES + g * HEAD_DIM
            wop_ref[to : to + HEAD_DIM, :] = wo_ref[g * wide + LANES : (g + 1) * wide, :]
        gvec_ref[...] = jnp.zeros_like(gvec_ref)
        gbu_ref[...] = jnp.zeros_like(gbu_ref)

    low = lax.broadcasted_iota(jnp.int32, (BLOCK, LANES), 1) < HEAD_DIM
    subs = range(tok_ref.shape[0] // ROWS)
    spans = [slice(n * ROWS, (n + 1) * ROWS) for n in subs]
    chunks = [slice(f, f + CHUNK) for f in range(0, hidden, CHUNK)]
    for n in subs:
        for g in range(groups):
            mix_ref[spans[n], g * LANES : (g + 1) * LANES] = ctx_ref[g, n, :ROWS, :]
        for g in range(0, groups, 2):
            to = groups * LANES + g * HEAD_DIM
            for m in range(ROWS // (2 * BLOCK)):
                at = ROWS + m * BLOCK
                a = ctx_ref[g, n, at : at + BLOCK, :].astype(f32)
                b = ctx_ref[g + 1, n, at : at + BLOCK, :].astype(f32)
                even = jnp.where(low, a, pltpu.roll(b, HEAD_DIM, 1))
                odd = jnp.where(low, pltpu.roll(a, HEAD_DIM, 1), b)
                r = n * ROWS + 2 * m * BLOCK
                mix_ref[r : r + BLOCK, to : to + LANES] = even.astype(bf16)
                mix_ref[r + BLOCK : r + 2 * BLOCK, to : to + LANES] = odd.astype(bf16)

    bo, g1, s1 = vec_ref[0:1, :], vec_ref[1:2, :], vec_ref[2:3, :]
    bd, g2, s2 = vec_ref[3:4, :], vec_ref[4:5, :], vec_ref[5:6, :]
    projs = [dot(mix_ref[rows, :], wop_ref[...]) for rows in spans]
    norms = [norm(tok_ref[rows, :].astype(f32) + proj + bo) for rows, proj in zip(spans, projs)]
    hids = [n1 * g1 + s1 for n1, _ in norms]
    lows = [hid.astype(bf16) for hid in hids]
    for rows, hid_low in zip(spans, lows):
        hid_ref[rows, :] = hid_low
    scale = np.sqrt(2.0 / np.pi).astype(np.float32)
    work = [(n, cols) for cols in chunks for n in subs]

    def behind(start, end):
        held = start(*work[0])
        for k, item in enumerate(work):
            now = held
            if k + 1 < len(work):
                held = start(*work[k + 1])
            end(*item, now)

    def up_start(n, cols):
        return dot(lows[n], wu_ref[:, cols])

    def up_end(n, cols, raw):
        u = raw + bu_ref[:, cols]
        square = u * u
        t = jnp.tanh(u * (scale + (scale * 0.044715) * square))
        half = 0.5 + 0.5 * t
        act_ref[spans[n], cols] = (u * half).astype(bf16)
        slope = half + (0.5 * u) * (1.0 - t * t) * (scale + (3 * 0.044715 * scale) * square)
        slope_ref[spans[n], cols] = slope.astype(bf16)

    behind(up_start, up_end)
    ffns = [dot(act_ref[rows, :], wd_ref[...]) for rows in spans]
    dres2s, dffns = [], []
    for n, rows in enumerate(spans):
        n2, rstd2 = norm(hids[n] + ffns[n] + bd)
        out_ref[rows, :] = (n2 * g2 + s2).astype(bf16)
        og = og_ref[rows, :].astype(f32)
        gvec_ref[4:5, :] += rowsum(og * n2)
        gvec_ref[5:6, :] += rowsum(og)
        dres2 = norm_back(og * g2, n2, rstd2)
        dffn = dres2.astype(bf16)
        dffn_ref[rows, :] = dffn
        gvec_ref[3:4, :] += rowsum(dffn.astype(f32))
        dres2s.append(dres2)
        dffns.append(dffn)

    if direct:
        remote, own, swap, keep = transfers(step)

        @pl.when(me.stays)
        def _():
            keep.start()

        @pl.when(jnp.logical_not(me.stays))
        def _():
            swap.start()

    def down_start(n, cols):
        return dot_nt(dffns[n], wd_ref[cols, :])

    def down_end(n, cols, dact):
        dpre = (dact * slope_ref[spans[n], cols].astype(f32)).astype(bf16)
        dpre_ref[spans[n], cols] = dpre
        gbu_ref[0:1, cols] += rowsum(dpre.astype(f32))

    behind(down_start, down_end)
    dhs = [dres2 + dot_nt(dpre_ref[rows, :], wu_ref[...]) for rows, dres2 in zip(spans, dres2s)]
    dmixes = []
    for rows, dh, (n1, rstd1) in zip(spans, dhs, norms):
        gvec_ref[1:2, :] += rowsum(dh * n1)
        gvec_ref[2:3, :] += rowsum(dh)
        dres1 = norm_back(dh * g1, n1, rstd1)
        dres_ref[rows, :] = dres1
        dproj = dres1.astype(bf16)
        dproj_ref[rows, :] = dproj
        gvec_ref[0:1, :] += rowsum(dproj.astype(f32))
        dmixes.append(dot_nt(dproj, wop_ref[...]))
    for n, dmix in enumerate(dmixes):
        for g in range(groups):
            dctx_ref[g, n, :ROWS, :] = dmix[:, g * LANES : (g + 1) * LANES].astype(bf16)
        for g in range(0, groups, 2):
            to = groups * LANES + g * HEAD_DIM
            for m in range(ROWS // (2 * BLOCK)):
                at = ROWS + m * BLOCK
                r = 2 * m * BLOCK
                even = dmix[r : r + BLOCK, to : to + LANES]
                odd = dmix[r + BLOCK : r + 2 * BLOCK, to : to + LANES]
                a = jnp.where(low, even, pltpu.roll(odd, HEAD_DIM, 1))
                b = jnp.where(low, pltpu.roll(even, HEAD_DIM, 1), odd)
                dctx_ref[g, n, at : at + BLOCK, :] = a.astype(bf16)
                dctx_ref[g + 1, n, at : at + BLOCK, :] = b.astype(bf16)

    if direct:
        for copy in remote:
            copy.start()
        own.start()

        @pl.when(step == pl.num_programs(0) - 1)
        def _():
            for t in range(dctx_stage.shape[0]):
                remote, own, swap, keep = transfers(t)
                for copy in remote:
                    copy.wait()
                own.wait()

                @pl.when(me.stays)
                def _():
                    keep.wait()

                @pl.when(jnp.logical_not(me.stays))
                def _():
                    swap.wait()


def chain(ctx, tok, og, wo, wu, wd, vec, bu, direct):
    rows, width = tok.shape
    hidden = wu.shape[1]
    groups = ctx.shape[0]
    once = pl.Buffered(1)

    def tiled(cols):
        return pl.BlockSpec((SUBS * ROWS, cols), lambda t: (t, 0))

    def fixed(shape):
        return pl.BlockSpec(shape, lambda t: (0, 0), pipeline_mode=once)

    packed = pl.BlockSpec((groups, SUBS) + ctx.shape[2:], lambda t: (0, t, 0, 0))
    shape = jax.ShapeDtypeStruct
    steps = rows // (SUBS * ROWS)
    hbm = pl.BlockSpec(memory_space=pltpu.HBM)
    scratch = [pltpu.VMEM((SUBS * ROWS, hidden), bf16), pltpu.VMEM(wo.shape, bf16)]
    params = pltpu.CompilerParams(vmem_limit_bytes=VMEM_BYTES)
    out_shape = (rows, width)
    if direct:
        out_shape = (steps, SUBS * ROWS, width)
        scratch += [
            pltpu.VMEM(out_shape, bf16),
            pltpu.VMEM((steps, groups, SUBS) + ctx.shape[2:], bf16),
            pltpu.SemaphoreType.DMA((steps, 4)),
            pltpu.SemaphoreType.DMA((steps, 4)),
            pltpu.SemaphoreType.DMA((steps, 2)),
        ]
        params = pltpu.CompilerParams(
            vmem_limit_bytes=VMEM_BYTES, collective_id=2, has_side_effects=True
        )
    return pl.pallas_call(
        partial(chain_kernel, groups, direct),
        grid=(steps,),
        out_shape=(
            shape(out_shape, bf16),
            shape((rows, width), f32),
            shape(ctx.shape, bf16),
            shape((rows, width), bf16),
            shape((rows, width), bf16),
            shape((rows, hidden), bf16),
            shape((rows, hidden), bf16),
            shape((rows, width), bf16),
            shape((rows, width), bf16),
            shape((8, width), f32),
            shape((8, hidden), f32),
        ),
        in_specs=[
            packed,
            tiled(width),
            tiled(width),
            fixed(wo.shape),
            fixed(wu.shape),
            fixed(wd.shape),
            fixed(vec.shape),
            fixed(bu.shape),
        ],
        out_specs=(
            hbm if direct else tiled(width),
            tiled(width),
            hbm if direct else packed,
            tiled(width),
            tiled(width),
            tiled(hidden),
            tiled(hidden),
            tiled(width),
            tiled(width),
            pl.BlockSpec((8, width), lambda t: (0, 0)),
            pl.BlockSpec((8, hidden), lambda t: (0, 0)),
        ),
        scratch_shapes=scratch,
        compiler_params=params,
        name="chain",
    )(ctx, tok, og, wo, wu, wd, vec, bu)


def gather_item(me, copies, shard, full, cols, x_first):
    y, x, core, zh, zl = me.y, me.x, me.core, me.zh, me.zl
    mine = shard.at[:, cols]
    own = copies.local(mine, full.at[y, x, core, me.z, :, cols])
    first = copies.remote(mine, full.at[y, x, core, me.z, :, cols], me.by_zl)
    own.start()
    first.start()
    yield 1
    own.wait()
    first.wait()
    pair = full.at[y, x, core, pl.ds(zh * 2, 2), :, cols]
    pair_far = full.at[y, x, core, pl.ds((1 - zh) * 2, 2), :, cols]
    middle = copies.remote(pair, pair, me.by_mid)
    onward = copies.remote(pair_far, pair_far, me.by_zl)

    @pl.when(me.inner)
    def _():
        middle.start()

    yield 1

    @pl.when(me.inner)
    def _():
        middle.wait()
        onward.start()

    yield 1

    @pl.when(me.inner)
    def _():
        onward.wait_send()

    @pl.when(jnp.logical_not(me.inner))
    def _():
        onward.wait_recv()

    line = full.at[y, x, core, :, :, cols]
    near = copies.remote(line, line, me.by_x if x_first else me.by_y)
    near.start()
    across = [copies.remote(line, line, me.by_core)]
    across[0].start()
    yield 1
    near.wait()
    if x_first:
        block = full.at[y, :, core, :, :, cols]
        got = full.at[y, 1 - x, core, :, :, cols]
        rest = full.at[1 - y, :, core, :, :, cols]
    else:
        block = full.at[:, x, core, :, :, cols]
        got = full.at[1 - y, x, core, :, :, cols]
        rest = full.at[:, 1 - x, core, :, :, cols]
    far = copies.remote(block, block, me.by_y if x_first else me.by_x)
    far.start()
    across.append(copies.remote(got, got, me.by_core))
    across[1].start()
    yield 1
    far.wait()
    across.append(copies.remote(rest, rest, me.by_core))
    across[2].start()
    yield 1
    for copy in across:
        copy.wait()


def tokens_item(me, copies, tok, x_all, piece):
    place = me.core * 2 + me.zl
    there = (1 - me.core) * 2 + me.zl
    held = x_all.at[place, piece]
    out = copies.remote(tok.at[piece], x_all.at[there, piece], me.by_swap)
    keep = copies.local(tok.at[piece], held)
    along = copies.remote(held, held, me.by_zl)
    over = copies.remote(held, held, me.by_core)

    @pl.when(me.stays)
    def _():
        keep.start()

    @pl.when(jnp.logical_not(me.stays))
    def _():
        out.start()

    yield 1

    @pl.when(me.stays)
    def _():
        keep.wait()
        along.start()
        over.start()

    yield 1

    @pl.when(jnp.logical_not(me.stays))
    def _():
        out.wait()
        along.start()
        over.start()

    yield 1
    along.wait()
    came = x_all.at[me.core * 2 + 1 - me.zl, piece]
    onto = copies.remote(came, came, me.by_core)
    onto.start()
    yield 1
    over.wait()
    onto.wait()


def exchange_item(me, copies, src, dst):
    out = copies.remote(src, dst, me.by_swap)
    keep = copies.local(src, dst)

    @pl.when(me.stays)
    def _():
        keep.start()

    @pl.when(jnp.logical_not(me.stays))
    def _():
        out.start()

    yield 1

    @pl.when(me.stays)
    def _():
        keep.wait()

    @pl.when(jnp.logical_not(me.stays))
    def _():
        out.wait()


PIECES = 4


def weight_item(me, copies, src, parts, whole, bias):
    y, x, core, zh, zl = me.y, me.x, me.core, me.zh, me.zl
    place = core * 2 + zl
    keep = copies.local(src.at[place], parts.at[place])
    moves = [
        copies.remote(src.at[core * 2 + 1 - zl], parts.at[place], me.by_zl),
        copies.remote(src.at[(1 - core) * 2 + zl], parts.at[place], me.by_core),
        copies.remote(src.at[(1 - core) * 2 + 1 - zl], parts.at[place], me.by_both),
    ]
    keep.start()
    for move in moves:
        move.start()
    yield 1
    keep.wait()
    for move in moves:
        move.wait()
    own = whole.shape[4] // 2
    for b in range(2):
        both = jnp.concatenate([parts[2 * b, :own, :], parts[2 * b + 1, :own, :]], axis=0)
        whole[y, x, b, zh] = both.astype(bf16)
    tail = pl.ds(own, 8)
    bias[y, x, zh] = parts[0, tail, :] + parts[1, tail, :] + parts[2, tail, :] + parts[3, tail, :]
    for spot, bias_spot, other in (
        (whole.at[y, x, :, zh], bias.at[y, x, zh], me.by_zh),
        (whole.at[y, x], bias.at[y, x], me.by_x),
        (whole.at[y], bias.at[y], me.by_y),
    ):
        moves = [copies.remote(spot, spot, other), copies.remote(bias_spot, bias_spot, other)]
        for move in moves:
            move.start()
        yield 1
        for move in moves:
            move.wait()


def finish(*generators):
    for phases in generators:
        for _ in phases:
            pass


def front_kernel(heads, randoms, *refs):
    rand_ref, tok, og, wq, w_out, up, down, small = refs[:8]
    x_hbm, tok_own, og_own, w_own, qkv_hbm, res_hbm, ctx_all, out_all, up_all, down_all, small_all = refs[8:19]
    x_all, parts, whole, bias, qkv_ref, res_ref, ends_ref, ctx_ref = refs[19:27]
    me = Where()
    me.greet()
    copies = Copies(*refs[27:])
    blocks = qkv_ref.shape[0]
    length = blocks * BLOCK
    quarter = length // 4
    core, zl = me.core, me.zl
    place = core * 2 + zl
    near = core * 2 + 1 - zl
    beside = (1 - core) * 2 + zl
    across = (1 - core) * 2 + 1 - zl

    weights = weight_item(me, copies, wq, parts, whole, bias)
    tokens = [tokens_item(me, copies, tok, x_all, piece) for piece in range(PIECES)]
    smalls = gather_item(me, copies, small, small_all, slice(0, LANES), True)
    turn = 0

    def gathers(*arrays):
        nonlocal turn
        made = []
        for shard, full, splits in arrays:
            width = shard.shape[1] // splits
            for n in range(splits):
                cols = slice(n * width, (n + 1) * width)
                made.append(gather_item(me, copies, shard, full, cols, turn % 2 == 0))
                turn += 1
        return made

    def advance(group):
        group[:] = [phases for phases in group if next(phases, None) is not None]

    early = gathers((up, up_all, 2))
    late = gathers((down, down_all, 2), (w_out, out_all, 2))
    last = [exchange_item(me, copies, og, og_own)]
    idle = [smalls]
    outs = []

    def write(src, dst):
        copy = copies.local(src, dst)
        copy.start()
        outs.append(copy)

    def project(where):
        bias_row = jnp.sum(bias[...].reshape(-1, 8, bias.shape[-1]), axis=0)[0:1]
        matrix = whole[...].reshape(-1, whole.shape[-1])
        for piece in range(PIECES):
            raw = dot(x_all[where, piece], matrix) + bias_row
            step = ROWS // BLOCK
            at = (where * PIECES + piece) * step
            qkv_ref[pl.ds(at, step)] = raw.astype(bf16).reshape(step, BLOCK, raw.shape[1])

    def forward_tokens():
        for item in tokens:
            next(item)

    next(weights)
    advance(early)
    next(weights)
    forward_tokens()
    forward_tokens()
    advance(early)
    next(weights)
    advance(idle)
    next(weights)
    advance(early)
    forward_tokens()
    advance(idle)
    finish(weights)
    advance(late)
    project(place)
    advance(early)
    write(whole, w_own)
    write(x_all.at[place], tok_own)
    advance(late)
    forward_tokens()
    project(near)
    finish(*tokens)
    advance(last)
    advance(early)
    project(beside)
    project(across)
    advance(late)
    advance(idle)
    write(x_all, x_hbm)
    write(qkv_ref, qkv_hbm)
    for h, both in enumerate(global_blocks(qkv_ref, heads, length)):
        ends_ref[h] = both
    advance(late)
    advance(early)
    advance(idle)

    def middle(t, carry):
        middle_blocks(qkv_ref, rand_ref, res_ref, t * PAIR, heads, randoms, blocks)
        return carry

    sends = []
    turns = quarter // BLOCK // PAIR
    for where, other in ((across, me.by_both), (near, me.by_zl), (beside, me.by_core), (place, None)):
        lax.fori_loop(where * turns, (where + 1) * turns, middle, 0)

        @pl.when(where == 0)
        def _():
            for h in range(heads):
                res_ref[h, 0:BLOCK, :] = ends_ref[h, 0:BLOCK, :]

        @pl.when(where == 3)
        def _():
            for h in range(heads):
                res_ref[h, length - BLOCK : length, :] = ends_ref[h, BLOCK : 2 * BLOCK, :]

        for piece in range(PIECES):
            pack_rows(res_ref, ctx_ref, where * quarter + piece * ROWS, where, piece)
        rows = rows_at(where * quarter, quarter)
        write(res_ref.at[:, rows], res_hbm.at[:, rows])
        if other is None:
            write(ctx_ref.at[where], ctx_all.at[place])
        else:
            send = copies.remote(ctx_ref.at[where], ctx_all.at[place], other)
            send.start()
            sends.append(send)
        advance(late if where is near or where is place else idle)
    finish(*early, *late, *last, *idle)
    for copy in sends + outs:
        copy.wait()


def front(rand, tok, og, wq, mats, small, heads):
    rows, width = tok.shape
    members = 4
    length = rows * members
    randoms = rand.size // (heads * (length // BLOCK - 2))
    hbm = pl.BlockSpec(memory_space=pltpu.HBM)
    shape = jax.ShapeDtypeStruct
    tok = tok.reshape(PIECES, rows // PIECES, width)
    cols = heads * SLOT
    own = mats[0].shape[0]
    packed = (members, rows // ROWS, ROWS * 3 // 2, LANES)
    outs = [
        shape((members,) + tok.shape, bf16),
        shape(tok.shape, bf16),
        shape(og.shape, bf16),
        shape((2, 2, 2, 2, 2 * own, cols), bf16),
        shape((length // BLOCK, BLOCK, cols), bf16),
        shape((heads, length, LANES), f32),
        shape(packed, bf16),
    ]
    outs += [shape((2, 2, 2, 4) + a.shape, bf16) for a in (*mats, small)]
    return pl.pallas_call(
        partial(front_kernel, heads, randoms),
        out_shape=tuple(outs),
        in_specs=[pl.BlockSpec(memory_space=pltpu.SMEM)] + [hbm] * 7,
        out_specs=(hbm,) * 11,
        scratch_shapes=[
            pltpu.VMEM((members,) + tok.shape, bf16),
            pltpu.VMEM(wq.shape, f32),
            pltpu.VMEM((2, 2, 2, 2, 2 * own, cols), bf16),
            pltpu.VMEM((2, 2, 2, 8, cols), f32),
            pltpu.VMEM((length // BLOCK, BLOCK, cols), bf16),
            pltpu.VMEM((heads, length, LANES), f32),
            pltpu.VMEM((heads, 2 * BLOCK, LANES), f32),
            pltpu.VMEM(packed, bf16),
            pltpu.SemaphoreType.DMA((112,)),
            pltpu.SemaphoreType.DMA((112,)),
            pltpu.SemaphoreType.DMA((32,)),
        ],
        compiler_params=pltpu.CompilerParams(
            collective_id=0, has_side_effects=True, vmem_limit_bytes=VMEM_BYTES
        ),
        name="front",
    )(rand, tok, og, wq, *mats, small)


def add_rows(dst, a, b, rows):
    step = next(n for n in (48, 32, 24, 16, 8) if rows % n == 0)

    def body(t, carry):
        at = rows_at(t * step, step)
        dst[at, :] = (a[at, :].astype(f32) + b[at, :].astype(f32)).astype(dst.dtype)
        return carry

    lax.fori_loop(0, rows // step, body, 0)


def scatter_item(me, copies, src, cols, acc, from_core, from_first, from_second, from_zh, part, from_zl, out, x_first):
    y, x, core, zh, zl = me.y, me.x, me.core, me.zh, me.zl
    rows = acc.shape[2]
    own = copies.local(src.at[:, :, core, :, cols], acc)
    over = copies.remote(src.at[:, :, 1 - core, :, cols], from_core, me.by_core)
    own.start()
    over.start()
    yield 1
    own.wait()
    over.wait()
    for a in range(2):
        for b in range(2):
            add_rows(acc.at[a, b], acc.at[a, b], from_core.at[a, b], rows)
    if x_first:
        first = copies.remote(acc.at[:, 1 - x], from_first, me.by_x)
    else:
        first = copies.remote(acc.at[1 - y], from_first, me.by_y)
    first.start()
    yield 1
    first.wait()
    for a in range(2):
        block = acc.at[a, x] if x_first else acc.at[y, a]
        add_rows(block, block, from_first.at[a], rows)
    if x_first:
        second = copies.remote(acc.at[1 - y, x], from_second, me.by_y)
    else:
        second = copies.remote(acc.at[y, 1 - x], from_second, me.by_x)
    second.start()
    yield 1
    second.wait()
    block = acc.at[y, x]
    add_rows(block, block, from_second, rows)
    half = rows // 2
    third = copies.remote(block.at[rows_at((1 - zh) * half, half)], from_zh, me.by_zh)
    third.start()
    yield 1
    third.wait()
    add_rows(part, block.at[rows_at(zh * half, half)], from_zh, half)
    last = half // 2
    fourth = copies.remote(part.at[rows_at((1 - zl) * last, last)], from_zl, me.by_zl)
    fourth.start()
    yield 1
    fourth.wait()
    add_rows(out, part.at[rows_at(zl * last, last)], from_zl, last)


def scatter_buffers(rows, cols, kind):
    return [
        pltpu.VMEM((2, 2, rows, cols), kind),
        pltpu.VMEM((2, 2, rows, cols), kind),
        pltpu.VMEM((2, rows, cols), kind),
        pltpu.VMEM((rows, cols), kind),
        pltpu.VMEM((rows // 2, cols), kind),
        pltpu.VMEM((rows // 2, cols), f32),
        pltpu.VMEM((rows // 4, cols), f32),
    ]


def own_columns_item(me, copies, src, acc, from_x, from_y, from_zh, part, out):
    y, x, core, zh, zl = me.y, me.x, me.core, me.zh, me.zl
    rows = src.shape[4]
    keep = copies.local(src.at[:, x], acc)
    first = copies.remote(src.at[:, 1 - x], from_x, me.by_x)
    keep.start()
    first.start()
    yield 1
    keep.wait()
    first.wait()
    for a in range(2):
        for b in range(2):
            for c in range(2):
                add_rows(acc.at[a, b, c], acc.at[a, b, c], from_x.at[a, b, c], rows)
    second = copies.remote(acc.at[1 - y], from_y, me.by_y)
    second.start()
    yield 1
    second.wait()
    for b in range(2):
        for c in range(2):
            block = acc.at[y, b, c]
            add_rows(block, block, from_y.at[b, c], rows)
    third = copies.remote(acc.at[y, :, 1 - zh], from_zh, me.by_zh)
    third.start()
    yield 1
    third.wait()
    half = rows // 2
    for b in range(2):
        add_rows(part.at[b], acc.at[y, b, zh], from_zh.at[b], rows)
    place = core * 2 + zl
    mine = rows_at(zl * half, half)
    other = rows_at((1 - zl) * half, half)
    keep = copies.local(part.at[core, mine], out.at[place])
    keep.start()
    moves = [
        copies.remote(part.at[core, other], out.at[place], me.by_zl),
        copies.remote(part.at[1 - core, mine], out.at[place], me.by_core),
        copies.remote(part.at[1 - core, other], out.at[place], me.by_both),
    ]
    for move in moves:
        move.start()
    yield 1
    keep.wait()
    for move in moves:
        move.wait()


def input_grad_item(me, copies, dx, dres, piece, acc, from_core, from_zl, res, send, out):
    core, zl = me.core, me.zl
    rows = acc.shape[1]
    keep = copies.local(dx.at[core, :, piece], acc)
    more = copies.local(dres.at[piece], res)
    over = copies.remote(dx.at[1 - core, :, piece], from_core, me.by_core)
    keep.start()
    more.start()
    over.start()
    yield 1
    keep.wait()
    over.wait()
    add_rows(acc.at[1 - zl], acc.at[1 - zl], from_core.at[1 - zl], rows)
    along = copies.remote(acc.at[1 - zl], from_zl, me.by_zl)
    along.start()
    add_rows(acc.at[zl], acc.at[zl], from_core.at[zl], rows)
    more.wait()
    add_rows(res, res, acc.at[zl], rows)
    yield 1
    along.wait()
    add_rows(send, res, from_zl, rows)
    yield from exchange_item(me, copies, send, out.at[piece])


SPLITS = ((0, 2), (1, 4), (2, 1), (3, 1))


def scatter_kernel(*refs):
    down, up, proj, vecs, qkv, dx, dres = refs[:7]
    outs = refs[7:13]
    sems, scratch = refs[13:16], list(refs[16:])
    me = Where()
    me.greet()
    copies = Copies(*sems)
    items = []

    def take(n):
        got = scratch[:n]
        del scratch[:n]
        return got

    for piece in range(PIECES):
        items.append((piece, input_grad_item(me, copies, dx, dres, piece, *take(5), outs[5])))
    items.append((0, own_columns_item(me, copies, qkv, *take(5), outs[4])))
    step = 0
    for n, splits in SPLITS:
        src = refs[n]
        width = src.shape[4] // splits
        for part in range(splits):
            cols = slice(part * width, (part + 1) * width)
            item = scatter_item(me, copies, src, cols, *take(7), outs[n].at[:, cols], step % 2 == 0)
            items.append((step // 2, item))
            step += 1
    items.sort(key=lambda item: item[0])
    run_phases(items)


def scatter(down, up, proj, vecs, qkv, dx, dres):
    hbm = pl.BlockSpec(memory_space=pltpu.HBM)
    vmem = pl.BlockSpec(memory_space=pltpu.VMEM)
    shape = jax.ShapeDtypeStruct
    grads = (down, up, proj, vecs)
    outs = [shape((a.shape[3] // 4, a.shape[4]), f32) for a in grads]
    rows, cols = qkv.shape[4:]
    outs.append(shape((4, rows // 2, cols), f32))
    outs.append(shape(dres.shape, bf16))
    buffers = []
    for _ in range(PIECES):
        tile = dres.shape[1:]
        buffers += [
            pltpu.VMEM((2,) + tile, bf16),
            pltpu.VMEM((2,) + tile, bf16),
            pltpu.VMEM(tile, bf16),
            pltpu.VMEM(tile, f32),
            pltpu.VMEM(tile, bf16),
        ]
    buffers += [
        pltpu.VMEM((2, 2, 2, rows, cols), bf16),
        pltpu.VMEM((2, 2, 2, rows, cols), bf16),
        pltpu.VMEM((2, 2, rows, cols), bf16),
        pltpu.VMEM((2, rows, cols), bf16),
        pltpu.VMEM((2, rows, cols), f32),
    ]
    for n, splits in SPLITS:
        a = grads[n]
        for _ in range(splits):
            buffers += scatter_buffers(a.shape[3], a.shape[4] // splits, a.dtype)
    return pl.pallas_call(
        scatter_kernel,
        out_shape=tuple(outs),
        in_specs=[hbm] * 7,
        out_specs=(vmem,) * 5 + (hbm,),
        scratch_shapes=[
            pltpu.SemaphoreType.DMA((80,)),
            pltpu.SemaphoreType.DMA((80,)),
            pltpu.SemaphoreType.DMA((32,)),
        ]
        + buffers,
        compiler_params=pltpu.CompilerParams(
            collective_id=1, has_side_effects=True, vmem_limit_bytes=VMEM_BYTES
        ),
        name="scatter",
    )(down, up, proj, vecs, qkv, dx, dres)


def per_device(
    tokens,
    qkv_weight,
    query_value_bias,
    out_weight,
    out_bias,
    norm1_gain,
    norm1_bias,
    up_weight,
    up_bias,
    down_weight,
    down_bias,
    norm2_gain,
    norm2_bias,
    rand_blocks,
    out_grad,
):
    members = lax.axis_size(GROUP)
    devices = lax.axis_size(ALL)
    swap = [(0, 0), (1, 2), (2, 1), (3, 3)]

    def move(a):
        return lax.ppermute(a, ("core", "zh"), swap)

    rand = move(rand_blocks[0])
    heads = rand.shape[0]
    rows, width = tokens.shape[1:]
    cols = heads * HEAD_DIM
    group = lax.axis_index(GROUP)
    own = width // devices
    rand_flat = rand.reshape(-1)

    def lay_out(a):
        a = a.reshape(a.shape[:-2] + (3, heads, HEAD_DIM))
        q, k, v = a[..., 0, :, :], a[..., 1, :, :], a[..., 2, :, :]
        q = q * jnp.asarray(HEAD_DIM**-0.5, a.dtype)
        laid = jnp.stack([q, jnp.zeros_like(q), k, v], axis=-2)
        return laid.reshape(laid.shape[:-3] + (heads * SLOT,))

    bias_part = jnp.stack([query_value_bias[0], jnp.zeros((own,), bf16), query_value_bias[1]])
    small = [out_bias, norm1_gain, norm1_bias, down_bias, norm2_gain, norm2_bias, up_bias]
    small = jnp.concatenate(small)
    direct = lax.axis_size("c") == 4 and members == 4 and own % 8 == 0
    if direct:
        count = small.shape[0]
        padded = jnp.pad(small, (0, 16 * LANES - count)).reshape(16, LANES)
        spread = lax.dynamic_update_slice(
            jnp.zeros((3, width), f32), bias_part.astype(f32), (0, lax.axis_index(ALL) * own)
        )
        spread = lay_out(jnp.transpose(spread.reshape(3, members, cols), (1, 0, 2)))
        wq = jnp.transpose(qkv_weight.astype(f32).reshape(own, 3, members, cols), (2, 0, 1, 3))
        wq = jnp.concatenate([lay_out(wq), spread[:, None], jnp.zeros((members, 7, heads * SLOT), f32)], axis=1)
        mats = (out_weight, up_weight, down_weight)
        x, tok, og, w_own, qkv, res, ctx, *full = front(
            rand_flat, tokens[0], out_grad[0], wq, mats, padded, heads
        )
        x, tok = x.reshape(-1, width), tok.reshape(-1, width)
        w_own = w_own.reshape(width, -1)
        w_out, w_up, w_down = (a.reshape(-1, a.shape[-1]) for a in full[:3])
        small = full[3].reshape(devices, -1)[:, :count].astype(f32)
    else:
        tok = move(tokens[0])
        og = move(out_grad[0])
        x = lax.all_gather(tok, GROUP, axis=0, tiled=True)
        mats = (qkv_weight, out_weight, up_weight, down_weight)
        w_qkv, w_out, w_up, w_down = (lax.all_gather(a, ALL, axis=0, tiled=True) for a in mats)
        small = lax.all_gather(small, ALL, axis=0).astype(f32)
        w_own = lax.dynamic_slice_in_dim(
            w_qkv.reshape(width, 3, members, cols), group, 1, axis=2
        ).reshape(width, 3, cols)
        w_own = lay_out(w_own)
        bias3 = lax.all_gather(bias_part, ALL, axis=1, tiled=True).astype(f32).reshape(3, members, cols)
        b_own = lay_out(lax.dynamic_slice_in_dim(bias3, group, 1, axis=1).reshape(1, 3, cols))
        qkv, res, ctx_send = attend(rand_flat, x, w_own, b_own, members, heads)
        ctx = lax.all_to_all(ctx_send, GROUP, split_axis=0, concat_axis=0, tiled=True)
    vecs = jnp.transpose(small[:, : 6 * own].reshape(devices, 6, own), (1, 0, 2)).reshape(6, width)
    bias_up = small[:, 6 * own :].reshape(1, -1)
    chain_vecs = jnp.concatenate([vecs, jnp.zeros((2, width), f32)], axis=0)
    out, dres1, dctx, mix, hid, act, dpre, dffn, dproj, gvec, gbu = chain(
        ctx, tok, og, w_out, w_up, w_down, chain_vecs, bias_up, direct
    )
    if direct:
        out = out.reshape(rows, width)
    else:
        dctx = lax.all_to_all(dctx, GROUP, split_axis=0, concat_axis=0, tiled=True)
        out = move(out)

    g_down = dot_tn(act, dffn).astype(bf16)
    g_up = dot_tn(hid, dpre).astype(bf16)
    g_mix = dot_tn(mix, dproj).astype(bf16)
    pairs = g_mix[: members * LANES].reshape(members, LANES, width)
    thirds = g_mix[members * LANES :].reshape(members, HEAD_DIM, width)
    g_out = jnp.concatenate([pairs, thirds], axis=1).reshape(width, width)

    draw, sums = attend_back(rand_flat, qkv, res, dctx, heads)
    dx = dot_nt(draw, w_own).astype(bf16)
    g_qkv = dot_tn(x, draw)

    def strip(a):
        a = a.reshape(a.shape[:-1] + (heads, 4, HEAD_DIM))
        q, k, v = a[..., 0, :] * (HEAD_DIM**-0.5), a[..., 2, :], a[..., 3, :]
        return jnp.stack([q, k, v], axis=-3).reshape(a.shape[:-3] + (3, cols))

    col_sums = strip(sums[0:1])[0]
    pair = jnp.stack([col_sums[0], col_sums[2]]).reshape(2, 1, cols)
    mine = (jnp.arange(members) == group)[None, :, None]
    pair = jnp.where(mine, pair, 0.0).reshape(2, width)
    vec_grads = jnp.concatenate([pair, gvec[0:6]], axis=0).reshape(8, devices, own)
    vec_grads = jnp.transpose(vec_grads, (1, 0, 2)).reshape(devices, 8 * own)
    vec_grads = jnp.concatenate([vec_grads, gbu[0].reshape(devices, -1)], axis=1)
    count = vec_grads.shape[1]

    if direct:
        lines = 8
        padded = jnp.pad(vec_grads, ((0, 0), (0, lines * LANES - count)))
        g_down, g_up, g_out, vec_grads, g_qkv, input_grad = scatter(
            g_down.reshape(2, 2, 2, -1, width),
            g_up.reshape(2, 2, 2, -1, g_up.shape[1]),
            g_out.reshape(2, 2, 2, -1, width),
            padded.reshape(2, 2, 2, 4 * lines, LANES),
            g_qkv.astype(bf16).reshape(2, 2, 2, 2, 2 * own, -1),
            dx.reshape(2, 2, PIECES, -1, width),
            dres1.reshape(PIECES, -1, width),
        )
        vec_grads = vec_grads.reshape(-1)[:count]
        input_grad = input_grad.reshape(rows, width).astype(f32)
        g_qkv = strip(g_qkv)
    else:

        def reduce(a):
            return lax.psum_scatter(a, ALL, scatter_dimension=0, tiled=True).astype(f32)

        g_down, g_up, g_out, vec_grads = reduce(g_down), reduce(g_up), reduce(g_out), reduce(vec_grads)[0]
        dx = lax.psum_scatter(dx, GROUP, scatter_dimension=0, tiled=True)
        input_grad = move((dres1 + dx.astype(f32)).astype(bf16)).astype(f32)
        g_qkv = strip(g_qkv).reshape(-1, 2, 2, members // 2, own, 3 * cols)
        g_qkv = jnp.transpose(g_qkv, (0, 2, 1, 3, 4, 5)).reshape(-1, members, own, 3 * cols)
        g_qkv = g_qkv.reshape(-1, 3 * cols).astype(bf16)
        g_qkv = lax.psum_scatter(g_qkv, REST, scatter_dimension=0, tiled=True)
        g_qkv = g_qkv.reshape(members, own, 3 * cols)
        g_qkv = lax.all_to_all(g_qkv, GROUP, split_axis=0, concat_axis=0, tiled=True).astype(f32)
    g_qkv = jnp.transpose(g_qkv.reshape(members, own, 3, cols), (1, 2, 0, 3)).reshape(own, -1)
    v8 = vec_grads[: 8 * own].reshape(8, own)
    return (
        out[None],
        input_grad[None],
        g_qkv,
        v8[0:2],
        g_out,
        v8[2],
        v8[3],
        v8[4],
        g_up,
        vec_grads[8 * own :],
        g_down,
        v8[5],
        v8[6],
        v8[7],
    )


def solution(mesh):
    dp, sp = mesh.shape["dp"], mesh.shape["sp"]
    fine = Mesh(mesh.devices.reshape(dp // 2, 2, 2, sp // 2), ALL)
    dp, sp = ("c", "core"), ("zh", "zl")
    act = P(dp, sp, None)
    mat = P(ALL, None)
    pair = P(None, ALL)
    vec = P(ALL)
    rand = P(dp, sp, None, None)
    return jax.shard_map(
        per_device,
        mesh=fine,
        in_specs=(act, mat, pair, mat, vec, vec, vec, mat, vec, mat, vec, vec, vec, rand, act),
        out_specs=(act, act, mat, pair, mat, vec, vec, vec, mat, vec, mat, vec, vec, vec),
        check_vma=False,
    )
```

```python
from functools import partial

import jax
import jax.numpy as jnp
import numpy as np
from jax import lax
from jax.experimental import pallas as pl
from jax.experimental.pallas import tpu as pltpu
from jax.sharding import Mesh
from jax.sharding import PartitionSpec as P

HEAD_DIM = 64
BLOCK = 64
LANES = 128
SLOT = 4 * HEAD_DIM
EPS = 1e-05
MASKED = -1e30
ALL = ("c", "core", "zh", "zl")
GROUP = ("core", "zl")
REST = ("c", "zh")
CHUNK = 512
ROWS = 256
PAIR = 2
SUBS = 1
PAIR_BACK = 2
VMEM_BYTES = 60 * 1024 * 1024

f32 = jnp.float32
bf16 = jnp.bfloat16
NT = (((1,), (1,)), ((), ()))
TN = (((0,), (0,)), ((), ()))


def dot(a, b):
    return jnp.dot(a, b, preferred_element_type=f32)


def dot_nt(a, b):
    return lax.dot_general(a, b, NT, preferred_element_type=f32)


def dot_tn(a, b):
    return lax.dot_general(a, b, TN, preferred_element_type=f32)


def rows_at(start, size):
    return pl.ds(pl.multiple_of(start, size), size)


def listed(ref, rand_ref, head, i, blocks, randoms):
    cols = slice(head * SLOT + LANES, head * SLOT + SLOT)
    near = jnp.clip(i - 1, 0, blocks - 3)
    parts = [ref[0, :, cols], ref[blocks - 1, :, cols]]
    parts += [ref[near + n, :, cols] for n in range(3)]
    base = (head * (blocks - 2) + near) * randoms
    parts += [ref[rand_ref[base + r], :, cols] for r in range(randoms)]
    return jnp.concatenate(parts, axis=0)


def keys_values(ref, head, t, size):
    cols = slice(head * SLOT + LANES, head * SLOT + SLOT)
    return ref[pl.ds(t * (size // BLOCK), size // BLOCK), :, cols].reshape(size, LANES)


def mask_globals(s, i, blocks):
    lane = lax.broadcasted_iota(jnp.int32, (BLOCK, LANES), 1)
    low = lane < BLOCK
    dead = (low & (i == 1)) | (~low & (i == blocks - 2))
    return jnp.concatenate([jnp.where(dead, MASKED, s[:, :LANES]), s[:, LANES:]], axis=1)


def middle_blocks(qkv_ref, rand_ref, res_ref, first, heads, randoms, blocks):
    lane = lax.broadcasted_iota(jnp.int32, (BLOCK, LANES), 1)
    work = [(first + n, h) for n in range(PAIR) for h in range(heads)]
    kvs = [listed(qkv_ref, rand_ref, h, i, blocks, randoms) for i, h in work]
    qs = [qkv_ref[i, :, h * SLOT : h * SLOT + LANES] for i, h in work]
    ss = [mask_globals(dot_nt(q, kv), i, blocks) for q, kv, (i, h) in zip(qs, kvs, work)]
    tops = [jnp.max(s, axis=1, keepdims=True) for s in ss]
    es = [jnp.exp(s - top) for s, top in zip(ss, tops)]
    totals = [jnp.sum(e, axis=1, keepdims=True) for e in es]
    os = [dot(e.astype(bf16), kv) for e, kv in zip(es, kvs)]
    for o, top, total, (i, h) in zip(os, tops, totals, work):
        both = jnp.where(lane < HEAD_DIM, top + jnp.log(total), o / total)
        res_ref[h, rows_at(i * BLOCK, BLOCK), :] = both


def global_blocks(qkv_ref, heads, length):
    last = length // BLOCK - 1

    def ends(h):
        cols = slice(h * SLOT, h * SLOT + LANES)
        return jnp.concatenate([qkv_ref[0, :, cols], qkv_ref[last, :, cols]], axis=0)

    qs = [ends(h) for h in range(heads)]

    def whole(t, carry):
        kvs = [keys_values(qkv_ref, h, t, CHUNK) for h in range(heads)]
        ss = [dot_nt(q, kv) for q, kv in zip(qs, kvs)]
        news = [jnp.maximum(c[0], jnp.max(s, axis=1, keepdims=True)) for c, s in zip(carry, ss)]
        fades = [jnp.exp(c[0] - new) for c, new in zip(carry, news)]
        es = [jnp.exp(s - new) for s, new in zip(ss, news)]
        sums = [jnp.sum(e, axis=1, keepdims=True) for e in es]
        os = [dot(e.astype(bf16), kv) for e, kv in zip(es, kvs)]
        return tuple(
            (new, c[1] * fade + total, c[2] * fade + o)
            for c, new, fade, total, o in zip(carry, news, fades, sums, os)
        )

    start = (
        jnp.full((2 * BLOCK, 1), MASKED, f32),
        jnp.zeros((2 * BLOCK, 1), f32),
        jnp.zeros((2 * BLOCK, LANES), f32),
    )
    done = lax.fori_loop(0, length // CHUNK, whole, (start,) * heads)
    lane = lax.broadcasted_iota(jnp.int32, (2 * BLOCK, LANES), 1)
    return [jnp.where(lane < HEAD_DIM, top + jnp.log(total), acc / total) for top, total, acc in done]


def pack_rows(res_ref, ctx_ref, start, part, piece):
    low = lax.broadcasted_iota(jnp.int32, (BLOCK, LANES), 1) < HEAD_DIM
    for n in range(ROWS // BLOCK):
        rows = rows_at(start + n * BLOCK, BLOCK)
        first = pltpu.roll(res_ref[0, rows, :], HEAD_DIM, 1)
        pair = jnp.where(low, first, res_ref[1, rows, :])
        ctx_ref[part, piece, n * BLOCK : (n + 1) * BLOCK, :] = pair.astype(bf16)
    for n in range(ROWS // (2 * BLOCK)):
        rows = rows_at(start + 2 * n * BLOCK, BLOCK)
        odd = rows_at(start + (2 * n + 1) * BLOCK, BLOCK)
        first = pltpu.roll(res_ref[2, rows, :], HEAD_DIM, 1)
        both = jnp.where(low, first, res_ref[2, odd, :])
        ctx_ref[part, piece, ROWS + n * BLOCK : ROWS + (n + 1) * BLOCK, :] = both.astype(bf16)


def attend_kernel(heads, randoms, rand_ref, x_ref, w_ref, b_ref, qkv_ref, res_ref, ctx_ref):
    length = x_ref.shape[0]
    blocks = length // BLOCK

    def project(t, carry):
        raw = dot(x_ref[rows_at(t * CHUNK, CHUNK), :], w_ref[...]) + b_ref[...]
        step = CHUNK // BLOCK
        qkv_ref[pl.ds(t * step, step)] = raw.astype(bf16).reshape(step, BLOCK, raw.shape[1])
        return carry

    lax.fori_loop(0, length // CHUNK, project, 0)

    def middle(t, carry):
        middle_blocks(qkv_ref, rand_ref, res_ref, t * PAIR, heads, randoms, blocks)
        return carry

    lax.fori_loop(0, blocks // PAIR, middle, 0)
    for h, both in enumerate(global_blocks(qkv_ref, heads, length)):
        res_ref[h, 0:BLOCK, :] = both[:BLOCK]
        res_ref[h, length - BLOCK : length, :] = both[BLOCK:]
    per_quarter = ctx_ref.shape[1]

    def pack(t, carry):
        pack_rows(res_ref, ctx_ref, t * ROWS, t // per_quarter, t % per_quarter)
        return carry

    lax.fori_loop(0, length // ROWS, pack, 0)


def attend(rand, x, w, b, parts, heads):
    length = x.shape[0]
    randoms = rand.size // (heads * (length // BLOCK - 2))
    vmem = pl.BlockSpec(memory_space=pltpu.VMEM)
    return pl.pallas_call(
        partial(attend_kernel, heads, randoms),
        out_shape=(
            jax.ShapeDtypeStruct((length // BLOCK, BLOCK, heads * SLOT), bf16),
            jax.ShapeDtypeStruct((heads, length, LANES), f32),
            jax.ShapeDtypeStruct((parts, length // parts // ROWS, ROWS * 3 // 2, LANES), bf16),
        ),
        in_specs=[pl.BlockSpec(memory_space=pltpu.SMEM), vmem, vmem, vmem],
        out_specs=(vmem, vmem, vmem),
        compiler_params=pltpu.CompilerParams(vmem_limit_bytes=VMEM_BYTES),
        name="attend",
    )(rand, x, w, b)


def attend_back_kernel(
    heads, randoms, rand_ref, qkv_ref, res_ref, dctx_ref, draw_ref, sums_ref, *scratch
):
    dout, acc = scratch[:heads], scratch[heads:]
    blocks = qkv_ref.shape[0]
    length = blocks * BLOCK
    last = (blocks - 1) * BLOCK
    per_quarter = dctx_ref.shape[1]

    def unpack(t, carry):
        part, piece = t // per_quarter, t % per_quarter
        lane = lax.broadcasted_iota(jnp.int32, (BLOCK, LANES), 1)
        low = lane < HEAD_DIM
        for n in range(ROWS // BLOCK):
            rows = rows_at(t * ROWS + n * BLOCK, BLOCK)
            pair = dctx_ref[part, piece, n * BLOCK : (n + 1) * BLOCK, :].astype(f32)
            dout[0][rows, :] = jnp.where(low, 0.0, pltpu.roll(pair, HEAD_DIM, 1)).astype(bf16)
            dout[1][rows, :] = jnp.where(low, 0.0, pair).astype(bf16)
        for n in range(ROWS // (2 * BLOCK)):
            rows = rows_at(t * ROWS + 2 * n * BLOCK, BLOCK)
            odd = rows_at(t * ROWS + (2 * n + 1) * BLOCK, BLOCK)
            both = dctx_ref[part, piece, ROWS + n * BLOCK : ROWS + (n + 1) * BLOCK, :].astype(f32)
            dout[2][rows, :] = jnp.where(low, 0.0, pltpu.roll(both, HEAD_DIM, 1)).astype(bf16)
            dout[2][odd, :] = jnp.where(low, 0.0, both).astype(bf16)
        return carry

    lax.fori_loop(0, length // ROWS, unpack, 0)

    step = 256

    def ends(ref, cols):
        return jnp.concatenate([ref[0:BLOCK, cols], ref[last : last + BLOCK, cols]], axis=0)

    every = slice(0, LANES)
    gs = [ends(dout[h], every) for h in range(heads)]
    reses = [ends(res_ref.at[h], every) for h in range(heads)]
    alls = [
        jnp.concatenate(
            [qkv_ref[n, :, h * SLOT : h * SLOT + LANES] for n in (0, blocks - 1)] + [gs[h]], axis=0
        )
        for h in range(heads)
    ]
    logs = [res[:, 0:1] for res in reses]
    deltas = [jnp.sum(g.astype(f32) * res, axis=1, keepdims=True) for g, res in zip(gs, reses)]

    def whole(t, dqs):
        rows = rows_at(t * step, step)
        kvs = [keys_values(qkv_ref, h, t, step) for h in range(heads)]
        sds = [dot_nt(both, kv) for both, kv in zip(alls, kvs)]
        ps = [jnp.exp(sd[: 2 * BLOCK] - log) for sd, log in zip(sds, logs)]
        dss = [(p * (sd[2 * BLOCK :] - d)).astype(bf16) for p, sd, d in zip(ps, sds, deltas)]
        dkvs = [
            dot_tn(jnp.concatenate([ds, p.astype(bf16)], axis=0), both)
            for ds, p, both in zip(dss, ps, alls)
        ]
        news = tuple(dq + dot(ds, kv) for dq, ds, kv in zip(dqs, dss, kvs))
        for h in range(heads):
            acc[h][rows, :] = dkvs[h]
        return news

    dqs = lax.fori_loop(
        0, length // step, whole, (jnp.zeros((2 * BLOCK, LANES), f32),) * heads
    )
    for h in range(heads):
        cols = slice(h * SLOT, h * SLOT + LANES)
        lane = lax.broadcasted_iota(jnp.int32, (2 * BLOCK, LANES), 1)
        dq = jnp.where(lane < HEAD_DIM, dqs[h], 0.0).astype(bf16)
        draw_ref[0:BLOCK, cols] = dq[:BLOCK]
        draw_ref[last : last + BLOCK, cols] = dq[BLOCK:]

    def middle(t, carry):
        lane = lax.broadcasted_iota(jnp.int32, (BLOCK, LANES), 1)
        work = [(1 + t * PAIR_BACK + n, h) for n in range(PAIR_BACK) for h in range(heads)]
        kvs = [listed(qkv_ref, rand_ref, h, i, blocks, randoms) for i, h in work]
        places = [(rows_at(i * BLOCK, BLOCK), slice(h * SLOT, h * SLOT + LANES)) for i, h in work]
        gs = [dout[h][rows, :] for (rows, _), (_, h) in zip(places, work)]
        reses = [res_ref[h, rows, :] for (rows, _), (_, h) in zip(places, work)]
        alls = [
            jnp.concatenate([qkv_ref[i, :, cols], g], axis=0)
            for (_, cols), (i, _), g in zip(places, work, gs)
        ]
        sds = [dot_nt(both, kv) for both, kv in zip(alls, kvs)]
        deltas = [jnp.sum(g.astype(f32) * res, axis=1, keepdims=True) for g, res in zip(gs, reses)]
        ps = [
            jnp.exp(mask_globals(sd[:BLOCK], i, blocks) - res[:, 0:1])
            for sd, res, (i, h) in zip(sds, reses, work)
        ]
        dss = [(p * (sd[BLOCK:] - d)).astype(bf16) for p, sd, d in zip(ps, sds, deltas)]
        dkvs = [
            dot_tn(jnp.concatenate([ds, p.astype(bf16)], axis=0), both)
            for ds, p, both in zip(dss, ps, alls)
        ]
        dqs = [dot(ds, kv) for ds, kv in zip(dss, kvs)]
        for dq, (rows, cols) in zip(dqs, places):
            draw_ref[rows, cols] = jnp.where(lane < HEAD_DIM, dq, 0.0).astype(bf16)
        for dkv, (i, h) in zip(dkvs, work):
            acc[h][0:BLOCK, :] += dkv[0:BLOCK]
            acc[h][last : last + BLOCK, :] += dkv[BLOCK : 2 * BLOCK]
            near = pl.ds(pl.multiple_of((i - 1) * BLOCK, BLOCK), 3 * BLOCK)
            acc[h][near, :] += dkv[2 * BLOCK : 5 * BLOCK]
            base = (h * (blocks - 2) + i - 1) * randoms
            for r in range(randoms):
                far = rows_at(rand_ref[base + r] * BLOCK, BLOCK)
                acc[h][far, :] += dkv[(5 + r) * BLOCK : (6 + r) * BLOCK]
        return carry

    lax.fori_loop(0, (blocks - 2) // PAIR_BACK, middle, 0)
    sums_ref[...] = jnp.zeros_like(sums_ref)

    def finish(t, carry):
        rows = rows_at(t * CHUNK, CHUNK)
        for h in range(heads):
            at = h * SLOT
            draw_ref[rows, at + LANES : at + SLOT] = acc[h][rows, :].astype(bf16)
        sums_ref[0:1, :] += jnp.sum(draw_ref[rows, :].astype(f32), axis=0, keepdims=True)
        return carry

    lax.fori_loop(0, length // CHUNK, finish, 0)


def attend_back(rand, qkv, res, dctx, heads):
    length = qkv.shape[0] * BLOCK
    randoms = rand.size // (heads * (length // BLOCK - 2))
    vmem = pl.BlockSpec(memory_space=pltpu.VMEM)
    return pl.pallas_call(
        partial(attend_back_kernel, heads, randoms),
        out_shape=(
            jax.ShapeDtypeStruct((length, heads * SLOT), bf16),
            jax.ShapeDtypeStruct((8, heads * SLOT), f32),
        ),
        in_specs=[pl.BlockSpec(memory_space=pltpu.SMEM), vmem, vmem, vmem],
        out_specs=(vmem, vmem),
        scratch_shapes=[pltpu.VMEM((length, LANES), bf16)] * heads
        + [pltpu.VMEM((length, LANES), f32)] * heads,
        compiler_params=pltpu.CompilerParams(vmem_limit_bytes=VMEM_BYTES),
        name="attend_back",
    )(rand, qkv, res, dctx)


def mean_of(a):
    return jnp.mean(a, axis=1, keepdims=True)


def norm(r):
    center = r - mean_of(r)
    rstd = lax.rsqrt(mean_of(center * center) + EPS)
    return center * rstd, rstd


def norm_back(dn, n, rstd):
    return rstd * (dn - mean_of(dn) - n * mean_of(dn * n))


def rowsum(a):
    return jnp.sum(a, axis=0, keepdims=True)


MESH = pl.DeviceIdType.MESH


def run_phases(items):
    step = 0
    live = list(items)
    while live:
        after = []
        for first, phases in live:
            if first > step or next(phases, None) is not None:
                after.append((first, phases))
        live = after
        step += 1


class Where:
    def __init__(self):
        c, core, zh, zl = (lax.axis_index(a) for a in ALL)
        self.y, self.x, self.core, self.zh, self.zl = c // 2, c % 2, core, zh, zl
        self.z = zh * 2 + zl
        self.by_x = (self.y * 2 + 1 - self.x, core, zh, zl)
        self.by_y = ((1 - self.y) * 2 + self.x, core, zh, zl)
        self.by_core = (c, 1 - core, zh, zl)
        self.by_zl = (c, core, zh, 1 - zl)
        self.by_zh = (c, core, 1 - zh, zl)
        self.by_mid = (c, core, 1 - zh, 1 - zl)
        self.by_swap = (c, 1 - core, 1 - zh, zl)
        self.by_both = (c, 1 - core, zh, 1 - zl)
        self.inner = zh != zl
        self.stays = core == zh

    def greet(self):
        barrier = pltpu.get_barrier_semaphore()
        others = (self.by_x, self.by_y, self.by_core, self.by_zl)
        others += (self.by_zh, self.by_mid, self.by_swap, self.by_both)
        for other in others:
            pl.semaphore_signal(barrier, inc=1, device_id=other, device_id_type=MESH)
        pl.semaphore_wait(barrier, len(others))


class Copies:
    def __init__(self, send, recv, local):
        self.send, self.recv, self.local_sems = send, recv, local
        self.n = self.m = 0

    def remote(self, src, dst, device):
        n = self.n
        self.n += 1
        return pltpu.make_async_remote_copy(
            src_ref=src,
            dst_ref=dst,
            send_sem=self.send.at[n],
            recv_sem=self.recv.at[n],
            device_id=device,
            device_id_type=MESH,
        )

    def local(self, src, dst):
        m = self.m
        self.m += 1
        return pltpu.make_async_copy(src, dst, self.local_sems.at[m])


def chain_kernel(
    groups,
    direct,
    ctx_ref,
    tok_ref,
    og_ref,
    wo_ref,
    wu_ref,
    wd_ref,
    vec_ref,
    bu_ref,
    out_ref,
    dres_ref,
    dctx_ref,
    mix_ref,
    hid_ref,
    act_ref,
    dpre_ref,
    dffn_ref,
    dproj_ref,
    gvec_ref,
    gbu_ref,
    slope_ref,
    wop_ref,
    *stage,
):
    width = tok_ref.shape[1]
    hidden = wu_ref.shape[1]
    wide = 3 * HEAD_DIM
    step = pl.program_id(0)
    if direct:
        me = Where()
        out_far, dctx_far = out_ref, dctx_ref
        out_stage, dctx_stage, send, recv, local = stage
        out_ref, dctx_ref = out_stage.at[step], dctx_stage.at[step]

        @pl.when(step == 0)
        def _():
            me.greet()

    def transfers(t):
        place = me.core * 2 + me.zl
        near, beside = me.core * 2 + 1 - me.zl, (1 - me.core) * 2 + me.zl
        across = (1 - me.core) * 2 + 1 - me.zl
        others = ((near, me.by_zl), (beside, me.by_core), (across, me.by_both))
        remote = [
            pltpu.make_async_remote_copy(
                src_ref=dctx_stage.at[t, where],
                dst_ref=dctx_far.at[place, pl.ds(t * SUBS, SUBS)],
                send_sem=send.at[t, n],
                recv_sem=recv.at[t, n],
                device_id=other,
                device_id_type=MESH,
            )
            for n, (where, other) in enumerate(others)
        ]
        swap = pltpu.make_async_remote_copy(
            src_ref=out_stage.at[t],
            dst_ref=out_far.at[t],
            send_sem=send.at[t, 3],
            recv_sem=recv.at[t, 3],
            device_id=me.by_swap,
            device_id_type=MESH,
        )
        keep = pltpu.make_async_copy(out_stage.at[t], out_far.at[t], local.at[t, 0])
        own = pltpu.make_async_copy(
            dctx_stage.at[t, place], dctx_far.at[place, pl.ds(t * SUBS, SUBS)], local.at[t, 1]
        )
        return remote, own, swap, keep

    @pl.when(step == 0)
    def _():
        for g in range(groups):
            wop_ref[g * LANES : (g + 1) * LANES, :] = wo_ref[g * wide : g * wide + LANES, :]
            to = groups * LANES + g * HEAD_DIM
            wop_ref[to : to + HEAD_DIM, :] = wo_ref[g * wide + LANES : (g + 1) * wide, :]
        gvec_ref[...] = jnp.zeros_like(gvec_ref)
        gbu_ref[...] = jnp.zeros_like(gbu_ref)

    low = lax.broadcasted_iota(jnp.int32, (BLOCK, LANES), 1) < HEAD_DIM
    subs = range(tok_ref.shape[0] // ROWS)
    spans = [slice(n * ROWS, (n + 1) * ROWS) for n in subs]
    chunks = [slice(f, f + CHUNK) for f in range(0, hidden, CHUNK)]
    for n in subs:
        for g in range(groups):
            mix_ref[spans[n], g * LANES : (g + 1) * LANES] = ctx_ref[g, n, :ROWS, :]
        for g in range(0, groups, 2):
            to = groups * LANES + g * HEAD_DIM
            for m in range(ROWS // (2 * BLOCK)):
                at = ROWS + m * BLOCK
                a = ctx_ref[g, n, at : at + BLOCK, :].astype(f32)
                b = ctx_ref[g + 1, n, at : at + BLOCK, :].astype(f32)
                even = jnp.where(low, a, pltpu.roll(b, HEAD_DIM, 1))
                odd = jnp.where(low, pltpu.roll(a, HEAD_DIM, 1), b)
                r = n * ROWS + 2 * m * BLOCK
                mix_ref[r : r + BLOCK, to : to + LANES] = even.astype(bf16)
                mix_ref[r + BLOCK : r + 2 * BLOCK, to : to + LANES] = odd.astype(bf16)

    bo, g1, s1 = vec_ref[0:1, :], vec_ref[1:2, :], vec_ref[2:3, :]
    bd, g2, s2 = vec_ref[3:4, :], vec_ref[4:5, :], vec_ref[5:6, :]
    projs = [dot(mix_ref[rows, :], wop_ref[...]) for rows in spans]
    norms = [norm(tok_ref[rows, :].astype(f32) + proj + bo) for rows, proj in zip(spans, projs)]
    hids = [n1 * g1 + s1 for n1, _ in norms]
    lows = [hid.astype(bf16) for hid in hids]
    for rows, hid_low in zip(spans, lows):
        hid_ref[rows, :] = hid_low
    scale = np.sqrt(2.0 / np.pi).astype(np.float32)
    work = [(n, cols) for cols in chunks for n in subs]

    def behind(start, end):
        held = start(*work[0])
        for k, item in enumerate(work):
            now = held
            if k + 1 < len(work):
                held = start(*work[k + 1])
            end(*item, now)

    def up_start(n, cols):
        return dot(lows[n], wu_ref[:, cols])

    def up_end(n, cols, raw):
        u = raw + bu_ref[:, cols]
        square = u * u
        t = jnp.tanh(u * (scale + (scale * 0.044715) * square))
        half = 0.5 + 0.5 * t
        act_ref[spans[n], cols] = (u * half).astype(bf16)
        slope = half + (0.5 * u) * (1.0 - t * t) * (scale + (3 * 0.044715 * scale) * square)
        slope_ref[spans[n], cols] = slope.astype(bf16)

    behind(up_start, up_end)
    ffns = [dot(act_ref[rows, :], wd_ref[...]) for rows in spans]
    dres2s, dffns = [], []
    for n, rows in enumerate(spans):
        n2, rstd2 = norm(hids[n] + ffns[n] + bd)
        out_ref[rows, :] = (n2 * g2 + s2).astype(bf16)
        og = og_ref[rows, :].astype(f32)
        gvec_ref[4:5, :] += rowsum(og * n2)
        gvec_ref[5:6, :] += rowsum(og)
        dres2 = norm_back(og * g2, n2, rstd2)
        dffn = dres2.astype(bf16)
        dffn_ref[rows, :] = dffn
        gvec_ref[3:4, :] += rowsum(dffn.astype(f32))
        dres2s.append(dres2)
        dffns.append(dffn)

    if direct:
        remote, own, swap, keep = transfers(step)

        @pl.when(me.stays)
        def _():
            keep.start()

        @pl.when(jnp.logical_not(me.stays))
        def _():
            swap.start()

    def down_start(n, cols):
        return dot_nt(dffns[n], wd_ref[cols, :])

    def down_end(n, cols, dact):
        dpre = (dact * slope_ref[spans[n], cols].astype(f32)).astype(bf16)
        dpre_ref[spans[n], cols] = dpre
        gbu_ref[0:1, cols] += rowsum(dpre.astype(f32))

    behind(down_start, down_end)
    dhs = [dres2 + dot_nt(dpre_ref[rows, :], wu_ref[...]) for rows, dres2 in zip(spans, dres2s)]
    dmixes = []
    for rows, dh, (n1, rstd1) in zip(spans, dhs, norms):
        gvec_ref[1:2, :] += rowsum(dh * n1)
        gvec_ref[2:3, :] += rowsum(dh)
        dres1 = norm_back(dh * g1, n1, rstd1)
        dres_ref[rows, :] = dres1
        dproj = dres1.astype(bf16)
        dproj_ref[rows, :] = dproj
        gvec_ref[0:1, :] += rowsum(dproj.astype(f32))
        dmixes.append(dot_nt(dproj, wop_ref[...]))
    for n, dmix in enumerate(dmixes):
        for g in range(groups):
            dctx_ref[g, n, :ROWS, :] = dmix[:, g * LANES : (g + 1) * LANES].astype(bf16)
        for g in range(0, groups, 2):
            to = groups * LANES + g * HEAD_DIM
            for m in range(ROWS // (2 * BLOCK)):
                at = ROWS + m * BLOCK
                r = 2 * m * BLOCK
                even = dmix[r : r + BLOCK, to : to + LANES]
                odd = dmix[r + BLOCK : r + 2 * BLOCK, to : to + LANES]
                a = jnp.where(low, even, pltpu.roll(odd, HEAD_DIM, 1))
                b = jnp.where(low, pltpu.roll(even, HEAD_DIM, 1), odd)
                dctx_ref[g, n, at : at + BLOCK, :] = a.astype(bf16)
                dctx_ref[g + 1, n, at : at + BLOCK, :] = b.astype(bf16)

    if direct:
        for copy in remote:
            copy.start()
        own.start()

        @pl.when(step == pl.num_programs(0) - 1)
        def _():
            for t in range(dctx_stage.shape[0]):
                remote, own, swap, keep = transfers(t)
                for copy in remote:
                    copy.wait()
                own.wait()

                @pl.when(me.stays)
                def _():
                    keep.wait()

                @pl.when(jnp.logical_not(me.stays))
                def _():
                    swap.wait()


def chain(ctx, tok, og, wo, wu, wd, vec, bu, direct):
    rows, width = tok.shape
    hidden = wu.shape[1]
    groups = ctx.shape[0]
    once = pl.Buffered(1)

    def tiled(cols):
        return pl.BlockSpec((SUBS * ROWS, cols), lambda t: (t, 0))

    def fixed(shape):
        return pl.BlockSpec(shape, lambda t: (0, 0), pipeline_mode=once)

    packed = pl.BlockSpec((groups, SUBS) + ctx.shape[2:], lambda t: (0, t, 0, 0))
    shape = jax.ShapeDtypeStruct
    steps = rows // (SUBS * ROWS)
    hbm = pl.BlockSpec(memory_space=pltpu.HBM)
    scratch = [pltpu.VMEM((SUBS * ROWS, hidden), bf16), pltpu.VMEM(wo.shape, bf16)]
    params = pltpu.CompilerParams(vmem_limit_bytes=VMEM_BYTES)
    out_shape = (rows, width)
    if direct:
        out_shape = (steps, SUBS * ROWS, width)
        scratch += [
            pltpu.VMEM(out_shape, bf16),
            pltpu.VMEM((steps, groups, SUBS) + ctx.shape[2:], bf16),
            pltpu.SemaphoreType.DMA((steps, 4)),
            pltpu.SemaphoreType.DMA((steps, 4)),
            pltpu.SemaphoreType.DMA((steps, 2)),
        ]
        params = pltpu.CompilerParams(
            vmem_limit_bytes=VMEM_BYTES, collective_id=2, has_side_effects=True
        )
    return pl.pallas_call(
        partial(chain_kernel, groups, direct),
        grid=(steps,),
        out_shape=(
            shape(out_shape, bf16),
            shape((rows, width), f32),
            shape(ctx.shape, bf16),
            shape((rows, width), bf16),
            shape((rows, width), bf16),
            shape((rows, hidden), bf16),
            shape((rows, hidden), bf16),
            shape((rows, width), bf16),
            shape((rows, width), bf16),
            shape((8, width), f32),
            shape((8, hidden), f32),
        ),
        in_specs=[
            packed,
            tiled(width),
            tiled(width),
            fixed(wo.shape),
            fixed(wu.shape),
            fixed(wd.shape),
            fixed(vec.shape),
            fixed(bu.shape),
        ],
        out_specs=(
            hbm if direct else tiled(width),
            tiled(width),
            hbm if direct else packed,
            tiled(width),
            tiled(width),
            tiled(hidden),
            tiled(hidden),
            tiled(width),
            tiled(width),
            pl.BlockSpec((8, width), lambda t: (0, 0)),
            pl.BlockSpec((8, hidden), lambda t: (0, 0)),
        ),
        scratch_shapes=scratch,
        compiler_params=params,
        name="chain",
    )(ctx, tok, og, wo, wu, wd, vec, bu)


def gather_item(me, copies, shard, full, cols, x_first):
    y, x, core, zh, zl = me.y, me.x, me.core, me.zh, me.zl
    mine = shard.at[:, cols]
    own = copies.local(mine, full.at[y, x, core, me.z, :, cols])
    spot = full.at[y, x, core, me.z, :, cols]
    along = [copies.remote(mine, spot, other) for other in (me.by_zl, me.by_mid, me.by_zh)]
    own.start()
    for copy in along:
        copy.start()
    yield 1
    own.wait()
    for copy in along:
        copy.wait()
    line = full.at[y, x, core, :, :, cols]
    near = copies.remote(line, line, me.by_x if x_first else me.by_y)
    near.start()
    across = [copies.remote(line, line, me.by_core)]
    across[0].start()
    yield 1
    near.wait()
    if x_first:
        block = full.at[y, :, core, :, :, cols]
        got = full.at[y, 1 - x, core, :, :, cols]
        rest = full.at[1 - y, :, core, :, :, cols]
    else:
        block = full.at[:, x, core, :, :, cols]
        got = full.at[1 - y, x, core, :, :, cols]
        rest = full.at[:, 1 - x, core, :, :, cols]
    far = copies.remote(block, block, me.by_y if x_first else me.by_x)
    far.start()
    across.append(copies.remote(got, got, me.by_core))
    across[1].start()
    yield 1
    far.wait()
    across.append(copies.remote(rest, rest, me.by_core))
    across[2].start()
    yield 1
    for copy in across:
        copy.wait()


def tokens_item(me, copies, tok, x_all, piece):
    place = me.core * 2 + me.zl
    there = (1 - me.core) * 2 + me.zl
    held = x_all.at[place, piece]
    out = copies.remote(tok.at[piece], x_all.at[there, piece], me.by_swap)
    keep = copies.local(tok.at[piece], held)
    along = copies.remote(held, held, me.by_zl)
    over = copies.remote(held, held, me.by_core)

    @pl.when(me.stays)
    def _():
        keep.start()

    @pl.when(jnp.logical_not(me.stays))
    def _():
        out.start()

    yield 1

    @pl.when(me.stays)
    def _():
        keep.wait()
        along.start()
        over.start()

    yield 1

    @pl.when(jnp.logical_not(me.stays))
    def _():
        out.wait()
        along.start()
        over.start()

    yield 1
    along.wait()
    came = x_all.at[me.core * 2 + 1 - me.zl, piece]
    onto = copies.remote(came, came, me.by_core)
    onto.start()
    yield 1
    over.wait()
    onto.wait()


def exchange_item(me, copies, src, dst):
    out = copies.remote(src, dst, me.by_swap)
    keep = copies.local(src, dst)

    @pl.when(me.stays)
    def _():
        keep.start()

    @pl.when(jnp.logical_not(me.stays))
    def _():
        out.start()

    yield 1

    @pl.when(me.stays)
    def _():
        keep.wait()

    @pl.when(jnp.logical_not(me.stays))
    def _():
        out.wait()


PIECES = 4


def weight_item(me, copies, src, parts, whole, bias):
    y, x, core, zh, zl = me.y, me.x, me.core, me.zh, me.zl
    place = core * 2 + zl
    keep = copies.local(src.at[place], parts.at[place])
    moves = [
        copies.remote(src.at[core * 2 + 1 - zl], parts.at[place], me.by_zl),
        copies.remote(src.at[(1 - core) * 2 + zl], parts.at[place], me.by_core),
        copies.remote(src.at[(1 - core) * 2 + 1 - zl], parts.at[place], me.by_both),
    ]
    keep.start()
    for move in moves:
        move.start()
    yield 1
    keep.wait()
    for move in moves:
        move.wait()
    own = whole.shape[4] // 2
    for b in range(2):
        both = jnp.concatenate([parts[2 * b, :own, :], parts[2 * b + 1, :own, :]], axis=0)
        whole[y, x, b, zh] = both.astype(bf16)
    tail = pl.ds(own, 8)
    bias[y, x, zh] = parts[0, tail, :] + parts[1, tail, :] + parts[2, tail, :] + parts[3, tail, :]
    for spot, bias_spot, other in (
        (whole.at[y, x, :, zh], bias.at[y, x, zh], me.by_zh),
        (whole.at[y, x], bias.at[y, x], me.by_x),
        (whole.at[y], bias.at[y], me.by_y),
    ):
        moves = [copies.remote(spot, spot, other), copies.remote(bias_spot, bias_spot, other)]
        for move in moves:
            move.start()
        yield 1
        for move in moves:
            move.wait()


def finish(*generators):
    for phases in generators:
        for _ in phases:
            pass


def front_kernel(heads, randoms, *refs):
    rand_ref, tok, og, wq, w_out, up, down, small = refs[:8]
    x_hbm, tok_own, og_own, w_own, qkv_hbm, res_hbm, ctx_all, out_all, up_all, down_all, small_all = refs[8:19]
    x_all, parts, whole, bias, qkv_ref, res_ref, ends_ref, ctx_ref = refs[19:27]
    me = Where()
    me.greet()
    copies = Copies(*refs[27:])
    blocks = qkv_ref.shape[0]
    length = blocks * BLOCK
    quarter = length // 4
    core, zl = me.core, me.zl
    place = core * 2 + zl
    near = core * 2 + 1 - zl
    beside = (1 - core) * 2 + zl
    across = (1 - core) * 2 + 1 - zl

    weights = weight_item(me, copies, wq, parts, whole, bias)
    tokens = [tokens_item(me, copies, tok, x_all, piece) for piece in range(PIECES)]
    smalls = gather_item(me, copies, small, small_all, slice(0, LANES), True)
    turn = 0

    def gathers(*arrays):
        nonlocal turn
        made = []
        for shard, full, splits in arrays:
            width = shard.shape[1] // splits
            for n in range(splits):
                cols = slice(n * width, (n + 1) * width)
                made.append(gather_item(me, copies, shard, full, cols, turn % 2 == 0))
                turn += 1
        return made

    def advance(group):
        group[:] = [phases for phases in group if next(phases, None) is not None]

    early = gathers((up, up_all, 2))
    late = gathers((down, down_all, 2), (w_out, out_all, 2))
    last = [exchange_item(me, copies, og, og_own)]
    idle = [smalls]
    outs = []

    def write(src, dst):
        copy = copies.local(src, dst)
        copy.start()
        outs.append(copy)

    def project(where):
        bias_row = jnp.sum(bias[...].reshape(-1, 8, bias.shape[-1]), axis=0)[0:1]
        matrix = whole[...].reshape(-1, whole.shape[-1])
        for piece in range(PIECES):
            raw = dot(x_all[where, piece], matrix) + bias_row
            step = ROWS // BLOCK
            at = (where * PIECES + piece) * step
            qkv_ref[pl.ds(at, step)] = raw.astype(bf16).reshape(step, BLOCK, raw.shape[1])

    def forward_tokens():
        for item in tokens:
            next(item)

    next(weights)
    advance(early)
    next(weights)
    forward_tokens()
    forward_tokens()
    next(weights)
    advance(idle)
    advance(early)
    next(weights)
    advance(idle)
    forward_tokens()
    advance(late)
    finish(weights)
    advance(early)
    project(place)
    write(whole, w_own)
    write(x_all.at[place], tok_own)
    forward_tokens()
    advance(late)
    project(near)
    finish(*tokens)
    advance(last)
    advance(early)
    project(beside)
    project(across)
    advance(idle)
    write(x_all, x_hbm)
    write(qkv_ref, qkv_hbm)
    for h, both in enumerate(global_blocks(qkv_ref, heads, length)):
        ends_ref[h] = both
    advance(late)
    advance(early)
    advance(idle)

    def middle(t, carry):
        middle_blocks(qkv_ref, rand_ref, res_ref, t * PAIR, heads, randoms, blocks)
        return carry

    sends = []
    turns = quarter // BLOCK // PAIR
    for where, other in ((across, me.by_both), (near, me.by_zl), (beside, me.by_core), (place, None)):
        lax.fori_loop(where * turns, (where + 1) * turns, middle, 0)

        @pl.when(where == 0)
        def _():
            for h in range(heads):
                res_ref[h, 0:BLOCK, :] = ends_ref[h, 0:BLOCK, :]

        @pl.when(where == 3)
        def _():
            for h in range(heads):
                res_ref[h, length - BLOCK : length, :] = ends_ref[h, BLOCK : 2 * BLOCK, :]

        for piece in range(PIECES):
            pack_rows(res_ref, ctx_ref, where * quarter + piece * ROWS, where, piece)
        rows = rows_at(where * quarter, quarter)
        write(res_ref.at[:, rows], res_hbm.at[:, rows])
        if other is None:
            write(ctx_ref.at[where], ctx_all.at[place])
        else:
            send = copies.remote(ctx_ref.at[where], ctx_all.at[place], other)
            send.start()
            sends.append(send)
        advance(late if where is near or where is place else idle)
    finish(*early, *late, *last, *idle)
    for copy in sends + outs:
        copy.wait()


def front(rand, tok, og, wq, mats, small, heads):
    rows, width = tok.shape
    members = 4
    length = rows * members
    randoms = rand.size // (heads * (length // BLOCK - 2))
    hbm = pl.BlockSpec(memory_space=pltpu.HBM)
    shape = jax.ShapeDtypeStruct
    tok = tok.reshape(PIECES, rows // PIECES, width)
    cols = heads * SLOT
    own = mats[0].shape[0]
    packed = (members, rows // ROWS, ROWS * 3 // 2, LANES)
    outs = [
        shape((members,) + tok.shape, bf16),
        shape(tok.shape, bf16),
        shape(og.shape, bf16),
        shape((2, 2, 2, 2, 2 * own, cols), bf16),
        shape((length // BLOCK, BLOCK, cols), bf16),
        shape((heads, length, LANES), f32),
        shape(packed, bf16),
    ]
    outs += [shape((2, 2, 2, 4) + a.shape, bf16) for a in (*mats, small)]
    return pl.pallas_call(
        partial(front_kernel, heads, randoms),
        out_shape=tuple(outs),
        in_specs=[pl.BlockSpec(memory_space=pltpu.SMEM)] + [hbm] * 7,
        out_specs=(hbm,) * 11,
        scratch_shapes=[
            pltpu.VMEM((members,) + tok.shape, bf16),
            pltpu.VMEM(wq.shape, f32),
            pltpu.VMEM((2, 2, 2, 2, 2 * own, cols), bf16),
            pltpu.VMEM((2, 2, 2, 8, cols), f32),
            pltpu.VMEM((length // BLOCK, BLOCK, cols), bf16),
            pltpu.VMEM((heads, length, LANES), f32),
            pltpu.VMEM((heads, 2 * BLOCK, LANES), f32),
            pltpu.VMEM(packed, bf16),
            pltpu.SemaphoreType.DMA((112,)),
            pltpu.SemaphoreType.DMA((112,)),
            pltpu.SemaphoreType.DMA((32,)),
        ],
        compiler_params=pltpu.CompilerParams(
            collective_id=0, has_side_effects=True, vmem_limit_bytes=VMEM_BYTES
        ),
        name="front",
    )(rand, tok, og, wq, *mats, small)


def add_rows(dst, a, b, rows):
    step = next(n for n in (48, 32, 24, 16, 8) if rows % n == 0)

    def body(t, carry):
        at = rows_at(t * step, step)
        dst[at, :] = (a[at, :].astype(f32) + b[at, :].astype(f32)).astype(dst.dtype)
        return carry

    lax.fori_loop(0, rows // step, body, 0)


def scatter_item(me, copies, src, cols, acc, from_core, from_first, from_second, slabs, from_line, out, x_first):
    y, x, core, zh, zl = me.y, me.x, me.core, me.zh, me.zl
    rows = acc.shape[2]
    own = copies.local(src.at[:, :, core, :, cols], acc)
    over = copies.remote(src.at[:, :, 1 - core, :, cols], from_core, me.by_core)
    own.start()
    over.start()
    yield 1
    own.wait()
    over.wait()
    for a in range(2):
        for b in range(2):
            add_rows(acc.at[a, b], acc.at[a, b], from_core.at[a, b], rows)
    if x_first:
        first = copies.remote(acc.at[:, 1 - x], from_first, me.by_x)
    else:
        first = copies.remote(acc.at[1 - y], from_first, me.by_y)
    first.start()
    yield 1
    first.wait()
    for a in range(2):
        block = acc.at[a, x] if x_first else acc.at[y, a]
        add_rows(block, block, from_first.at[a], rows)
    if x_first:
        second = copies.remote(acc.at[1 - y, x], from_second, me.by_y)
    else:
        second = copies.remote(acc.at[y, 1 - x], from_second, me.by_x)
    second.start()
    yield 1
    second.wait()
    rest = rows // 4
    summed = acc[y, x].astype(f32) + from_second[...].astype(f32)
    for z in range(4):
        slabs[z] = summed[z * rest : (z + 1) * rest].astype(slabs.dtype)
    moves = [
        copies.remote(slabs.at[(1 - zh) * 2 + zl], from_line.at[0], me.by_zh),
        copies.remote(slabs.at[(1 - zh) * 2 + 1 - zl], from_line.at[1], me.by_mid),
        copies.remote(slabs.at[zh * 2 + 1 - zl], from_line.at[2], me.by_zl),
    ]
    for move in moves:
        move.start()
    yield 1
    for move in moves:
        move.wait()
    near = slabs[me.z].astype(f32) + from_line[2].astype(f32)
    out[...] = near + (from_line[0].astype(f32) + from_line[1].astype(f32))


def scatter_buffers(rows, cols, kind):
    return [
        pltpu.VMEM((2, 2, rows, cols), kind),
        pltpu.VMEM((2, 2, rows, cols), kind),
        pltpu.VMEM((2, rows, cols), kind),
        pltpu.VMEM((rows, cols), kind),
        pltpu.VMEM((4, rows // 4, cols), kind),
        pltpu.VMEM((3, rows // 4, cols), kind),
    ]


def own_columns_item(me, copies, acc, from_x, from_y, from_zh, part, out):
    y, x, core, zh, zl = me.y, me.x, me.core, me.zh, me.zl
    rows = acc.shape[4]
    first = copies.remote(acc.at[1 - x], from_x, me.by_x)
    first.start()
    yield 1
    first.wait()
    for a in range(2):
        for b in range(2):
            for c in range(2):
                add_rows(acc.at[x, a, b, c], acc.at[x, a, b, c], from_x.at[a, b, c], rows)
    acc = acc.at[x]
    second = copies.remote(acc.at[1 - y], from_y, me.by_y)
    second.start()
    yield 1
    second.wait()
    for b in range(2):
        for c in range(2):
            block = acc.at[y, b, c]
            add_rows(block, block, from_y.at[b, c], rows)
    third = copies.remote(acc.at[y, :, 1 - zh], from_zh, me.by_zh)
    third.start()
    yield 1
    third.wait()
    half = rows // 2
    for b in range(2):
        add_rows(part.at[b], acc.at[y, b, zh], from_zh.at[b], rows)
    place = core * 2 + zl
    mine = rows_at(zl * half, half)
    other = rows_at((1 - zl) * half, half)
    keep = copies.local(part.at[core, mine], out.at[place])
    keep.start()
    moves = [
        copies.remote(part.at[core, other], out.at[place], me.by_zl),
        copies.remote(part.at[1 - core, mine], out.at[place], me.by_core),
        copies.remote(part.at[1 - core, other], out.at[place], me.by_both),
    ]
    for move in moves:
        move.start()
    yield 1
    keep.wait()
    for move in moves:
        move.wait()


def input_grad_item(me, copies, draw, w, dres, piece, stage, from_core, far, from_zl, res, send, out):
    core, zl = me.core, me.zl
    more = copies.local(dres.at[piece], res)
    more.start()
    for b in range(2):
        stage[b] = dot_nt(draw[(1 - core) * 2 + b, piece], w[...]).astype(bf16)
    over = copies.remote(stage, from_core, me.by_core)
    over.start()
    yield 1
    mine = dot_nt(draw[core * 2 + 1 - zl, piece], w[...])
    over.wait()
    far[...] = (mine + from_core[1 - zl].astype(f32)).astype(bf16)
    along = copies.remote(far, from_zl, me.by_zl)
    along.start()
    mine = dot_nt(draw[core * 2 + zl, piece], w[...])
    more.wait()
    res[...] = res[...] + (mine + from_core[zl].astype(f32))
    yield 1
    along.wait()
    send[...] = (res[...] + from_zl[...].astype(f32)).astype(bf16)
    yield from exchange_item(me, copies, send, out.at[piece])


SPLITS = ((0, 2), (1, 4), (2, 1), (3, 1))


def scatter_kernel(*refs):
    down, up, proj, vecs, draw, x_hbm, w, dres = refs[:8]
    outs = refs[8:14]
    sems, scratch = refs[14:17], list(refs[17:])
    me = Where()
    me.greet()
    copies = Copies(*sems)

    def take(n):
        got = scratch[:n]
        del scratch[:n]
        return got

    def advance(group):
        group[:] = [phases for phases in group if next(phases, None) is not None]

    pieces = [
        input_grad_item(me, copies, draw, w, dres, piece, *take(6), outs[5]) for piece in range(PIECES)
    ]
    x_all, total, acc, *buffers = take(7)
    fetch = copies.local(x_hbm, x_all)
    fetch.start()
    columns = [own_columns_item(me, copies, acc, *buffers, outs[4])]
    items = []
    for n, splits in SPLITS:
        src = refs[n]
        width = src.shape[4] // splits
        for part in range(splits):
            cols = slice(part * width, (part + 1) * width)
            dst = outs[n].at[:, cols]
            items.append(scatter_item(me, copies, src, cols, *take(6), dst, len(items) % 2 == 0))

    def weight_grad(t, carry):
        place, piece = t // PIECES, t % PIECES
        total[...] += dot_tn(x_all[place, piece], draw[place, piece])
        return carry

    next(pieces[0])
    next(pieces[1])
    advance(items)
    next(pieces[0])
    next(pieces[1])
    next(pieces[2])
    next(pieces[3])
    advance(items)
    next(pieces[0])
    next(pieces[2])
    total[...] = jnp.zeros_like(total)
    fetch.wait()
    lax.fori_loop(0, 2 * PIECES, weight_grad, 0)
    next(pieces[1])
    next(pieces[3])
    lax.fori_loop(2 * PIECES, 4 * PIECES, weight_grad, 0)
    laid = total[...].reshape((2, 2) + acc.shape[2:])
    for a in range(2):
        for b in range(2):
            acc[b, a] = laid[a, b].astype(bf16)
    advance(columns)
    next(pieces[2])
    advance(items)
    next(pieces[3])
    while pieces or columns or items:
        advance(items)
        advance(columns)
        if not items:
            advance(pieces)


def scatter(down, up, proj, vecs, draw, x_all, w, dres, own):
    hbm = pl.BlockSpec(memory_space=pltpu.HBM)
    vmem = pl.BlockSpec(memory_space=pltpu.VMEM)
    shape = jax.ShapeDtypeStruct
    grads = (down, up, proj, vecs)
    outs = [shape((a.shape[3] // 4, a.shape[4]), f32) for a in grads]
    width, cols = w.shape
    rows = 2 * own
    outs.append(shape((4, own, cols), f32))
    outs.append(shape(dres.shape, bf16))
    buffers = []
    for _ in range(PIECES):
        tile = dres.shape[1:]
        buffers += [
            pltpu.VMEM((2,) + tile, bf16),
            pltpu.VMEM((2,) + tile, bf16),
            pltpu.VMEM(tile, bf16),
            pltpu.VMEM(tile, bf16),
            pltpu.VMEM(tile, f32),
            pltpu.VMEM(tile, bf16),
        ]
    buffers += [
        pltpu.VMEM(x_all.shape, bf16),
        pltpu.VMEM((width, cols), f32),
        pltpu.VMEM((2, 2, 2, 2, rows, cols), bf16),
        pltpu.VMEM((2, 2, 2, rows, cols), bf16),
        pltpu.VMEM((2, 2, rows, cols), bf16),
        pltpu.VMEM((2, rows, cols), bf16),
        pltpu.VMEM((2, rows, cols), f32),
    ]
    for n, splits in SPLITS:
        a = grads[n]
        for _ in range(splits):
            buffers += scatter_buffers(a.shape[3], a.shape[4] // splits, a.dtype)
    return pl.pallas_call(
        scatter_kernel,
        out_shape=tuple(outs),
        in_specs=[hbm] * 4 + [vmem, hbm, vmem, hbm],
        out_specs=(vmem,) * 5 + (hbm,),
        scratch_shapes=[
            pltpu.SemaphoreType.DMA((80,)),
            pltpu.SemaphoreType.DMA((80,)),
            pltpu.SemaphoreType.DMA((32,)),
        ]
        + buffers,
        compiler_params=pltpu.CompilerParams(
            collective_id=1, has_side_effects=True, vmem_limit_bytes=VMEM_BYTES
        ),
        name="scatter",
    )(down, up, proj, vecs, draw, x_all, w, dres)


def per_device(
    tokens,
    qkv_weight,
    query_value_bias,
    out_weight,
    out_bias,
    norm1_gain,
    norm1_bias,
    up_weight,
    up_bias,
    down_weight,
    down_bias,
    norm2_gain,
    norm2_bias,
    rand_blocks,
    out_grad,
):
    members = lax.axis_size(GROUP)
    devices = lax.axis_size(ALL)
    swap = [(0, 0), (1, 2), (2, 1), (3, 3)]

    def move(a):
        return lax.ppermute(a, ("core", "zh"), swap)

    rand = move(rand_blocks[0])
    heads = rand.shape[0]
    rows, width = tokens.shape[1:]
    cols = heads * HEAD_DIM
    group = lax.axis_index(GROUP)
    own = width // devices
    rand_flat = rand.reshape(-1)

    def lay_out(a):
        a = a.reshape(a.shape[:-2] + (3, heads, HEAD_DIM))
        q, k, v = a[..., 0, :, :], a[..., 1, :, :], a[..., 2, :, :]
        q = q * jnp.asarray(HEAD_DIM**-0.5, a.dtype)
        laid = jnp.stack([q, jnp.zeros_like(q), k, v], axis=-2)
        return laid.reshape(laid.shape[:-3] + (heads * SLOT,))

    bias_part = jnp.stack([query_value_bias[0], jnp.zeros((own,), bf16), query_value_bias[1]])
    small = [out_bias, norm1_gain, norm1_bias, down_bias, norm2_gain, norm2_bias, up_bias]
    small = jnp.concatenate(small)
    direct = lax.axis_size("c") == 4 and members == 4 and own % 8 == 0
    if direct:
        count = small.shape[0]
        padded = jnp.pad(small, (0, 16 * LANES - count)).reshape(16, LANES)
        spread = lax.dynamic_update_slice(
            jnp.zeros((3, width), f32), bias_part.astype(f32), (0, lax.axis_index(ALL) * own)
        )
        spread = lay_out(jnp.transpose(spread.reshape(3, members, cols), (1, 0, 2)))
        wq = jnp.transpose(qkv_weight.astype(f32).reshape(own, 3, members, cols), (2, 0, 1, 3))
        wq = jnp.concatenate([lay_out(wq), spread[:, None], jnp.zeros((members, 7, heads * SLOT), f32)], axis=1)
        mats = (out_weight, up_weight, down_weight)
        x, tok, og, w_own, qkv, res, ctx, *full = front(
            rand_flat, tokens[0], out_grad[0], wq, mats, padded, heads
        )
        x, tok = x.reshape(-1, width), tok.reshape(-1, width)
        w_own = w_own.reshape(width, -1)
        w_out, w_up, w_down = (a.reshape(-1, a.shape[-1]) for a in full[:3])
        small = full[3].reshape(devices, -1)[:, :count].astype(f32)
    else:
        tok = move(tokens[0])
        og = move(out_grad[0])
        x = lax.all_gather(tok, GROUP, axis=0, tiled=True)
        mats = (qkv_weight, out_weight, up_weight, down_weight)
        w_qkv, w_out, w_up, w_down = (lax.all_gather(a, ALL, axis=0, tiled=True) for a in mats)
        small = lax.all_gather(small, ALL, axis=0).astype(f32)
        w_own = lax.dynamic_slice_in_dim(
            w_qkv.reshape(width, 3, members, cols), group, 1, axis=2
        ).reshape(width, 3, cols)
        w_own = lay_out(w_own)
        bias3 = lax.all_gather(bias_part, ALL, axis=1, tiled=True).astype(f32).reshape(3, members, cols)
        b_own = lay_out(lax.dynamic_slice_in_dim(bias3, group, 1, axis=1).reshape(1, 3, cols))
        qkv, res, ctx_send = attend(rand_flat, x, w_own, b_own, members, heads)
        ctx = lax.all_to_all(ctx_send, GROUP, split_axis=0, concat_axis=0, tiled=True)
    vecs = jnp.transpose(small[:, : 6 * own].reshape(devices, 6, own), (1, 0, 2)).reshape(6, width)
    bias_up = small[:, 6 * own :].reshape(1, -1)
    chain_vecs = jnp.concatenate([vecs, jnp.zeros((2, width), f32)], axis=0)
    out, dres1, dctx, mix, hid, act, dpre, dffn, dproj, gvec, gbu = chain(
        ctx, tok, og, w_out, w_up, w_down, chain_vecs, bias_up, direct
    )
    if direct:
        out = out.reshape(rows, width)
    else:
        dctx = lax.all_to_all(dctx, GROUP, split_axis=0, concat_axis=0, tiled=True)
        out = move(out)

    g_down = dot_tn(act, dffn).astype(bf16)
    g_up = dot_tn(hid, dpre).astype(bf16)
    g_mix = dot_tn(mix, dproj).astype(bf16)
    pairs = g_mix[: members * LANES].reshape(members, LANES, width)
    thirds = g_mix[members * LANES :].reshape(members, HEAD_DIM, width)
    g_out = jnp.concatenate([pairs, thirds], axis=1).reshape(width, width)

    draw, sums = attend_back(rand_flat, qkv, res, dctx, heads)

    def strip(a):
        a = a.reshape(a.shape[:-1] + (heads, 4, HEAD_DIM))
        q, k, v = a[..., 0, :] * (HEAD_DIM**-0.5), a[..., 2, :], a[..., 3, :]
        return jnp.stack([q, k, v], axis=-3).reshape(a.shape[:-3] + (3, cols))

    col_sums = strip(sums[0:1])[0]
    pair = jnp.stack([col_sums[0], col_sums[2]]).reshape(2, 1, cols)
    mine = (jnp.arange(members) == group)[None, :, None]
    pair = jnp.where(mine, pair, 0.0).reshape(2, width)
    vec_grads = jnp.concatenate([pair, gvec[0:6]], axis=0).reshape(8, devices, own)
    vec_grads = jnp.transpose(vec_grads, (1, 0, 2)).reshape(devices, 8 * own)
    vec_grads = jnp.concatenate([vec_grads, gbu[0].reshape(devices, -1)], axis=1)
    count = vec_grads.shape[1]

    if direct:
        lines = 8
        padded = jnp.pad(vec_grads, ((0, 0), (0, lines * LANES - count)))
        g_down, g_up, g_out, vec_grads, g_qkv, input_grad = scatter(
            g_down.reshape(2, 2, 2, -1, width),
            g_up.reshape(2, 2, 2, -1, g_up.shape[1]),
            g_out.reshape(2, 2, 2, -1, width),
            padded.reshape(2, 2, 2, 4 * lines, LANES),
            draw.reshape(members, PIECES, -1, draw.shape[1]),
            x.reshape(members, PIECES, -1, width),
            w_own,
            dres1.reshape(PIECES, -1, width),
            own,
        )
        vec_grads = vec_grads.reshape(-1)[:count]
        input_grad = input_grad.reshape(rows, width).astype(f32)
        g_qkv = strip(g_qkv)
    else:

        def reduce(a):
            return lax.psum_scatter(a, ALL, scatter_dimension=0, tiled=True).astype(f32)

        g_down, g_up, g_out, vec_grads = reduce(g_down), reduce(g_up), reduce(g_out), reduce(vec_grads)[0]
        dx = dot_nt(draw, w_own).astype(bf16)
        dx = lax.psum_scatter(dx, GROUP, scatter_dimension=0, tiled=True)
        input_grad = move((dres1 + dx.astype(f32)).astype(bf16)).astype(f32)
        g_qkv = strip(dot_tn(x, draw)).reshape(-1, 2, 2, members // 2, own, 3 * cols)
        g_qkv = jnp.transpose(g_qkv, (0, 2, 1, 3, 4, 5)).reshape(-1, members, own, 3 * cols)
        g_qkv = g_qkv.reshape(-1, 3 * cols).astype(bf16)
        g_qkv = lax.psum_scatter(g_qkv, REST, scatter_dimension=0, tiled=True)
        g_qkv = g_qkv.reshape(members, own, 3 * cols)
        g_qkv = lax.all_to_all(g_qkv, GROUP, split_axis=0, concat_axis=0, tiled=True).astype(f32)
    g_qkv = jnp.transpose(g_qkv.reshape(members, own, 3, cols), (1, 2, 0, 3)).reshape(own, -1)
    v8 = vec_grads[: 8 * own].reshape(8, own)
    return (
        out[None],
        input_grad[None],
        g_qkv,
        v8[0:2],
        g_out,
        v8[2],
        v8[3],
        v8[4],
        g_up,
        vec_grads[8 * own :],
        g_down,
        v8[5],
        v8[6],
        v8[7],
    )


def solution(mesh):
    dp, sp = mesh.shape["dp"], mesh.shape["sp"]
    fine = Mesh(mesh.devices.reshape(dp // 2, 2, 2, sp // 2), ALL)
    dp, sp = ("c", "core"), ("zh", "zl")
    act = P(dp, sp, None)
    mat = P(ALL, None)
    pair = P(None, ALL)
    vec = P(ALL)
    rand = P(dp, sp, None, None)
    return jax.shard_map(
        per_device,
        mesh=fine,
        in_specs=(act, mat, pair, mat, vec, vec, vec, mat, vec, mat, vec, vec, vec, rand, act),
        out_specs=(act, act, mat, pair, mat, vec, vec, vec, mat, vec, mat, vec, vec, vec),
        check_vma=False,
    )
```

```python
from functools import partial

import jax
import jax.numpy as jnp
import numpy as np
from jax import lax
from jax.experimental import pallas as pl
from jax.experimental.pallas import tpu as pltpu
from jax.sharding import Mesh
from jax.sharding import PartitionSpec as P

HEAD_DIM = 64
BLOCK = 64
LANES = 128
SLOT = 4 * HEAD_DIM
EPS = 1e-05
MASKED = -1e30
ALL = ("c", "core", "zh", "zl")
GROUP = ("core", "zl")
REST = ("c", "zh")
CHUNK = 512
ROWS = 256
PAIR = 2
SUBS = 1
PAIR_BACK = 2
VMEM_BYTES = 60 * 1024 * 1024

f32 = jnp.float32
bf16 = jnp.bfloat16
NT = (((1,), (1,)), ((), ()))
TN = (((0,), (0,)), ((), ()))


def dot(a, b):
    return jnp.dot(a, b, preferred_element_type=f32)


def dot_nt(a, b):
    return lax.dot_general(a, b, NT, preferred_element_type=f32)


def dot_tn(a, b):
    return lax.dot_general(a, b, TN, preferred_element_type=f32)


def rows_at(start, size):
    return pl.ds(pl.multiple_of(start, size), size)


def listed(ref, rand_ref, head, i, blocks, randoms):
    cols = slice(head * SLOT + LANES, head * SLOT + SLOT)
    near = jnp.clip(i - 1, 0, blocks - 3)
    parts = [ref[0, :, cols], ref[blocks - 1, :, cols]]
    parts += [ref[near + n, :, cols] for n in range(3)]
    base = (head * (blocks - 2) + near) * randoms
    parts += [ref[rand_ref[base + r], :, cols] for r in range(randoms)]
    return jnp.concatenate(parts, axis=0)


def keys_values(ref, head, t, size):
    cols = slice(head * SLOT + LANES, head * SLOT + SLOT)
    return ref[pl.ds(t * (size // BLOCK), size // BLOCK), :, cols].reshape(size, LANES)


def mask_globals(s, i, blocks):
    lane = lax.broadcasted_iota(jnp.int32, (BLOCK, LANES), 1)
    low = lane < BLOCK
    dead = (low & (i == 1)) | (~low & (i == blocks - 2))
    return jnp.concatenate([jnp.where(dead, MASKED, s[:, :LANES]), s[:, LANES:]], axis=1)


def middle_blocks(qkv_ref, rand_ref, res_ref, first, heads, randoms, blocks):
    lane = lax.broadcasted_iota(jnp.int32, (BLOCK, LANES), 1)
    work = [(first + n, h) for n in range(PAIR) for h in range(heads)]
    kvs = [listed(qkv_ref, rand_ref, h, i, blocks, randoms) for i, h in work]
    qs = [qkv_ref[i, :, h * SLOT : h * SLOT + LANES] for i, h in work]
    ss = [mask_globals(dot_nt(q, kv), i, blocks) for q, kv, (i, h) in zip(qs, kvs, work)]
    tops = [jnp.max(s, axis=1, keepdims=True) for s in ss]
    es = [jnp.exp(s - top) for s, top in zip(ss, tops)]
    totals = [jnp.sum(e, axis=1, keepdims=True) for e in es]
    os = [dot(e.astype(bf16), kv) for e, kv in zip(es, kvs)]
    for o, top, total, (i, h) in zip(os, tops, totals, work):
        both = jnp.where(lane < HEAD_DIM, top + jnp.log(total), o / total)
        res_ref[h, rows_at(i * BLOCK, BLOCK), :] = both


def global_blocks(qkv_ref, heads, length):
    last = length // BLOCK - 1

    def ends(h):
        cols = slice(h * SLOT, h * SLOT + LANES)
        return jnp.concatenate([qkv_ref[0, :, cols], qkv_ref[last, :, cols]], axis=0)

    qs = [ends(h) for h in range(heads)]

    def whole(t, carry):
        kvs = [keys_values(qkv_ref, h, t, CHUNK) for h in range(heads)]
        ss = [dot_nt(q, kv) for q, kv in zip(qs, kvs)]
        news = [jnp.maximum(c[0], jnp.max(s, axis=1, keepdims=True)) for c, s in zip(carry, ss)]
        fades = [jnp.exp(c[0] - new) for c, new in zip(carry, news)]
        es = [jnp.exp(s - new) for s, new in zip(ss, news)]
        sums = [jnp.sum(e, axis=1, keepdims=True) for e in es]
        os = [dot(e.astype(bf16), kv) for e, kv in zip(es, kvs)]
        return tuple(
            (new, c[1] * fade + total, c[2] * fade + o)
            for c, new, fade, total, o in zip(carry, news, fades, sums, os)
        )

    start = (
        jnp.full((2 * BLOCK, 1), MASKED, f32),
        jnp.zeros((2 * BLOCK, 1), f32),
        jnp.zeros((2 * BLOCK, LANES), f32),
    )
    done = lax.fori_loop(0, length // CHUNK, whole, (start,) * heads)
    lane = lax.broadcasted_iota(jnp.int32, (2 * BLOCK, LANES), 1)
    return [jnp.where(lane < HEAD_DIM, top + jnp.log(total), acc / total) for top, total, acc in done]


def pack_rows(res_ref, ctx_ref, start, part, piece):
    low = lax.broadcasted_iota(jnp.int32, (BLOCK, LANES), 1) < HEAD_DIM
    for n in range(ROWS // BLOCK):
        rows = rows_at(start + n * BLOCK, BLOCK)
        first = pltpu.roll(res_ref[0, rows, :], HEAD_DIM, 1)
        pair = jnp.where(low, first, res_ref[1, rows, :])
        ctx_ref[part, piece, n * BLOCK : (n + 1) * BLOCK, :] = pair.astype(bf16)
    for n in range(ROWS // (2 * BLOCK)):
        rows = rows_at(start + 2 * n * BLOCK, BLOCK)
        odd = rows_at(start + (2 * n + 1) * BLOCK, BLOCK)
        first = pltpu.roll(res_ref[2, rows, :], HEAD_DIM, 1)
        both = jnp.where(low, first, res_ref[2, odd, :])
        ctx_ref[part, piece, ROWS + n * BLOCK : ROWS + (n + 1) * BLOCK, :] = both.astype(bf16)


def attend_kernel(heads, randoms, rand_ref, x_ref, w_ref, b_ref, qkv_ref, res_ref, ctx_ref):
    length = x_ref.shape[0]
    blocks = length // BLOCK

    def project(t, carry):
        raw = dot(x_ref[rows_at(t * CHUNK, CHUNK), :], w_ref[...]) + b_ref[...]
        step = CHUNK // BLOCK
        qkv_ref[pl.ds(t * step, step)] = raw.astype(bf16).reshape(step, BLOCK, raw.shape[1])
        return carry

    lax.fori_loop(0, length // CHUNK, project, 0)

    def middle(t, carry):
        middle_blocks(qkv_ref, rand_ref, res_ref, t * PAIR, heads, randoms, blocks)
        return carry

    lax.fori_loop(0, blocks // PAIR, middle, 0)
    for h, both in enumerate(global_blocks(qkv_ref, heads, length)):
        res_ref[h, 0:BLOCK, :] = both[:BLOCK]
        res_ref[h, length - BLOCK : length, :] = both[BLOCK:]
    per_quarter = ctx_ref.shape[1]

    def pack(t, carry):
        pack_rows(res_ref, ctx_ref, t * ROWS, t // per_quarter, t % per_quarter)
        return carry

    lax.fori_loop(0, length // ROWS, pack, 0)


def attend(rand, x, w, b, parts, heads):
    length = x.shape[0]
    randoms = rand.size // (heads * (length // BLOCK - 2))
    vmem = pl.BlockSpec(memory_space=pltpu.VMEM)
    return pl.pallas_call(
        partial(attend_kernel, heads, randoms),
        out_shape=(
            jax.ShapeDtypeStruct((length // BLOCK, BLOCK, heads * SLOT), bf16),
            jax.ShapeDtypeStruct((heads, length, LANES), f32),
            jax.ShapeDtypeStruct((parts, length // parts // ROWS, ROWS * 3 // 2, LANES), bf16),
        ),
        in_specs=[pl.BlockSpec(memory_space=pltpu.SMEM), vmem, vmem, vmem],
        out_specs=(vmem, vmem, vmem),
        compiler_params=pltpu.CompilerParams(vmem_limit_bytes=VMEM_BYTES),
        name="attend",
    )(rand, x, w, b)


def attend_back_kernel(
    heads, randoms, rand_ref, qkv_ref, res_ref, dctx_ref, draw_ref, sums_ref, *scratch
):
    dout, acc = scratch[:heads], scratch[heads:]
    blocks = qkv_ref.shape[0]
    length = blocks * BLOCK
    last = (blocks - 1) * BLOCK
    per_quarter = dctx_ref.shape[1]

    def unpack(t, carry):
        part, piece = t // per_quarter, t % per_quarter
        lane = lax.broadcasted_iota(jnp.int32, (BLOCK, LANES), 1)
        low = lane < HEAD_DIM
        for n in range(ROWS // BLOCK):
            rows = rows_at(t * ROWS + n * BLOCK, BLOCK)
            pair = dctx_ref[part, piece, n * BLOCK : (n + 1) * BLOCK, :].astype(f32)
            dout[0][rows, :] = jnp.where(low, 0.0, pltpu.roll(pair, HEAD_DIM, 1)).astype(bf16)
            dout[1][rows, :] = jnp.where(low, 0.0, pair).astype(bf16)
        for n in range(ROWS // (2 * BLOCK)):
            rows = rows_at(t * ROWS + 2 * n * BLOCK, BLOCK)
            odd = rows_at(t * ROWS + (2 * n + 1) * BLOCK, BLOCK)
            both = dctx_ref[part, piece, ROWS + n * BLOCK : ROWS + (n + 1) * BLOCK, :].astype(f32)
            dout[2][rows, :] = jnp.where(low, 0.0, pltpu.roll(both, HEAD_DIM, 1)).astype(bf16)
            dout[2][odd, :] = jnp.where(low, 0.0, both).astype(bf16)
        return carry

    lax.fori_loop(0, length // ROWS, unpack, 0)

    step = 256

    def ends(ref, cols):
        return jnp.concatenate([ref[0:BLOCK, cols], ref[last : last + BLOCK, cols]], axis=0)

    every = slice(0, LANES)
    gs = [ends(dout[h], every) for h in range(heads)]
    reses = [ends(res_ref.at[h], every) for h in range(heads)]
    alls = [
        jnp.concatenate(
            [qkv_ref[n, :, h * SLOT : h * SLOT + LANES] for n in (0, blocks - 1)] + [gs[h]], axis=0
        )
        for h in range(heads)
    ]
    logs = [res[:, 0:1] for res in reses]
    deltas = [jnp.sum(g.astype(f32) * res, axis=1, keepdims=True) for g, res in zip(gs, reses)]

    def whole(t, dqs):
        rows = rows_at(t * step, step)
        kvs = [keys_values(qkv_ref, h, t, step) for h in range(heads)]
        sds = [dot_nt(both, kv) for both, kv in zip(alls, kvs)]
        ps = [jnp.exp(sd[: 2 * BLOCK] - log) for sd, log in zip(sds, logs)]
        dss = [(p * (sd[2 * BLOCK :] - d)).astype(bf16) for p, sd, d in zip(ps, sds, deltas)]
        dkvs = [
            dot_tn(jnp.concatenate([ds, p.astype(bf16)], axis=0), both)
            for ds, p, both in zip(dss, ps, alls)
        ]
        news = tuple(dq + dot(ds, kv) for dq, ds, kv in zip(dqs, dss, kvs))
        for h in range(heads):
            acc[h][rows, :] = dkvs[h]
        return news

    dqs = lax.fori_loop(
        0, length // step, whole, (jnp.zeros((2 * BLOCK, LANES), f32),) * heads
    )
    for h in range(heads):
        cols = slice(h * SLOT, h * SLOT + LANES)
        lane = lax.broadcasted_iota(jnp.int32, (2 * BLOCK, LANES), 1)
        dq = jnp.where(lane < HEAD_DIM, dqs[h], 0.0).astype(bf16)
        draw_ref[0:BLOCK, cols] = dq[:BLOCK]
        draw_ref[last : last + BLOCK, cols] = dq[BLOCK:]

    def middle(t, carry):
        lane = lax.broadcasted_iota(jnp.int32, (BLOCK, LANES), 1)
        work = [(1 + t * PAIR_BACK + n, h) for n in range(PAIR_BACK) for h in range(heads)]
        kvs = [listed(qkv_ref, rand_ref, h, i, blocks, randoms) for i, h in work]
        places = [(rows_at(i * BLOCK, BLOCK), slice(h * SLOT, h * SLOT + LANES)) for i, h in work]
        gs = [dout[h][rows, :] for (rows, _), (_, h) in zip(places, work)]
        reses = [res_ref[h, rows, :] for (rows, _), (_, h) in zip(places, work)]
        alls = [
            jnp.concatenate([qkv_ref[i, :, cols], g], axis=0)
            for (_, cols), (i, _), g in zip(places, work, gs)
        ]
        sds = [dot_nt(both, kv) for both, kv in zip(alls, kvs)]
        deltas = [jnp.sum(g.astype(f32) * res, axis=1, keepdims=True) for g, res in zip(gs, reses)]
        ps = [
            jnp.exp(mask_globals(sd[:BLOCK], i, blocks) - res[:, 0:1])
            for sd, res, (i, h) in zip(sds, reses, work)
        ]
        dss = [(p * (sd[BLOCK:] - d)).astype(bf16) for p, sd, d in zip(ps, sds, deltas)]
        dkvs = [
            dot_tn(jnp.concatenate([ds, p.astype(bf16)], axis=0), both)
            for ds, p, both in zip(dss, ps, alls)
        ]
        dqs = [dot(ds, kv) for ds, kv in zip(dss, kvs)]
        for dq, (rows, cols) in zip(dqs, places):
            draw_ref[rows, cols] = jnp.where(lane < HEAD_DIM, dq, 0.0).astype(bf16)
        for dkv, (i, h) in zip(dkvs, work):
            acc[h][0:BLOCK, :] += dkv[0:BLOCK]
            acc[h][last : last + BLOCK, :] += dkv[BLOCK : 2 * BLOCK]
            near = pl.ds(pl.multiple_of((i - 1) * BLOCK, BLOCK), 3 * BLOCK)
            acc[h][near, :] += dkv[2 * BLOCK : 5 * BLOCK]
            base = (h * (blocks - 2) + i - 1) * randoms
            for r in range(randoms):
                far = rows_at(rand_ref[base + r] * BLOCK, BLOCK)
                acc[h][far, :] += dkv[(5 + r) * BLOCK : (6 + r) * BLOCK]
        return carry

    lax.fori_loop(0, (blocks - 2) // PAIR_BACK, middle, 0)
    sums_ref[...] = jnp.zeros_like(sums_ref)

    def finish(t, carry):
        rows = rows_at(t * CHUNK, CHUNK)
        for h in range(heads):
            at = h * SLOT
            draw_ref[rows, at + LANES : at + SLOT] = acc[h][rows, :].astype(bf16)
        sums_ref[0:1, :] += jnp.sum(draw_ref[rows, :].astype(f32), axis=0, keepdims=True)
        return carry

    lax.fori_loop(0, length // CHUNK, finish, 0)


def attend_back(rand, qkv, res, dctx, heads):
    length = qkv.shape[0] * BLOCK
    randoms = rand.size // (heads * (length // BLOCK - 2))
    vmem = pl.BlockSpec(memory_space=pltpu.VMEM)
    return pl.pallas_call(
        partial(attend_back_kernel, heads, randoms),
        out_shape=(
            jax.ShapeDtypeStruct((length, heads * SLOT), bf16),
            jax.ShapeDtypeStruct((8, heads * SLOT), f32),
        ),
        in_specs=[pl.BlockSpec(memory_space=pltpu.SMEM), vmem, vmem, vmem],
        out_specs=(vmem, vmem),
        scratch_shapes=[pltpu.VMEM((length, LANES), bf16)] * heads
        + [pltpu.VMEM((length, LANES), f32)] * heads,
        compiler_params=pltpu.CompilerParams(vmem_limit_bytes=VMEM_BYTES),
        name="attend_back",
    )(rand, qkv, res, dctx)


def mean_of(a):
    return jnp.mean(a, axis=1, keepdims=True)


def norm(r):
    center = r - mean_of(r)
    rstd = lax.rsqrt(mean_of(center * center) + EPS)
    return center * rstd, rstd


def norm_back(dn, n, rstd):
    return rstd * (dn - mean_of(dn) - n * mean_of(dn * n))


def rowsum(a):
    return jnp.sum(a, axis=0, keepdims=True)


MESH = pl.DeviceIdType.MESH


def run_phases(items):
    step = 0
    live = list(items)
    while live:
        after = []
        for first, phases in live:
            if first > step or next(phases, None) is not None:
                after.append((first, phases))
        live = after
        step += 1


class Where:
    def __init__(self):
        c, core, zh, zl = (lax.axis_index(a) for a in ALL)
        self.y, self.x, self.core, self.zh, self.zl = c // 2, c % 2, core, zh, zl
        self.z = zh * 2 + zl
        self.by_x = (self.y * 2 + 1 - self.x, core, zh, zl)
        self.by_y = ((1 - self.y) * 2 + self.x, core, zh, zl)
        self.by_core = (c, 1 - core, zh, zl)
        self.by_zl = (c, core, zh, 1 - zl)
        self.by_zh = (c, core, 1 - zh, zl)
        self.by_mid = (c, core, 1 - zh, 1 - zl)
        self.by_swap = (c, 1 - core, 1 - zh, zl)
        self.by_both = (c, 1 - core, zh, 1 - zl)
        self.inner = zh != zl
        self.stays = core == zh

    def greet(self):
        barrier = pltpu.get_barrier_semaphore()
        others = (self.by_x, self.by_y, self.by_core, self.by_zl)
        others += (self.by_zh, self.by_mid, self.by_swap, self.by_both)
        for other in others:
            pl.semaphore_signal(barrier, inc=1, device_id=other, device_id_type=MESH)
        pl.semaphore_wait(barrier, len(others))


class Copies:
    def __init__(self, send, recv, local):
        self.send, self.recv, self.local_sems = send, recv, local
        self.n = self.m = 0

    def remote(self, src, dst, device):
        n = self.n
        self.n += 1
        return pltpu.make_async_remote_copy(
            src_ref=src,
            dst_ref=dst,
            send_sem=self.send.at[n],
            recv_sem=self.recv.at[n],
            device_id=device,
            device_id_type=MESH,
        )

    def local(self, src, dst):
        m = self.m
        self.m += 1
        return pltpu.make_async_copy(src, dst, self.local_sems.at[m])


def chain_kernel(
    groups,
    direct,
    ctx_ref,
    tok_ref,
    og_ref,
    wo_ref,
    wu_ref,
    wd_ref,
    vec_ref,
    bu_ref,
    out_ref,
    dres_ref,
    dctx_ref,
    mix_ref,
    hid_ref,
    act_ref,
    dpre_ref,
    dffn_ref,
    dproj_ref,
    gvec_ref,
    gbu_ref,
    slope_ref,
    wop_ref,
    *stage,
):
    width = tok_ref.shape[1]
    hidden = wu_ref.shape[1]
    wide = 3 * HEAD_DIM
    step = pl.program_id(0)
    if direct:
        me = Where()
        out_far, dctx_far = out_ref, dctx_ref
        out_stage, dctx_stage, send, recv, local = stage
        out_ref, dctx_ref = out_stage.at[step], dctx_stage.at[step]

        @pl.when(step == 0)
        def _():
            me.greet()

    def transfers(t):
        place = me.core * 2 + me.zl
        near, beside = me.core * 2 + 1 - me.zl, (1 - me.core) * 2 + me.zl
        across = (1 - me.core) * 2 + 1 - me.zl
        others = ((near, me.by_zl), (beside, me.by_core), (across, me.by_both))
        remote = [
            pltpu.make_async_remote_copy(
                src_ref=dctx_stage.at[t, where],
                dst_ref=dctx_far.at[place, pl.ds(t * SUBS, SUBS)],
                send_sem=send.at[t, n],
                recv_sem=recv.at[t, n],
                device_id=other,
                device_id_type=MESH,
            )
            for n, (where, other) in enumerate(others)
        ]
        swap = pltpu.make_async_remote_copy(
            src_ref=out_stage.at[t],
            dst_ref=out_far.at[t],
            send_sem=send.at[t, 3],
            recv_sem=recv.at[t, 3],
            device_id=me.by_swap,
            device_id_type=MESH,
        )
        keep = pltpu.make_async_copy(out_stage.at[t], out_far.at[t], local.at[t, 0])
        own = pltpu.make_async_copy(
            dctx_stage.at[t, place], dctx_far.at[place, pl.ds(t * SUBS, SUBS)], local.at[t, 1]
        )
        return remote, own, swap, keep

    @pl.when(step == 0)
    def _():
        for g in range(groups):
            wop_ref[g * LANES : (g + 1) * LANES, :] = wo_ref[g * wide : g * wide + LANES, :]
            to = groups * LANES + g * HEAD_DIM
            wop_ref[to : to + HEAD_DIM, :] = wo_ref[g * wide + LANES : (g + 1) * wide, :]
        gvec_ref[...] = jnp.zeros_like(gvec_ref)
        gbu_ref[...] = jnp.zeros_like(gbu_ref)

    low = lax.broadcasted_iota(jnp.int32, (BLOCK, LANES), 1) < HEAD_DIM
    subs = range(tok_ref.shape[0] // ROWS)
    spans = [slice(n * ROWS, (n + 1) * ROWS) for n in subs]
    chunks = [slice(f, f + CHUNK) for f in range(0, hidden, CHUNK)]
    for n in subs:
        for g in range(groups):
            mix_ref[spans[n], g * LANES : (g + 1) * LANES] = ctx_ref[g, n, :ROWS, :]
        for g in range(0, groups, 2):
            to = groups * LANES + g * HEAD_DIM
            for m in range(ROWS // (2 * BLOCK)):
                at = ROWS + m * BLOCK
                a = ctx_ref[g, n, at : at + BLOCK, :].astype(f32)
                b = ctx_ref[g + 1, n, at : at + BLOCK, :].astype(f32)
                even = jnp.where(low, a, pltpu.roll(b, HEAD_DIM, 1))
                odd = jnp.where(low, pltpu.roll(a, HEAD_DIM, 1), b)
                r = n * ROWS + 2 * m * BLOCK
                mix_ref[r : r + BLOCK, to : to + LANES] = even.astype(bf16)
                mix_ref[r + BLOCK : r + 2 * BLOCK, to : to + LANES] = odd.astype(bf16)

    bo, g1, s1 = vec_ref[0:1, :], vec_ref[1:2, :], vec_ref[2:3, :]
    bd, g2, s2 = vec_ref[3:4, :], vec_ref[4:5, :], vec_ref[5:6, :]
    projs = [dot(mix_ref[rows, :], wop_ref[...]) for rows in spans]
    norms = [norm(tok_ref[rows, :].astype(f32) + proj + bo) for rows, proj in zip(spans, projs)]
    hids = [n1 * g1 + s1 for n1, _ in norms]
    lows = [hid.astype(bf16) for hid in hids]
    for rows, hid_low in zip(spans, lows):
        hid_ref[rows, :] = hid_low
    scale = np.sqrt(2.0 / np.pi).astype(np.float32)
    work = [(n, cols) for cols in chunks for n in subs]

    def behind(start, end):
        held = start(*work[0])
        for k, item in enumerate(work):
            now = held
            if k + 1 < len(work):
                held = start(*work[k + 1])
            end(*item, now)

    def up_start(n, cols):
        return dot(lows[n], wu_ref[:, cols])

    def up_end(n, cols, raw):
        u = raw + bu_ref[:, cols]
        square = u * u
        t = jnp.tanh(u * (scale + (scale * 0.044715) * square))
        half = 0.5 + 0.5 * t
        act_ref[spans[n], cols] = (u * half).astype(bf16)
        slope = half + (0.5 * u) * (1.0 - t * t) * (scale + (3 * 0.044715 * scale) * square)
        slope_ref[spans[n], cols] = slope.astype(bf16)

    behind(up_start, up_end)
    ffns = [dot(act_ref[rows, :], wd_ref[...]) for rows in spans]
    dres2s, dffns = [], []
    for n, rows in enumerate(spans):
        n2, rstd2 = norm(hids[n] + ffns[n] + bd)
        out_ref[rows, :] = (n2 * g2 + s2).astype(bf16)
        og = og_ref[rows, :].astype(f32)
        gvec_ref[4:5, :] += rowsum(og * n2)
        gvec_ref[5:6, :] += rowsum(og)
        dres2 = norm_back(og * g2, n2, rstd2)
        dffn = dres2.astype(bf16)
        dffn_ref[rows, :] = dffn
        gvec_ref[3:4, :] += rowsum(dffn.astype(f32))
        dres2s.append(dres2)
        dffns.append(dffn)

    if direct:
        remote, own, swap, keep = transfers(step)

        @pl.when(me.stays)
        def _():
            keep.start()

        @pl.when(jnp.logical_not(me.stays))
        def _():
            swap.start()

    def down_start(n, cols):
        return dot_nt(dffns[n], wd_ref[cols, :])

    def down_end(n, cols, dact):
        dpre = (dact * slope_ref[spans[n], cols].astype(f32)).astype(bf16)
        dpre_ref[spans[n], cols] = dpre
        gbu_ref[0:1, cols] += rowsum(dpre.astype(f32))

    behind(down_start, down_end)
    dhs = [dres2 + dot_nt(dpre_ref[rows, :], wu_ref[...]) for rows, dres2 in zip(spans, dres2s)]
    dmixes = []
    for rows, dh, (n1, rstd1) in zip(spans, dhs, norms):
        gvec_ref[1:2, :] += rowsum(dh * n1)
        gvec_ref[2:3, :] += rowsum(dh)
        dres1 = norm_back(dh * g1, n1, rstd1)
        dres_ref[rows, :] = dres1
        dproj = dres1.astype(bf16)
        dproj_ref[rows, :] = dproj
        gvec_ref[0:1, :] += rowsum(dproj.astype(f32))
        dmixes.append(dot_nt(dproj, wop_ref[...]))
    for n, dmix in enumerate(dmixes):
        for g in range(groups):
            dctx_ref[g, n, :ROWS, :] = dmix[:, g * LANES : (g + 1) * LANES].astype(bf16)
        for g in range(0, groups, 2):
            to = groups * LANES + g * HEAD_DIM
            for m in range(ROWS // (2 * BLOCK)):
                at = ROWS + m * BLOCK
                r = 2 * m * BLOCK
                even = dmix[r : r + BLOCK, to : to + LANES]
                odd = dmix[r + BLOCK : r + 2 * BLOCK, to : to + LANES]
                a = jnp.where(low, even, pltpu.roll(odd, HEAD_DIM, 1))
                b = jnp.where(low, pltpu.roll(even, HEAD_DIM, 1), odd)
                dctx_ref[g, n, at : at + BLOCK, :] = a.astype(bf16)
                dctx_ref[g + 1, n, at : at + BLOCK, :] = b.astype(bf16)

    if direct:
        for copy in remote:
            copy.start()
        own.start()

        @pl.when(step == pl.num_programs(0) - 1)
        def _():
            for t in range(dctx_stage.shape[0]):
                remote, own, swap, keep = transfers(t)
                for copy in remote:
                    copy.wait()
                own.wait()

                @pl.when(me.stays)
                def _():
                    keep.wait()

                @pl.when(jnp.logical_not(me.stays))
                def _():
                    swap.wait()


def chain(ctx, tok, og, wo, wu, wd, vec, bu, direct):
    rows, width = tok.shape
    hidden = wu.shape[1]
    groups = ctx.shape[0]
    once = pl.Buffered(1)

    def tiled(cols):
        return pl.BlockSpec((SUBS * ROWS, cols), lambda t: (t, 0))

    def fixed(shape):
        return pl.BlockSpec(shape, lambda t: (0, 0), pipeline_mode=once)

    packed = pl.BlockSpec((groups, SUBS) + ctx.shape[2:], lambda t: (0, t, 0, 0))
    shape = jax.ShapeDtypeStruct
    steps = rows // (SUBS * ROWS)
    hbm = pl.BlockSpec(memory_space=pltpu.HBM)
    scratch = [pltpu.VMEM((SUBS * ROWS, hidden), bf16), pltpu.VMEM(wo.shape, bf16)]
    params = pltpu.CompilerParams(vmem_limit_bytes=VMEM_BYTES)
    out_shape = (rows, width)
    if direct:
        out_shape = (steps, SUBS * ROWS, width)
        scratch += [
            pltpu.VMEM(out_shape, bf16),
            pltpu.VMEM((steps, groups, SUBS) + ctx.shape[2:], bf16),
            pltpu.SemaphoreType.DMA((steps, 4)),
            pltpu.SemaphoreType.DMA((steps, 4)),
            pltpu.SemaphoreType.DMA((steps, 2)),
        ]
        params = pltpu.CompilerParams(
            vmem_limit_bytes=VMEM_BYTES, collective_id=2, has_side_effects=True
        )
    return pl.pallas_call(
        partial(chain_kernel, groups, direct),
        grid=(steps,),
        out_shape=(
            shape(out_shape, bf16),
            shape((rows, width), f32),
            shape(ctx.shape, bf16),
            shape((rows, width), bf16),
            shape((rows, width), bf16),
            shape((rows, hidden), bf16),
            shape((rows, hidden), bf16),
            shape((rows, width), bf16),
            shape((rows, width), bf16),
            shape((8, width), f32),
            shape((8, hidden), f32),
        ),
        in_specs=[
            packed,
            tiled(width),
            tiled(width),
            fixed(wo.shape),
            fixed(wu.shape),
            fixed(wd.shape),
            fixed(vec.shape),
            fixed(bu.shape),
        ],
        out_specs=(
            hbm if direct else tiled(width),
            tiled(width),
            hbm if direct else packed,
            tiled(width),
            tiled(width),
            tiled(hidden),
            tiled(hidden),
            tiled(width),
            tiled(width),
            pl.BlockSpec((8, width), lambda t: (0, 0)),
            pl.BlockSpec((8, hidden), lambda t: (0, 0)),
        ),
        scratch_shapes=scratch,
        compiler_params=params,
        name="chain",
    )(ctx, tok, og, wo, wu, wd, vec, bu)


def gather_item(me, copies, shard, full, cols, x_first):
    y, x, core, zh, zl = me.y, me.x, me.core, me.zh, me.zl
    mine = shard.at[:, cols]
    own = copies.local(mine, full.at[y, x, core, me.z, :, cols])
    spot = full.at[y, x, core, me.z, :, cols]
    along = [copies.remote(mine, spot, other) for other in (me.by_zl, me.by_mid, me.by_zh)]
    own.start()
    for copy in along:
        copy.start()
    yield 1
    own.wait()
    for copy in along:
        copy.wait()
    line = full.at[y, x, core, :, :, cols]
    near = copies.remote(line, line, me.by_x if x_first else me.by_y)
    near.start()
    across = [copies.remote(line, line, me.by_core)]
    across[0].start()
    yield 1
    near.wait()
    if x_first:
        block = full.at[y, :, core, :, :, cols]
        got = full.at[y, 1 - x, core, :, :, cols]
        rest = full.at[1 - y, :, core, :, :, cols]
    else:
        block = full.at[:, x, core, :, :, cols]
        got = full.at[1 - y, x, core, :, :, cols]
        rest = full.at[:, 1 - x, core, :, :, cols]
    far = copies.remote(block, block, me.by_y if x_first else me.by_x)
    far.start()
    across.append(copies.remote(got, got, me.by_core))
    across[1].start()
    yield 1
    far.wait()
    across.append(copies.remote(rest, rest, me.by_core))
    across[2].start()
    yield 1
    for copy in across:
        copy.wait()


def tokens_item(me, copies, tok, x_all, piece):
    place = me.core * 2 + me.zl
    there = (1 - me.core) * 2 + me.zl
    held = x_all.at[place, piece]
    out = copies.remote(tok.at[piece], x_all.at[there, piece], me.by_swap)
    keep = copies.local(tok.at[piece], held)
    along = copies.remote(held, held, me.by_zl)
    over = copies.remote(held, held, me.by_core)

    @pl.when(me.stays)
    def _():
        keep.start()

    @pl.when(jnp.logical_not(me.stays))
    def _():
        out.start()

    yield 1

    @pl.when(me.stays)
    def _():
        keep.wait()
        along.start()
        over.start()

    yield 1

    @pl.when(jnp.logical_not(me.stays))
    def _():
        out.wait()
        along.start()
        over.start()

    yield 1
    along.wait()
    came = x_all.at[me.core * 2 + 1 - me.zl, piece]
    onto = copies.remote(came, came, me.by_core)
    onto.start()
    yield 1
    over.wait()
    onto.wait()


def exchange_item(me, copies, src, dst):
    out = copies.remote(src, dst, me.by_swap)
    keep = copies.local(src, dst)

    @pl.when(me.stays)
    def _():
        keep.start()

    @pl.when(jnp.logical_not(me.stays))
    def _():
        out.start()

    yield 1

    @pl.when(me.stays)
    def _():
        keep.wait()

    @pl.when(jnp.logical_not(me.stays))
    def _():
        out.wait()


PIECES = 4


def weight_item(me, copies, src, parts, whole, bias):
    y, x, core, zh, zl = me.y, me.x, me.core, me.zh, me.zl
    place = core * 2 + zl
    keep = copies.local(src.at[place], parts.at[place])
    moves = [
        copies.remote(src.at[core * 2 + 1 - zl], parts.at[place], me.by_zl),
        copies.remote(src.at[(1 - core) * 2 + zl], parts.at[place], me.by_core),
        copies.remote(src.at[(1 - core) * 2 + 1 - zl], parts.at[place], me.by_both),
    ]
    keep.start()
    for move in moves:
        move.start()
    yield 1
    keep.wait()
    for move in moves:
        move.wait()
    own = whole.shape[4] // 2
    for b in range(2):
        both = jnp.concatenate([parts[2 * b, :own, :], parts[2 * b + 1, :own, :]], axis=0)
        whole[y, x, b, zh] = both.astype(bf16)
    tail = pl.ds(own, 8)
    bias[y, x, zh] = parts[0, tail, :] + parts[1, tail, :] + parts[2, tail, :] + parts[3, tail, :]
    for spot, bias_spot, other in (
        (whole.at[y, x, :, zh], bias.at[y, x, zh], me.by_zh),
        (whole.at[y, x], bias.at[y, x], me.by_x),
        (whole.at[y], bias.at[y], me.by_y),
    ):
        moves = [copies.remote(spot, spot, other), copies.remote(bias_spot, bias_spot, other)]
        for move in moves:
            move.start()
        yield 1
        for move in moves:
            move.wait()


def finish(*generators):
    for phases in generators:
        for _ in phases:
            pass


def front_kernel(heads, randoms, *refs):
    rand_ref, tok, og, wq, w_out, up, down, small = refs[:8]
    x_hbm, tok_own, og_own, w_own, qkv_hbm, res_hbm, ctx_all, out_all, up_all, down_all, small_all = refs[8:19]
    x_all, parts, whole, bias, qkv_ref, res_ref, ends_ref, ctx_ref = refs[19:27]
    me = Where()
    me.greet()
    copies = Copies(*refs[27:])
    blocks = qkv_ref.shape[0]
    length = blocks * BLOCK
    quarter = length // 4
    core, zl = me.core, me.zl
    place = core * 2 + zl
    near = core * 2 + 1 - zl
    beside = (1 - core) * 2 + zl
    across = (1 - core) * 2 + 1 - zl

    weights = weight_item(me, copies, wq, parts, whole, bias)
    tokens = [tokens_item(me, copies, tok, x_all, piece) for piece in range(PIECES)]
    smalls = gather_item(me, copies, small, small_all, slice(0, LANES), True)
    turn = 0

    def gathers(*arrays):
        nonlocal turn
        made = []
        for shard, full, splits in arrays:
            width = shard.shape[1] // splits
            for n in range(splits):
                cols = slice(n * width, (n + 1) * width)
                made.append(gather_item(me, copies, shard, full, cols, turn % 2 == 0))
                turn += 1
        return made

    def advance(group):
        group[:] = [phases for phases in group if next(phases, None) is not None]

    early = gathers((up, up_all, 2))
    late = gathers((down, down_all, 2), (w_out, out_all, 2))
    last = [exchange_item(me, copies, og.at[n], og_own.at[n]) for n in range(PIECES)]
    idle = [smalls]
    outs = []

    def write(src, dst):
        copy = copies.local(src, dst)
        copy.start()
        outs.append(copy)

    def project(where):
        bias_row = jnp.sum(bias[...].reshape(-1, 8, bias.shape[-1]), axis=0)[0:1]
        matrix = whole[...].reshape(-1, whole.shape[-1])
        for piece in range(PIECES):
            raw = dot(x_all[where, piece], matrix) + bias_row
            step = ROWS // BLOCK
            at = (where * PIECES + piece) * step
            qkv_ref[pl.ds(at, step)] = raw.astype(bf16).reshape(step, BLOCK, raw.shape[1])

    def forward_tokens():
        for item in tokens:
            next(item)

    next(weights)
    advance(early)
    next(weights)
    forward_tokens()
    forward_tokens()
    next(weights)
    advance(idle)
    advance(early)
    next(weights)
    advance(idle)
    forward_tokens()
    advance(late)
    finish(weights)
    advance(early)
    next(last[0])
    project(place)
    write(whole, w_own)
    write(x_all.at[place], tok_own)
    forward_tokens()
    advance(late)
    next(last[1])
    project(near)
    finish(*tokens)
    next(last[2])
    next(last[3])
    advance(early)
    project(beside)
    project(across)
    advance(idle)
    write(x_all, x_hbm)
    write(qkv_ref, qkv_hbm)
    for h, both in enumerate(global_blocks(qkv_ref, heads, length)):
        ends_ref[h] = both
    advance(late)
    advance(early)
    advance(idle)

    def middle(t, carry):
        middle_blocks(qkv_ref, rand_ref, res_ref, t * PAIR, heads, randoms, blocks)
        return carry

    sends = []
    turns = quarter // BLOCK // PAIR
    for where, other in ((across, me.by_both), (near, me.by_zl), (beside, me.by_core), (place, None)):
        lax.fori_loop(where * turns, (where + 1) * turns, middle, 0)

        @pl.when(where == 0)
        def _():
            for h in range(heads):
                res_ref[h, 0:BLOCK, :] = ends_ref[h, 0:BLOCK, :]

        @pl.when(where == 3)
        def _():
            for h in range(heads):
                res_ref[h, length - BLOCK : length, :] = ends_ref[h, BLOCK : 2 * BLOCK, :]

        for piece in range(PIECES):
            pack_rows(res_ref, ctx_ref, where * quarter + piece * ROWS, where, piece)
        rows = rows_at(where * quarter, quarter)
        write(res_ref.at[:, rows], res_hbm.at[:, rows])
        if other is None:
            write(ctx_ref.at[where], ctx_all.at[place])
        else:
            send = copies.remote(ctx_ref.at[where], ctx_all.at[place], other)
            send.start()
            sends.append(send)
        advance(late if where is near or where is place else idle)
    finish(*early, *late, *last, *idle)
    for copy in sends + outs:
        copy.wait()


def front(rand, tok, og, wq, mats, small, heads):
    rows, width = tok.shape
    members = 4
    length = rows * members
    randoms = rand.size // (heads * (length // BLOCK - 2))
    hbm = pl.BlockSpec(memory_space=pltpu.HBM)
    shape = jax.ShapeDtypeStruct
    tok = tok.reshape(PIECES, rows // PIECES, width)
    og = og.reshape(tok.shape)
    cols = heads * SLOT
    own = mats[0].shape[0]
    packed = (members, rows // ROWS, ROWS * 3 // 2, LANES)
    outs = [
        shape((members,) + tok.shape, bf16),
        shape(tok.shape, bf16),
        shape(og.shape, bf16),
        shape((2, 2, 2, 2, 2 * own, cols), bf16),
        shape((length // BLOCK, BLOCK, cols), bf16),
        shape((heads, length, LANES), f32),
        shape(packed, bf16),
    ]
    outs += [shape((2, 2, 2, 4) + a.shape, bf16) for a in (*mats, small)]
    return pl.pallas_call(
        partial(front_kernel, heads, randoms),
        out_shape=tuple(outs),
        in_specs=[pl.BlockSpec(memory_space=pltpu.SMEM)] + [hbm] * 7,
        out_specs=(hbm,) * 11,
        scratch_shapes=[
            pltpu.VMEM((members,) + tok.shape, bf16),
            pltpu.VMEM(wq.shape, f32),
            pltpu.VMEM((2, 2, 2, 2, 2 * own, cols), bf16),
            pltpu.VMEM((2, 2, 2, 8, cols), f32),
            pltpu.VMEM((length // BLOCK, BLOCK, cols), bf16),
            pltpu.VMEM((heads, length, LANES), f32),
            pltpu.VMEM((heads, 2 * BLOCK, LANES), f32),
            pltpu.VMEM(packed, bf16),
            pltpu.SemaphoreType.DMA((112,)),
            pltpu.SemaphoreType.DMA((112,)),
            pltpu.SemaphoreType.DMA((32,)),
        ],
        compiler_params=pltpu.CompilerParams(
            collective_id=0, has_side_effects=True, vmem_limit_bytes=VMEM_BYTES
        ),
        name="front",
    )(rand, tok, og, wq, *mats, small)


def add_rows(dst, a, b, rows):
    step = next(n for n in (48, 32, 24, 16, 8) if rows % n == 0)

    def body(t, carry):
        at = rows_at(t * step, step)
        dst[at, :] = (a[at, :].astype(f32) + b[at, :].astype(f32)).astype(dst.dtype)
        return carry

    lax.fori_loop(0, rows // step, body, 0)


def scatter_item(me, copies, src, cols, acc, from_core, from_first, from_second, slabs, from_line, out, x_first):
    y, x, core, zh, zl = me.y, me.x, me.core, me.zh, me.zl
    rows = acc.shape[2]
    own = copies.local(src.at[:, :, core, :, cols], acc)
    over = copies.remote(src.at[:, :, 1 - core, :, cols], from_core, me.by_core)
    own.start()
    over.start()
    yield 1
    own.wait()
    over.wait()
    for a in range(2):
        for b in range(2):
            add_rows(acc.at[a, b], acc.at[a, b], from_core.at[a, b], rows)
    if x_first:
        first = copies.remote(acc.at[:, 1 - x], from_first, me.by_x)
    else:
        first = copies.remote(acc.at[1 - y], from_first, me.by_y)
    first.start()
    yield 1
    first.wait()
    for a in range(2):
        block = acc.at[a, x] if x_first else acc.at[y, a]
        add_rows(block, block, from_first.at[a], rows)
    if x_first:
        second = copies.remote(acc.at[1 - y, x], from_second, me.by_y)
    else:
        second = copies.remote(acc.at[y, 1 - x], from_second, me.by_x)
    second.start()
    yield 1
    second.wait()
    rest = rows // 4
    summed = acc[y, x].astype(f32) + from_second[...].astype(f32)
    for z in range(4):
        slabs[z] = summed[z * rest : (z + 1) * rest].astype(slabs.dtype)
    moves = [
        copies.remote(slabs.at[(1 - zh) * 2 + zl], from_line.at[0], me.by_zh),
        copies.remote(slabs.at[(1 - zh) * 2 + 1 - zl], from_line.at[1], me.by_mid),
        copies.remote(slabs.at[zh * 2 + 1 - zl], from_line.at[2], me.by_zl),
    ]
    for move in moves:
        move.start()
    yield 1
    for move in moves:
        move.wait()
    near = slabs[me.z].astype(f32) + from_line[2].astype(f32)
    out[...] = near + (from_line[0].astype(f32) + from_line[1].astype(f32))


def scatter_buffers(rows, cols, kind):
    return [
        pltpu.VMEM((2, 2, rows, cols), kind),
        pltpu.VMEM((2, 2, rows, cols), kind),
        pltpu.VMEM((2, rows, cols), kind),
        pltpu.VMEM((rows, cols), kind),
        pltpu.VMEM((4, rows // 4, cols), kind),
        pltpu.VMEM((3, rows // 4, cols), kind),
    ]


def own_columns_item(me, copies, acc, from_x, from_y, from_zh, part, blocks, out):
    y, x, core, zh, zl = me.y, me.x, me.core, me.zh, me.zl
    rows = acc.shape[4]
    first = copies.remote(acc.at[1 - x], from_x, me.by_x)
    first.start()
    yield 1
    first.wait()
    for a in range(2):
        for b in range(2):
            for c in range(2):
                add_rows(acc.at[x, a, b, c], acc.at[x, a, b, c], from_x.at[a, b, c], rows)
    acc = acc.at[x]
    second = copies.remote(acc.at[1 - y], from_y, me.by_y)
    second.start()
    yield 1
    second.wait()
    for b in range(2):
        for c in range(2):
            block = acc.at[y, b, c]
            add_rows(block, block, from_y.at[b, c], rows)
    third = copies.remote(acc.at[y, :, 1 - zh], from_zh, me.by_zh)
    third.start()
    yield 1
    third.wait()
    half = rows // 2
    for b in range(2):
        add_rows(part.at[b], acc.at[y, b, zh], from_zh.at[b], rows)
    place = core * 2 + zl
    mine = rows_at(zl * half, half)
    other = rows_at((1 - zl) * half, half)
    keep = copies.local(part.at[core, mine], blocks.at[place])
    keep.start()
    moves = [
        copies.remote(part.at[core, other], blocks.at[place], me.by_zl),
        copies.remote(part.at[1 - core, mine], blocks.at[place], me.by_core),
        copies.remote(part.at[1 - core, other], blocks.at[place], me.by_both),
    ]
    for move in moves:
        move.start()
    yield 1
    keep.wait()
    for move in moves:
        move.wait()
    heads = blocks.shape[2] // SLOT
    low = lax.broadcasted_iota(jnp.int32, (blocks.shape[1], LANES), 1) < HEAD_DIM
    for kind in range(3):
        for n in range(0, 4 * heads, 2):
            pair = []
            for head in (n, n + 1):
                at = head % heads * SLOT + (0 if kind == 0 else LANES)
                pair.append(blocks[head // heads, :, at : at + LANES])
            if kind == 2:
                tile = jnp.where(low, pltpu.roll(pair[0], HEAD_DIM, 1), pair[1])
            else:
                tile = jnp.where(low, pair[0], pltpu.roll(pair[1], HEAD_DIM, 1))
            if kind == 0:
                tile = tile * HEAD_DIM**-0.5
            to = (kind * 4 * heads + n) * HEAD_DIM
            out[:, to : to + LANES] = tile


def input_grad_item(me, copies, draw, w, dres, piece, stage, from_core, far, from_zl, res, send, out):
    core, zl = me.core, me.zl
    more = copies.local(dres.at[piece], res)
    more.start()
    for b in range(2):
        stage[b] = dot_nt(draw[(1 - core) * 2 + b, piece], w[...]).astype(bf16)
    over = copies.remote(stage, from_core, me.by_core)
    over.start()
    yield 1
    mine = dot_nt(draw[core * 2 + 1 - zl, piece], w[...])
    over.wait()
    far[...] = (mine + from_core[1 - zl].astype(f32)).astype(bf16)
    along = copies.remote(far, from_zl, me.by_zl)
    along.start()
    mine = dot_nt(draw[core * 2 + zl, piece], w[...])
    more.wait()
    res[...] = res[...] + (mine + from_core[zl].astype(f32))
    yield 1
    along.wait()
    send[...] = (res[...] + from_zl[...].astype(f32)).astype(bf16)
    yield from exchange_item(me, copies, send, out.at[piece])


SPLITS = ((0, 2), (1, 4), (2, 1), (3, 1))


def scatter_kernel(*refs):
    down, up, proj, vecs, draw, x_hbm, w, dres = refs[:8]
    outs = refs[8:14]
    sems, scratch = refs[14:17], list(refs[17:])
    me = Where()
    me.greet()
    copies = Copies(*sems)

    def take(n):
        got = scratch[:n]
        del scratch[:n]
        return got

    def advance(group):
        group[:] = [phases for phases in group if next(phases, None) is not None]

    pieces = [
        input_grad_item(me, copies, draw, w, dres, piece, *take(6), outs[5]) for piece in range(PIECES)
    ]
    x_all, total, acc, *buffers = take(8)
    fetch = copies.local(x_hbm, x_all)
    fetch.start()
    columns = [own_columns_item(me, copies, acc, *buffers, outs[4])]
    items = []
    for n, splits in SPLITS:
        src = refs[n]
        width = src.shape[4] // splits
        for part in range(splits):
            cols = slice(part * width, (part + 1) * width)
            dst = outs[n].at[:, cols]
            items.append(scatter_item(me, copies, src, cols, *take(6), dst, len(items) % 2 == 0))

    def weight_grad(t, carry):
        place, piece = t // PIECES, t % PIECES
        total[...] += dot_tn(x_all[place, piece], draw[place, piece])
        return carry

    next(pieces[0])
    next(pieces[1])
    advance(items)
    next(pieces[0])
    next(pieces[1])
    next(pieces[2])
    next(pieces[3])
    advance(items)
    next(pieces[0])
    next(pieces[2])
    total[...] = jnp.zeros_like(total)
    fetch.wait()
    lax.fori_loop(0, 2 * PIECES, weight_grad, 0)
    next(pieces[1])
    next(pieces[3])
    lax.fori_loop(2 * PIECES, 4 * PIECES, weight_grad, 0)
    laid = total[...].reshape((2, 2) + acc.shape[2:])
    for a in range(2):
        for b in range(2):
            acc[b, a] = laid[a, b].astype(bf16)
    advance(columns)
    next(pieces[2])
    advance(items)
    next(pieces[3])
    while pieces or columns or items:
        advance(items)
        advance(columns)
        if not items:
            advance(pieces)


def scatter(down, up, proj, vecs, draw, x_all, w, dres, own):
    hbm = pl.BlockSpec(memory_space=pltpu.HBM)
    vmem = pl.BlockSpec(memory_space=pltpu.VMEM)
    shape = jax.ShapeDtypeStruct
    grads = (down, up, proj, vecs)
    outs = [shape((a.shape[3] // 4, a.shape[4]), f32) for a in grads]
    width, cols = w.shape
    rows = 2 * own
    outs.append(shape((own, 3 * cols), f32))
    outs.append(shape(dres.shape, bf16))
    buffers = []
    for _ in range(PIECES):
        tile = dres.shape[1:]
        buffers += [
            pltpu.VMEM((2,) + tile, bf16),
            pltpu.VMEM((2,) + tile, bf16),
            pltpu.VMEM(tile, bf16),
            pltpu.VMEM(tile, bf16),
            pltpu.VMEM(tile, f32),
            pltpu.VMEM(tile, bf16),
        ]
    buffers += [
        pltpu.VMEM(x_all.shape, bf16),
        pltpu.VMEM((width, cols), f32),
        pltpu.VMEM((2, 2, 2, 2, rows, cols), bf16),
        pltpu.VMEM((2, 2, 2, rows, cols), bf16),
        pltpu.VMEM((2, 2, rows, cols), bf16),
        pltpu.VMEM((2, rows, cols), bf16),
        pltpu.VMEM((2, rows, cols), f32),
        pltpu.VMEM((4, own, cols), f32),
    ]
    for n, splits in SPLITS:
        a = grads[n]
        for _ in range(splits):
            buffers += scatter_buffers(a.shape[3], a.shape[4] // splits, a.dtype)
    return pl.pallas_call(
        scatter_kernel,
        out_shape=tuple(outs),
        in_specs=[hbm] * 4 + [vmem, hbm, vmem, hbm],
        out_specs=(vmem,) * 5 + (hbm,),
        scratch_shapes=[
            pltpu.SemaphoreType.DMA((80,)),
            pltpu.SemaphoreType.DMA((80,)),
            pltpu.SemaphoreType.DMA((32,)),
        ]
        + buffers,
        compiler_params=pltpu.CompilerParams(
            collective_id=1, has_side_effects=True, vmem_limit_bytes=VMEM_BYTES
        ),
        name="scatter",
    )(down, up, proj, vecs, draw, x_all, w, dres)


def per_device(
    tokens,
    qkv_weight,
    query_value_bias,
    out_weight,
    out_bias,
    norm1_gain,
    norm1_bias,
    up_weight,
    up_bias,
    down_weight,
    down_bias,
    norm2_gain,
    norm2_bias,
    rand_blocks,
    out_grad,
):
    members = lax.axis_size(GROUP)
    devices = lax.axis_size(ALL)
    swap = [(0, 0), (1, 2), (2, 1), (3, 3)]

    def move(a):
        return lax.ppermute(a, ("core", "zh"), swap)

    rand = move(rand_blocks[0])
    heads = rand.shape[0]
    rows, width = tokens.shape[1:]
    cols = heads * HEAD_DIM
    group = lax.axis_index(GROUP)
    own = width // devices
    rand_flat = rand.reshape(-1)

    def lay_out(a):
        a = a.reshape(a.shape[:-2] + (3, heads, HEAD_DIM))
        q, k, v = a[..., 0, :, :], a[..., 1, :, :], a[..., 2, :, :]
        q = q * jnp.asarray(HEAD_DIM**-0.5, a.dtype)
        laid = jnp.stack([q, jnp.zeros_like(q), k, v], axis=-2)
        return laid.reshape(laid.shape[:-3] + (heads * SLOT,))

    bias_part = jnp.stack([query_value_bias[0], jnp.zeros((own,), bf16), query_value_bias[1]])
    small = [out_bias, norm1_gain, norm1_bias, down_bias, norm2_gain, norm2_bias, up_bias]
    small = jnp.concatenate(small)
    direct = lax.axis_size("c") == 4 and members == 4 and own % 8 == 0
    if direct:
        count = small.shape[0]
        padded = jnp.pad(small, (0, 16 * LANES - count)).reshape(16, LANES)
        spread = lax.dynamic_update_slice(
            jnp.zeros((3, width), f32), bias_part.astype(f32), (0, lax.axis_index(ALL) * own)
        )
        spread = lay_out(jnp.transpose(spread.reshape(3, members, cols), (1, 0, 2)))
        wq = jnp.transpose(qkv_weight.astype(f32).reshape(own, 3, members, cols), (2, 0, 1, 3))
        wq = jnp.concatenate([lay_out(wq), spread[:, None], jnp.zeros((members, 7, heads * SLOT), f32)], axis=1)
        mats = (out_weight, up_weight, down_weight)
        x, tok, og, w_own, qkv, res, ctx, *full = front(
            rand_flat, tokens[0], out_grad[0], wq, mats, padded, heads
        )
        x, tok, og = (a.reshape(-1, width) for a in (x, tok, og))
        w_own = w_own.reshape(width, -1)
        w_out, w_up, w_down = (a.reshape(-1, a.shape[-1]) for a in full[:3])
        small = full[3].reshape(devices, -1)[:, :count].astype(f32)
    else:
        tok = move(tokens[0])
        og = move(out_grad[0])
        x = lax.all_gather(tok, GROUP, axis=0, tiled=True)
        mats = (qkv_weight, out_weight, up_weight, down_weight)
        w_qkv, w_out, w_up, w_down = (lax.all_gather(a, ALL, axis=0, tiled=True) for a in mats)
        small = lax.all_gather(small, ALL, axis=0).astype(f32)
        w_own = lax.dynamic_slice_in_dim(
            w_qkv.reshape(width, 3, members, cols), group, 1, axis=2
        ).reshape(width, 3, cols)
        w_own = lay_out(w_own)
        bias3 = lax.all_gather(bias_part, ALL, axis=1, tiled=True).astype(f32).reshape(3, members, cols)
        b_own = lay_out(lax.dynamic_slice_in_dim(bias3, group, 1, axis=1).reshape(1, 3, cols))
        qkv, res, ctx_send = attend(rand_flat, x, w_own, b_own, members, heads)
        ctx = lax.all_to_all(ctx_send, GROUP, split_axis=0, concat_axis=0, tiled=True)
    vecs = jnp.transpose(small[:, : 6 * own].reshape(devices, 6, own), (1, 0, 2)).reshape(6, width)
    bias_up = small[:, 6 * own :].reshape(1, -1)
    chain_vecs = jnp.concatenate([vecs, jnp.zeros((2, width), f32)], axis=0)
    out, dres1, dctx, mix, hid, act, dpre, dffn, dproj, gvec, gbu = chain(
        ctx, tok, og, w_out, w_up, w_down, chain_vecs, bias_up, direct
    )
    if direct:
        out = out.reshape(rows, width)
    else:
        dctx = lax.all_to_all(dctx, GROUP, split_axis=0, concat_axis=0, tiled=True)
        out = move(out)

    g_down = dot_tn(act, dffn).astype(bf16)
    g_up = dot_tn(hid, dpre).astype(bf16)
    g_mix = dot_tn(mix, dproj).astype(bf16)
    pairs = g_mix[: members * LANES].reshape(members, LANES, width)
    thirds = g_mix[members * LANES :].reshape(members, HEAD_DIM, width)
    g_out = jnp.concatenate([pairs, thirds], axis=1).reshape(width, width)

    draw, sums = attend_back(rand_flat, qkv, res, dctx, heads)

    def strip(a):
        a = a.reshape(a.shape[:-1] + (heads, 4, HEAD_DIM))
        q, k, v = a[..., 0, :] * (HEAD_DIM**-0.5), a[..., 2, :], a[..., 3, :]
        return jnp.stack([q, k, v], axis=-3).reshape(a.shape[:-3] + (3, cols))

    col_sums = strip(sums[0:1])[0]
    pair = jnp.stack([col_sums[0], col_sums[2]]).reshape(2, 1, cols)
    mine = (jnp.arange(members) == group)[None, :, None]
    pair = jnp.where(mine, pair, 0.0).reshape(2, width)
    vec_grads = jnp.concatenate([pair, gvec[0:6]], axis=0).reshape(8, devices, own)
    vec_grads = jnp.transpose(vec_grads, (1, 0, 2)).reshape(devices, 8 * own)
    vec_grads = jnp.concatenate([vec_grads, gbu[0].reshape(devices, -1)], axis=1)
    count = vec_grads.shape[1]

    if direct:
        lines = 8
        padded = jnp.pad(vec_grads, ((0, 0), (0, lines * LANES - count)))
        g_down, g_up, g_out, vec_grads, g_qkv, input_grad = scatter(
            g_down.reshape(2, 2, 2, -1, width),
            g_up.reshape(2, 2, 2, -1, g_up.shape[1]),
            g_out.reshape(2, 2, 2, -1, width),
            padded.reshape(2, 2, 2, 4 * lines, LANES),
            draw.reshape(members, PIECES, -1, draw.shape[1]),
            x.reshape(members, PIECES, -1, width),
            w_own,
            dres1.reshape(PIECES, -1, width),
            own,
        )
        vec_grads = vec_grads.reshape(-1)[:count]
        input_grad = input_grad.reshape(rows, width).astype(f32)
    else:

        def reduce(a):
            return lax.psum_scatter(a, ALL, scatter_dimension=0, tiled=True).astype(f32)

        g_down, g_up, g_out, vec_grads = reduce(g_down), reduce(g_up), reduce(g_out), reduce(vec_grads)[0]
        dx = dot_nt(draw, w_own).astype(bf16)
        dx = lax.psum_scatter(dx, GROUP, scatter_dimension=0, tiled=True)
        input_grad = move((dres1 + dx.astype(f32)).astype(bf16)).astype(f32)
        g_qkv = strip(dot_tn(x, draw)).reshape(-1, 2, 2, members // 2, own, 3 * cols)
        g_qkv = jnp.transpose(g_qkv, (0, 2, 1, 3, 4, 5)).reshape(-1, members, own, 3 * cols)
        g_qkv = g_qkv.reshape(-1, 3 * cols).astype(bf16)
        g_qkv = lax.psum_scatter(g_qkv, REST, scatter_dimension=0, tiled=True)
        g_qkv = g_qkv.reshape(members, own, 3 * cols)
        g_qkv = lax.all_to_all(g_qkv, GROUP, split_axis=0, concat_axis=0, tiled=True).astype(f32)
        g_qkv = jnp.transpose(g_qkv.reshape(members, own, 3, cols), (1, 2, 0, 3)).reshape(own, -1)
    v8 = vec_grads[: 8 * own].reshape(8, own)
    return (
        out[None],
        input_grad[None],
        g_qkv,
        v8[0:2],
        g_out,
        v8[2],
        v8[3],
        v8[4],
        g_up,
        vec_grads[8 * own :],
        g_down,
        v8[5],
        v8[6],
        v8[7],
    )


def solution(mesh):
    dp, sp = mesh.shape["dp"], mesh.shape["sp"]
    fine = Mesh(mesh.devices.reshape(dp // 2, 2, 2, sp // 2), ALL)
    dp, sp = ("c", "core"), ("zh", "zl")
    act = P(dp, sp, None)
    mat = P(ALL, None)
    pair = P(None, ALL)
    vec = P(ALL)
    rand = P(dp, sp, None, None)
    return jax.shard_map(
        per_device,
        mesh=fine,
        in_specs=(act, mat, pair, mat, vec, vec, vec, mat, vec, mat, vec, vec, vec, rand, act),
        out_specs=(act, act, mat, pair, mat, vec, vec, vec, mat, vec, mat, vec, vec, vec),
        check_vma=False,
    )
```

```python
from functools import partial

import jax
import jax.numpy as jnp
import numpy as np
from jax import lax
from jax.experimental import pallas as pl
from jax.experimental.pallas import tpu as pltpu
from jax.sharding import Mesh
from jax.sharding import PartitionSpec as P

HEAD_DIM = 64
BLOCK = 64
LANES = 128
SLOT = 4 * HEAD_DIM
EPS = 1e-05
MASKED = -1e30
ALL = ("c", "core", "zh", "zl")
GROUP = ("core", "zl")
REST = ("c", "zh")
CHUNK = 512
ROWS = 256
PAIR = 2
SUBS = 1
PAIR_BACK = 2
VMEM_BYTES = 60 * 1024 * 1024

f32 = jnp.float32
bf16 = jnp.bfloat16
NT = (((1,), (1,)), ((), ()))
TN = (((0,), (0,)), ((), ()))


def dot(a, b):
    return jnp.dot(a, b, preferred_element_type=f32)


def dot_nt(a, b):
    return lax.dot_general(a, b, NT, preferred_element_type=f32)


def dot_tn(a, b):
    return lax.dot_general(a, b, TN, preferred_element_type=f32)


def rows_at(start, size):
    return pl.ds(pl.multiple_of(start, size), size)


def listed(ref, rand_ref, head, i, blocks, randoms):
    cols = slice(head * SLOT + LANES, head * SLOT + SLOT)
    near = jnp.clip(i - 1, 0, blocks - 3)
    parts = [ref[0, :, cols], ref[blocks - 1, :, cols]]
    parts += [ref[near + n, :, cols] for n in range(3)]
    base = (head * (blocks - 2) + near) * randoms
    parts += [ref[rand_ref[base + r], :, cols] for r in range(randoms)]
    return jnp.concatenate(parts, axis=0)


def keys_values(ref, head, t, size):
    cols = slice(head * SLOT + LANES, head * SLOT + SLOT)
    return ref[pl.ds(t * (size // BLOCK), size // BLOCK), :, cols].reshape(size, LANES)


def mask_globals(s, i, blocks):
    lane = lax.broadcasted_iota(jnp.int32, (BLOCK, LANES), 1)
    low = lane < BLOCK
    dead = (low & (i == 1)) | (~low & (i == blocks - 2))
    return jnp.concatenate([jnp.where(dead, MASKED, s[:, :LANES]), s[:, LANES:]], axis=1)


def middle_blocks(qkv_ref, rand_ref, res_ref, first, heads, randoms, blocks):
    lane = lax.broadcasted_iota(jnp.int32, (BLOCK, LANES), 1)
    work = [(first + n, h) for n in range(PAIR) for h in range(heads)]
    kvs = [listed(qkv_ref, rand_ref, h, i, blocks, randoms) for i, h in work]
    qs = [qkv_ref[i, :, h * SLOT : h * SLOT + LANES] for i, h in work]
    ss = [mask_globals(dot_nt(q, kv), i, blocks) for q, kv, (i, h) in zip(qs, kvs, work)]
    tops = [jnp.max(s, axis=1, keepdims=True) for s in ss]
    es = [jnp.exp(s - top) for s, top in zip(ss, tops)]
    totals = [jnp.sum(e, axis=1, keepdims=True) for e in es]
    os = [dot(e.astype(bf16), kv) for e, kv in zip(es, kvs)]
    for o, top, total, (i, h) in zip(os, tops, totals, work):
        both = jnp.where(lane < HEAD_DIM, top + jnp.log(total), o / total)
        res_ref[h, rows_at(i * BLOCK, BLOCK), :] = both


def global_blocks(qkv_ref, heads, length):
    last = length // BLOCK - 1

    def ends(h):
        cols = slice(h * SLOT, h * SLOT + LANES)
        return jnp.concatenate([qkv_ref[0, :, cols], qkv_ref[last, :, cols]], axis=0)

    qs = [ends(h) for h in range(heads)]

    def whole(t, carry):
        kvs = [keys_values(qkv_ref, h, t, CHUNK) for h in range(heads)]
        ss = [dot_nt(q, kv) for q, kv in zip(qs, kvs)]
        news = [jnp.maximum(c[0], jnp.max(s, axis=1, keepdims=True)) for c, s in zip(carry, ss)]
        fades = [jnp.exp(c[0] - new) for c, new in zip(carry, news)]
        es = [jnp.exp(s - new) for s, new in zip(ss, news)]
        sums = [jnp.sum(e, axis=1, keepdims=True) for e in es]
        os = [dot(e.astype(bf16), kv) for e, kv in zip(es, kvs)]
        return tuple(
            (new, c[1] * fade + total, c[2] * fade + o)
            for c, new, fade, total, o in zip(carry, news, fades, sums, os)
        )

    start = (
        jnp.full((2 * BLOCK, 1), MASKED, f32),
        jnp.zeros((2 * BLOCK, 1), f32),
        jnp.zeros((2 * BLOCK, LANES), f32),
    )
    done = lax.fori_loop(0, length // CHUNK, whole, (start,) * heads)
    lane = lax.broadcasted_iota(jnp.int32, (2 * BLOCK, LANES), 1)
    return [jnp.where(lane < HEAD_DIM, top + jnp.log(total), acc / total) for top, total, acc in done]


def pack_rows(res_ref, ctx_ref, start, part, piece):
    low = lax.broadcasted_iota(jnp.int32, (BLOCK, LANES), 1) < HEAD_DIM
    for n in range(ROWS // BLOCK):
        rows = rows_at(start + n * BLOCK, BLOCK)
        first = pltpu.roll(res_ref[0, rows, :], HEAD_DIM, 1)
        pair = jnp.where(low, first, res_ref[1, rows, :])
        ctx_ref[part, piece, n * BLOCK : (n + 1) * BLOCK, :] = pair.astype(bf16)
    for n in range(ROWS // (2 * BLOCK)):
        rows = rows_at(start + 2 * n * BLOCK, BLOCK)
        odd = rows_at(start + (2 * n + 1) * BLOCK, BLOCK)
        first = pltpu.roll(res_ref[2, rows, :], HEAD_DIM, 1)
        both = jnp.where(low, first, res_ref[2, odd, :])
        ctx_ref[part, piece, ROWS + n * BLOCK : ROWS + (n + 1) * BLOCK, :] = both.astype(bf16)


def attend_kernel(heads, randoms, rand_ref, x_ref, w_ref, b_ref, qkv_ref, res_ref, ctx_ref):
    length = x_ref.shape[0]
    blocks = length // BLOCK

    def project(t, carry):
        raw = dot(x_ref[rows_at(t * CHUNK, CHUNK), :], w_ref[...]) + b_ref[...]
        step = CHUNK // BLOCK
        qkv_ref[pl.ds(t * step, step)] = raw.astype(bf16).reshape(step, BLOCK, raw.shape[1])
        return carry

    lax.fori_loop(0, length // CHUNK, project, 0)

    def middle(t, carry):
        middle_blocks(qkv_ref, rand_ref, res_ref, t * PAIR, heads, randoms, blocks)
        return carry

    lax.fori_loop(0, blocks // PAIR, middle, 0)
    for h, both in enumerate(global_blocks(qkv_ref, heads, length)):
        res_ref[h, 0:BLOCK, :] = both[:BLOCK]
        res_ref[h, length - BLOCK : length, :] = both[BLOCK:]
    per_quarter = ctx_ref.shape[1]

    def pack(t, carry):
        pack_rows(res_ref, ctx_ref, t * ROWS, t // per_quarter, t % per_quarter)
        return carry

    lax.fori_loop(0, length // ROWS, pack, 0)


def attend(rand, x, w, b, parts, heads):
    length = x.shape[0]
    randoms = rand.size // (heads * (length // BLOCK - 2))
    vmem = pl.BlockSpec(memory_space=pltpu.VMEM)
    return pl.pallas_call(
        partial(attend_kernel, heads, randoms),
        out_shape=(
            jax.ShapeDtypeStruct((length // BLOCK, BLOCK, heads * SLOT), bf16),
            jax.ShapeDtypeStruct((heads, length, LANES), f32),
            jax.ShapeDtypeStruct((parts, length // parts // ROWS, ROWS * 3 // 2, LANES), bf16),
        ),
        in_specs=[pl.BlockSpec(memory_space=pltpu.SMEM), vmem, vmem, vmem],
        out_specs=(vmem, vmem, vmem),
        compiler_params=pltpu.CompilerParams(vmem_limit_bytes=VMEM_BYTES),
        name="attend",
    )(rand, x, w, b)


def attend_back_kernel(
    heads, randoms, rand_ref, qkv_ref, res_ref, dctx_ref, draw_ref, sums_ref, *scratch
):
    dout, acc = scratch[:heads], scratch[heads:]
    blocks = qkv_ref.shape[0]
    length = blocks * BLOCK
    last = (blocks - 1) * BLOCK
    per_quarter = dctx_ref.shape[1]

    def unpack(t, carry):
        part, piece = t // per_quarter, t % per_quarter
        lane = lax.broadcasted_iota(jnp.int32, (BLOCK, LANES), 1)
        low = lane < HEAD_DIM
        for n in range(ROWS // BLOCK):
            rows = rows_at(t * ROWS + n * BLOCK, BLOCK)
            pair = dctx_ref[part, piece, n * BLOCK : (n + 1) * BLOCK, :].astype(f32)
            dout[0][rows, :] = jnp.where(low, 0.0, pltpu.roll(pair, HEAD_DIM, 1)).astype(bf16)
            dout[1][rows, :] = jnp.where(low, 0.0, pair).astype(bf16)
        for n in range(ROWS // (2 * BLOCK)):
            rows = rows_at(t * ROWS + 2 * n * BLOCK, BLOCK)
            odd = rows_at(t * ROWS + (2 * n + 1) * BLOCK, BLOCK)
            both = dctx_ref[part, piece, ROWS + n * BLOCK : ROWS + (n + 1) * BLOCK, :].astype(f32)
            dout[2][rows, :] = jnp.where(low, 0.0, pltpu.roll(both, HEAD_DIM, 1)).astype(bf16)
            dout[2][odd, :] = jnp.where(low, 0.0, both).astype(bf16)
        return carry

    lax.fori_loop(0, length // ROWS, unpack, 0)

    step = 256

    def ends(ref, cols):
        return jnp.concatenate([ref[0:BLOCK, cols], ref[last : last + BLOCK, cols]], axis=0)

    every = slice(0, LANES)
    gs = [ends(dout[h], every) for h in range(heads)]
    reses = [ends(res_ref.at[h], every) for h in range(heads)]
    alls = [
        jnp.concatenate(
            [qkv_ref[n, :, h * SLOT : h * SLOT + LANES] for n in (0, blocks - 1)] + [gs[h]], axis=0
        )
        for h in range(heads)
    ]
    logs = [res[:, 0:1] for res in reses]
    deltas = [jnp.sum(g.astype(f32) * res, axis=1, keepdims=True) for g, res in zip(gs, reses)]

    def whole(t, dqs):
        rows = rows_at(t * step, step)
        kvs = [keys_values(qkv_ref, h, t, step) for h in range(heads)]
        sds = [dot_nt(both, kv) for both, kv in zip(alls, kvs)]
        ps = [jnp.exp(sd[: 2 * BLOCK] - log) for sd, log in zip(sds, logs)]
        dss = [(p * (sd[2 * BLOCK :] - d)).astype(bf16) for p, sd, d in zip(ps, sds, deltas)]
        dkvs = [
            dot_tn(jnp.concatenate([ds, p.astype(bf16)], axis=0), both)
            for ds, p, both in zip(dss, ps, alls)
        ]
        news = tuple(dq + dot(ds, kv) for dq, ds, kv in zip(dqs, dss, kvs))
        for h in range(heads):
            acc[h][rows, :] = dkvs[h]
        return news

    dqs = lax.fori_loop(
        0, length // step, whole, (jnp.zeros((2 * BLOCK, LANES), f32),) * heads
    )
    for h in range(heads):
        cols = slice(h * SLOT, h * SLOT + LANES)
        lane = lax.broadcasted_iota(jnp.int32, (2 * BLOCK, LANES), 1)
        dq = jnp.where(lane < HEAD_DIM, dqs[h], 0.0).astype(bf16)
        draw_ref[0:BLOCK, cols] = dq[:BLOCK]
        draw_ref[last : last + BLOCK, cols] = dq[BLOCK:]

    def middle(t, carry):
        lane = lax.broadcasted_iota(jnp.int32, (BLOCK, LANES), 1)
        work = [(1 + t * PAIR_BACK + n, h) for n in range(PAIR_BACK) for h in range(heads)]
        kvs = [listed(qkv_ref, rand_ref, h, i, blocks, randoms) for i, h in work]
        places = [(rows_at(i * BLOCK, BLOCK), slice(h * SLOT, h * SLOT + LANES)) for i, h in work]
        gs = [dout[h][rows, :] for (rows, _), (_, h) in zip(places, work)]
        reses = [res_ref[h, rows, :] for (rows, _), (_, h) in zip(places, work)]
        alls = [
            jnp.concatenate([qkv_ref[i, :, cols], g], axis=0)
            for (_, cols), (i, _), g in zip(places, work, gs)
        ]
        sds = [dot_nt(both, kv) for both, kv in zip(alls, kvs)]
        deltas = [jnp.sum(g.astype(f32) * res, axis=1, keepdims=True) for g, res in zip(gs, reses)]
        ps = [
            jnp.exp(mask_globals(sd[:BLOCK], i, blocks) - res[:, 0:1])
            for sd, res, (i, h) in zip(sds, reses, work)
        ]
        dss = [(p * (sd[BLOCK:] - d)).astype(bf16) for p, sd, d in zip(ps, sds, deltas)]
        dkvs = [
            dot_tn(jnp.concatenate([ds, p.astype(bf16)], axis=0), both)
            for ds, p, both in zip(dss, ps, alls)
        ]
        dqs = [dot(ds, kv) for ds, kv in zip(dss, kvs)]
        for dq, (rows, cols) in zip(dqs, places):
            draw_ref[rows, cols] = jnp.where(lane < HEAD_DIM, dq, 0.0).astype(bf16)
        for dkv, (i, h) in zip(dkvs, work):
            acc[h][0:BLOCK, :] += dkv[0:BLOCK]
            acc[h][last : last + BLOCK, :] += dkv[BLOCK : 2 * BLOCK]
            near = pl.ds(pl.multiple_of((i - 1) * BLOCK, BLOCK), 3 * BLOCK)
            acc[h][near, :] += dkv[2 * BLOCK : 5 * BLOCK]
            base = (h * (blocks - 2) + i - 1) * randoms
            for r in range(randoms):
                far = rows_at(rand_ref[base + r] * BLOCK, BLOCK)
                acc[h][far, :] += dkv[(5 + r) * BLOCK : (6 + r) * BLOCK]
        return carry

    lax.fori_loop(0, (blocks - 2) // PAIR_BACK, middle, 0)
    sums_ref[...] = jnp.zeros_like(sums_ref)

    def finish(t, carry):
        rows = rows_at(t * CHUNK, CHUNK)
        for h in range(heads):
            at = h * SLOT
            draw_ref[rows, at + LANES : at + SLOT] = acc[h][rows, :].astype(bf16)
        sums_ref[0:1, :] += jnp.sum(draw_ref[rows, :].astype(f32), axis=0, keepdims=True)
        return carry

    lax.fori_loop(0, length // CHUNK, finish, 0)


def attend_back(rand, qkv, res, dctx, heads):
    length = qkv.shape[0] * BLOCK
    randoms = rand.size // (heads * (length // BLOCK - 2))
    vmem = pl.BlockSpec(memory_space=pltpu.VMEM)
    return pl.pallas_call(
        partial(attend_back_kernel, heads, randoms),
        out_shape=(
            jax.ShapeDtypeStruct((length, heads * SLOT), bf16),
            jax.ShapeDtypeStruct((8, heads * SLOT), f32),
        ),
        in_specs=[pl.BlockSpec(memory_space=pltpu.SMEM), vmem, vmem, vmem],
        out_specs=(vmem, vmem),
        scratch_shapes=[pltpu.VMEM((length, LANES), bf16)] * heads
        + [pltpu.VMEM((length, LANES), f32)] * heads,
        compiler_params=pltpu.CompilerParams(vmem_limit_bytes=VMEM_BYTES),
        name="attend_back",
    )(rand, qkv, res, dctx)


def mean_of(a):
    return jnp.mean(a, axis=1, keepdims=True)


def norm(r):
    center = r - mean_of(r)
    rstd = lax.rsqrt(mean_of(center * center) + EPS)
    return center * rstd, rstd


def norm_back(dn, n, rstd):
    return rstd * (dn - mean_of(dn) - n * mean_of(dn * n))


def rowsum(a):
    return jnp.sum(a, axis=0, keepdims=True)


MESH = pl.DeviceIdType.MESH


def run_phases(items):
    step = 0
    live = list(items)
    while live:
        after = []
        for first, phases in live:
            if first > step or next(phases, None) is not None:
                after.append((first, phases))
        live = after
        step += 1


class Where:
    def __init__(self):
        c, core, zh, zl = (lax.axis_index(a) for a in ALL)
        self.y, self.x, self.core, self.zh, self.zl = c // 2, c % 2, core, zh, zl
        self.z = zh * 2 + zl
        self.by_x = (self.y * 2 + 1 - self.x, core, zh, zl)
        self.by_y = ((1 - self.y) * 2 + self.x, core, zh, zl)
        self.by_core = (c, 1 - core, zh, zl)
        self.by_zl = (c, core, zh, 1 - zl)
        self.by_zh = (c, core, 1 - zh, zl)
        self.by_mid = (c, core, 1 - zh, 1 - zl)
        self.by_swap = (c, 1 - core, 1 - zh, zl)
        self.by_both = (c, 1 - core, zh, 1 - zl)
        self.inner = zh != zl
        self.stays = core == zh

    def greet(self):
        barrier = pltpu.get_barrier_semaphore()
        others = (self.by_x, self.by_y, self.by_core, self.by_zl)
        others += (self.by_zh, self.by_mid, self.by_swap, self.by_both)
        for other in others:
            pl.semaphore_signal(barrier, inc=1, device_id=other, device_id_type=MESH)
        pl.semaphore_wait(barrier, len(others))


class Copies:
    def __init__(self, send, recv, local):
        self.send, self.recv, self.local_sems = send, recv, local
        self.n = self.m = 0

    def remote(self, src, dst, device):
        n = self.n
        self.n += 1
        return pltpu.make_async_remote_copy(
            src_ref=src,
            dst_ref=dst,
            send_sem=self.send.at[n],
            recv_sem=self.recv.at[n],
            device_id=device,
            device_id_type=MESH,
        )

    def local(self, src, dst):
        m = self.m
        self.m += 1
        return pltpu.make_async_copy(src, dst, self.local_sems.at[m])


def chain_kernel(
    groups,
    direct,
    ctx_ref,
    tok_ref,
    og_ref,
    wo_ref,
    wu_ref,
    wd_ref,
    vec_ref,
    bu_ref,
    out_ref,
    dres_ref,
    dctx_ref,
    mix_ref,
    hid_ref,
    act_ref,
    dpre_ref,
    dffn_ref,
    dproj_ref,
    gvec_ref,
    gbu_ref,
    slope_ref,
    wop_ref,
    *stage,
):
    width = tok_ref.shape[1]
    hidden = wu_ref.shape[1]
    wide = 3 * HEAD_DIM
    step = pl.program_id(0)
    if direct:
        me = Where()
        out_far, dctx_far = out_ref, dctx_ref
        out_stage, dctx_stage, send, recv, local = stage
        out_ref, dctx_ref = out_stage.at[step], dctx_stage.at[step]

        @pl.when(step == 0)
        def _():
            me.greet()

    def transfers(t):
        place = me.core * 2 + me.zl
        near, beside = me.core * 2 + 1 - me.zl, (1 - me.core) * 2 + me.zl
        across = (1 - me.core) * 2 + 1 - me.zl
        others = ((near, me.by_zl), (beside, me.by_core), (across, me.by_both))
        remote = [
            pltpu.make_async_remote_copy(
                src_ref=dctx_stage.at[t, where],
                dst_ref=dctx_far.at[place, pl.ds(t * SUBS, SUBS)],
                send_sem=send.at[t, n],
                recv_sem=recv.at[t, n],
                device_id=other,
                device_id_type=MESH,
            )
            for n, (where, other) in enumerate(others)
        ]
        swap = pltpu.make_async_remote_copy(
            src_ref=out_stage.at[t],
            dst_ref=out_far.at[t],
            send_sem=send.at[t, 3],
            recv_sem=recv.at[t, 3],
            device_id=me.by_swap,
            device_id_type=MESH,
        )
        keep = pltpu.make_async_copy(out_stage.at[t], out_far.at[t], local.at[t, 0])
        own = pltpu.make_async_copy(
            dctx_stage.at[t, place], dctx_far.at[place, pl.ds(t * SUBS, SUBS)], local.at[t, 1]
        )
        return remote, own, swap, keep

    @pl.when(step == 0)
    def _():
        for g in range(groups):
            wop_ref[g * LANES : (g + 1) * LANES, :] = wo_ref[g * wide : g * wide + LANES, :]
            to = groups * LANES + g * HEAD_DIM
            wop_ref[to : to + HEAD_DIM, :] = wo_ref[g * wide + LANES : (g + 1) * wide, :]
        gvec_ref[...] = jnp.zeros_like(gvec_ref)
        gbu_ref[...] = jnp.zeros_like(gbu_ref)

    low = lax.broadcasted_iota(jnp.int32, (BLOCK, LANES), 1) < HEAD_DIM
    subs = range(tok_ref.shape[0] // ROWS)
    spans = [slice(n * ROWS, (n + 1) * ROWS) for n in subs]
    chunks = [slice(f, f + CHUNK) for f in range(0, hidden, CHUNK)]
    for n in subs:
        for g in range(groups):
            mix_ref[spans[n], g * LANES : (g + 1) * LANES] = ctx_ref[g, n, :ROWS, :]
        for g in range(0, groups, 2):
            to = groups * LANES + g * HEAD_DIM
            for m in range(ROWS // (2 * BLOCK)):
                at = ROWS + m * BLOCK
                a = ctx_ref[g, n, at : at + BLOCK, :].astype(f32)
                b = ctx_ref[g + 1, n, at : at + BLOCK, :].astype(f32)
                even = jnp.where(low, a, pltpu.roll(b, HEAD_DIM, 1))
                odd = jnp.where(low, pltpu.roll(a, HEAD_DIM, 1), b)
                r = n * ROWS + 2 * m * BLOCK
                mix_ref[r : r + BLOCK, to : to + LANES] = even.astype(bf16)
                mix_ref[r + BLOCK : r + 2 * BLOCK, to : to + LANES] = odd.astype(bf16)

    bo, g1, s1 = vec_ref[0:1, :], vec_ref[1:2, :], vec_ref[2:3, :]
    bd, g2, s2 = vec_ref[3:4, :], vec_ref[4:5, :], vec_ref[5:6, :]
    projs = [dot(mix_ref[rows, :], wop_ref[...]) for rows in spans]
    norms = [norm(tok_ref[rows, :].astype(f32) + proj + bo) for rows, proj in zip(spans, projs)]
    hids = [n1 * g1 + s1 for n1, _ in norms]
    lows = [hid.astype(bf16) for hid in hids]
    for rows, hid_low in zip(spans, lows):
        hid_ref[rows, :] = hid_low
    scale = np.sqrt(2.0 / np.pi).astype(np.float32)
    work = [(n, cols) for cols in chunks for n in subs]

    def behind(start, end):
        held = start(*work[0])
        for k, item in enumerate(work):
            now = held
            if k + 1 < len(work):
                held = start(*work[k + 1])
            end(*item, now)

    def up_start(n, cols):
        return dot(lows[n], wu_ref[:, cols])

    def up_end(n, cols, raw):
        u = raw + bu_ref[:, cols]
        square = u * u
        t = jnp.tanh(u * (scale + (scale * 0.044715) * square))
        half = 0.5 + 0.5 * t
        act_ref[spans[n], cols] = (u * half).astype(bf16)
        slope = half + (0.5 * u) * (1.0 - t * t) * (scale + (3 * 0.044715 * scale) * square)
        slope_ref[spans[n], cols] = slope.astype(bf16)

    behind(up_start, up_end)
    ffns = [dot(act_ref[rows, :], wd_ref[...]) for rows in spans]
    dres2s, dffns = [], []
    for n, rows in enumerate(spans):
        n2, rstd2 = norm(hids[n] + ffns[n] + bd)
        out_ref[rows, :] = (n2 * g2 + s2).astype(bf16)
        og = og_ref[rows, :].astype(f32)
        gvec_ref[4:5, :] += rowsum(og * n2)
        gvec_ref[5:6, :] += rowsum(og)
        dres2 = norm_back(og * g2, n2, rstd2)
        dffn = dres2.astype(bf16)
        dffn_ref[rows, :] = dffn
        gvec_ref[3:4, :] += rowsum(dffn.astype(f32))
        dres2s.append(dres2)
        dffns.append(dffn)

    if direct:
        remote, own, swap, keep = transfers(step)

        @pl.when(me.stays)
        def _():
            keep.start()

        @pl.when(jnp.logical_not(me.stays))
        def _():
            swap.start()

    def down_start(n, cols):
        return dot_nt(dffns[n], wd_ref[cols, :])

    def down_end(n, cols, dact):
        dpre = (dact * slope_ref[spans[n], cols].astype(f32)).astype(bf16)
        dpre_ref[spans[n], cols] = dpre
        gbu_ref[0:1, cols] += rowsum(dpre.astype(f32))

    behind(down_start, down_end)
    dhs = [dres2 + dot_nt(dpre_ref[rows, :], wu_ref[...]) for rows, dres2 in zip(spans, dres2s)]
    dmixes = []
    for rows, dh, (n1, rstd1) in zip(spans, dhs, norms):
        gvec_ref[1:2, :] += rowsum(dh * n1)
        gvec_ref[2:3, :] += rowsum(dh)
        dres1 = norm_back(dh * g1, n1, rstd1)
        dres_ref[rows, :] = dres1
        dproj = dres1.astype(bf16)
        dproj_ref[rows, :] = dproj
        gvec_ref[0:1, :] += rowsum(dproj.astype(f32))
        dmixes.append(dot_nt(dproj, wop_ref[...]))
    for n, dmix in enumerate(dmixes):
        for g in range(groups):
            dctx_ref[g, n, :ROWS, :] = dmix[:, g * LANES : (g + 1) * LANES].astype(bf16)
        for g in range(0, groups, 2):
            to = groups * LANES + g * HEAD_DIM
            for m in range(ROWS // (2 * BLOCK)):
                at = ROWS + m * BLOCK
                r = 2 * m * BLOCK
                even = dmix[r : r + BLOCK, to : to + LANES]
                odd = dmix[r + BLOCK : r + 2 * BLOCK, to : to + LANES]
                a = jnp.where(low, even, pltpu.roll(odd, HEAD_DIM, 1))
                b = jnp.where(low, pltpu.roll(even, HEAD_DIM, 1), odd)
                dctx_ref[g, n, at : at + BLOCK, :] = a.astype(bf16)
                dctx_ref[g + 1, n, at : at + BLOCK, :] = b.astype(bf16)

    if direct:
        for copy in remote:
            copy.start()
        own.start()

        @pl.when(step == pl.num_programs(0) - 1)
        def _():
            for t in range(dctx_stage.shape[0]):
                remote, own, swap, keep = transfers(t)
                for copy in remote:
                    copy.wait()
                own.wait()

                @pl.when(me.stays)
                def _():
                    keep.wait()

                @pl.when(jnp.logical_not(me.stays))
                def _():
                    swap.wait()


def chain(ctx, tok, og, wo, wu, wd, vec, bu, direct):
    rows, width = tok.shape
    hidden = wu.shape[1]
    groups = ctx.shape[0]
    once = pl.Buffered(1)

    def tiled(cols):
        return pl.BlockSpec((SUBS * ROWS, cols), lambda t: (t, 0))

    def fixed(shape):
        return pl.BlockSpec(shape, lambda t: (0, 0), pipeline_mode=once)

    packed = pl.BlockSpec((groups, SUBS) + ctx.shape[2:], lambda t: (0, t, 0, 0))
    shape = jax.ShapeDtypeStruct
    steps = rows // (SUBS * ROWS)
    hbm = pl.BlockSpec(memory_space=pltpu.HBM)
    scratch = [pltpu.VMEM((SUBS * ROWS, hidden), bf16), pltpu.VMEM(wo.shape, bf16)]
    params = pltpu.CompilerParams(vmem_limit_bytes=VMEM_BYTES)
    out_shape = (rows, width)
    if direct:
        out_shape = (steps, SUBS * ROWS, width)
        scratch += [
            pltpu.VMEM(out_shape, bf16),
            pltpu.VMEM((steps, groups, SUBS) + ctx.shape[2:], bf16),
            pltpu.SemaphoreType.DMA((steps, 4)),
            pltpu.SemaphoreType.DMA((steps, 4)),
            pltpu.SemaphoreType.DMA((steps, 2)),
        ]
        params = pltpu.CompilerParams(
            vmem_limit_bytes=VMEM_BYTES, collective_id=2, has_side_effects=True
        )
    return pl.pallas_call(
        partial(chain_kernel, groups, direct),
        grid=(steps,),
        out_shape=(
            shape(out_shape, bf16),
            shape((rows, width), f32),
            shape(ctx.shape, bf16),
            shape((rows, width), bf16),
            shape((rows, width), bf16),
            shape((rows, hidden), bf16),
            shape((rows, hidden), bf16),
            shape((rows, width), bf16),
            shape((rows, width), bf16),
            shape((8, width), f32),
            shape((8, hidden), f32),
        ),
        in_specs=[
            packed,
            tiled(width),
            tiled(width),
            fixed(wo.shape),
            fixed(wu.shape),
            fixed(wd.shape),
            fixed(vec.shape),
            fixed(bu.shape),
        ],
        out_specs=(
            hbm if direct else tiled(width),
            tiled(width),
            hbm if direct else packed,
            tiled(width),
            tiled(width),
            tiled(hidden),
            tiled(hidden),
            tiled(width),
            tiled(width),
            pl.BlockSpec((8, width), lambda t: (0, 0)),
            pl.BlockSpec((8, hidden), lambda t: (0, 0)),
        ),
        scratch_shapes=scratch,
        compiler_params=params,
        name="chain",
    )(ctx, tok, og, wo, wu, wd, vec, bu)


def gather_item(me, copies, shard, full, cols, x_first):
    y, x, core, zh, zl = me.y, me.x, me.core, me.zh, me.zl
    mine = shard.at[:, cols]
    own = copies.local(mine, full.at[y, x, core, me.z, :, cols])
    spot = full.at[y, x, core, me.z, :, cols]
    along = [copies.remote(mine, spot, other) for other in (me.by_zl, me.by_mid, me.by_zh)]
    own.start()
    for copy in along:
        copy.start()
    yield 1
    own.wait()
    for copy in along:
        copy.wait()
    line = full.at[y, x, core, :, :, cols]
    near = copies.remote(line, line, me.by_x if x_first else me.by_y)
    near.start()
    across = [copies.remote(line, line, me.by_core)]
    across[0].start()
    yield 1
    near.wait()
    if x_first:
        block = full.at[y, :, core, :, :, cols]
        got = full.at[y, 1 - x, core, :, :, cols]
        rest = full.at[1 - y, :, core, :, :, cols]
    else:
        block = full.at[:, x, core, :, :, cols]
        got = full.at[1 - y, x, core, :, :, cols]
        rest = full.at[:, 1 - x, core, :, :, cols]
    far = copies.remote(block, block, me.by_y if x_first else me.by_x)
    far.start()
    across.append(copies.remote(got, got, me.by_core))
    across[1].start()
    yield 1
    far.wait()
    across.append(copies.remote(rest, rest, me.by_core))
    across[2].start()
    yield 1
    for copy in across:
        copy.wait()


def tokens_item(me, copies, tok, x_all, piece):
    place = me.core * 2 + me.zl
    there = (1 - me.core) * 2 + me.zl
    held = x_all.at[place, piece]
    out = copies.remote(tok.at[piece], x_all.at[there, piece], me.by_swap)
    keep = copies.local(tok.at[piece], held)
    along = copies.remote(held, held, me.by_zl)
    over = copies.remote(held, held, me.by_core)

    @pl.when(me.stays)
    def _():
        keep.start()

    @pl.when(jnp.logical_not(me.stays))
    def _():
        out.start()

    yield 1

    @pl.when(me.stays)
    def _():
        keep.wait()
        along.start()
        over.start()

    yield 1

    @pl.when(jnp.logical_not(me.stays))
    def _():
        out.wait()
        along.start()
        over.start()

    yield 1
    along.wait()
    came = x_all.at[me.core * 2 + 1 - me.zl, piece]
    onto = copies.remote(came, came, me.by_core)
    onto.start()
    yield 1
    over.wait()
    onto.wait()


def exchange_item(me, copies, src, dst):
    out = copies.remote(src, dst, me.by_swap)
    keep = copies.local(src, dst)

    @pl.when(me.stays)
    def _():
        keep.start()

    @pl.when(jnp.logical_not(me.stays))
    def _():
        out.start()

    yield 1

    @pl.when(me.stays)
    def _():
        keep.wait()

    @pl.when(jnp.logical_not(me.stays))
    def _():
        out.wait()


PIECES = 4


def weight_item(me, copies, src, parts, whole, bias):
    y, x, core, zh, zl = me.y, me.x, me.core, me.zh, me.zl
    place = core * 2 + zl
    keep = copies.local(src.at[place], parts.at[place])
    moves = [
        copies.remote(src.at[core * 2 + 1 - zl], parts.at[place], me.by_zl),
        copies.remote(src.at[(1 - core) * 2 + zl], parts.at[place], me.by_core),
        copies.remote(src.at[(1 - core) * 2 + 1 - zl], parts.at[place], me.by_both),
    ]
    keep.start()
    for move in moves:
        move.start()
    yield 1
    keep.wait()
    for move in moves:
        move.wait()
    own = whole.shape[4] // 2
    for b in range(2):
        both = jnp.concatenate([parts[2 * b, :own, :], parts[2 * b + 1, :own, :]], axis=0)
        whole[y, x, b, zh] = both.astype(bf16)
    tail = pl.ds(own, 8)
    bias[y, x, zh] = parts[0, tail, :] + parts[1, tail, :] + parts[2, tail, :] + parts[3, tail, :]
    for spot, bias_spot, other in (
        (whole.at[y, x, :, zh], bias.at[y, x, zh], me.by_zh),
        (whole.at[y, x], bias.at[y, x], me.by_x),
        (whole.at[y], bias.at[y], me.by_y),
    ):
        moves = [copies.remote(spot, spot, other), copies.remote(bias_spot, bias_spot, other)]
        for move in moves:
            move.start()
        yield 1
        for move in moves:
            move.wait()


def finish(*generators):
    for phases in generators:
        for _ in phases:
            pass


def front_kernel(heads, randoms, *refs):
    rand_ref, tok, og, wq, w_out, up, down, small = refs[:8]
    x_hbm, tok_own, og_own, w_own, qkv_hbm, res_hbm, ctx_all, out_all, up_all, down_all, small_all = refs[8:19]
    x_all, parts, whole, bias, qkv_ref, res_ref, ends_ref, ctx_ref = refs[19:27]
    me = Where()
    me.greet()
    copies = Copies(*refs[27:])
    blocks = qkv_ref.shape[0]
    length = blocks * BLOCK
    quarter = length // 4
    core, zl = me.core, me.zl
    place = core * 2 + zl
    near = core * 2 + 1 - zl
    beside = (1 - core) * 2 + zl
    across = (1 - core) * 2 + 1 - zl

    weights = weight_item(me, copies, wq, parts, whole, bias)
    tokens = [tokens_item(me, copies, tok, x_all, piece) for piece in range(PIECES)]
    smalls = gather_item(me, copies, small, small_all, slice(0, LANES), True)
    turn = 0

    def gathers(*arrays):
        nonlocal turn
        made = []
        for shard, full, splits in arrays:
            width = shard.shape[1] // splits
            for n in range(splits):
                cols = slice(n * width, (n + 1) * width)
                made.append(gather_item(me, copies, shard, full, cols, turn % 2 == 0))
                turn += 1
        return made

    def advance(group):
        group[:] = [phases for phases in group if next(phases, None) is not None]

    early = gathers((up, up_all, 2))
    late = gathers((down, down_all, 2), (w_out, out_all, 2))
    last = [exchange_item(me, copies, og.at[n], og_own.at[n]) for n in range(PIECES)]
    idle = [smalls]
    outs = []

    def write(src, dst):
        copy = copies.local(src, dst)
        copy.start()
        outs.append(copy)

    def project(where):
        bias_row = jnp.sum(bias[...].reshape(-1, 8, bias.shape[-1]), axis=0)[0:1]
        matrix = whole[...].reshape(-1, whole.shape[-1])
        for piece in range(PIECES):
            raw = dot(x_all[where, piece], matrix) + bias_row
            step = ROWS // BLOCK
            at = (where * PIECES + piece) * step
            qkv_ref[pl.ds(at, step)] = raw.astype(bf16).reshape(step, BLOCK, raw.shape[1])

    def forward_tokens():
        for item in tokens:
            next(item)

    next(weights)
    advance(early)
    next(weights)
    forward_tokens()
    forward_tokens()
    next(weights)
    advance(idle)
    advance(early)
    next(weights)
    advance(idle)
    forward_tokens()
    advance(late)
    finish(weights)
    advance(early)
    next(last[0])
    project(place)
    write(whole, w_own)
    write(x_all.at[place], tok_own)
    forward_tokens()
    advance(late)
    next(last[1])
    project(near)
    finish(*tokens)
    next(last[2])
    next(last[3])
    advance(early)
    project(beside)
    project(across)
    advance(idle)
    write(x_all, x_hbm)
    write(qkv_ref, qkv_hbm)
    for h, both in enumerate(global_blocks(qkv_ref, heads, length)):
        ends_ref[h] = both
    advance(late)
    advance(early)
    advance(idle)

    def middle(t, carry):
        middle_blocks(qkv_ref, rand_ref, res_ref, t * PAIR, heads, randoms, blocks)
        return carry

    sends = []
    turns = quarter // BLOCK // PAIR
    for where, other in ((across, me.by_both), (near, me.by_zl), (beside, me.by_core), (place, None)):
        lax.fori_loop(where * turns, (where + 1) * turns, middle, 0)

        @pl.when(where == 0)
        def _():
            for h in range(heads):
                res_ref[h, 0:BLOCK, :] = ends_ref[h, 0:BLOCK, :]

        @pl.when(where == 3)
        def _():
            for h in range(heads):
                res_ref[h, length - BLOCK : length, :] = ends_ref[h, BLOCK : 2 * BLOCK, :]

        for piece in range(PIECES):
            pack_rows(res_ref, ctx_ref, where * quarter + piece * ROWS, where, piece)
        rows = rows_at(where * quarter, quarter)
        write(res_ref.at[:, rows], res_hbm.at[:, rows])
        if other is None:
            write(ctx_ref.at[where], ctx_all.at[place])
        else:
            send = copies.remote(ctx_ref.at[where], ctx_all.at[place], other)
            send.start()
            sends.append(send)
        advance(late if where is near or where is place else idle)
    finish(*early, *late, *last, *idle)
    for copy in sends + outs:
        copy.wait()


def front(rand, tok, og, wq, mats, small, heads):
    rows, width = tok.shape
    members = 4
    length = rows * members
    randoms = rand.size // (heads * (length // BLOCK - 2))
    hbm = pl.BlockSpec(memory_space=pltpu.HBM)
    shape = jax.ShapeDtypeStruct
    tok = tok.reshape(PIECES, rows // PIECES, width)
    og = og.reshape(tok.shape)
    cols = heads * SLOT
    own = mats[0].shape[0]
    packed = (members, rows // ROWS, ROWS * 3 // 2, LANES)
    outs = [
        shape((members,) + tok.shape, bf16),
        shape(tok.shape, bf16),
        shape(og.shape, bf16),
        shape((2, 2, 2, 2, 2 * own, cols), bf16),
        shape((length // BLOCK, BLOCK, cols), bf16),
        shape((heads, length, LANES), f32),
        shape(packed, bf16),
    ]
    outs += [shape((2, 2, 2, 4) + a.shape, bf16) for a in (*mats, small)]
    return pl.pallas_call(
        partial(front_kernel, heads, randoms),
        out_shape=tuple(outs),
        in_specs=[pl.BlockSpec(memory_space=pltpu.SMEM)] + [hbm] * 7,
        out_specs=(hbm,) * 11,
        scratch_shapes=[
            pltpu.VMEM((members,) + tok.shape, bf16),
            pltpu.VMEM(wq.shape, f32),
            pltpu.VMEM((2, 2, 2, 2, 2 * own, cols), bf16),
            pltpu.VMEM((2, 2, 2, 8, cols), f32),
            pltpu.VMEM((length // BLOCK, BLOCK, cols), bf16),
            pltpu.VMEM((heads, length, LANES), f32),
            pltpu.VMEM((heads, 2 * BLOCK, LANES), f32),
            pltpu.VMEM(packed, bf16),
            pltpu.SemaphoreType.DMA((112,)),
            pltpu.SemaphoreType.DMA((112,)),
            pltpu.SemaphoreType.DMA((32,)),
        ],
        compiler_params=pltpu.CompilerParams(
            collective_id=0, has_side_effects=True, vmem_limit_bytes=VMEM_BYTES
        ),
        name="front",
    )(rand, tok, og, wq, *mats, small)


def add_rows(dst, a, b, rows):
    step = next(n for n in (48, 32, 24, 16, 8) if rows % n == 0)

    def body(t, carry):
        at = rows_at(t * step, step)
        dst[at, :] = (a[at, :].astype(f32) + b[at, :].astype(f32)).astype(dst.dtype)
        return carry

    lax.fori_loop(0, rows // step, body, 0)


def scatter_item(me, copies, src, cols, acc, from_core, from_first, from_second, slabs, from_line, out, x_first):
    y, x, core, zh, zl = me.y, me.x, me.core, me.zh, me.zl
    rows = acc.shape[2]
    own = None
    if cols is not None:
        own = copies.local(src.at[:, :, core, :, cols], acc)
        own.start()
        src = src.at[:, :, 1 - core, :, cols]
    over = copies.remote(src, from_core, me.by_core)
    over.start()
    yield 1
    if own is not None:
        own.wait()
    over.wait()
    for a in range(2):
        for b in range(2):
            add_rows(acc.at[a, b], acc.at[a, b], from_core.at[a, b], rows)
    if x_first:
        first = copies.remote(acc.at[:, 1 - x], from_first, me.by_x)
    else:
        first = copies.remote(acc.at[1 - y], from_first, me.by_y)
    first.start()
    yield 1
    first.wait()
    for a in range(2):
        block = acc.at[a, x] if x_first else acc.at[y, a]
        add_rows(block, block, from_first.at[a], rows)
    if x_first:
        second = copies.remote(acc.at[1 - y, x], from_second, me.by_y)
    else:
        second = copies.remote(acc.at[y, 1 - x], from_second, me.by_x)
    second.start()
    yield 1
    second.wait()
    rest = rows // 4
    summed = acc[y, x].astype(f32) + from_second[...].astype(f32)
    for z in range(4):
        slabs[z] = summed[z * rest : (z + 1) * rest].astype(slabs.dtype)
    moves = [
        copies.remote(slabs.at[(1 - zh) * 2 + zl], from_line.at[0], me.by_zh),
        copies.remote(slabs.at[(1 - zh) * 2 + 1 - zl], from_line.at[1], me.by_mid),
        copies.remote(slabs.at[zh * 2 + 1 - zl], from_line.at[2], me.by_zl),
    ]
    for move in moves:
        move.start()
    yield 1
    for move in moves:
        move.wait()
    near = slabs[me.z].astype(f32) + from_line[2].astype(f32)
    out[...] = near + (from_line[0].astype(f32) + from_line[1].astype(f32))


def scatter_buffers(rows, cols, kind):
    return [
        pltpu.VMEM((2, 2, rows, cols), kind),
        pltpu.VMEM((2, 2, rows, cols), kind),
        pltpu.VMEM((2, rows, cols), kind),
        pltpu.VMEM((rows, cols), kind),
        pltpu.VMEM((4, rows // 4, cols), kind),
        pltpu.VMEM((3, rows // 4, cols), kind),
    ]


def own_columns_item(me, copies, acc, from_x, from_y, from_zh, part, blocks, out):
    y, x, core, zh, zl = me.y, me.x, me.core, me.zh, me.zl
    rows = acc.shape[4]
    first = copies.remote(acc.at[1 - x], from_x, me.by_x)
    first.start()
    yield 1
    first.wait()
    for a in range(2):
        for b in range(2):
            for c in range(2):
                add_rows(acc.at[x, a, b, c], acc.at[x, a, b, c], from_x.at[a, b, c], rows)
    acc = acc.at[x]
    second = copies.remote(acc.at[1 - y], from_y, me.by_y)
    second.start()
    yield 1
    second.wait()
    for b in range(2):
        for c in range(2):
            block = acc.at[y, b, c]
            add_rows(block, block, from_y.at[b, c], rows)
    third = copies.remote(acc.at[y, :, 1 - zh], from_zh, me.by_zh)
    third.start()
    yield 1
    third.wait()
    half = rows // 2
    for b in range(2):
        add_rows(part.at[b], acc.at[y, b, zh], from_zh.at[b], rows)
    place = core * 2 + zl
    mine = rows_at(zl * half, half)
    other = rows_at((1 - zl) * half, half)
    keep = copies.local(part.at[core, mine], blocks.at[place])
    keep.start()
    moves = [
        copies.remote(part.at[core, other], blocks.at[place], me.by_zl),
        copies.remote(part.at[1 - core, mine], blocks.at[place], me.by_core),
        copies.remote(part.at[1 - core, other], blocks.at[place], me.by_both),
    ]
    for move in moves:
        move.start()
    yield 1
    keep.wait()
    for move in moves:
        move.wait()
    heads = blocks.shape[2] // SLOT
    low = lax.broadcasted_iota(jnp.int32, (blocks.shape[1], LANES), 1) < HEAD_DIM
    for kind in range(3):
        for n in range(0, 4 * heads, 2):
            pair = []
            for head in (n, n + 1):
                at = head % heads * SLOT + (0 if kind == 0 else LANES)
                pair.append(blocks[head // heads, :, at : at + LANES])
            if kind == 2:
                tile = jnp.where(low, pltpu.roll(pair[0], HEAD_DIM, 1), pair[1])
            else:
                tile = jnp.where(low, pair[0], pltpu.roll(pair[1], HEAD_DIM, 1))
            if kind == 0:
                tile = tile * HEAD_DIM**-0.5
            to = (kind * 4 * heads + n) * HEAD_DIM
            out[:, to : to + LANES] = tile


def input_grad_item(me, copies, draw, w, dres, piece, stage, from_core, from_zl, res, out):
    core, zl = me.core, me.zl
    more = copies.local(dres.at[piece], res)
    more.start()
    for b in range(2):
        stage[b] = dot_nt(draw[(1 - core) * 2 + b, piece], w[...]).astype(bf16)
    over = copies.remote(stage, from_core, me.by_core)
    over.start()
    yield 1
    mine = dot_nt(draw[core * 2 + 1 - zl, piece], w[...])
    over.wait()
    far, send = stage.at[0], stage.at[1]
    far[...] = (mine + from_core[1 - zl].astype(f32)).astype(bf16)
    along = copies.remote(far, from_zl, me.by_zl)
    along.start()
    mine = dot_nt(draw[core * 2 + zl, piece], w[...])
    more.wait()
    res[...] = res[...] + (mine + from_core[zl].astype(f32))
    yield 1
    along.wait()
    send[...] = (res[...] + from_zl[...].astype(f32)).astype(bf16)
    yield from exchange_item(me, copies, send, out.at[piece])


def scatter_kernel(*refs):
    act, dffn, hid, dpre, proj, vecs, draw, x_hbm, w, dres = refs[:10]
    outs = refs[10:16]
    sems, scratch = refs[16:19], list(refs[19:])
    me = Where()
    me.greet()
    copies = Copies(*sems)

    def take(n):
        got = scratch[:n]
        del scratch[:n]
        return got

    def advance(group):
        group[:] = [phases for phases in group if next(phases, None) is not None]

    pieces = [
        input_grad_item(me, copies, draw, w, dres, piece, *take(4), outs[5]) for piece in range(PIECES)
    ]
    x_all, total, acc, *buffers = take(8)
    columns = [own_columns_item(me, copies, acc, *buffers, outs[4])]
    halves, quarters, stage_down, stage_up = take(4)
    first, second = [], []
    for n in range(2):
        cols = outs[0].shape[1] // 2
        part = outs[0].at[:, n * cols : (n + 1) * cols]
        first.append(
            scatter_item(me, copies, stage_down.at[n], None, halves.at[n], *take(5), part, n % 2 == 0)
        )
    for n in range(4):
        cols = outs[1].shape[1] // 4
        part = outs[1].at[:, n * cols : (n + 1) * cols]
        second.append(
            scatter_item(me, copies, stage_up.at[n], None, quarters.at[n], *take(5), part, n % 2 == 0)
        )
    for src, out, group in ((proj, outs[2], first), (vecs, outs[3], second)):
        whole = slice(0, src.shape[4])
        group.append(scatter_item(me, copies, src, whole, *take(6), out, True))

    def fetch(src):
        wide = x_all.shape[3]
        got = [copies.local(src.at[:, :, c * wide : (c + 1) * wide], x_all.at[c]) for c in range(4)]
        for copy in got:
            copy.start()
        return got

    def flat(value):
        return value.reshape(-1, value.shape[-1])

    def down_grad(c, carry):
        g = dot_tn(flat(x_all[c]), flat(dffn[...])).astype(bf16)
        rows, cols = g.shape[0] // 2, g.shape[1] // 2
        for n in range(2):
            low, high = g[:rows, n * cols : (n + 1) * cols], g[rows:, n * cols : (n + 1) * cols]
            halves[n, c // 2, c % 2] = jnp.where(me.core == 0, low, high)
            stage_down[n, c // 2, c % 2] = jnp.where(me.core == 0, high, low)
        return carry

    def up_grad(c, carry):
        g = dot_tn(flat(hid[...]), flat(x_all[c])).astype(bf16)
        rows = g.shape[0] // 8
        for k in range(4):
            low, high = g[2 * k * rows : (2 * k + 1) * rows], g[(2 * k + 1) * rows : (2 * k + 2) * rows]
            quarters[c, k // 2, k % 2] = jnp.where(me.core == 0, low, high)
            stage_up[c, k // 2, k % 2] = jnp.where(me.core == 0, high, low)
        return carry

    def weight_grad(t, carry):
        place, piece = t // PIECES, t % PIECES
        total[...] += dot_tn(x_all[place, piece], draw[place, piece])
        return carry

    got = fetch(act)
    next(pieces[0])
    next(pieces[1])
    next(pieces[0])
    next(pieces[1])
    for copy in got:
        copy.wait()
    lax.fori_loop(0, 4, down_grad, 0)
    got = fetch(dpre)
    advance(first)
    next(pieces[2])
    next(pieces[3])
    next(pieces[2])
    next(pieces[3])
    for copy in got:
        copy.wait()
    advance(first)
    lax.fori_loop(0, 4, up_grad, 0)
    got = copies.local(x_hbm, x_all)
    got.start()
    advance(second)
    next(pieces[0])
    total[...] = jnp.zeros_like(total)
    got.wait()
    advance(second)
    next(pieces[1])
    lax.fori_loop(0, 2 * PIECES, weight_grad, 0)
    next(pieces[2])
    advance(first)
    lax.fori_loop(2 * PIECES, 4 * PIECES, weight_grad, 0)
    laid = total[...].reshape((2, 2) + acc.shape[2:])
    for a in range(2):
        for b in range(2):
            acc[b, a] = laid[a, b].astype(bf16)
    advance(columns)
    next(pieces[3])
    advance(first)
    advance(second)
    while pieces or columns or first or second:
        advance(columns)
        advance(second)
        advance(first)
        if not second:
            advance(pieces)


def scatter(act, dffn, hid, dpre, proj, vecs, draw, x_all, w, dres, own):
    hbm = pl.BlockSpec(memory_space=pltpu.HBM)
    vmem = pl.BlockSpec(memory_space=pltpu.VMEM)
    shape = jax.ShapeDtypeStruct
    hidden = act.shape[-1]
    outs = [shape((hidden // 32, w.shape[0]), f32), shape((own, hidden), f32)]
    outs += [shape((a.shape[3] // 4, a.shape[4]), f32) for a in (proj, vecs)]
    width, cols = w.shape
    rows = 2 * own
    outs.append(shape((own, 3 * cols), f32))
    outs.append(shape(dres.shape, bf16))
    buffers = []
    for _ in range(PIECES):
        tile = dres.shape[1:]
        buffers += [
            pltpu.VMEM((2,) + tile, bf16),
            pltpu.VMEM((2,) + tile, bf16),
            pltpu.VMEM(tile, bf16),
            pltpu.VMEM(tile, f32),
        ]
    buffers += [
        pltpu.VMEM(x_all.shape, bf16),
        pltpu.VMEM((width, cols), f32),
        pltpu.VMEM((2, 2, 2, 2, rows, cols), bf16),
        pltpu.VMEM((2, 2, 2, rows, cols), bf16),
        pltpu.VMEM((2, 2, rows, cols), bf16),
        pltpu.VMEM((2, rows, cols), bf16),
        pltpu.VMEM((2, rows, cols), f32),
        pltpu.VMEM((4, own, cols), f32),
    ]
    down = (hidden // 8, width // 2)
    up = (4 * own, hidden // 4)
    buffers += [
        pltpu.VMEM((2, 2, 2) + down, bf16),
        pltpu.VMEM((4, 2, 2) + up, bf16),
        pltpu.VMEM((2, 2, 2) + down, bf16),
        pltpu.VMEM((4, 2, 2) + up, bf16),
    ]
    for tile in [down] * 2 + [up] * 4:
        buffers += scatter_buffers(*tile, bf16)[1:]
    for a in (proj, vecs):
        buffers += scatter_buffers(*a.shape[3:], a.dtype)
    return pl.pallas_call(
        scatter_kernel,
        out_shape=tuple(outs),
        in_specs=[hbm, vmem, vmem, hbm, hbm, hbm, vmem, hbm, vmem, hbm],
        out_specs=(vmem,) * 5 + (hbm,),
        scratch_shapes=[
            pltpu.SemaphoreType.DMA((80,)),
            pltpu.SemaphoreType.DMA((80,)),
            pltpu.SemaphoreType.DMA((32,)),
        ]
        + buffers,
        compiler_params=pltpu.CompilerParams(
            collective_id=1, has_side_effects=True, vmem_limit_bytes=VMEM_BYTES
        ),
        name="scatter",
    )(act, dffn, hid, dpre, proj, vecs, draw, x_all, w, dres)


def per_device(
    tokens,
    qkv_weight,
    query_value_bias,
    out_weight,
    out_bias,
    norm1_gain,
    norm1_bias,
    up_weight,
    up_bias,
    down_weight,
    down_bias,
    norm2_gain,
    norm2_bias,
    rand_blocks,
    out_grad,
):
    members = lax.axis_size(GROUP)
    devices = lax.axis_size(ALL)
    swap = [(0, 0), (1, 2), (2, 1), (3, 3)]

    def move(a):
        return lax.ppermute(a, ("core", "zh"), swap)

    rand = move(rand_blocks[0])
    heads = rand.shape[0]
    rows, width = tokens.shape[1:]
    cols = heads * HEAD_DIM
    group = lax.axis_index(GROUP)
    own = width // devices
    rand_flat = rand.reshape(-1)

    def lay_out(a):
        a = a.reshape(a.shape[:-2] + (3, heads, HEAD_DIM))
        q, k, v = a[..., 0, :, :], a[..., 1, :, :], a[..., 2, :, :]
        q = q * jnp.asarray(HEAD_DIM**-0.5, a.dtype)
        laid = jnp.stack([q, jnp.zeros_like(q), k, v], axis=-2)
        return laid.reshape(laid.shape[:-3] + (heads * SLOT,))

    bias_part = jnp.stack([query_value_bias[0], jnp.zeros((own,), bf16), query_value_bias[1]])
    small = [out_bias, norm1_gain, norm1_bias, down_bias, norm2_gain, norm2_bias, up_bias]
    small = jnp.concatenate(small)
    direct = lax.axis_size("c") == 4 and members == 4 and own % 8 == 0
    if direct:
        count = small.shape[0]
        padded = jnp.pad(small, (0, 16 * LANES - count)).reshape(16, LANES)
        spread = lax.dynamic_update_slice(
            jnp.zeros((3, width), f32), bias_part.astype(f32), (0, lax.axis_index(ALL) * own)
        )
        spread = lay_out(jnp.transpose(spread.reshape(3, members, cols), (1, 0, 2)))
        wq = jnp.transpose(qkv_weight.astype(f32).reshape(own, 3, members, cols), (2, 0, 1, 3))
        wq = jnp.concatenate([lay_out(wq), spread[:, None], jnp.zeros((members, 7, heads * SLOT), f32)], axis=1)
        mats = (out_weight, up_weight, down_weight)
        x, tok, og, w_own, qkv, res, ctx, *full = front(
            rand_flat, tokens[0], out_grad[0], wq, mats, padded, heads
        )
        x, tok, og = (a.reshape(-1, width) for a in (x, tok, og))
        w_own = w_own.reshape(width, -1)
        w_out, w_up, w_down = (a.reshape(-1, a.shape[-1]) for a in full[:3])
        small = full[3].reshape(devices, -1)[:, :count].astype(f32)
    else:
        tok = move(tokens[0])
        og = move(out_grad[0])
        x = lax.all_gather(tok, GROUP, axis=0, tiled=True)
        mats = (qkv_weight, out_weight, up_weight, down_weight)
        w_qkv, w_out, w_up, w_down = (lax.all_gather(a, ALL, axis=0, tiled=True) for a in mats)
        small = lax.all_gather(small, ALL, axis=0).astype(f32)
        w_own = lax.dynamic_slice_in_dim(
            w_qkv.reshape(width, 3, members, cols), group, 1, axis=2
        ).reshape(width, 3, cols)
        w_own = lay_out(w_own)
        bias3 = lax.all_gather(bias_part, ALL, axis=1, tiled=True).astype(f32).reshape(3, members, cols)
        b_own = lay_out(lax.dynamic_slice_in_dim(bias3, group, 1, axis=1).reshape(1, 3, cols))
        qkv, res, ctx_send = attend(rand_flat, x, w_own, b_own, members, heads)
        ctx = lax.all_to_all(ctx_send, GROUP, split_axis=0, concat_axis=0, tiled=True)
    vecs = jnp.transpose(small[:, : 6 * own].reshape(devices, 6, own), (1, 0, 2)).reshape(6, width)
    bias_up = small[:, 6 * own :].reshape(1, -1)
    chain_vecs = jnp.concatenate([vecs, jnp.zeros((2, width), f32)], axis=0)
    out, dres1, dctx, mix, hid, act, dpre, dffn, dproj, gvec, gbu = chain(
        ctx, tok, og, w_out, w_up, w_down, chain_vecs, bias_up, direct
    )
    if direct:
        out = out.reshape(rows, width)
    else:
        dctx = lax.all_to_all(dctx, GROUP, split_axis=0, concat_axis=0, tiled=True)
        out = move(out)

    g_mix = dot_tn(mix, dproj).astype(bf16)
    pairs = g_mix[: members * LANES].reshape(members, LANES, width)
    thirds = g_mix[members * LANES :].reshape(members, HEAD_DIM, width)
    g_out = jnp.concatenate([pairs, thirds], axis=1).reshape(width, width)

    draw, sums = attend_back(rand_flat, qkv, res, dctx, heads)

    def strip(a):
        a = a.reshape(a.shape[:-1] + (heads, 4, HEAD_DIM))
        q, k, v = a[..., 0, :] * (HEAD_DIM**-0.5), a[..., 2, :], a[..., 3, :]
        return jnp.stack([q, k, v], axis=-3).reshape(a.shape[:-3] + (3, cols))

    col_sums = strip(sums[0:1])[0]
    pair = jnp.stack([col_sums[0], col_sums[2]]).reshape(2, 1, cols)
    mine = (jnp.arange(members) == group)[None, :, None]
    pair = jnp.where(mine, pair, 0.0).reshape(2, width)
    vec_grads = jnp.concatenate([pair, gvec[0:6]], axis=0).reshape(8, devices, own)
    vec_grads = jnp.transpose(vec_grads, (1, 0, 2)).reshape(devices, 8 * own)
    vec_grads = jnp.concatenate([vec_grads, gbu[0].reshape(devices, -1)], axis=1)
    count = vec_grads.shape[1]

    if direct:
        lines = 8
        padded = jnp.pad(vec_grads, ((0, 0), (0, lines * LANES - count)))
        g_down, g_up, g_out, vec_grads, g_qkv, input_grad = scatter(
            act.reshape(PIECES, -1, act.shape[1]),
            dffn.reshape(PIECES, -1, width),
            hid.reshape(PIECES, -1, width),
            dpre.reshape(PIECES, -1, dpre.shape[1]),
            g_out.reshape(2, 2, 2, -1, width),
            padded.reshape(2, 2, 2, 4 * lines, LANES),
            draw.reshape(members, PIECES, -1, draw.shape[1]),
            x.reshape(members, PIECES, -1, width),
            w_own,
            dres1.reshape(PIECES, -1, width),
            own,
        )
        vec_grads = vec_grads.reshape(-1)[:count]
        input_grad = input_grad.reshape(rows, width).astype(f32)
    else:

        def reduce(a):
            return lax.psum_scatter(a, ALL, scatter_dimension=0, tiled=True).astype(f32)

        g_down, g_up = reduce(dot_tn(act, dffn).astype(bf16)), reduce(dot_tn(hid, dpre).astype(bf16))
        g_out, vec_grads = reduce(g_out), reduce(vec_grads)[0]
        dx = dot_nt(draw, w_own).astype(bf16)
        dx = lax.psum_scatter(dx, GROUP, scatter_dimension=0, tiled=True)
        input_grad = move((dres1 + dx.astype(f32)).astype(bf16)).astype(f32)
        g_qkv = strip(dot_tn(x, draw)).reshape(-1, 2, 2, members // 2, own, 3 * cols)
        g_qkv = jnp.transpose(g_qkv, (0, 2, 1, 3, 4, 5)).reshape(-1, members, own, 3 * cols)
        g_qkv = g_qkv.reshape(-1, 3 * cols).astype(bf16)
        g_qkv = lax.psum_scatter(g_qkv, REST, scatter_dimension=0, tiled=True)
        g_qkv = g_qkv.reshape(members, own, 3 * cols)
        g_qkv = lax.all_to_all(g_qkv, GROUP, split_axis=0, concat_axis=0, tiled=True).astype(f32)
        g_qkv = jnp.transpose(g_qkv.reshape(members, own, 3, cols), (1, 2, 0, 3)).reshape(own, -1)
    v8 = vec_grads[: 8 * own].reshape(8, own)
    return (
        out[None],
        input_grad[None],
        g_qkv,
        v8[0:2],
        g_out,
        v8[2],
        v8[3],
        v8[4],
        g_up,
        vec_grads[8 * own :],
        g_down,
        v8[5],
        v8[6],
        v8[7],
    )


def solution(mesh):
    dp, sp = mesh.shape["dp"], mesh.shape["sp"]
    fine = Mesh(mesh.devices.reshape(dp // 2, 2, 2, sp // 2), ALL)
    dp, sp = ("c", "core"), ("zh", "zl")
    act = P(dp, sp, None)
    mat = P(ALL, None)
    pair = P(None, ALL)
    vec = P(ALL)
    rand = P(dp, sp, None, None)
    return jax.shard_map(
        per_device,
        mesh=fine,
        in_specs=(act, mat, pair, mat, vec, vec, vec, mat, vec, mat, vec, vec, vec, rand, act),
        out_specs=(act, act, mat, pair, mat, vec, vec, vec, mat, vec, mat, vec, vec, vec),
        check_vma=False,
    )
```

```python
from functools import partial

import jax
import jax.numpy as jnp
import numpy as np
from jax import lax
from jax.experimental import pallas as pl
from jax.experimental.pallas import tpu as pltpu
from jax.sharding import Mesh
from jax.sharding import PartitionSpec as P

HEAD_DIM = 64
BLOCK = 64
LANES = 128
SLOT = 4 * HEAD_DIM
EPS = 1e-05
MASKED = -1e30
ALL = ("c", "core", "zh", "zl")
GROUP = ("core", "zl")
REST = ("c", "zh")
CHUNK = 512
ROWS = 256
PAIR = 2
SUBS = 1
PAIR_BACK = 2
VMEM_BYTES = 60 * 1024 * 1024

f32 = jnp.float32
bf16 = jnp.bfloat16
NT = (((1,), (1,)), ((), ()))
TN = (((0,), (0,)), ((), ()))


def dot(a, b):
    return jnp.dot(a, b, preferred_element_type=f32)


def dot_nt(a, b):
    return lax.dot_general(a, b, NT, preferred_element_type=f32)


def dot_tn(a, b):
    return lax.dot_general(a, b, TN, preferred_element_type=f32)


def rows_at(start, size):
    return pl.ds(pl.multiple_of(start, size), size)


def listed(ref, rand_ref, head, i, blocks, randoms):
    cols = slice(head * SLOT + LANES, head * SLOT + SLOT)
    near = jnp.clip(i - 1, 0, blocks - 3)
    parts = [ref[0, :, cols], ref[blocks - 1, :, cols]]
    parts += [ref[near + n, :, cols] for n in range(3)]
    base = (head * (blocks - 2) + near) * randoms
    parts += [ref[rand_ref[base + r], :, cols] for r in range(randoms)]
    return jnp.concatenate(parts, axis=0)


def keys_values(ref, head, t, size):
    cols = slice(head * SLOT + LANES, head * SLOT + SLOT)
    return ref[pl.ds(t * (size // BLOCK), size // BLOCK), :, cols].reshape(size, LANES)


def mask_globals(s, i, blocks):
    lane = lax.broadcasted_iota(jnp.int32, (BLOCK, LANES), 1)
    low = lane < BLOCK
    dead = (low & (i == 1)) | (~low & (i == blocks - 2))
    return jnp.concatenate([jnp.where(dead, MASKED, s[:, :LANES]), s[:, LANES:]], axis=1)


def middle_blocks(qkv_ref, rand_ref, res_ref, first, heads, randoms, blocks):
    lane = lax.broadcasted_iota(jnp.int32, (BLOCK, LANES), 1)
    work = [(first + n, h) for n in range(PAIR) for h in range(heads)]
    kvs = [listed(qkv_ref, rand_ref, h, i, blocks, randoms) for i, h in work]
    qs = [qkv_ref[i, :, h * SLOT : h * SLOT + LANES] for i, h in work]
    ss = [mask_globals(dot_nt(q, kv), i, blocks) for q, kv, (i, h) in zip(qs, kvs, work)]
    tops = [jnp.max(s, axis=1, keepdims=True) for s in ss]
    es = [jnp.exp(s - top) for s, top in zip(ss, tops)]
    totals = [jnp.sum(e, axis=1, keepdims=True) for e in es]
    os = [dot(e.astype(bf16), kv) for e, kv in zip(es, kvs)]
    for o, top, total, (i, h) in zip(os, tops, totals, work):
        both = jnp.where(lane < HEAD_DIM, top + jnp.log(total), o / total)
        res_ref[h, rows_at(i * BLOCK, BLOCK), :] = both


def global_blocks(qkv_ref, heads, length):
    last = length // BLOCK - 1

    def ends(h):
        cols = slice(h * SLOT, h * SLOT + LANES)
        return jnp.concatenate([qkv_ref[0, :, cols], qkv_ref[last, :, cols]], axis=0)

    qs = [ends(h) for h in range(heads)]

    def whole(t, carry):
        kvs = [keys_values(qkv_ref, h, t, CHUNK) for h in range(heads)]
        ss = [dot_nt(q, kv) for q, kv in zip(qs, kvs)]
        news = [jnp.maximum(c[0], jnp.max(s, axis=1, keepdims=True)) for c, s in zip(carry, ss)]
        fades = [jnp.exp(c[0] - new) for c, new in zip(carry, news)]
        es = [jnp.exp(s - new) for s, new in zip(ss, news)]
        sums = [jnp.sum(e, axis=1, keepdims=True) for e in es]
        os = [dot(e.astype(bf16), kv) for e, kv in zip(es, kvs)]
        return tuple(
            (new, c[1] * fade + total, c[2] * fade + o)
            for c, new, fade, total, o in zip(carry, news, fades, sums, os)
        )

    start = (
        jnp.full((2 * BLOCK, 1), MASKED, f32),
        jnp.zeros((2 * BLOCK, 1), f32),
        jnp.zeros((2 * BLOCK, LANES), f32),
    )
    done = lax.fori_loop(0, length // CHUNK, whole, (start,) * heads)
    lane = lax.broadcasted_iota(jnp.int32, (2 * BLOCK, LANES), 1)
    return [jnp.where(lane < HEAD_DIM, top + jnp.log(total), acc / total) for top, total, acc in done]


def pack_rows(res_ref, ctx_ref, start, part, piece):
    low = lax.broadcasted_iota(jnp.int32, (BLOCK, LANES), 1) < HEAD_DIM
    for n in range(ROWS // BLOCK):
        rows = rows_at(start + n * BLOCK, BLOCK)
        first = pltpu.roll(res_ref[0, rows, :], HEAD_DIM, 1)
        pair = jnp.where(low, first, res_ref[1, rows, :])
        ctx_ref[part, piece, n * BLOCK : (n + 1) * BLOCK, :] = pair.astype(bf16)
    for n in range(ROWS // (2 * BLOCK)):
        rows = rows_at(start + 2 * n * BLOCK, BLOCK)
        odd = rows_at(start + (2 * n + 1) * BLOCK, BLOCK)
        first = pltpu.roll(res_ref[2, rows, :], HEAD_DIM, 1)
        both = jnp.where(low, first, res_ref[2, odd, :])
        ctx_ref[part, piece, ROWS + n * BLOCK : ROWS + (n + 1) * BLOCK, :] = both.astype(bf16)


def attend_kernel(heads, randoms, rand_ref, x_ref, w_ref, b_ref, qkv_ref, res_ref, ctx_ref):
    length = x_ref.shape[0]
    blocks = length // BLOCK

    def project(t, carry):
        raw = dot(x_ref[rows_at(t * CHUNK, CHUNK), :], w_ref[...]) + b_ref[...]
        step = CHUNK // BLOCK
        qkv_ref[pl.ds(t * step, step)] = raw.astype(bf16).reshape(step, BLOCK, raw.shape[1])
        return carry

    lax.fori_loop(0, length // CHUNK, project, 0)

    def middle(t, carry):
        middle_blocks(qkv_ref, rand_ref, res_ref, t * PAIR, heads, randoms, blocks)
        return carry

    lax.fori_loop(0, blocks // PAIR, middle, 0)
    for h, both in enumerate(global_blocks(qkv_ref, heads, length)):
        res_ref[h, 0:BLOCK, :] = both[:BLOCK]
        res_ref[h, length - BLOCK : length, :] = both[BLOCK:]
    per_quarter = ctx_ref.shape[1]

    def pack(t, carry):
        pack_rows(res_ref, ctx_ref, t * ROWS, t // per_quarter, t % per_quarter)
        return carry

    lax.fori_loop(0, length // ROWS, pack, 0)


def attend(rand, x, w, b, parts, heads):
    length = x.shape[0]
    randoms = rand.size // (heads * (length // BLOCK - 2))
    vmem = pl.BlockSpec(memory_space=pltpu.VMEM)
    return pl.pallas_call(
        partial(attend_kernel, heads, randoms),
        out_shape=(
            jax.ShapeDtypeStruct((length // BLOCK, BLOCK, heads * SLOT), bf16),
            jax.ShapeDtypeStruct((heads, length, LANES), f32),
            jax.ShapeDtypeStruct((parts, length // parts // ROWS, ROWS * 3 // 2, LANES), bf16),
        ),
        in_specs=[pl.BlockSpec(memory_space=pltpu.SMEM), vmem, vmem, vmem],
        out_specs=(vmem, vmem, vmem),
        compiler_params=pltpu.CompilerParams(vmem_limit_bytes=VMEM_BYTES),
        name="attend",
    )(rand, x, w, b)


def attend_back_kernel(
    heads, randoms, rand_ref, qkv_ref, res_ref, dctx_ref, draw_ref, sums_ref, *scratch
):
    dout, acc = scratch[:heads], scratch[heads:]
    blocks = qkv_ref.shape[0]
    length = blocks * BLOCK
    last = (blocks - 1) * BLOCK
    per_quarter = dctx_ref.shape[1]

    def unpack(t, carry):
        part, piece = t // per_quarter, t % per_quarter
        lane = lax.broadcasted_iota(jnp.int32, (BLOCK, LANES), 1)
        low = lane < HEAD_DIM
        for n in range(ROWS // BLOCK):
            rows = rows_at(t * ROWS + n * BLOCK, BLOCK)
            pair = dctx_ref[part, piece, n * BLOCK : (n + 1) * BLOCK, :].astype(f32)
            dout[0][rows, :] = jnp.where(low, 0.0, pltpu.roll(pair, HEAD_DIM, 1)).astype(bf16)
            dout[1][rows, :] = jnp.where(low, 0.0, pair).astype(bf16)
        for n in range(ROWS // (2 * BLOCK)):
            rows = rows_at(t * ROWS + 2 * n * BLOCK, BLOCK)
            odd = rows_at(t * ROWS + (2 * n + 1) * BLOCK, BLOCK)
            both = dctx_ref[part, piece, ROWS + n * BLOCK : ROWS + (n + 1) * BLOCK, :].astype(f32)
            dout[2][rows, :] = jnp.where(low, 0.0, pltpu.roll(both, HEAD_DIM, 1)).astype(bf16)
            dout[2][odd, :] = jnp.where(low, 0.0, both).astype(bf16)
        return carry

    lax.fori_loop(0, length // ROWS, unpack, 0)

    step = 512

    def ends(ref, cols):
        return jnp.concatenate([ref[0:BLOCK, cols], ref[last : last + BLOCK, cols]], axis=0)

    every = slice(0, LANES)
    gs = [ends(dout[h], every) for h in range(heads)]
    reses = [ends(res_ref.at[h], every) for h in range(heads)]
    alls = [
        jnp.concatenate(
            [qkv_ref[n, :, h * SLOT : h * SLOT + LANES] for n in (0, blocks - 1)] + [gs[h]], axis=0
        )
        for h in range(heads)
    ]
    logs = [res[:, 0:1] for res in reses]
    deltas = [jnp.sum(g.astype(f32) * res, axis=1, keepdims=True) for g, res in zip(gs, reses)]

    def whole(t, dqs):
        rows = rows_at(t * step, step)
        kvs = [keys_values(qkv_ref, h, t, step) for h in range(heads)]
        sds = [dot_nt(both, kv) for both, kv in zip(alls, kvs)]
        ps = [jnp.exp(sd[: 2 * BLOCK] - log) for sd, log in zip(sds, logs)]
        dss = [(p * (sd[2 * BLOCK :] - d)).astype(bf16) for p, sd, d in zip(ps, sds, deltas)]
        dkvs = [
            dot_tn(jnp.concatenate([ds, p.astype(bf16)], axis=0), both)
            for ds, p, both in zip(dss, ps, alls)
        ]
        news = tuple(dq + dot(ds, kv) for dq, ds, kv in zip(dqs, dss, kvs))
        for h in range(heads):
            acc[h][rows, :] = dkvs[h]
        return news

    dqs = lax.fori_loop(
        0, length // step, whole, (jnp.zeros((2 * BLOCK, LANES), f32),) * heads
    )
    for h in range(heads):
        cols = slice(h * SLOT, h * SLOT + LANES)
        lane = lax.broadcasted_iota(jnp.int32, (2 * BLOCK, LANES), 1)
        dq = jnp.where(lane < HEAD_DIM, dqs[h], 0.0).astype(bf16)
        draw_ref[0:BLOCK, cols] = dq[:BLOCK]
        draw_ref[last : last + BLOCK, cols] = dq[BLOCK:]

    def middle(t, carry):
        lane = lax.broadcasted_iota(jnp.int32, (BLOCK, LANES), 1)
        work = [(1 + t * PAIR_BACK + n, h) for n in range(PAIR_BACK) for h in range(heads)]
        kvs = [listed(qkv_ref, rand_ref, h, i, blocks, randoms) for i, h in work]
        places = [(rows_at(i * BLOCK, BLOCK), slice(h * SLOT, h * SLOT + LANES)) for i, h in work]
        gs = [dout[h][rows, :] for (rows, _), (_, h) in zip(places, work)]
        reses = [res_ref[h, rows, :] for (rows, _), (_, h) in zip(places, work)]
        alls = [
            jnp.concatenate([qkv_ref[i, :, cols], g], axis=0)
            for (_, cols), (i, _), g in zip(places, work, gs)
        ]
        sds = [dot_nt(both, kv) for both, kv in zip(alls, kvs)]
        deltas = [jnp.sum(g.astype(f32) * res, axis=1, keepdims=True) for g, res in zip(gs, reses)]
        ps = [
            jnp.exp(mask_globals(sd[:BLOCK], i, blocks) - res[:, 0:1])
            for sd, res, (i, h) in zip(sds, reses, work)
        ]
        dss = [(p * (sd[BLOCK:] - d)).astype(bf16) for p, sd, d in zip(ps, sds, deltas)]
        dkvs = [
            dot_tn(jnp.concatenate([ds, p.astype(bf16)], axis=0), both)
            for ds, p, both in zip(dss, ps, alls)
        ]
        dqs = [dot(ds, kv) for ds, kv in zip(dss, kvs)]
        for dq, (rows, cols) in zip(dqs, places):
            draw_ref[rows, cols] = jnp.where(lane < HEAD_DIM, dq, 0.0).astype(bf16)
        for dkv, (i, h) in zip(dkvs, work):
            acc[h][0:BLOCK, :] += dkv[0:BLOCK]
            acc[h][last : last + BLOCK, :] += dkv[BLOCK : 2 * BLOCK]
            near = pl.ds(pl.multiple_of((i - 1) * BLOCK, BLOCK), 3 * BLOCK)
            acc[h][near, :] += dkv[2 * BLOCK : 5 * BLOCK]
            base = (h * (blocks - 2) + i - 1) * randoms
            for r in range(randoms):
                far = rows_at(rand_ref[base + r] * BLOCK, BLOCK)
                acc[h][far, :] += dkv[(5 + r) * BLOCK : (6 + r) * BLOCK]
        return carry

    lax.fori_loop(0, (blocks - 2) // PAIR_BACK, middle, 0)
    sums_ref[...] = jnp.zeros_like(sums_ref)

    def finish(t, carry):
        rows = rows_at(t * CHUNK, CHUNK)
        for h in range(heads):
            at = h * SLOT
            draw_ref[rows, at + LANES : at + SLOT] = acc[h][rows, :].astype(bf16)
        sums_ref[0:1, :] += jnp.sum(draw_ref[rows, :].astype(f32), axis=0, keepdims=True)
        return carry

    lax.fori_loop(0, length // CHUNK, finish, 0)


def attend_back(rand, qkv, res, dctx, heads):
    length = qkv.shape[0] * BLOCK
    randoms = rand.size // (heads * (length // BLOCK - 2))
    vmem = pl.BlockSpec(memory_space=pltpu.VMEM)
    return pl.pallas_call(
        partial(attend_back_kernel, heads, randoms),
        out_shape=(
            jax.ShapeDtypeStruct((length, heads * SLOT), bf16),
            jax.ShapeDtypeStruct((8, heads * SLOT), f32),
        ),
        in_specs=[pl.BlockSpec(memory_space=pltpu.SMEM), vmem, vmem, vmem],
        out_specs=(vmem, vmem),
        scratch_shapes=[pltpu.VMEM((length, LANES), bf16)] * heads
        + [pltpu.VMEM((length, LANES), f32)] * heads,
        compiler_params=pltpu.CompilerParams(vmem_limit_bytes=VMEM_BYTES),
        name="attend_back",
    )(rand, qkv, res, dctx)


def mean_of(a):
    return jnp.mean(a, axis=1, keepdims=True)


def norm(r):
    center = r - mean_of(r)
    rstd = lax.rsqrt(mean_of(center * center) + EPS)
    return center * rstd, rstd


def norm_back(dn, n, rstd):
    return rstd * (dn - mean_of(dn) - n * mean_of(dn * n))


def rowsum(a):
    return jnp.sum(a, axis=0, keepdims=True)


MESH = pl.DeviceIdType.MESH


def run_phases(items):
    step = 0
    live = list(items)
    while live:
        after = []
        for first, phases in live:
            if first > step or next(phases, None) is not None:
                after.append((first, phases))
        live = after
        step += 1


class Where:
    def __init__(self):
        c, core, zh, zl = (lax.axis_index(a) for a in ALL)
        self.y, self.x, self.core, self.zh, self.zl = c // 2, c % 2, core, zh, zl
        self.z = zh * 2 + zl
        self.by_x = (self.y * 2 + 1 - self.x, core, zh, zl)
        self.by_y = ((1 - self.y) * 2 + self.x, core, zh, zl)
        self.by_core = (c, 1 - core, zh, zl)
        self.by_zl = (c, core, zh, 1 - zl)
        self.by_zh = (c, core, 1 - zh, zl)
        self.by_mid = (c, core, 1 - zh, 1 - zl)
        self.by_swap = (c, 1 - core, 1 - zh, zl)
        self.by_both = (c, 1 - core, zh, 1 - zl)
        self.inner = zh != zl
        self.stays = core == zh

    def greet(self):
        barrier = pltpu.get_barrier_semaphore()
        others = (self.by_x, self.by_y, self.by_core, self.by_zl)
        others += (self.by_zh, self.by_mid, self.by_swap, self.by_both)
        for other in others:
            pl.semaphore_signal(barrier, inc=1, device_id=other, device_id_type=MESH)
        pl.semaphore_wait(barrier, len(others))


class Copies:
    def __init__(self, send, recv, local):
        self.send, self.recv, self.local_sems = send, recv, local
        self.n = self.m = 0

    def remote(self, src, dst, device):
        n = self.n
        self.n += 1
        return pltpu.make_async_remote_copy(
            src_ref=src,
            dst_ref=dst,
            send_sem=self.send.at[n],
            recv_sem=self.recv.at[n],
            device_id=device,
            device_id_type=MESH,
        )

    def local(self, src, dst):
        m = self.m
        self.m += 1
        return pltpu.make_async_copy(src, dst, self.local_sems.at[m])


def chain_kernel(
    groups,
    direct,
    ctx_ref,
    tok_ref,
    og_ref,
    wo_ref,
    wu_ref,
    wd_ref,
    vec_ref,
    bu_ref,
    out_ref,
    dres_ref,
    dctx_ref,
    mix_ref,
    hid_ref,
    act_ref,
    dpre_ref,
    dffn_ref,
    dproj_ref,
    gvec_ref,
    gbu_ref,
    slope_ref,
    wop_ref,
    *stage,
):
    width = tok_ref.shape[1]
    hidden = wu_ref.shape[1]
    wide = 3 * HEAD_DIM
    step = pl.program_id(0)
    if direct:
        me = Where()
        out_far, dctx_far = out_ref, dctx_ref
        out_stage, dctx_stage, send, recv, local = stage
        out_ref, dctx_ref = out_stage.at[step], dctx_stage.at[step]

        @pl.when(step == 0)
        def _():
            me.greet()

    def transfers(t):
        place = me.core * 2 + me.zl
        near, beside = me.core * 2 + 1 - me.zl, (1 - me.core) * 2 + me.zl
        across = (1 - me.core) * 2 + 1 - me.zl
        others = ((near, me.by_zl), (beside, me.by_core), (across, me.by_both))
        remote = [
            pltpu.make_async_remote_copy(
                src_ref=dctx_stage.at[t, where],
                dst_ref=dctx_far.at[place, pl.ds(t * SUBS, SUBS)],
                send_sem=send.at[t, n],
                recv_sem=recv.at[t, n],
                device_id=other,
                device_id_type=MESH,
            )
            for n, (where, other) in enumerate(others)
        ]
        swap = pltpu.make_async_remote_copy(
            src_ref=out_stage.at[t],
            dst_ref=out_far.at[t],
            send_sem=send.at[t, 3],
            recv_sem=recv.at[t, 3],
            device_id=me.by_swap,
            device_id_type=MESH,
        )
        keep = pltpu.make_async_copy(out_stage.at[t], out_far.at[t], local.at[t, 0])
        own = pltpu.make_async_copy(
            dctx_stage.at[t, place], dctx_far.at[place, pl.ds(t * SUBS, SUBS)], local.at[t, 1]
        )
        return remote, own, swap, keep

    @pl.when(step == 0)
    def _():
        for g in range(groups):
            wop_ref[g * LANES : (g + 1) * LANES, :] = wo_ref[g * wide : g * wide + LANES, :]
            to = groups * LANES + g * HEAD_DIM
            wop_ref[to : to + HEAD_DIM, :] = wo_ref[g * wide + LANES : (g + 1) * wide, :]
        gvec_ref[...] = jnp.zeros_like(gvec_ref)
        gbu_ref[...] = jnp.zeros_like(gbu_ref)

    low = lax.broadcasted_iota(jnp.int32, (BLOCK, LANES), 1) < HEAD_DIM
    subs = range(tok_ref.shape[0] // ROWS)
    spans = [slice(n * ROWS, (n + 1) * ROWS) for n in subs]
    chunks = [slice(f, f + CHUNK) for f in range(0, hidden, CHUNK)]
    for n in subs:
        for g in range(groups):
            mix_ref[spans[n], g * LANES : (g + 1) * LANES] = ctx_ref[g, n, :ROWS, :]
        for g in range(0, groups, 2):
            to = groups * LANES + g * HEAD_DIM
            for m in range(ROWS // (2 * BLOCK)):
                at = ROWS + m * BLOCK
                a = ctx_ref[g, n, at : at + BLOCK, :].astype(f32)
                b = ctx_ref[g + 1, n, at : at + BLOCK, :].astype(f32)
                even = jnp.where(low, a, pltpu.roll(b, HEAD_DIM, 1))
                odd = jnp.where(low, pltpu.roll(a, HEAD_DIM, 1), b)
                r = n * ROWS + 2 * m * BLOCK
                mix_ref[r : r + BLOCK, to : to + LANES] = even.astype(bf16)
                mix_ref[r + BLOCK : r + 2 * BLOCK, to : to + LANES] = odd.astype(bf16)

    bo, g1, s1 = vec_ref[0:1, :], vec_ref[1:2, :], vec_ref[2:3, :]
    bd, g2, s2 = vec_ref[3:4, :], vec_ref[4:5, :], vec_ref[5:6, :]
    projs = [dot(mix_ref[rows, :], wop_ref[...]) for rows in spans]
    norms = [norm(tok_ref[rows, :].astype(f32) + proj + bo) for rows, proj in zip(spans, projs)]
    hids = [n1 * g1 + s1 for n1, _ in norms]
    lows = [hid.astype(bf16) for hid in hids]
    for rows, hid_low in zip(spans, lows):
        hid_ref[rows, :] = hid_low
    scale = np.sqrt(2.0 / np.pi).astype(np.float32)
    work = [(n, cols) for cols in chunks for n in subs]

    def behind(start, end):
        held = start(*work[0])
        for k, item in enumerate(work):
            now = held
            if k + 1 < len(work):
                held = start(*work[k + 1])
            end(*item, now)

    def up_start(n, cols):
        return dot(lows[n], wu_ref[:, cols])

    def up_end(n, cols, raw):
        u = raw + bu_ref[:, cols]
        square = u * u
        t = jnp.tanh(u * (scale + (scale * 0.044715) * square))
        half = 0.5 + 0.5 * t
        act_ref[spans[n], cols] = (u * half).astype(bf16)
        slope = half + (0.5 * u) * (1.0 - t * t) * (scale + (3 * 0.044715 * scale) * square)
        slope_ref[spans[n], cols] = slope.astype(bf16)

    behind(up_start, up_end)
    ffns = [dot(act_ref[rows, :], wd_ref[...]) for rows in spans]
    dres2s, dffns = [], []
    for n, rows in enumerate(spans):
        n2, rstd2 = norm(hids[n] + ffns[n] + bd)
        out_ref[rows, :] = (n2 * g2 + s2).astype(bf16)
        og = og_ref[rows, :].astype(f32)
        gvec_ref[4:5, :] += rowsum(og * n2)
        gvec_ref[5:6, :] += rowsum(og)
        dres2 = norm_back(og * g2, n2, rstd2)
        dffn = dres2.astype(bf16)
        dffn_ref[rows, :] = dffn
        gvec_ref[3:4, :] += rowsum(dffn.astype(f32))
        dres2s.append(dres2)
        dffns.append(dffn)

    if direct:
        remote, own, swap, keep = transfers(step)

        @pl.when(me.stays)
        def _():
            keep.start()

        @pl.when(jnp.logical_not(me.stays))
        def _():
            swap.start()

    def down_start(n, cols):
        return dot_nt(dffns[n], wd_ref[cols, :])

    def down_end(n, cols, dact):
        dpre = (dact * slope_ref[spans[n], cols].astype(f32)).astype(bf16)
        dpre_ref[spans[n], cols] = dpre
        gbu_ref[0:1, cols] += rowsum(dpre.astype(f32))

    behind(down_start, down_end)
    dhs = [dres2 + dot_nt(dpre_ref[rows, :], wu_ref[...]) for rows, dres2 in zip(spans, dres2s)]
    dmixes = []
    for rows, dh, (n1, rstd1) in zip(spans, dhs, norms):
        gvec_ref[1:2, :] += rowsum(dh * n1)
        gvec_ref[2:3, :] += rowsum(dh)
        dres1 = norm_back(dh * g1, n1, rstd1)
        dres_ref[rows, :] = dres1
        dproj = dres1.astype(bf16)
        dproj_ref[rows, :] = dproj
        gvec_ref[0:1, :] += rowsum(dproj.astype(f32))
        dmixes.append(dot_nt(dproj, wop_ref[...]))
    for n, dmix in enumerate(dmixes):
        for g in range(groups):
            dctx_ref[g, n, :ROWS, :] = dmix[:, g * LANES : (g + 1) * LANES].astype(bf16)
        for g in range(0, groups, 2):
            to = groups * LANES + g * HEAD_DIM
            for m in range(ROWS // (2 * BLOCK)):
                at = ROWS + m * BLOCK
                r = 2 * m * BLOCK
                even = dmix[r : r + BLOCK, to : to + LANES]
                odd = dmix[r + BLOCK : r + 2 * BLOCK, to : to + LANES]
                a = jnp.where(low, even, pltpu.roll(odd, HEAD_DIM, 1))
                b = jnp.where(low, pltpu.roll(even, HEAD_DIM, 1), odd)
                dctx_ref[g, n, at : at + BLOCK, :] = a.astype(bf16)
                dctx_ref[g + 1, n, at : at + BLOCK, :] = b.astype(bf16)

    if direct:
        for copy in remote:
            copy.start()
        own.start()

        @pl.when(step == pl.num_programs(0) - 1)
        def _():
            for t in range(dctx_stage.shape[0]):
                remote, own, swap, keep = transfers(t)
                for copy in remote:
                    copy.wait()
                own.wait()

                @pl.when(me.stays)
                def _():
                    keep.wait()

                @pl.when(jnp.logical_not(me.stays))
                def _():
                    swap.wait()


def chain(ctx, tok, og, wo, wu, wd, vec, bu, direct):
    rows, width = tok.shape
    hidden = wu.shape[1]
    groups = ctx.shape[0]
    once = pl.Buffered(1)

    def tiled(cols):
        return pl.BlockSpec((SUBS * ROWS, cols), lambda t: (t, 0))

    def fixed(shape):
        return pl.BlockSpec(shape, lambda t: (0, 0), pipeline_mode=once)

    packed = pl.BlockSpec((groups, SUBS) + ctx.shape[2:], lambda t: (0, t, 0, 0))
    shape = jax.ShapeDtypeStruct
    steps = rows // (SUBS * ROWS)
    hbm = pl.BlockSpec(memory_space=pltpu.HBM)
    scratch = [pltpu.VMEM((SUBS * ROWS, hidden), bf16), pltpu.VMEM(wo.shape, bf16)]
    params = pltpu.CompilerParams(vmem_limit_bytes=VMEM_BYTES)
    out_shape = (rows, width)
    if direct:
        out_shape = (steps, SUBS * ROWS, width)
        scratch += [
            pltpu.VMEM(out_shape, bf16),
            pltpu.VMEM((steps, groups, SUBS) + ctx.shape[2:], bf16),
            pltpu.SemaphoreType.DMA((steps, 4)),
            pltpu.SemaphoreType.DMA((steps, 4)),
            pltpu.SemaphoreType.DMA((steps, 2)),
        ]
        params = pltpu.CompilerParams(
            vmem_limit_bytes=VMEM_BYTES, collective_id=2, has_side_effects=True
        )
    return pl.pallas_call(
        partial(chain_kernel, groups, direct),
        grid=(steps,),
        out_shape=(
            shape(out_shape, bf16),
            shape((rows, width), f32),
            shape(ctx.shape, bf16),
            shape((rows, width), bf16),
            shape((rows, width), bf16),
            shape((rows, hidden), bf16),
            shape((rows, hidden), bf16),
            shape((rows, width), bf16),
            shape((rows, width), bf16),
            shape((8, width), f32),
            shape((8, hidden), f32),
        ),
        in_specs=[
            packed,
            tiled(width),
            tiled(width),
            fixed(wo.shape),
            fixed(wu.shape),
            fixed(wd.shape),
            fixed(vec.shape),
            fixed(bu.shape),
        ],
        out_specs=(
            hbm if direct else tiled(width),
            tiled(width),
            hbm if direct else packed,
            tiled(width),
            tiled(width),
            tiled(hidden),
            tiled(hidden),
            tiled(width),
            tiled(width),
            pl.BlockSpec((8, width), lambda t: (0, 0)),
            pl.BlockSpec((8, hidden), lambda t: (0, 0)),
        ),
        scratch_shapes=scratch,
        compiler_params=params,
        name="chain",
    )(ctx, tok, og, wo, wu, wd, vec, bu)


def gather_item(me, copies, shard, full, cols, x_first):
    y, x, core, zh, zl = me.y, me.x, me.core, me.zh, me.zl
    mine = shard.at[:, cols]
    own = copies.local(mine, full.at[y, x, core, me.z, :, cols])
    spot = full.at[y, x, core, me.z, :, cols]
    along = [copies.remote(mine, spot, other) for other in (me.by_zl, me.by_mid, me.by_zh)]
    own.start()
    for copy in along:
        copy.start()
    yield 1
    own.wait()
    for copy in along:
        copy.wait()
    line = full.at[y, x, core, :, :, cols]
    near = copies.remote(line, line, me.by_x if x_first else me.by_y)
    near.start()
    across = [copies.remote(line, line, me.by_core)]
    across[0].start()
    yield 1
    near.wait()
    if x_first:
        block = full.at[y, :, core, :, :, cols]
        got = full.at[y, 1 - x, core, :, :, cols]
        rest = full.at[1 - y, :, core, :, :, cols]
    else:
        block = full.at[:, x, core, :, :, cols]
        got = full.at[1 - y, x, core, :, :, cols]
        rest = full.at[:, 1 - x, core, :, :, cols]
    far = copies.remote(block, block, me.by_y if x_first else me.by_x)
    far.start()
    across.append(copies.remote(got, got, me.by_core))
    across[1].start()
    yield 1
    far.wait()
    across.append(copies.remote(rest, rest, me.by_core))
    across[2].start()
    yield 1
    for copy in across:
        copy.wait()


def tokens_item(me, copies, tok, x_all, piece):
    place = me.core * 2 + me.zl
    there = (1 - me.core) * 2 + me.zl
    held = x_all.at[place, piece]
    out = copies.remote(tok.at[piece], x_all.at[there, piece], me.by_swap)
    keep = copies.local(tok.at[piece], held)
    along = copies.remote(held, held, me.by_zl)
    over = copies.remote(held, held, me.by_core)

    @pl.when(me.stays)
    def _():
        keep.start()

    @pl.when(jnp.logical_not(me.stays))
    def _():
        out.start()

    yield 1

    @pl.when(me.stays)
    def _():
        keep.wait()
        along.start()
        over.start()

    yield 1

    @pl.when(jnp.logical_not(me.stays))
    def _():
        out.wait()
        along.start()
        over.start()

    yield 1
    along.wait()
    came = x_all.at[me.core * 2 + 1 - me.zl, piece]
    onto = copies.remote(came, came, me.by_core)
    onto.start()
    yield 1
    over.wait()
    onto.wait()


def exchange_item(me, copies, src, dst):
    out = copies.remote(src, dst, me.by_swap)
    keep = copies.local(src, dst)

    @pl.when(me.stays)
    def _():
        keep.start()

    @pl.when(jnp.logical_not(me.stays))
    def _():
        out.start()

    yield 1

    @pl.when(me.stays)
    def _():
        keep.wait()

    @pl.when(jnp.logical_not(me.stays))
    def _():
        out.wait()


PIECES = 4


def weight_item(me, copies, src, parts, whole, bias):
    y, x, core, zh, zl = me.y, me.x, me.core, me.zh, me.zl
    place = core * 2 + zl
    keep = copies.local(src.at[place], parts.at[place])
    moves = [
        copies.remote(src.at[core * 2 + 1 - zl], parts.at[place], me.by_zl),
        copies.remote(src.at[(1 - core) * 2 + zl], parts.at[place], me.by_core),
        copies.remote(src.at[(1 - core) * 2 + 1 - zl], parts.at[place], me.by_both),
    ]
    keep.start()
    for move in moves:
        move.start()
    yield 1
    keep.wait()
    for move in moves:
        move.wait()
    own = whole.shape[4] // 2
    for b in range(2):
        both = jnp.concatenate([parts[2 * b, :own, :], parts[2 * b + 1, :own, :]], axis=0)
        whole[y, x, b, zh] = both.astype(bf16)
    tail = pl.ds(own, 8)
    bias[y, x, zh] = parts[0, tail, :] + parts[1, tail, :] + parts[2, tail, :] + parts[3, tail, :]
    for spot, bias_spot, other in (
        (whole.at[y, x, :, zh], bias.at[y, x, zh], me.by_zh),
        (whole.at[y, x], bias.at[y, x], me.by_x),
        (whole.at[y], bias.at[y], me.by_y),
    ):
        moves = [copies.remote(spot, spot, other), copies.remote(bias_spot, bias_spot, other)]
        for move in moves:
            move.start()
        yield 1
        for move in moves:
            move.wait()


def finish(*generators):
    for phases in generators:
        for _ in phases:
            pass


def front_kernel(heads, randoms, *refs):
    rand_ref, tok, og, wq, w_out, up, down, small = refs[:8]
    x_hbm, tok_own, og_own, w_own, qkv_hbm, res_hbm, ctx_all, out_all, up_all, down_all, small_all = refs[8:19]
    x_all, parts, whole, bias, qkv_ref, res_ref, ends_ref, ctx_ref = refs[19:27]
    me = Where()
    me.greet()
    copies = Copies(*refs[27:])
    blocks = qkv_ref.shape[0]
    length = blocks * BLOCK
    quarter = length // 4
    core, zl = me.core, me.zl
    place = core * 2 + zl
    near = core * 2 + 1 - zl
    beside = (1 - core) * 2 + zl
    across = (1 - core) * 2 + 1 - zl

    weights = weight_item(me, copies, wq, parts, whole, bias)
    tokens = [tokens_item(me, copies, tok, x_all, piece) for piece in range(PIECES)]
    smalls = gather_item(me, copies, small, small_all, slice(0, LANES), True)
    turn = 0

    def gathers(*arrays):
        nonlocal turn
        made = []
        for shard, full, splits in arrays:
            width = shard.shape[1] // splits
            for n in range(splits):
                cols = slice(n * width, (n + 1) * width)
                made.append(gather_item(me, copies, shard, full, cols, turn % 2 == 0))
                turn += 1
        return made

    def advance(group):
        group[:] = [phases for phases in group if next(phases, None) is not None]

    early = gathers((up, up_all, 2))
    late = gathers((down, down_all, 2), (w_out, out_all, 2))
    last = [exchange_item(me, copies, og.at[n], og_own.at[n]) for n in range(PIECES)]
    idle = [smalls]
    outs = []

    def write(src, dst):
        copy = copies.local(src, dst)
        copy.start()
        outs.append(copy)

    def project(where):
        bias_row = jnp.sum(bias[...].reshape(-1, 8, bias.shape[-1]), axis=0)[0:1]
        matrix = whole[...].reshape(-1, whole.shape[-1])
        for piece in range(PIECES):
            raw = dot(x_all[where, piece], matrix) + bias_row
            step = ROWS // BLOCK
            at = (where * PIECES + piece) * step
            qkv_ref[pl.ds(at, step)] = raw.astype(bf16).reshape(step, BLOCK, raw.shape[1])

    def forward_tokens():
        for item in tokens:
            next(item)

    next(weights)
    advance(early)
    next(weights)
    forward_tokens()
    forward_tokens()
    next(weights)
    advance(idle)
    advance(early)
    next(weights)
    advance(idle)
    forward_tokens()
    advance(late)
    finish(weights)
    advance(early)
    next(last[0])
    project(place)
    write(whole, w_own)
    write(x_all.at[place], tok_own)
    forward_tokens()
    advance(late)
    next(last[1])
    project(near)
    finish(*tokens)
    next(last[2])
    next(last[3])
    advance(early)
    project(beside)
    project(across)
    advance(idle)
    write(x_all, x_hbm)
    write(qkv_ref, qkv_hbm)
    for h, both in enumerate(global_blocks(qkv_ref, heads, length)):
        ends_ref[h] = both
    advance(late)
    advance(early)
    advance(idle)

    def middle(t, carry):
        middle_blocks(qkv_ref, rand_ref, res_ref, t * PAIR, heads, randoms, blocks)
        return carry

    sends = []
    turns = quarter // BLOCK // PAIR
    for where, other in ((across, me.by_both), (near, me.by_zl), (beside, me.by_core), (place, None)):
        lax.fori_loop(where * turns, (where + 1) * turns, middle, 0)

        @pl.when(where == 0)
        def _():
            for h in range(heads):
                res_ref[h, 0:BLOCK, :] = ends_ref[h, 0:BLOCK, :]

        @pl.when(where == 3)
        def _():
            for h in range(heads):
                res_ref[h, length - BLOCK : length, :] = ends_ref[h, BLOCK : 2 * BLOCK, :]

        for piece in range(PIECES):
            pack_rows(res_ref, ctx_ref, where * quarter + piece * ROWS, where, piece)
        rows = rows_at(where * quarter, quarter)
        write(res_ref.at[:, rows], res_hbm.at[:, rows])
        if other is None:
            write(ctx_ref.at[where], ctx_all.at[place])
        else:
            send = copies.remote(ctx_ref.at[where], ctx_all.at[place], other)
            send.start()
            sends.append(send)
        advance(late if where is near or where is place else idle)
    finish(*early, *late, *last, *idle)
    for copy in sends + outs:
        copy.wait()


def front(rand, tok, og, wq, mats, small, heads):
    rows, width = tok.shape
    members = 4
    length = rows * members
    randoms = rand.size // (heads * (length // BLOCK - 2))
    hbm = pl.BlockSpec(memory_space=pltpu.HBM)
    shape = jax.ShapeDtypeStruct
    tok = tok.reshape(PIECES, rows // PIECES, width)
    og = og.reshape(tok.shape)
    cols = heads * SLOT
    own = mats[0].shape[0]
    packed = (members, rows // ROWS, ROWS * 3 // 2, LANES)
    outs = [
        shape((members,) + tok.shape, bf16),
        shape(tok.shape, bf16),
        shape(og.shape, bf16),
        shape((2, 2, 2, 2, 2 * own, cols), bf16),
        shape((length // BLOCK, BLOCK, cols), bf16),
        shape((heads, length, LANES), f32),
        shape(packed, bf16),
    ]
    outs += [shape((2, 2, 2, 4) + a.shape, bf16) for a in (*mats, small)]
    return pl.pallas_call(
        partial(front_kernel, heads, randoms),
        out_shape=tuple(outs),
        in_specs=[pl.BlockSpec(memory_space=pltpu.SMEM)] + [hbm] * 7,
        out_specs=(hbm,) * 11,
        scratch_shapes=[
            pltpu.VMEM((members,) + tok.shape, bf16),
            pltpu.VMEM(wq.shape, f32),
            pltpu.VMEM((2, 2, 2, 2, 2 * own, cols), bf16),
            pltpu.VMEM((2, 2, 2, 8, cols), f32),
            pltpu.VMEM((length // BLOCK, BLOCK, cols), bf16),
            pltpu.VMEM((heads, length, LANES), f32),
            pltpu.VMEM((heads, 2 * BLOCK, LANES), f32),
            pltpu.VMEM(packed, bf16),
            pltpu.SemaphoreType.DMA((112,)),
            pltpu.SemaphoreType.DMA((112,)),
            pltpu.SemaphoreType.DMA((32,)),
        ],
        compiler_params=pltpu.CompilerParams(
            collective_id=0, has_side_effects=True, vmem_limit_bytes=VMEM_BYTES
        ),
        name="front",
    )(rand, tok, og, wq, *mats, small)


def add_rows(dst, a, b, rows):
    step = next(n for n in (48, 32, 24, 16, 8) if rows % n == 0)

    def body(t, carry):
        at = rows_at(t * step, step)
        dst[at, :] = (a[at, :].astype(f32) + b[at, :].astype(f32)).astype(dst.dtype)
        return carry

    lax.fori_loop(0, rows // step, body, 0)


def scatter_item(me, copies, src, cols, acc, from_core, from_first, from_second, slabs, from_line, out, x_first):
    y, x, core, zh, zl = me.y, me.x, me.core, me.zh, me.zl
    rows = acc.shape[2]
    own = None
    if cols is not None:
        own = copies.local(src.at[:, :, core, :, cols], acc)
        own.start()
        src = src.at[:, :, 1 - core, :, cols]
    over = copies.remote(src, from_core, me.by_core)
    over.start()
    yield 1
    if own is not None:
        own.wait()
    over.wait()
    for a in range(2):
        for b in range(2):
            add_rows(acc.at[a, b], acc.at[a, b], from_core.at[a, b], rows)
    if x_first:
        first = copies.remote(acc.at[:, 1 - x], from_first, me.by_x)
    else:
        first = copies.remote(acc.at[1 - y], from_first, me.by_y)
    first.start()
    yield 1
    first.wait()
    for a in range(2):
        block = acc.at[a, x] if x_first else acc.at[y, a]
        add_rows(block, block, from_first.at[a], rows)
    if x_first:
        second = copies.remote(acc.at[1 - y, x], from_second, me.by_y)
    else:
        second = copies.remote(acc.at[y, 1 - x], from_second, me.by_x)
    second.start()
    yield 1
    second.wait()
    rest = rows // 4
    summed = acc[y, x].astype(f32) + from_second[...].astype(f32)
    for z in range(4):
        slabs[z] = summed[z * rest : (z + 1) * rest].astype(slabs.dtype)
    moves = [
        copies.remote(slabs.at[(1 - zh) * 2 + zl], from_line.at[0], me.by_zh),
        copies.remote(slabs.at[(1 - zh) * 2 + 1 - zl], from_line.at[1], me.by_mid),
        copies.remote(slabs.at[zh * 2 + 1 - zl], from_line.at[2], me.by_zl),
    ]
    for move in moves:
        move.start()
    yield 1
    for move in moves:
        move.wait()
    near = slabs[me.z].astype(f32) + from_line[2].astype(f32)
    out[...] = near + (from_line[0].astype(f32) + from_line[1].astype(f32))


def scatter_buffers(rows, cols, kind):
    return [
        pltpu.VMEM((2, 2, rows, cols), kind),
        pltpu.VMEM((2, 2, rows, cols), kind),
        pltpu.VMEM((2, rows, cols), kind),
        pltpu.VMEM((rows, cols), kind),
        pltpu.VMEM((4, rows // 4, cols), kind),
        pltpu.VMEM((3, rows // 4, cols), kind),
    ]


def own_columns_item(me, copies, acc, from_x, from_y, from_zh, part, blocks, out):
    y, x, core, zh, zl = me.y, me.x, me.core, me.zh, me.zl
    rows = acc.shape[4]
    first = copies.remote(acc.at[1 - x], from_x, me.by_x)
    first.start()
    yield 1
    first.wait()
    for a in range(2):
        for b in range(2):
            for c in range(2):
                add_rows(acc.at[x, a, b, c], acc.at[x, a, b, c], from_x.at[a, b, c], rows)
    acc = acc.at[x]
    second = copies.remote(acc.at[1 - y], from_y, me.by_y)
    second.start()
    yield 1
    second.wait()
    for b in range(2):
        for c in range(2):
            block = acc.at[y, b, c]
            add_rows(block, block, from_y.at[b, c], rows)
    third = copies.remote(acc.at[y, :, 1 - zh], from_zh, me.by_zh)
    third.start()
    yield 1
    third.wait()
    half = rows // 2
    for b in range(2):
        add_rows(part.at[b], acc.at[y, b, zh], from_zh.at[b], rows)
    place = core * 2 + zl
    mine = rows_at(zl * half, half)
    other = rows_at((1 - zl) * half, half)
    keep = copies.local(part.at[core, mine], blocks.at[place])
    keep.start()
    moves = [
        copies.remote(part.at[core, other], blocks.at[place], me.by_zl),
        copies.remote(part.at[1 - core, mine], blocks.at[place], me.by_core),
        copies.remote(part.at[1 - core, other], blocks.at[place], me.by_both),
    ]
    for move in moves:
        move.start()
    yield 1
    keep.wait()
    for move in moves:
        move.wait()
    heads = blocks.shape[2] // SLOT
    low = lax.broadcasted_iota(jnp.int32, (blocks.shape[1], LANES), 1) < HEAD_DIM
    for kind in range(3):
        for n in range(0, 4 * heads, 2):
            pair = []
            for head in (n, n + 1):
                at = head % heads * SLOT + (0 if kind == 0 else LANES)
                pair.append(blocks[head // heads, :, at : at + LANES])
            if kind == 2:
                tile = jnp.where(low, pltpu.roll(pair[0], HEAD_DIM, 1), pair[1])
            else:
                tile = jnp.where(low, pair[0], pltpu.roll(pair[1], HEAD_DIM, 1))
            if kind == 0:
                tile = tile * HEAD_DIM**-0.5
            to = (kind * 4 * heads + n) * HEAD_DIM
            out[:, to : to + LANES] = tile


def input_grad_item(me, copies, draw, w, dres, piece, stage, from_core, from_zl, res, out):
    core, zl = me.core, me.zl
    more = copies.local(dres.at[piece], res)
    more.start()
    for b in range(2):
        stage[b] = dot_nt(draw[(1 - core) * 2 + b, piece], w[...]).astype(bf16)
    over = copies.remote(stage, from_core, me.by_core)
    over.start()
    yield 1
    mine = dot_nt(draw[core * 2 + 1 - zl, piece], w[...])
    over.wait()
    far, send = stage.at[0], stage.at[1]
    far[...] = (mine + from_core[1 - zl].astype(f32)).astype(bf16)
    along = copies.remote(far, from_zl, me.by_zl)
    along.start()
    mine = dot_nt(draw[core * 2 + zl, piece], w[...])
    more.wait()
    res[...] = res[...] + (mine + from_core[zl].astype(f32))
    yield 1
    along.wait()
    send[...] = (res[...] + from_zl[...].astype(f32)).astype(bf16)
    yield from exchange_item(me, copies, send, out.at[piece])


def scatter_kernel(*refs):
    act, dffn, hid, dpre, proj, vecs, draw, x_hbm, w, dres = refs[:10]
    outs = refs[10:16]
    sems, scratch = refs[16:19], list(refs[19:])
    me = Where()
    me.greet()
    copies = Copies(*sems)

    def take(n):
        got = scratch[:n]
        del scratch[:n]
        return got

    def advance(group):
        group[:] = [phases for phases in group if next(phases, None) is not None]

    pieces = [
        input_grad_item(me, copies, draw, w, dres, piece, *take(4), outs[5]) for piece in range(PIECES)
    ]
    x_all, total, acc, *buffers = take(8)
    columns = [own_columns_item(me, copies, acc, *buffers, outs[4])]
    halves, quarters, stage_down, stage_up = take(4)
    first, second = [], []
    for n in range(2):
        cols = outs[0].shape[1] // 2
        part = outs[0].at[:, n * cols : (n + 1) * cols]
        first.append(
            scatter_item(me, copies, stage_down.at[n], None, halves.at[n], *take(5), part, n % 2 == 0)
        )
    for n in range(4):
        cols = outs[1].shape[1] // 4
        part = outs[1].at[:, n * cols : (n + 1) * cols]
        second.append(
            scatter_item(me, copies, stage_up.at[n], None, quarters.at[n], *take(5), part, n % 2 == 0)
        )
    for src, out, group in ((proj, outs[2], first), (vecs, outs[3], second)):
        whole = slice(0, src.shape[4])
        group.append(scatter_item(me, copies, src, whole, *take(6), out, True))

    def fetch(src):
        wide = x_all.shape[3]
        got = [copies.local(src.at[:, :, c * wide : (c + 1) * wide], x_all.at[c]) for c in range(4)]
        for copy in got:
            copy.start()
        return got

    def flat(value):
        return value.reshape(-1, value.shape[-1])

    def down_grad(c, carry):
        g = dot_tn(flat(x_all[c]), flat(dffn[...])).astype(bf16)
        rows, cols = g.shape[0] // 2, g.shape[1] // 2
        for n in range(2):
            low, high = g[:rows, n * cols : (n + 1) * cols], g[rows:, n * cols : (n + 1) * cols]
            halves[n, c // 2, c % 2] = jnp.where(me.core == 0, low, high)
            stage_down[n, c // 2, c % 2] = jnp.where(me.core == 0, high, low)
        return carry

    def up_grad(c, carry):
        g = dot_tn(flat(hid[...]), flat(x_all[c])).astype(bf16)
        rows = g.shape[0] // 8
        for k in range(4):
            low, high = g[2 * k * rows : (2 * k + 1) * rows], g[(2 * k + 1) * rows : (2 * k + 2) * rows]
            quarters[c, k // 2, k % 2] = jnp.where(me.core == 0, low, high)
            stage_up[c, k // 2, k % 2] = jnp.where(me.core == 0, high, low)
        return carry

    def weight_grad(t, carry):
        place, piece = t // PIECES, t % PIECES
        total[...] += dot_tn(x_all[place, piece], draw[place, piece])
        return carry

    got = fetch(act)
    next(pieces[0])
    next(pieces[1])
    next(pieces[0])
    next(pieces[1])
    for copy in got:
        copy.wait()
    lax.fori_loop(0, 4, down_grad, 0)
    got = fetch(dpre)
    advance(first)
    next(pieces[2])
    next(pieces[3])
    next(pieces[2])
    next(pieces[3])
    for copy in got:
        copy.wait()
    advance(first)
    lax.fori_loop(0, 4, up_grad, 0)
    got = copies.local(x_hbm, x_all)
    got.start()
    advance(second)
    next(pieces[0])
    total[...] = jnp.zeros_like(total)
    got.wait()
    advance(second)
    next(pieces[1])
    lax.fori_loop(0, 2 * PIECES, weight_grad, 0)
    next(pieces[2])
    advance(first)
    lax.fori_loop(2 * PIECES, 4 * PIECES, weight_grad, 0)
    laid = total[...].reshape((2, 2) + acc.shape[2:])
    for a in range(2):
        for b in range(2):
            acc[b, a] = laid[a, b].astype(bf16)
    advance(columns)
    next(pieces[3])
    advance(first)
    advance(second)
    while pieces or columns or first or second:
        advance(columns)
        advance(second)
        advance(first)
        if not second:
            advance(pieces)


def scatter(act, dffn, hid, dpre, proj, vecs, draw, x_all, w, dres, own):
    hbm = pl.BlockSpec(memory_space=pltpu.HBM)
    vmem = pl.BlockSpec(memory_space=pltpu.VMEM)
    shape = jax.ShapeDtypeStruct
    hidden = act.shape[-1]
    outs = [shape((hidden // 32, w.shape[0]), f32), shape((own, hidden), f32)]
    outs += [shape((a.shape[3] // 4, a.shape[4]), f32) for a in (proj, vecs)]
    width, cols = w.shape
    rows = 2 * own
    outs.append(shape((own, 3 * cols), f32))
    outs.append(shape(dres.shape, bf16))
    buffers = []
    for _ in range(PIECES):
        tile = dres.shape[1:]
        buffers += [
            pltpu.VMEM((2,) + tile, bf16),
            pltpu.VMEM((2,) + tile, bf16),
            pltpu.VMEM(tile, bf16),
            pltpu.VMEM(tile, f32),
        ]
    buffers += [
        pltpu.VMEM(x_all.shape, bf16),
        pltpu.VMEM((width, cols), f32),
        pltpu.VMEM((2, 2, 2, 2, rows, cols), bf16),
        pltpu.VMEM((2, 2, 2, rows, cols), bf16),
        pltpu.VMEM((2, 2, rows, cols), bf16),
        pltpu.VMEM((2, rows, cols), bf16),
        pltpu.VMEM((2, rows, cols), f32),
        pltpu.VMEM((4, own, cols), f32),
    ]
    down = (hidden // 8, width // 2)
    up = (4 * own, hidden // 4)
    buffers += [
        pltpu.VMEM((2, 2, 2) + down, bf16),
        pltpu.VMEM((4, 2, 2) + up, bf16),
        pltpu.VMEM((2, 2, 2) + down, bf16),
        pltpu.VMEM((4, 2, 2) + up, bf16),
    ]
    for tile in [down] * 2 + [up] * 4:
        buffers += scatter_buffers(*tile, bf16)[1:]
    for a in (proj, vecs):
        buffers += scatter_buffers(*a.shape[3:], a.dtype)
    return pl.pallas_call(
        scatter_kernel,
        out_shape=tuple(outs),
        in_specs=[hbm, vmem, vmem, hbm, hbm, hbm, vmem, hbm, vmem, hbm],
        out_specs=(vmem,) * 5 + (hbm,),
        scratch_shapes=[
            pltpu.SemaphoreType.DMA((80,)),
            pltpu.SemaphoreType.DMA((80,)),
            pltpu.SemaphoreType.DMA((32,)),
        ]
        + buffers,
        compiler_params=pltpu.CompilerParams(
            collective_id=1, has_side_effects=True, vmem_limit_bytes=VMEM_BYTES
        ),
        name="scatter",
    )(act, dffn, hid, dpre, proj, vecs, draw, x_all, w, dres)


def per_device(
    tokens,
    qkv_weight,
    query_value_bias,
    out_weight,
    out_bias,
    norm1_gain,
    norm1_bias,
    up_weight,
    up_bias,
    down_weight,
    down_bias,
    norm2_gain,
    norm2_bias,
    rand_blocks,
    out_grad,
):
    members = lax.axis_size(GROUP)
    devices = lax.axis_size(ALL)
    swap = [(0, 0), (1, 2), (2, 1), (3, 3)]

    def move(a):
        return lax.ppermute(a, ("core", "zh"), swap)

    rand = move(rand_blocks[0])
    heads = rand.shape[0]
    rows, width = tokens.shape[1:]
    cols = heads * HEAD_DIM
    group = lax.axis_index(GROUP)
    own = width // devices
    rand_flat = rand.reshape(-1)

    def lay_out(a):
        a = a.reshape(a.shape[:-2] + (3, heads, HEAD_DIM))
        q, k, v = a[..., 0, :, :], a[..., 1, :, :], a[..., 2, :, :]
        q = q * jnp.asarray(HEAD_DIM**-0.5, a.dtype)
        laid = jnp.stack([q, jnp.zeros_like(q), k, v], axis=-2)
        return laid.reshape(laid.shape[:-3] + (heads * SLOT,))

    bias_part = jnp.stack([query_value_bias[0], jnp.zeros((own,), bf16), query_value_bias[1]])
    small = [out_bias, norm1_gain, norm1_bias, down_bias, norm2_gain, norm2_bias, up_bias]
    small = jnp.concatenate(small)
    direct = lax.axis_size("c") == 4 and members == 4 and own % 8 == 0
    if direct:
        count = small.shape[0]
        padded = jnp.pad(small, (0, 16 * LANES - count)).reshape(16, LANES)
        spread = lax.dynamic_update_slice(
            jnp.zeros((3, width), f32), bias_part.astype(f32), (0, lax.axis_index(ALL) * own)
        )
        spread = lay_out(jnp.transpose(spread.reshape(3, members, cols), (1, 0, 2)))
        wq = jnp.transpose(qkv_weight.astype(f32).reshape(own, 3, members, cols), (2, 0, 1, 3))
        wq = jnp.concatenate([lay_out(wq), spread[:, None], jnp.zeros((members, 7, heads * SLOT), f32)], axis=1)
        mats = (out_weight, up_weight, down_weight)
        x, tok, og, w_own, qkv, res, ctx, *full = front(
            rand_flat, tokens[0], out_grad[0], wq, mats, padded, heads
        )
        x, tok, og = (a.reshape(-1, width) for a in (x, tok, og))
        w_own = w_own.reshape(width, -1)
        w_out, w_up, w_down = (a.reshape(-1, a.shape[-1]) for a in full[:3])
        small = full[3].reshape(devices, -1)[:, :count].astype(f32)
    else:
        tok = move(tokens[0])
        og = move(out_grad[0])
        x = lax.all_gather(tok, GROUP, axis=0, tiled=True)
        mats = (qkv_weight, out_weight, up_weight, down_weight)
        w_qkv, w_out, w_up, w_down = (lax.all_gather(a, ALL, axis=0, tiled=True) for a in mats)
        small = lax.all_gather(small, ALL, axis=0).astype(f32)
        w_own = lax.dynamic_slice_in_dim(
            w_qkv.reshape(width, 3, members, cols), group, 1, axis=2
        ).reshape(width, 3, cols)
        w_own = lay_out(w_own)
        bias3 = lax.all_gather(bias_part, ALL, axis=1, tiled=True).astype(f32).reshape(3, members, cols)
        b_own = lay_out(lax.dynamic_slice_in_dim(bias3, group, 1, axis=1).reshape(1, 3, cols))
        qkv, res, ctx_send = attend(rand_flat, x, w_own, b_own, members, heads)
        ctx = lax.all_to_all(ctx_send, GROUP, split_axis=0, concat_axis=0, tiled=True)
    vecs = jnp.transpose(small[:, : 6 * own].reshape(devices, 6, own), (1, 0, 2)).reshape(6, width)
    bias_up = small[:, 6 * own :].reshape(1, -1)
    chain_vecs = jnp.concatenate([vecs, jnp.zeros((2, width), f32)], axis=0)
    out, dres1, dctx, mix, hid, act, dpre, dffn, dproj, gvec, gbu = chain(
        ctx, tok, og, w_out, w_up, w_down, chain_vecs, bias_up, direct
    )
    if direct:
        out = out.reshape(rows, width)
    else:
        dctx = lax.all_to_all(dctx, GROUP, split_axis=0, concat_axis=0, tiled=True)
        out = move(out)

    g_mix = dot_tn(mix, dproj).astype(bf16)
    pairs = g_mix[: members * LANES].reshape(members, LANES, width)
    thirds = g_mix[members * LANES :].reshape(members, HEAD_DIM, width)
    g_out = jnp.concatenate([pairs, thirds], axis=1).reshape(width, width)

    draw, sums = attend_back(rand_flat, qkv, res, dctx, heads)

    def strip(a):
        a = a.reshape(a.shape[:-1] + (heads, 4, HEAD_DIM))
        q, k, v = a[..., 0, :] * (HEAD_DIM**-0.5), a[..., 2, :], a[..., 3, :]
        return jnp.stack([q, k, v], axis=-3).reshape(a.shape[:-3] + (3, cols))

    col_sums = strip(sums[0:1])[0]
    pair = jnp.stack([col_sums[0], col_sums[2]]).reshape(2, 1, cols)
    mine = (jnp.arange(members) == group)[None, :, None]
    pair = jnp.where(mine, pair, 0.0).reshape(2, width)
    vec_grads = jnp.concatenate([pair, gvec[0:6]], axis=0).reshape(8, devices, own)
    vec_grads = jnp.transpose(vec_grads, (1, 0, 2)).reshape(devices, 8 * own)
    vec_grads = jnp.concatenate([vec_grads, gbu[0].reshape(devices, -1)], axis=1)
    count = vec_grads.shape[1]

    if direct:
        lines = 8
        padded = jnp.pad(vec_grads, ((0, 0), (0, lines * LANES - count)))
        g_down, g_up, g_out, vec_grads, g_qkv, input_grad = scatter(
            act.reshape(PIECES, -1, act.shape[1]),
            dffn.reshape(PIECES, -1, width),
            hid.reshape(PIECES, -1, width),
            dpre.reshape(PIECES, -1, dpre.shape[1]),
            g_out.reshape(2, 2, 2, -1, width),
            padded.reshape(2, 2, 2, 4 * lines, LANES),
            draw.reshape(members, PIECES, -1, draw.shape[1]),
            x.reshape(members, PIECES, -1, width),
            w_own,
            dres1.reshape(PIECES, -1, width),
            own,
        )
        vec_grads = vec_grads.reshape(-1)[:count]
        input_grad = input_grad.reshape(rows, width).astype(f32)
    else:

        def reduce(a):
            return lax.psum_scatter(a, ALL, scatter_dimension=0, tiled=True).astype(f32)

        g_down, g_up = reduce(dot_tn(act, dffn).astype(bf16)), reduce(dot_tn(hid, dpre).astype(bf16))
        g_out, vec_grads = reduce(g_out), reduce(vec_grads)[0]
        dx = dot_nt(draw, w_own).astype(bf16)
        dx = lax.psum_scatter(dx, GROUP, scatter_dimension=0, tiled=True)
        input_grad = move((dres1 + dx.astype(f32)).astype(bf16)).astype(f32)
        g_qkv = strip(dot_tn(x, draw)).reshape(-1, 2, 2, members // 2, own, 3 * cols)
        g_qkv = jnp.transpose(g_qkv, (0, 2, 1, 3, 4, 5)).reshape(-1, members, own, 3 * cols)
        g_qkv = g_qkv.reshape(-1, 3 * cols).astype(bf16)
        g_qkv = lax.psum_scatter(g_qkv, REST, scatter_dimension=0, tiled=True)
        g_qkv = g_qkv.reshape(members, own, 3 * cols)
        g_qkv = lax.all_to_all(g_qkv, GROUP, split_axis=0, concat_axis=0, tiled=True).astype(f32)
        g_qkv = jnp.transpose(g_qkv.reshape(members, own, 3, cols), (1, 2, 0, 3)).reshape(own, -1)
    v8 = vec_grads[: 8 * own].reshape(8, own)
    return (
        out[None],
        input_grad[None],
        g_qkv,
        v8[0:2],
        g_out,
        v8[2],
        v8[3],
        v8[4],
        g_up,
        vec_grads[8 * own :],
        g_down,
        v8[5],
        v8[6],
        v8[7],
    )


def solution(mesh):
    dp, sp = mesh.shape["dp"], mesh.shape["sp"]
    fine = Mesh(mesh.devices.reshape(dp // 2, 2, 2, sp // 2), ALL)
    dp, sp = ("c", "core"), ("zh", "zl")
    act = P(dp, sp, None)
    mat = P(ALL, None)
    pair = P(None, ALL)
    vec = P(ALL)
    rand = P(dp, sp, None, None)
    return jax.shard_map(
        per_device,
        mesh=fine,
        in_specs=(act, mat, pair, mat, vec, vec, vec, mat, vec, mat, vec, vec, vec, rand, act),
        out_specs=(act, act, mat, pair, mat, vec, vec, vec, mat, vec, mat, vec, vec, vec),
        check_vma=False,
    )
```
